32 devices in a mesh: seq: 4 (over z), expert: 4 (over y, core), rep: 2 (over x).
Axes of the slice: x: 2, y: 2, z: 4, core: 2. Of those that a mesh axis runs over, the one named last changes fastest.
Arguments:
- query_rows: bfloat16 [4, 1024, 512], P('expert', ('seq', 'rep')), may hold values from -150 to 150
- key_rows: bfloat16 [4, 1024, 512], P('expert', ('seq', 'rep')), may hold values from -150 to 150
- value_rows: bfloat16 [4, 1024, 512], P('expert', ('seq', 'rep')), may hold values from -6 to 6
- doc_lengths: int32 [4, 8], P('expert'), may hold values from 1 to 512, 1024 in all within a row
- residual: bfloat16 [4, 1024, 512], P('expert', ('seq', 'rep')), may hold values from -6 to 6
- out_proj: bfloat16 [512, 512], replicated, may hold values from -0.25 to 0.25
- router: bfloat16 [512, 4], replicated, may hold values from -0.5 to 0.5
- expert_choice: int32 [4, 1024, 1], P('expert', ('seq', 'rep')), may hold values from 0 to 3, as said below
- weight_in: bfloat16 [4, 512, 512], P('expert'), may hold values from -0.25 to 0.25
- weight_out: bfloat16 [4, 512, 512], P('expert'), may hold values from -0.5 to 0.5
- grad_out: bfloat16 [4, 1024, 512], P('expert', ('seq', 'rep')), may hold values from -6 to 6
Outputs:
- layer_out: bfloat16 [4, 1024, 512], P('expert', ('seq', 'rep'))
- grad_mixed: bfloat16 [4, 1024, 512], P('expert', ('seq', 'rep'))
- grad_weight_in: float32 [4, 512, 512], P('expert', ('seq', 'rep'))
- grad_weight_out: float32 [4, 512, 512], P('expert', ('seq', 'rep'))
The draws below stay inside these ranges and needn't reach their ends.
Inputs may be any that keep to these rules, and one draw needn't show every extreme that they name: `expert_choice`: A routing group is one index of seq and one of rep; each group has one hot expert, the same on all of the group's devices. Among one device's tokens, its group's hot expert is named between 49 and 64 times, exactly 64 times on some device and 48 + 1 times on some device; every other expert is named at most 48 times, and on every device some expert other than the hot one is named exactly 48 times. `doc_lengths`: each sequence's lengths sum to 1024; the longest is exactly half of 1024.
All inputs are finite; a program needn't handle non-finite values.
Results may differ from the reference program's by a relative error of at most 0.02.
Values may be sent and summed in bfloat16 or wider, within the bound.
No kernel may reach another device: no remote copies, remote signals or barrier semaphores. Data moves between devices by JAX's collectives and lax.ppermute only.
A program may use at most 64 MiB of HBM per device.

```python
import math
import jax
import jax.numpy as jnp
import numpy as np
from jax import lax

D = 512
H = 16
HD = 32
FF = 512
DOCS = 8
TOK_DEV = 128
SEQ_LEN = 1024
SEQS = 4
EXPERTS = 4
CAP = 48
HOT_CAP = 64
N_SEQ = 4
N_REP = 2


def paired_rows(key):
    query_key, key_key = jax.random.split(jax.random.fold_in(key, 17))
    queries = jnp.clip(jax.random.normal(query_key, (SEQS, SEQ_LEN, D), jnp.float32), -4.0, 4.0)
    keyed = jnp.clip(jax.random.normal(key_key, (SEQS, SEQ_LEN, D), jnp.float32), -4.0, 4.0)
    return (queries, keyed)


def draw_query_rows(key, part):
    return paired_rows(key)[0].astype(jnp.bfloat16)


def draw_key_rows(key, part):
    return paired_rows(key)[1].astype(jnp.bfloat16)


def routing_draw(key):
    base = jax.random.fold_in(key, 29)
    hot_key, count_key, block_key = jax.random.split(base, 3)
    groups = N_SEQ * N_REP
    blocks = SEQS * groups
    hot = jax.random.randint(hot_key, (N_SEQ, N_REP), 0, EXPERTS).astype(jnp.int32)
    hot_count = jax.random.randint(count_key, (blocks,), CAP + 1, HOT_CAP + 1).astype(jnp.int32)
    hot_count = hot_count.at[0].set(CAP + 1).at[1].set(HOT_CAP)
    block_hot = jnp.tile(hot.reshape(groups), SEQS)

    def one_block(single_key, hot_id, count):
        order_key, spot_key = jax.random.split(single_key)
        shuffled = jax.random.permutation(order_key, EXPERTS).astype(jnp.int32)
        ranking = jnp.where(shuffled == hot_id, EXPERTS, jnp.arange(EXPERTS, dtype=jnp.int32))
        others = shuffled[jnp.argsort(ranking)]
        places = jnp.arange(TOK_DEV, dtype=jnp.int32)
        cold_place = places - count
        cycled = 1 + (cold_place - CAP) % (EXPERTS - 2)
        pick = jnp.where(places < count, EXPERTS - 1, jnp.where(cold_place < CAP, 0, cycled))
        named = others[pick]
        spots = jax.random.permutation(spot_key, TOK_DEV)
        return named[spots].astype(jnp.int32)
    routed = jax.vmap(one_block)(jax.random.split(block_key, blocks), block_hot, hot_count)
    return routed.reshape(SEQS, SEQ_LEN, 1)


def draw_expert_choice(key, part):
    return routing_draw(key)


def levels(stream_key, dims, pieces, least, high):
    loudness, own = 1.0, jax.random.fold_in(stream_key, 6)
    for position, parts in pieces:
        steps = jnp.exp(jax.random.uniform(jax.random.fold_in(own, position), (parts,), jnp.float32, least / len(pieces), high / len(pieces)))
        loudness = loudness * jnp.repeat(steps, dims[position] // parts).reshape([-1 if axis == position else 1 for axis in range(len(dims))])
    return loudness


def split_up(amount, total, bound, lean):
    portions = [(1 << 20) // math.isqrt(grade ** lean) + 1 for grade in range(2, amount + 1)]
    rest, holding = total - bound - (amount - 1), [1] * (amount - 1)
    while rest > 0:
        candidates = [i for i in range(amount - 1) if holding[i] < bound]
        pool, left = sum([portions[i] for i in candidates]), rest
        for i in candidates:
            more = min(bound - holding[i], max(1, left * portions[i] // pool), rest)
            holding[i] = holding[i] + more
            rest = rest - more
    return np.array([bound] + holding)


def ragged(own_key, number_of, total, bound, skew):
    if number_of == 2:
        one = jax.random.randint(own_key, (), max(1, total - bound), min(bound, total - 1) + 1)
        return jnp.stack([one, total - one])
    tallies = jnp.asarray(split_up(number_of, total, bound, skew), jnp.int32)
    pairs = (number_of - 1) // 2
    source_of, taker = tallies[1:1 + 2 * pairs:2], tallies[2:2 + 2 * pairs:2]
    margin = jnp.minimum(source_of - 1, bound - taker)
    moved = jax.random.randint(jax.random.fold_in(own_key, 1), (pairs,), 0, 1 << 20) % (margin + 1)
    tallies = tallies.at[1:1 + 2 * pairs:2].set(source_of - moved).at[2:2 + 2 * pairs:2].set(taker + moved)
    return tallies[jax.random.permutation(jax.random.fold_in(own_key, 2), number_of)]


def gaussian(own_key, dims, spread, most, cuts=(), held_as=jnp.bfloat16):
    level = levels(own_key, dims, cuts, -0.22, 0.18) if cuts else 1.0
    drawn = jax.random.normal(own_key, dims, jnp.float32) * spread * level
    return jnp.minimum(jnp.maximum(drawn, -most), most).astype(held_as)


def setup_inputs(seed: int = 0) -> dict:
    key_list = jax.random.split(jax.random.key(seed), 12)
    query_rows = draw_query_rows(jax.random.fold_in(key_list[11], 71), 0)
    key_rows = draw_key_rows(jax.random.fold_in(key_list[11], 71), 0)
    value_rows = gaussian(key_list[2], (SEQS, SEQ_LEN, D), 1.0, 6.0, ((0, 4), (1, 8)))
    doc_lengths = jax.vmap(lambda own: ragged(own, DOCS, SEQ_LEN, SEQ_LEN // 2, 2))(jax.random.split(key_list[3], SEQS)).reshape((SEQS, DOCS)).astype(jnp.int32)
    residual = gaussian(key_list[4], (SEQS, SEQ_LEN, D), 1.0, 6.0, ((0, 4), (1, 8)))
    out_proj = gaussian(key_list[5], (D, D), D ** -0.5, 0.25)
    router = gaussian(key_list[6], (D, EXPERTS), (D // 4) ** -0.5, 0.5)
    expert_choice = draw_expert_choice(jax.random.fold_in(key_list[11], 71), 0)
    weight_in = gaussian(key_list[8], (EXPERTS, D, FF), D ** -0.5, 0.25, ((0, 4),))
    weight_out = gaussian(key_list[9], (EXPERTS, FF, D), (FF // 4) ** -0.5, 0.5, ((0, 4),))
    grad_out = gaussian(key_list[10], (SEQS, SEQ_LEN, D), 1.0, 6.0, ((0, 4), (1, 8)))
    return dict(query_rows=query_rows, key_rows=key_rows, value_rows=value_rows, doc_lengths=doc_lengths, residual=residual, out_proj=out_proj, router=router, expert_choice=expert_choice, weight_in=weight_in, weight_out=weight_out, grad_out=grad_out)


norm_eps = 1e-06
masked_score = -1e+30
row_block = 512

def document_ids(lengths, positions):
    boundaries = jnp.cumsum(lengths).astype(jnp.int32)
    return lax.optimization_barrier(jnp.sum((positions[:, None] >= boundaries[None, :-1]).astype(jnp.int32), axis=1)).astype(jnp.int32)

def expert_pass(token_rows, grad_rows, weight_up, weight_down):
    hidden_pre = jnp.dot(token_rows, weight_up, preferred_element_type=jnp.float32)
    sigmoid_pre = jax.nn.sigmoid(hidden_pre)
    activated = (hidden_pre * sigmoid_pre).astype(jnp.bfloat16)
    produced = jnp.dot(activated, weight_down, preferred_element_type=jnp.float32).astype(jnp.bfloat16)
    act_grad = jnp.dot(grad_rows, weight_down.T, preferred_element_type=jnp.float32)
    pre_grad = (act_grad * sigmoid_pre * (1.0 + hidden_pre * (1.0 - sigmoid_pre))).astype(jnp.bfloat16)
    token_grad = jnp.dot(pre_grad, weight_up.T, preferred_element_type=jnp.float32).astype(jnp.bfloat16)
    up_grad = jnp.dot(token_rows.T, pre_grad, preferred_element_type=jnp.float32)
    down_grad = jnp.dot(activated.T, grad_rows, preferred_element_type=jnp.float32)
    return (produced, token_grad, up_grad, down_grad)

def attend_sequence(operands):
    queries, keyed, valued, lengths = operands
    positions = jnp.arange(SEQ_LEN, dtype=jnp.int32)
    docs = document_ids(lengths, positions)
    query_heads = queries.reshape(SEQ_LEN, H, HD).astype(jnp.float32)
    key_heads = keyed.reshape(SEQ_LEN, H, HD).astype(jnp.float32)
    value_heads = valued.reshape(SEQ_LEN, H, HD).astype(jnp.float32)
    scores = jnp.einsum('qhd,khd->hqk', query_heads, key_heads) * (1.0 / math.sqrt(HD))
    visible = (positions[None, :] <= positions[:, None]) & (docs[None, :] == docs[:, None])
    scores = jnp.where(visible[None], scores, masked_score)
    highest = lax.optimization_barrier(jnp.max(scores, axis=2, keepdims=True))
    weights = jnp.where(visible[None], jnp.exp(scores - highest), 0.0)
    totals = lax.optimization_barrier(jnp.sum(weights, axis=2))
    rounded = lax.optimization_barrier(weights.astype(jnp.bfloat16))
    summed = jnp.einsum('hqk,khd->hqd', rounded.astype(jnp.float32), value_heads)
    result = summed / totals[:, :, None]
    return result.transpose(1, 0, 2).reshape(SEQ_LEN, D).astype(jnp.bfloat16)

def reference(query_rows, key_rows, value_rows, doc_lengths, residual, out_proj, router, expert_choice, weight_in, weight_out, grad_out):
    attended = lax.map(attend_sequence, (query_rows, key_rows, value_rows, doc_lengths))
    token_total = SEQS * SEQ_LEN
    mixed = (residual.reshape(token_total, D).astype(jnp.float32) + jnp.dot(attended.reshape(token_total, D), out_proj, preferred_element_type=jnp.float32)).astype(jnp.bfloat16)
    mixed_f = mixed.astype(jnp.float32)
    inv_rms = lax.rsqrt(lax.optimization_barrier(jnp.mean(mixed_f * mixed_f, axis=1, keepdims=True)) + norm_eps)
    normed = (mixed_f * inv_rms).astype(jnp.bfloat16)
    chosen = expert_choice.reshape(token_total).astype(jnp.int32)
    logits = jnp.dot(normed, router, preferred_element_type=jnp.float32)
    gate_value = jax.nn.sigmoid(jnp.take_along_axis(logits, chosen[:, None], axis=1)[:, 0])
    grad_rows = grad_out.reshape(token_total, D)
    scaled_grad = (gate_value[:, None] * grad_rows.astype(jnp.float32)).astype(jnp.bfloat16)
    ordering = jnp.argsort(chosen, stable=True).astype(jnp.int32)
    counts = jnp.zeros((EXPERTS,), jnp.int32).at[chosen].add(1).astype(jnp.int32)
    begins = (jnp.cumsum(counts) - counts).astype(jnp.int32)
    sorted_rows = jnp.concatenate([normed[ordering], jnp.zeros((row_block, D), jnp.bfloat16)], axis=0)
    sorted_grads = jnp.concatenate([scaled_grad[ordering], jnp.zeros((row_block, D), jnp.bfloat16)], axis=0)

    def expert_loop(expert_index, carry):
        made, grads_back, up_all, down_all = carry
        begin_row = begins[expert_index].astype(jnp.int32)
        count = counts[expert_index].astype(jnp.int32)
        weight_up = weight_in[expert_index]
        weight_down = weight_out[expert_index]

        def block_loop(block_index, inner):
            made_in, back_in, up_acc, down_acc = inner
            first = (begin_row + block_index * row_block).astype(jnp.int32)
            local = (block_index * row_block + jnp.arange(row_block, dtype=jnp.int32)).astype(jnp.int32)
            usable = (local < count)[:, None]
            rows_in = jnp.where(usable, lax.dynamic_slice_in_dim(sorted_rows, first, row_block, 0), jnp.zeros((), jnp.bfloat16))
            grads_in = jnp.where(usable, lax.dynamic_slice_in_dim(sorted_grads, first, row_block, 0), jnp.zeros((), jnp.bfloat16))
            produced, token_grad, up_grad, down_grad = expert_pass(rows_in, grads_in, weight_up, weight_down)
            old_made = lax.dynamic_slice_in_dim(made_in, first, row_block, 0)
            old_back = lax.dynamic_slice_in_dim(back_in, first, row_block, 0)
            made_in = lax.dynamic_update_slice_in_dim(made_in, jnp.where(usable, produced, old_made), first, 0)
            back_in = lax.dynamic_update_slice_in_dim(back_in, jnp.where(usable, token_grad, old_back), first, 0)
            return (made_in, back_in, up_acc + up_grad, down_acc + down_grad)
        block_count = ((count + row_block - 1) // row_block).astype(jnp.int32)
        start_state = (made, grads_back, jnp.zeros((D, FF), jnp.float32), jnp.zeros((FF, D), jnp.float32))
        made, grads_back, up_acc, down_acc = lax.fori_loop(jnp.int32(0), block_count, block_loop, start_state)
        up_all = lax.dynamic_update_index_in_dim(up_all, up_acc, expert_index, 0)
        down_all = lax.dynamic_update_index_in_dim(down_all, down_acc, expert_index, 0)
        return (made, grads_back, up_all, down_all)
    start_all = (jnp.zeros((token_total + row_block, D), jnp.bfloat16), jnp.zeros((token_total + row_block, D), jnp.bfloat16), jnp.zeros((EXPERTS, D, FF), jnp.float32), jnp.zeros((EXPERTS, FF, D), jnp.float32))
    made, grads_back, grad_weight_in, grad_weight_out = lax.fori_loop(jnp.int32(0), jnp.int32(EXPERTS), expert_loop, start_all)
    expert_result = jnp.zeros((token_total, D), jnp.bfloat16).at[ordering].set(made[:token_total])
    normed_grad = jnp.zeros((token_total, D), jnp.bfloat16).at[ordering].set(grads_back[:token_total])
    result_f = expert_result.astype(jnp.float32)
    layer_out = (mixed_f + gate_value[:, None] * result_f).astype(jnp.bfloat16)
    gate_grad = lax.optimization_barrier(jnp.sum(grad_rows.astype(jnp.float32) * result_f, axis=1))
    logit_grad = gate_grad * gate_value * (1.0 - gate_value)
    router_cols = router[:, chosen].T.astype(jnp.float32)
    total_grad = normed_grad.astype(jnp.float32) + logit_grad[:, None] * router_cols
    mean_term = lax.optimization_barrier(jnp.mean(total_grad * mixed_f, axis=1, keepdims=True))
    input_grad = inv_rms * total_grad - mixed_f * inv_rms * inv_rms * inv_rms * mean_term
    grad_mixed = (grad_rows.astype(jnp.float32) + input_grad).astype(jnp.bfloat16)
    return (layer_out.reshape(SEQS, SEQ_LEN, D), grad_mixed.reshape(SEQS, SEQ_LEN, D), grad_weight_in, grad_weight_out)
```

```python
import functools
import math

import jax
import jax.numpy as jnp
from jax import lax
from jax.experimental import pallas as pl
from jax.experimental.pallas import tpu as pltpu
from jax.sharding import PartitionSpec as P

HD = 32
norm_eps = 1e-06
masked_score = -1e30
VMEM_LIMIT = 48 * 1024 * 1024
NT = (((1,), (1,)), ((), ()))
TN = (((0,), (0,)), ((), ()))


def whole_vmem(count):
    return [pl.BlockSpec(memory_space=pltpu.VMEM)] * count


def params():
    return pltpu.CompilerParams(vmem_limit_bytes=VMEM_LIMIT)


def dot(a, b, dims=None):
    if dims is None:
        return jnp.dot(a, b, preferred_element_type=jnp.float32)
    return lax.dot_general(a, b, dims, preferred_element_type=jnp.float32)


def slot_matrix(choice, expert_count, hot_capacity):
    tok = choice.shape[1]
    one_hot = lax.broadcasted_iota(jnp.int32, (expert_count, tok), 0) == choice
    hits = one_hot.astype(jnp.float32).astype(jnp.bfloat16)
    earlier = lax.broadcasted_iota(jnp.int32, (tok, tok), 0) <= lax.broadcasted_iota(
        jnp.int32, (tok, tok), 1
    )
    counted = dot(hits, earlier.astype(jnp.float32).astype(jnp.bfloat16))
    rank = jnp.sum(jnp.where(one_hot, counted, 0.0), axis=0, keepdims=True) - 1.0
    slots = choice * hot_capacity + rank.astype(jnp.int32)
    rows = lax.broadcasted_iota(jnp.int32, (expert_count * hot_capacity, tok), 0)
    return (rows == slots).astype(jnp.float32).astype(jnp.bfloat16)


def pack_kernel(query_ref, key_ref, value_ref, sent_ref):
    ranks = sent_ref.shape[0]
    width = sent_ref.shape[1] // 3
    for place, ref in enumerate((query_ref, key_ref, value_ref)):
        turned = ref[...].T
        for rank in range(ranks):
            sent_ref[rank, place * width : (place + 1) * width, :] = turned[
                rank * width : (rank + 1) * width, :
            ]


def grad_dispatch_kernel(expert_count, hot_capacity, choice_ref, grad_ref, sent_ref):
    placed = slot_matrix(choice_ref[...], expert_count, hot_capacity)
    rows = dot(placed, grad_ref[...]).astype(jnp.bfloat16)
    for rep in range(sent_ref.shape[0]):
        sent_ref[rep] = rows


def attend_kernel(lengths_ref, got_ref, out_ref, keys_ref):
    ranks, width3, tok = got_ref.shape
    width = width3 // 3
    heads = width // HD
    reach = (ranks + 1) // 2
    for rank in range(ranks):
        keys_ref[rank * tok : (rank + 1) * tok, :] = got_ref[rank, width : 2 * width, :].T
    bounds = []
    total = jnp.int32(0)
    for doc in range(lengths_ref.shape[1] - 1):
        total = total + lengths_ref[0, doc]
        bounds.append(total)
    scale = math.log2(math.e) / math.sqrt(HD)
    head_of_row = lax.broadcasted_iota(jnp.int32, (width, tok), 0) // HD
    for block in range(ranks):
        first = max(0, block - reach)
        span = (block - first + 1) * tok
        query = got_ref[block, 0:width, :]
        spread = jnp.concatenate(
            [jnp.where(head_of_row == head, query, jnp.zeros_like(query)) for head in range(heads)],
            axis=1,
        )
        position = block * tok + lax.broadcasted_iota(jnp.int32, (1, tok), 1)
        begin = jnp.zeros((1, tok), jnp.int32)
        for bound in bounds:
            begin = jnp.maximum(begin, jnp.where(position >= bound, bound, 0))
        key_position = first * tok + lax.broadcasted_iota(jnp.int32, (span, tok), 0)
        visible = (key_position >= begin) & (key_position <= position)
        scores = dot(keys_ref[first * tok : first * tok + span, :], spread)
        values = jnp.concatenate(
            [got_ref[rank, 2 * width : 3 * width, :] for rank in range(first, block + 1)], axis=1
        )
        for head in range(heads):
            part = jnp.where(visible, scores[:, head * tok : (head + 1) * tok], masked_score)
            top = jnp.max(part, axis=0, keepdims=True)
            weights = jnp.exp2((part - top) * scale)
            totals = jnp.sum(weights, axis=0, keepdims=True)
            summed = dot(
                values[head * HD : (head + 1) * HD, :], weights.astype(jnp.bfloat16)
            )
            out_ref[block, head * HD : (head + 1) * HD, :] = (summed / totals).astype(jnp.bfloat16)


def mix_kernel(
    expert_count, hot_capacity, turned_ref, residual_ref, proj_ref, choice_ref, mixed_ref, sent_ref
):
    attended = turned_ref[...].T
    mixed = (residual_ref[...].astype(jnp.float32) + dot(attended, proj_ref[...])).astype(
        jnp.bfloat16
    )
    mixed_ref[...] = mixed
    mixed_f = mixed.astype(jnp.float32)
    inv_rms = lax.rsqrt(jnp.mean(mixed_f * mixed_f, axis=1, keepdims=True) + norm_eps)
    normed = (mixed_f * inv_rms).astype(jnp.bfloat16)
    placed = slot_matrix(choice_ref[...], expert_count, hot_capacity)
    rows = dot(placed, normed).astype(jnp.bfloat16)
    for rep in range(sent_ref.shape[0]):
        sent_ref[rep] = rows


def expert_kernel(
    ids_ref, rows_ref, grads_ref, up_ref, down_ref, router_ref, back_ref, terms_ref, up_acc, down_acc
):
    reps, count, width = rows_ref.shape
    sources, unused, capacity, unused_width = back_ref.shape
    parts, kinds, strip, unused_hidden = terms_ref.shape
    expert = ids_ref[0]
    own = ids_ref[1]
    up = up_ref[...]
    down = down_ref[...]
    router = router_ref[...]
    expert_lane = lax.broadcasted_iota(jnp.int32, (count, router.shape[0]), 1) == expert

    def chunk(rep, first):
        rows = rows_ref[rep]
        pre = dot(rows, up)
        sigmoid_pre = jax.nn.sigmoid(pre)
        activated = (pre * sigmoid_pre).astype(jnp.bfloat16)
        logits = dot(rows, router, NT)
        gate = jax.nn.sigmoid(
            jnp.sum(jnp.where(expert_lane, logits, 0.0), axis=1, keepdims=True)
        )
        scaled = (gate * grads_ref[rep].astype(jnp.float32)).astype(jnp.bfloat16)
        act_grad = dot(scaled, down, NT)
        pre_grad = (act_grad * sigmoid_pre * (1.0 + pre * (1.0 - sigmoid_pre))).astype(
            jnp.bfloat16
        )
        up_term = dot(rows, pre_grad, TN)
        down_term = dot(activated, scaled, TN)
        if first:
            up_acc[...] = up_term
            down_acc[...] = down_term
            produced = dot(activated, down).astype(jnp.bfloat16)
            token_grad = dot(pre_grad, up, NT).astype(jnp.bfloat16)
            for source in range(sources):
                back_ref[source, 0] = produced[source * capacity : (source + 1) * capacity]
                back_ref[source, 1] = token_grad[source * capacity : (source + 1) * capacity]
        else:
            up_acc[...] += up_term
            down_acc[...] += down_term

    chunk(own, True)

    def other(step, carry):
        chunk(lax.rem(own + step, reps), False)
        return carry

    if reps > 1:
        lax.fori_loop(1, reps, other, 0)
    for part in range(parts):
        first_row = pl.multiple_of((part * reps + own) * strip, strip)
        terms_ref[part, 0] = up_acc[pl.ds(first_row, strip), :].astype(jnp.bfloat16)
        terms_ref[part, 1] = down_acc[pl.ds(first_row, strip), :].astype(jnp.bfloat16)


def finish_kernel(
    hot_capacity, back_ref, mixed_ref, grad_ref, choice_ref, router_ref, layer_ref, grad_mixed_ref
):
    sources, kinds, capacity, width = back_ref.shape
    tok = mixed_ref.shape[0]
    choice = choice_ref[...]
    placed = slot_matrix(choice, sources, hot_capacity)
    router = router_ref[...]
    mixed_f = mixed_ref[...].astype(jnp.float32)
    inv_rms = lax.rsqrt(jnp.mean(mixed_f * mixed_f, axis=1, keepdims=True) + norm_eps)
    normed = (mixed_f * inv_rms).astype(jnp.bfloat16)
    one_hot = lax.broadcasted_iota(jnp.int32, (sources, tok), 0) == choice
    logits = dot(router, normed, NT)
    logit_row = jnp.sum(jnp.where(one_hot, logits, 0.0), axis=0, keepdims=True)
    logit = jnp.broadcast_to(logit_row, (8, tok)).T[:, 0:1]
    gate = jax.nn.sigmoid(logit)
    results = jnp.concatenate([back_ref[source, 0] for source in range(sources)], axis=0)
    grads = jnp.concatenate([back_ref[source, 1] for source in range(sources)], axis=0)
    result_f = dot(placed, results, TN)
    normed_grad = dot(placed, grads, TN)
    grad_f = grad_ref[...].astype(jnp.float32)
    layer_ref[...] = (mixed_f + gate * result_f).astype(jnp.bfloat16)
    gate_grad = jnp.sum(grad_f * result_f, axis=1, keepdims=True)
    logit_grad = gate_grad * gate * (1.0 - gate)
    router_cols = dot(one_hot.astype(jnp.float32).astype(jnp.bfloat16), router, TN)
    total_grad = normed_grad + logit_grad * router_cols
    mean_term = jnp.mean(total_grad * mixed_f, axis=1, keepdims=True)
    input_grad = inv_rms * total_grad - mixed_f * inv_rms * inv_rms * inv_rms * mean_term
    grad_mixed_ref[...] = (grad_f + input_grad).astype(jnp.bfloat16)


def sum_kernel(terms_ref, up_ref, down_ref):
    up_ref[...] = jnp.sum(terms_ref[:, 0].astype(jnp.float32), axis=0)
    down_ref[...] = jnp.sum(terms_ref[:, 1].astype(jnp.float32), axis=0)


def shape(dims, dtype=jnp.bfloat16):
    return jax.ShapeDtypeStruct(dims, dtype)


def local(
    seq_count,
    rep_count,
    query_rows,
    key_rows,
    value_rows,
    doc_lengths,
    residual,
    out_proj,
    router,
    expert_choice,
    weight_in,
    weight_out,
    grad_out,
):
    tok, width = query_rows.shape[1:]
    hidden = weight_in.shape[2]
    ranks = seq_count * rep_count
    share = width // ranks
    expert_count = router.shape[1]
    capacity = max(2, (3 * tok + 2 * expert_count - 1) // (2 * expert_count))
    hot_capacity = min(4 * capacity, tok // 2)
    slots = expert_count * hot_capacity
    choice = expert_choice.reshape(1, tok)
    router_rows = router.T

    def call(body, out_shape, specs, scratch=()):
        return pl.pallas_call(
            body,
            out_shape=out_shape,
            in_specs=specs,
            out_specs=jax.tree.map(lambda unused: pl.BlockSpec(memory_space=pltpu.VMEM), out_shape),
            scratch_shapes=list(scratch),
            compiler_params=params(),
        )

    packed = call(pack_kernel, shape((ranks, 3 * share, tok)), whole_vmem(3))(
        query_rows[0], key_rows[0], value_rows[0]
    )
    got = lax.all_to_all(packed, ("seq", "rep"), split_axis=0, concat_axis=0, tiled=True)
    sent_grads = call(
        functools.partial(grad_dispatch_kernel, expert_count, hot_capacity),
        shape((rep_count, slots, width)),
        whole_vmem(2),
    )(choice, grad_out[0])
    got_grads = lax.all_to_all(
        sent_grads.reshape(rep_count * expert_count, hot_capacity, width),
        ("rep", "expert"),
        split_axis=0,
        concat_axis=0,
        tiled=True,
    ).reshape(rep_count, slots, width)
    smem = pl.BlockSpec(memory_space=pltpu.SMEM)
    attended = call(
        attend_kernel,
        shape((ranks, share, tok)),
        [smem] + whole_vmem(1),
        [pltpu.VMEM((ranks * tok, share), jnp.bfloat16)],
    )(doc_lengths, got)
    turned = lax.all_to_all(
        attended, ("seq", "rep"), split_axis=0, concat_axis=0, tiled=True
    ).reshape(width, tok)
    mixed, sent_rows = call(
        functools.partial(mix_kernel, expert_count, hot_capacity),
        (shape((tok, width)), shape((rep_count, slots, width))),
        whole_vmem(4),
    )(turned, residual[0], out_proj, choice)
    got_rows = lax.all_to_all(
        sent_rows.reshape(rep_count * expert_count, hot_capacity, width),
        ("rep", "expert"),
        split_axis=0,
        concat_axis=0,
        tiled=True,
    ).reshape(rep_count, slots, width)
    ids = jnp.stack([lax.axis_index("expert"), lax.axis_index("rep")]).astype(jnp.int32)
    strip = width // ranks
    back, terms = call(
        expert_kernel,
        (
            shape((expert_count, 2, hot_capacity, width)),
            shape((seq_count, 2, strip, hidden)),
        ),
        [smem] + whole_vmem(5),
        [pltpu.VMEM((width, hidden), jnp.float32), pltpu.VMEM((hidden, width), jnp.float32)],
    )(ids, got_rows, got_grads, weight_in[0], weight_out[0], router_rows)
    got_terms = lax.all_to_all(terms, "seq", split_axis=0, concat_axis=0, tiled=True)
    got_back = lax.all_to_all(back, "expert", split_axis=0, concat_axis=0, tiled=True)
    layer_out, grad_mixed = call(
        functools.partial(finish_kernel, hot_capacity),
        (shape((tok, width)), shape((tok, width))),
        whole_vmem(5),
    )(got_back, mixed, grad_out[0], choice, router_rows)
    share_in, share_out = call(
        sum_kernel,
        (shape((strip, hidden), jnp.float32), shape((strip, width), jnp.float32)),
        whole_vmem(1),
    )(got_terms)
    return (layer_out[None], grad_mixed[None], share_in[None], share_out[None])


def solution(mesh):
    rows = P("expert", ("seq", "rep"), None)
    in_specs = (
        rows,
        rows,
        rows,
        P("expert", None),
        rows,
        P(),
        P(),
        rows,
        P("expert", None, None),
        P("expert", None, None),
        rows,
    )
    body = functools.partial(local, mesh.shape["seq"], mesh.shape["rep"])
    return jax.shard_map(
        body, mesh=mesh, in_specs=in_specs, out_specs=(rows, rows, rows, rows), check_vma=False
    )
```

```python
import functools
import math

import jax
import jax.numpy as jnp
from jax import lax
from jax.experimental import pallas as pl
from jax.experimental.pallas import tpu as pltpu
from jax.sharding import PartitionSpec as P

HD = 32
norm_eps = 1e-06
masked_score = -1e30
VMEM_LIMIT = 48 * 1024 * 1024
MOST_PERMUTES = 16
NT = (((1,), (1,)), ((), ()))
TN = (((0,), (0,)), ((), ()))


def dot(a, b, dims=None):
    if dims is None:
        return jnp.dot(a, b, preferred_element_type=jnp.float32)
    return lax.dot_general(a, b, dims, preferred_element_type=jnp.float32)


def away(index, offset, size):
    if size & (size - 1) == 0:
        return index ^ offset
    return (index + offset) % size


def back_from(index, offset, size):
    if size & (size - 1) == 0:
        return index ^ offset
    return (index - offset + size) % size


class Group:
    def __init__(self, axes, sizes):
        self.axes, self.sizes = tuple(axes), tuple(sizes)
        self.count = math.prod(sizes)

    def split(self, flat):
        coords = []
        for size in reversed(self.sizes):
            coords.append(flat % size)
            flat = flat // size
        return coords[::-1]

    def moved(self, flat, offset, step):
        place = 0
        for coord, part, size in zip(self.split(flat), self.split(offset), self.sizes):
            place = place * size + step(coord, part, size)
        return place

    def target(self, flat, offset):
        return self.moved(flat, offset, away)

    def source(self, flat, offset):
        return self.moved(flat, offset, back_from)

    def exchange(self, chunks, inverse=False):
        to, start = (self.source, self.target) if inverse else (self.target, self.source)
        if self.count <= MOST_PERMUTES:
            order = sorted(range(1, self.count), key=lambda k: -k)
            got = {0: chunks[0]}
            for k in order:
                pairs = [(i, to(i, k)) for i in range(self.count)]
                got[k] = lax.ppermute(chunks[k], self.axes, pairs)
            return [got[k] for k in range(self.count)]
        me = lax.axis_index(self.axes)
        steps = jnp.arange(self.count, dtype=jnp.int32)
        sent_to = jax.vmap(lambda k: to(me, k))(steps)
        placed = jnp.zeros((self.count,), jnp.int32).at[sent_to].set(steps)
        stacked = jnp.stack(chunks)[placed]
        got = lax.all_to_all(stacked, self.axes, split_axis=0, concat_axis=0, tiled=True)
        came_from = jax.vmap(lambda k: start(me, k))(steps)
        ordered = got[came_from]
        return [ordered[k] for k in range(self.count)]


def merged(chunks, most):
    if len(chunks) <= most:
        return list(chunks)
    return [jnp.concatenate(chunks, axis=0)]


def rows_of(refs):
    if len(refs) == 1:
        return refs[0][...]
    return jnp.concatenate([ref[...] for ref in refs], axis=0)


def slot_matrix(choice, own, expert_count, hot_capacity):
    tok = choice.shape[1]
    offset = back_from(choice, own, expert_count)
    one_hot = lax.broadcasted_iota(jnp.int32, (expert_count, tok), 0) == offset
    hits = one_hot.astype(jnp.float32).astype(jnp.bfloat16)
    earlier = lax.broadcasted_iota(jnp.int32, (tok, tok), 0) <= lax.broadcasted_iota(
        jnp.int32, (tok, tok), 1
    )
    counted = dot(hits, earlier.astype(jnp.float32).astype(jnp.bfloat16))
    rank = jnp.sum(jnp.where(one_hot, counted, 0.0), axis=0, keepdims=True) - 1.0
    slots = offset * hot_capacity + rank.astype(jnp.int32)
    rows = lax.broadcasted_iota(jnp.int32, (expert_count * hot_capacity, tok), 0)
    return (rows == slots).astype(jnp.float32).astype(jnp.bfloat16)


def pack_kernel(share, to_ref, query_ref, key_ref, value_ref, *refs):
    sent_refs, (held_ref, turned_ref, sems) = refs[:-3], refs[-3:]
    copies = [
        pltpu.make_async_copy(ref, held_ref.at[place], sems.at[place])
        for place, ref in enumerate((query_ref, key_ref, value_ref))
    ]
    for copy in copies:
        copy.start()
    for place, copy in enumerate(copies):
        copy.wait()
        turned_ref[place] = held_ref[place].T
        for k, sent_ref in enumerate(sent_refs):
            first = pl.multiple_of(to_ref[k] * share, share)
            sent_ref[place * share : (place + 1) * share, :] = turned_ref[
                place, pl.ds(first, share), :
            ]


def grad_dispatch_kernel(hot_capacity, own_ref, choice_ref, grad_ref, *sent_refs):
    placed = slot_matrix(choice_ref[...], own_ref[0], len(sent_refs), hot_capacity)
    rows = dot(placed, grad_ref[...]).astype(jnp.bfloat16)
    for k, sent_ref in enumerate(sent_refs):
        sent_ref[...] = rows[k * hot_capacity : (k + 1) * hot_capacity]


def attend_kernel(ranks, to_ref, from_ref, lengths_ref, *refs):
    got_refs, out_refs = refs[:ranks], refs[ranks : 2 * ranks]
    query_ref, keys_ref, values_ref, result_ref = refs[2 * ranks :]
    width, tok = out_refs[0].shape
    heads = width // HD
    reach = (ranks + 1) // 2
    for k, got_ref in enumerate(got_refs):
        rank = from_ref[k]
        query_ref[rank] = got_ref[0:width, :]
        keys_ref[pl.ds(pl.multiple_of(rank * tok, tok), tok), :] = got_ref[width : 2 * width, :].T
        values_ref[rank] = got_ref[2 * width : 3 * width, :]
    bounds = []
    total = jnp.int32(0)
    for doc in range(lengths_ref.shape[1] - 1):
        total = total + lengths_ref[0, doc]
        bounds.append(total)
    scale = math.log2(math.e) / math.sqrt(HD)
    head_of_row = lax.broadcasted_iota(jnp.int32, (width, tok), 0) // HD
    for block in range(ranks):
        first = max(0, block - reach)
        span = (block - first + 1) * tok
        query = query_ref[block]
        spread = jnp.concatenate(
            [jnp.where(head_of_row == head, query, jnp.zeros_like(query)) for head in range(heads)],
            axis=1,
        )
        position = block * tok + lax.broadcasted_iota(jnp.int32, (1, tok), 1)
        begin = jnp.zeros((1, tok), jnp.int32)
        for bound in bounds:
            begin = jnp.maximum(begin, jnp.where(position >= bound, bound, 0))
        key_position = first * tok + lax.broadcasted_iota(jnp.int32, (span, tok), 0)
        visible = (key_position >= begin) & (key_position <= position)
        scores = dot(keys_ref[first * tok : first * tok + span, :], spread)
        values = jnp.concatenate([values_ref[rank] for rank in range(first, block + 1)], axis=1)
        for head in range(heads):
            part = jnp.where(visible, scores[:, head * tok : (head + 1) * tok], masked_score)
            top = jnp.max(part, axis=0, keepdims=True)
            weights = jnp.exp2((part - top) * scale)
            totals = jnp.sum(weights, axis=0, keepdims=True)
            summed = dot(
                values[head * HD : (head + 1) * HD, :], weights.astype(jnp.bfloat16)
            )
            result_ref[block, head * HD : (head + 1) * HD, :] = (summed / totals).astype(
                jnp.bfloat16
            )
    for k, out_ref in enumerate(out_refs):
        out_ref[...] = result_ref[to_ref[k]]


def mix_kernel(
    ranks, hot_capacity, from_ref, own_ref, choice_ref, residual_ref, proj_ref, *refs
):
    got_refs, mixed_ref, sent_refs, turned_ref = refs[:ranks], refs[ranks], refs[ranks + 1 : -1], refs[-1]
    share = got_refs[0].shape[0]
    for k, got_ref in enumerate(got_refs):
        turned_ref[pl.ds(pl.multiple_of(from_ref[k] * share, share), share), :] = got_ref[...]
    attended = turned_ref[...].T
    mixed = (residual_ref[...].astype(jnp.float32) + dot(attended, proj_ref[...])).astype(
        jnp.bfloat16
    )
    mixed_ref[...] = mixed
    mixed_f = mixed.astype(jnp.float32)
    inv_rms = lax.rsqrt(jnp.mean(mixed_f * mixed_f, axis=1, keepdims=True) + norm_eps)
    normed = (mixed_f * inv_rms).astype(jnp.bfloat16)
    placed = slot_matrix(choice_ref[...], own_ref[0], len(sent_refs), hot_capacity)
    rows = dot(placed, normed).astype(jnp.bfloat16)
    for k, sent_ref in enumerate(sent_refs):
        sent_ref[...] = rows[k * hot_capacity : (k + 1) * hot_capacity]


def expert_kernel(
    reps, sources, parts, strip, own_ref, part_ref, up_ref, down_ref, router_ref, *refs
):
    per_rep = (len(refs) - 2 - sources - parts) // (2 * reps)
    row_refs = [refs[rep * per_rep : (rep + 1) * per_rep] for rep in range(reps)]
    refs = refs[reps * per_rep :]
    grad_refs = [refs[rep * per_rep : (rep + 1) * per_rep] for rep in range(reps)]
    refs = refs[reps * per_rep :]
    back_refs, term_refs, (kept_ref, up_acc, down_acc) = refs[:sources], refs[sources:-3], refs[-3:]
    capacity = back_refs[0].shape[0] // 2
    count = sources * capacity
    up = up_ref[...]
    down = down_ref[...]
    router = router_ref[...]
    expert_lane = lax.broadcasted_iota(jnp.int32, (count, router.shape[0]), 1) == own_ref[0]
    for rep in range(reps):
        rows = rows_of(row_refs[rep])
        pre = dot(rows, up)
        sigmoid_pre = jax.nn.sigmoid(pre)
        activated = (pre * sigmoid_pre).astype(jnp.bfloat16)
        logits = dot(rows, router, NT)
        gate = jax.nn.sigmoid(
            jnp.sum(jnp.where(expert_lane, logits, 0.0), axis=1, keepdims=True)
        )
        scaled = (gate * rows_of(grad_refs[rep]).astype(jnp.float32)).astype(jnp.bfloat16)
        act_grad = dot(scaled, down, NT)
        pre_grad = (act_grad * sigmoid_pre * (1.0 + pre * (1.0 - sigmoid_pre))).astype(
            jnp.bfloat16
        )
        up_term = dot(rows, pre_grad, TN)
        down_term = dot(activated, scaled, TN)
        if rep == 0:
            up_acc[...] = up_term
            down_acc[...] = down_term
            produced = dot(activated, down).astype(jnp.bfloat16)
            token_grad = dot(pre_grad, up, NT).astype(jnp.bfloat16)
            for k, back_ref in enumerate(back_refs):
                back_ref[0:capacity] = produced[k * capacity : (k + 1) * capacity]
                back_ref[capacity : 2 * capacity] = token_grad[k * capacity : (k + 1) * capacity]
        else:
            up_acc[...] += up_term
            down_acc[...] += down_term
    for k in range(parts):
        first = pl.multiple_of(part_ref[k] * strip, strip)
        up_part = up_acc[pl.ds(first, strip), :]
        down_part = down_acc[pl.ds(first, strip), :]
        if k == 0:
            kept_ref[0] = up_part
            kept_ref[1] = down_part
        else:
            term_refs[k - 1][0] = up_part.astype(jnp.bfloat16)
            term_refs[k - 1][1] = down_part.astype(jnp.bfloat16)


def finish_kernel(
    hot_capacity, own_ref, choice_ref, router_ref, mixed_ref, grad_ref, *refs
):
    back_refs, (layer_ref, grad_mixed_ref) = refs[:-2], refs[-2:]
    expert_count = router_ref.shape[0]
    tok = mixed_ref.shape[0]
    choice = choice_ref[...]
    placed = slot_matrix(choice, own_ref[0], expert_count, hot_capacity)
    router = router_ref[...]
    mixed_f = mixed_ref[...].astype(jnp.float32)
    inv_rms = lax.rsqrt(jnp.mean(mixed_f * mixed_f, axis=1, keepdims=True) + norm_eps)
    normed = (mixed_f * inv_rms).astype(jnp.bfloat16)
    one_hot = lax.broadcasted_iota(jnp.int32, (expert_count, tok), 0) == choice
    logits = dot(router, normed, NT)
    logit_row = jnp.sum(jnp.where(one_hot, logits, 0.0), axis=0, keepdims=True)
    logit = jnp.broadcast_to(logit_row, (8, tok)).T[:, 0:1]
    gate = jax.nn.sigmoid(logit)
    pair = 2 * hot_capacity
    chunks = [
        ref[first : first + pair] for ref in back_refs for first in range(0, ref.shape[0], pair)
    ]
    results = jnp.concatenate([chunk[:hot_capacity] for chunk in chunks], axis=0)
    grads = jnp.concatenate([chunk[hot_capacity:] for chunk in chunks], axis=0)
    result_f = dot(placed, results, TN)
    normed_grad = dot(placed, grads, TN)
    grad_f = grad_ref[...].astype(jnp.float32)
    layer_ref[...] = (mixed_f + gate * result_f).astype(jnp.bfloat16)
    gate_grad = jnp.sum(grad_f * result_f, axis=1, keepdims=True)
    logit_grad = gate_grad * gate * (1.0 - gate)
    router_cols = dot(one_hot.astype(jnp.float32).astype(jnp.bfloat16), router, TN)
    total_grad = normed_grad + logit_grad * router_cols
    mean_term = jnp.mean(total_grad * mixed_f, axis=1, keepdims=True)
    input_grad = inv_rms * total_grad - mixed_f * inv_rms * inv_rms * inv_rms * mean_term
    grad_mixed_ref[...] = (grad_f + input_grad).astype(jnp.bfloat16)


def sum_kernel(kept_ref, *refs):
    term_refs, (up_ref, down_ref) = refs[:-2], refs[-2:]
    for kind, out_ref in enumerate((up_ref, down_ref)):
        total = kept_ref[kind]
        for ref in term_refs:
            total = total + ref[kind].astype(jnp.float32)
        out_ref[...] = total


def shape(dims, dtype=jnp.bfloat16):
    return jax.ShapeDtypeStruct(dims, dtype)


SMEM = pl.BlockSpec(memory_space=pltpu.SMEM)
VMEM = pl.BlockSpec(memory_space=pltpu.VMEM)
HBM = pl.BlockSpec(memory_space=pltpu.HBM)


def call(body, out_shape, specs, scratch=()):
    return pl.pallas_call(
        body,
        out_shape=out_shape,
        in_specs=specs,
        out_specs=jax.tree.map(lambda unused: VMEM, out_shape),
        scratch_shapes=list(scratch),
        compiler_params=pltpu.CompilerParams(vmem_limit_bytes=VMEM_LIMIT),
    )


def local(
    seq_count,
    expert_count,
    rep_count,
    query_rows,
    key_rows,
    value_rows,
    doc_lengths,
    residual,
    out_proj,
    router,
    expert_choice,
    weight_in,
    weight_out,
    grad_out,
):
    tok, width = query_rows.shape[1:]
    hidden = weight_in.shape[2]
    positions = Group(("seq", "rep"), (seq_count, rep_count))
    owners = Group(("expert", "rep"), (expert_count, rep_count))
    experts = Group(("expert",), (expert_count,))
    parts = Group(("seq",), (seq_count,))
    ranks = positions.count
    share = width // ranks
    strip = width // ranks
    capacity = max(2, (3 * tok + 2 * expert_count - 1) // (2 * expert_count))
    hot_capacity = min(4 * capacity, tok // 2)
    choice = expert_choice.reshape(1, tok)
    router_rows = router.T
    seq_index = lax.axis_index("seq")
    rep_index = lax.axis_index("rep")
    rank = seq_index * rep_count + rep_index
    own = jnp.stack([lax.axis_index("expert")]).astype(jnp.int32)
    rank_to = jnp.stack([positions.target(rank, k) for k in range(ranks)]).astype(jnp.int32)
    rank_from = jnp.stack([positions.source(rank, k) for k in range(ranks)]).astype(jnp.int32)
    part_to = jnp.stack(
        [parts.target(seq_index, k) * rep_count + rep_index for k in range(seq_count)]
    ).astype(jnp.int32)

    packed = call(
        functools.partial(pack_kernel, share),
        [shape((3 * share, tok))] * ranks,
        [SMEM, HBM, HBM, HBM],
        [
            pltpu.VMEM((3, tok, width), jnp.bfloat16),
            pltpu.VMEM((3, width, tok), jnp.bfloat16),
            pltpu.SemaphoreType.DMA((3,)),
        ],
    )(rank_to, query_rows[0], key_rows[0], value_rows[0])
    got = positions.exchange(packed)

    def to_owners(chunks):
        arrived = owners.exchange([chunks[k // rep_count] for k in range(owners.count)])
        spread = []
        for rep in range(rep_count):
            spread += merged(arrived[rep::rep_count], MOST_PERMUTES)
        return spread

    sent_grads = call(
        functools.partial(grad_dispatch_kernel, hot_capacity),
        [shape((hot_capacity, width))] * expert_count,
        [SMEM, VMEM, VMEM],
    )(own, choice, grad_out[0])
    got_grads = to_owners(sent_grads)
    attended = call(
        functools.partial(attend_kernel, ranks),
        [shape((share, tok))] * ranks,
        [SMEM, SMEM, SMEM] + [VMEM] * ranks,
        [
            pltpu.VMEM((ranks, share, tok), jnp.bfloat16),
            pltpu.VMEM((ranks * tok, share), jnp.bfloat16),
            pltpu.VMEM((ranks, share, tok), jnp.bfloat16),
            pltpu.VMEM((ranks, share, tok), jnp.bfloat16),
        ],
    )(rank_to, rank_from, doc_lengths, *got)
    turned = positions.exchange(attended)
    mixed, *sent_rows = call(
        functools.partial(mix_kernel, ranks, hot_capacity),
        [shape((tok, width))] + [shape((hot_capacity, width))] * expert_count,
        [SMEM, SMEM] + [VMEM] * (3 + ranks),
        [pltpu.VMEM((width, tok), jnp.bfloat16)],
    )(rank_from, own, choice, residual[0], out_proj, *turned)
    got_rows = to_owners(sent_rows)
    outs = call(
        functools.partial(expert_kernel, rep_count, expert_count, seq_count, strip),
        [shape((2 * hot_capacity, width))] * expert_count
        + [shape((2, strip, hidden))] * (seq_count - 1)
        + [shape((2, strip, hidden), jnp.float32)],
        [SMEM, SMEM] + [VMEM] * (3 + len(got_rows) + len(got_grads)),
        [pltpu.VMEM((width, hidden), jnp.float32), pltpu.VMEM((hidden, width), jnp.float32)],
    )(own, part_to, weight_in[0], weight_out[0], router_rows, *got_rows, *got_grads)
    back, terms, kept = outs[:expert_count], outs[expert_count:-1], outs[-1]
    got_terms = parts.exchange([None] + list(terms))[1:]
    got_back = merged(experts.exchange(back, inverse=True), MOST_PERMUTES)
    layer_out, grad_mixed = call(
        functools.partial(finish_kernel, hot_capacity),
        [shape((tok, width)), shape((tok, width))],
        [SMEM] + [VMEM] * (4 + len(got_back)),
    )(own, choice, router_rows, mixed, grad_out[0], *got_back)
    share_in, share_out = call(
        sum_kernel,
        [shape((strip, hidden), jnp.float32), shape((strip, width), jnp.float32)],
        [VMEM] * seq_count,
    )(kept, *got_terms)
    return (layer_out[None], grad_mixed[None], share_in[None], share_out[None])


def solution(mesh):
    rows = P("expert", ("seq", "rep"), None)
    in_specs = (
        rows,
        rows,
        rows,
        P("expert", None),
        rows,
        P(),
        P(),
        rows,
        P("expert", None, None),
        P("expert", None, None),
        rows,
    )
    body = functools.partial(
        local, mesh.shape["seq"], mesh.shape["expert"], mesh.shape["rep"]
    )
    return jax.shard_map(
        body, mesh=mesh, in_specs=in_specs, out_specs=(rows, rows, rows, rows), check_vma=False
    )
```

```python
import functools
import math

import jax
import jax.numpy as jnp
from jax import lax
from jax.experimental import pallas as pl
from jax.experimental.pallas import tpu as pltpu
from jax.sharding import PartitionSpec as P

HD = 32
norm_eps = 1e-06
masked_score = -1e30
VMEM_LIMIT = 48 * 1024 * 1024
MOST_PERMUTES = 16
NT = (((1,), (1,)), ((), ()))
TN = (((0,), (0,)), ((), ()))


def dot(a, b, dims=None):
    if dims is None:
        return jnp.dot(a, b, preferred_element_type=jnp.float32)
    return lax.dot_general(a, b, dims, preferred_element_type=jnp.float32)


def away(index, offset, size):
    if size & (size - 1) == 0:
        return index ^ offset
    return (index + offset) % size


def back_from(index, offset, size):
    if size & (size - 1) == 0:
        return index ^ offset
    return (index - offset + size) % size


class Group:
    def __init__(self, axes, sizes):
        self.axes, self.sizes = tuple(axes), tuple(sizes)
        self.count = math.prod(sizes)

    def split(self, flat):
        coords = []
        for size in reversed(self.sizes):
            coords.append(flat % size)
            flat = flat // size
        return coords[::-1]

    def moved(self, flat, offset, step):
        place = 0
        for coord, part, size in zip(self.split(flat), self.split(offset), self.sizes):
            place = place * size + step(coord, part, size)
        return place

    def target(self, flat, offset):
        return self.moved(flat, offset, away)

    def source(self, flat, offset):
        return self.moved(flat, offset, back_from)

    def exchange(self, chunks, inverse=False):
        to, start = (self.source, self.target) if inverse else (self.target, self.source)
        if self.count <= MOST_PERMUTES:
            order = sorted(range(1, self.count), key=lambda k: -k)
            got = {0: chunks[0]}
            for k in order:
                pairs = [(i, to(i, k)) for i in range(self.count)]
                got[k] = lax.ppermute(chunks[k], self.axes, pairs)
            return [got[k] for k in range(self.count)]
        me = lax.axis_index(self.axes)
        steps = jnp.arange(self.count, dtype=jnp.int32)
        sent_to = jax.vmap(lambda k: to(me, k))(steps)
        placed = jnp.zeros((self.count,), jnp.int32).at[sent_to].set(steps)
        stacked = jnp.stack(chunks)[placed]
        got = lax.all_to_all(stacked, self.axes, split_axis=0, concat_axis=0, tiled=True)
        came_from = jax.vmap(lambda k: start(me, k))(steps)
        ordered = got[came_from]
        return [ordered[k] for k in range(self.count)]


def merged(chunks, most):
    if len(chunks) <= most:
        return list(chunks)
    return [jnp.concatenate(chunks, axis=0)]


def chunk_rows(refs, count, low, high):
    size = sum(ref.shape[0] for ref in refs) // count
    parts = []
    for chunk in range(count):
        ref, first = (refs[chunk], 0) if len(refs) == count else (refs[0], chunk * size)
        parts.append(ref[first + low : first + high, :])
    return parts[0] if count == 1 else jnp.concatenate(parts, axis=0)


def slot_matrix(choice, own, expert_count, hot_capacity):
    tok = choice.shape[1]
    offset = back_from(choice, own, expert_count)
    one_hot = lax.broadcasted_iota(jnp.int32, (expert_count, tok), 0) == offset
    hits = one_hot.astype(jnp.float32).astype(jnp.bfloat16)
    earlier = lax.broadcasted_iota(jnp.int32, (tok, tok), 0) <= lax.broadcasted_iota(
        jnp.int32, (tok, tok), 1
    )
    counted = dot(hits, earlier.astype(jnp.float32).astype(jnp.bfloat16))
    rank = jnp.sum(jnp.where(one_hot, counted, 0.0), axis=0, keepdims=True) - 1.0
    slots = offset * hot_capacity + rank.astype(jnp.int32)
    rows = lax.broadcasted_iota(jnp.int32, (expert_count * hot_capacity, tok), 0)
    return (rows == slots).astype(jnp.float32).astype(jnp.bfloat16)


def stack_kernel(key_ref, value_ref, out_ref, sems):
    tok = key_ref.shape[0]
    copies = [
        pltpu.make_async_copy(ref, out_ref.at[pl.ds(place * tok, tok), :], sems.at[place])
        for place, ref in enumerate((key_ref, value_ref))
    ]
    for copy in copies:
        copy.start()
    for copy in copies:
        copy.wait()


def dispatch_kernel(reps, hot_capacity, own_ref, *refs):
    choice_refs, row_refs, sent_refs = refs[:reps], refs[reps : 2 * reps], refs[2 * reps :]
    for rep in range(reps):
        placed = slot_matrix(choice_refs[rep][...], own_ref[0], len(sent_refs), hot_capacity)
        rows = dot(placed, row_refs[rep][...]).astype(jnp.bfloat16)
        for k, sent_ref in enumerate(sent_refs):
            sent_ref[rep * hot_capacity : (rep + 1) * hot_capacity] = rows[
                k * hot_capacity : (k + 1) * hot_capacity
            ]


def attend_blocks(block_ref, lengths_ref, query_ref, pair_refs, state_refs, bias_ref, first):
    top_ref, total_ref, sum_ref = state_refs
    tok, width = query_ref.shape
    lanes = 128
    per = lanes // HD
    scale = math.log2(math.e) / math.sqrt(HD)
    turned = query_ref[...].T
    head_of_row = lax.broadcasted_iota(jnp.int32, (lanes, tok), 0) // HD
    spread = []
    for group in range(width // lanes):
        part = turned[group * lanes : (group + 1) * lanes]
        spread.append(
            jnp.concatenate(
                [jnp.where(head_of_row == head, part, jnp.zeros_like(part)) for head in range(per)],
                axis=1,
            )
        )
    position = block_ref[0] * tok + lax.broadcasted_iota(jnp.int32, (1, tok), 1)
    begin = jnp.zeros((1, tok), jnp.int32)
    bound = jnp.int32(0)
    for doc in range(lengths_ref.shape[1] - 1):
        bound = bound + lengths_ref[0, doc]
        begin = jnp.maximum(begin, jnp.where(position >= bound, bound, 0))

    def fold(pair_ref, block, fresh):
        key_position = block * tok + lax.broadcasted_iota(jnp.int32, (tok, tok), 0)
        visible = (key_position >= begin) & (key_position <= position)
        bias_ref[...] = jnp.where(visible, 0.0, masked_score)
        bias = bias_ref[...]
        values = pair_ref[tok : 2 * tok, :].T
        for group in range(width // lanes):
            columns = slice(group * lanes, (group + 1) * lanes)
            scores = dot(pair_ref[0:tok, columns], spread[group])
            weights, factors = [], []
            for head in range(per):
                row = group * per + head
                part = scores[:, head * tok : (head + 1) * tok] + bias
                top = jnp.max(part, axis=0, keepdims=True)
                if not fresh:
                    old = top_ref[row : row + 1, :]
                    top = jnp.maximum(top, old)
                    factors.append(jnp.exp2((old - top) * scale))
                weight = jnp.exp2((part - top) * scale)
                total = jnp.sum(weight, axis=0, keepdims=True)
                if not fresh:
                    total = total + total_ref[row : row + 1, :] * factors[head]
                top_ref[row : row + 1, :] = top
                total_ref[row : row + 1, :] = total
                weights.append(weight.astype(jnp.bfloat16))
            summed = dot(values[columns], jnp.concatenate(weights, axis=1))
            for head in range(per):
                rows = slice((group * per + head) * HD, (group * per + head + 1) * HD)
                piece = summed[head * HD : (head + 1) * HD, head * tok : (head + 1) * tok]
                if not fresh:
                    piece = piece + sum_ref[rows, :] * factors[head]
                sum_ref[rows, :] = piece

    for place, pair_ref in enumerate(pair_refs):
        block = block_ref[1 + place]
        if first and place == 0:
            fold(pair_ref, block, True)
        else:

            @pl.when(block >= 0)
            def unused(pair_ref=pair_ref, block=block):
                fold(pair_ref, block, False)


def attend_kernel(count, first, block_ref, lengths_ref, query_ref, *refs):
    pair_refs, refs = refs[:count], refs[count:]
    if not first:
        for old_ref, new_ref in zip(refs[0:3], refs[3:6]):
            new_ref[...] = old_ref[...]
        refs = refs[3:]
    attend_blocks(block_ref, lengths_ref, query_ref, pair_refs, refs[0:3], refs[3], first)


def mix_kernel(
    count,
    hot_capacity,
    block_ref,
    own_ref,
    lengths_ref,
    query_ref,
    choice_ref,
    residual_ref,
    proj_ref,
    *refs,
):
    pair_refs, refs = refs[:count], refs[count:]
    old_refs, mixed_ref, normed_ref = refs[0:3], refs[3], refs[4]
    sent_refs, state_refs, bias_ref = refs[5:-4], refs[-4:-1], refs[-1]
    for old_ref, new_ref in zip(old_refs, state_refs):
        new_ref[...] = old_ref[...]
    attend_blocks(block_ref, lengths_ref, query_ref, pair_refs, state_refs, bias_ref, False)
    unused_top, total_ref, sum_ref = state_refs
    pieces = [
        (sum_ref[head * HD : (head + 1) * HD, :] / total_ref[head : head + 1, :]).astype(
            jnp.bfloat16
        )
        for head in range(total_ref.shape[0])
    ]
    attended = jnp.concatenate(pieces, axis=0).T
    mixed = (residual_ref[...].astype(jnp.float32) + dot(attended, proj_ref[...])).astype(
        jnp.bfloat16
    )
    mixed_ref[...] = mixed
    mixed_f = mixed.astype(jnp.float32)
    inv_rms = lax.rsqrt(jnp.mean(mixed_f * mixed_f, axis=1, keepdims=True) + norm_eps)
    normed = (mixed_f * inv_rms).astype(jnp.bfloat16)
    normed_ref[...] = normed
    placed = slot_matrix(choice_ref[...], own_ref[0], len(sent_refs), hot_capacity)
    rows = dot(placed, normed).astype(jnp.bfloat16)
    for k, sent_ref in enumerate(sent_refs):
        sent_ref[...] = rows[k * hot_capacity : (k + 1) * hot_capacity]


def expert_kernel(
    reps,
    rep_list,
    sources,
    strip,
    counts,
    own_ref,
    part_ref,
    up_ref,
    down_ref,
    router_ref,
    *refs,
):
    row_count, grad_count = counts
    row_refs, refs = refs[:row_count], refs[row_count:]
    grad_refs, refs = refs[:grad_count], refs[grad_count:]
    own_rows = rep_list[0] == 0
    held_ref, refs = refs[-1], refs[:-1]
    if own_rows:
        back_refs, (up_acc, down_acc) = refs[:-2], refs[-2:]
    else:
        up_old, down_old = refs[:2]
        term_refs, kept_ref = refs[2:-1], refs[-1]
    total_grads = sum(ref.shape[0] for ref in grad_refs)
    capacity = total_grads // (sources * reps)
    count = sources * capacity
    parts = part_ref.shape[0]
    up = up_ref[...]
    down = down_ref[...]
    router = router_ref[...]
    expert_lane = lax.broadcasted_iota(jnp.int32, (count, router.shape[0]), 1) == own_ref[0]

    def strips(rows, place):
        held_ref[place] = rows.T
        taken = []
        for k in range(parts):
            first = pl.multiple_of(part_ref[k] * strip, strip)
            taken.append(held_ref[place, pl.ds(first, strip), :])
        return jnp.concatenate(taken, axis=0)

    up_term = down_term = None
    for place, rep in enumerate(rep_list):
        rows = chunk_rows(row_refs, sources, place * capacity, (place + 1) * capacity)
        grads = chunk_rows(grad_refs, sources, rep * capacity, (rep + 1) * capacity)
        pre = dot(rows, up)
        sigmoid_pre = jax.nn.sigmoid(pre)
        activated = (pre * sigmoid_pre).astype(jnp.bfloat16)
        logits = dot(rows, router, NT)
        gate = jax.nn.sigmoid(
            jnp.sum(jnp.where(expert_lane, logits, 0.0), axis=1, keepdims=True)
        )
        scaled = (gate * grads.astype(jnp.float32)).astype(jnp.bfloat16)
        act_grad = dot(scaled, down, NT)
        pre_grad = (act_grad * sigmoid_pre * (1.0 + pre * (1.0 - sigmoid_pre))).astype(
            jnp.bfloat16
        )
        if own_rows:
            produced = dot(activated, down).astype(jnp.bfloat16)
            token_grad = dot(pre_grad, up, NT).astype(jnp.bfloat16)
            for k, back_ref in enumerate(back_refs):
                back_ref[0:capacity] = produced[k * capacity : (k + 1) * capacity]
                back_ref[capacity : 2 * capacity] = token_grad[k * capacity : (k + 1) * capacity]
        more_up = dot(strips(rows, 2 * place), pre_grad)
        more_down = dot(strips(activated, 2 * place + 1), scaled)
        up_term = more_up if up_term is None else up_term + more_up
        down_term = more_down if down_term is None else down_term + more_down
    if own_rows:
        up_acc[...] = up_term
        down_acc[...] = down_term
        return
    up_term = up_term + up_old[...]
    down_term = down_term + down_old[...]
    for k in range(parts):
        rows = slice(k * strip, (k + 1) * strip)
        if k == 0:
            kept_ref[0] = up_term[rows]
            kept_ref[1] = down_term[rows]
        else:
            term_refs[k - 1][0] = up_term[rows].astype(jnp.bfloat16)
            term_refs[k - 1][1] = down_term[rows].astype(jnp.bfloat16)


def finish_kernel(
    hot_capacity, own_ref, choice_ref, router_ref, mixed_ref, grad_ref, *refs
):
    back_refs, (layer_ref, grad_mixed_ref) = refs[:-2], refs[-2:]
    expert_count = router_ref.shape[0]
    tok = mixed_ref.shape[0]
    choice = choice_ref[...]
    placed = slot_matrix(choice, own_ref[0], expert_count, hot_capacity)
    router = router_ref[...]
    mixed_f = mixed_ref[...].astype(jnp.float32)
    inv_rms = lax.rsqrt(jnp.mean(mixed_f * mixed_f, axis=1, keepdims=True) + norm_eps)
    normed = (mixed_f * inv_rms).astype(jnp.bfloat16)
    one_hot = lax.broadcasted_iota(jnp.int32, (expert_count, tok), 0) == choice
    logits = dot(router, normed, NT)
    logit_row = jnp.sum(jnp.where(one_hot, logits, 0.0), axis=0, keepdims=True)
    logit = jnp.broadcast_to(logit_row, (8, tok)).T[:, 0:1]
    gate = jax.nn.sigmoid(logit)
    pair = 2 * hot_capacity
    chunks = [
        ref[first : first + pair] for ref in back_refs for first in range(0, ref.shape[0], pair)
    ]
    results = jnp.concatenate([chunk[:hot_capacity] for chunk in chunks], axis=0)
    grads = jnp.concatenate([chunk[hot_capacity:] for chunk in chunks], axis=0)
    result_f = dot(placed, results, TN)
    normed_grad = dot(placed, grads, TN)
    grad_f = grad_ref[...].astype(jnp.float32)
    layer_ref[...] = (mixed_f + gate * result_f).astype(jnp.bfloat16)
    gate_grad = jnp.sum(grad_f * result_f, axis=1, keepdims=True)
    logit_grad = gate_grad * gate * (1.0 - gate)
    router_cols = dot(one_hot.astype(jnp.float32).astype(jnp.bfloat16), router, TN)
    total_grad = normed_grad + logit_grad * router_cols
    mean_term = jnp.mean(total_grad * mixed_f, axis=1, keepdims=True)
    input_grad = inv_rms * total_grad - mixed_f * inv_rms * inv_rms * inv_rms * mean_term
    grad_mixed_ref[...] = (grad_f + input_grad).astype(jnp.bfloat16)


def sum_kernel(kept_ref, *refs):
    term_refs, (up_ref, down_ref) = refs[:-2], refs[-2:]
    for kind, out_ref in enumerate((up_ref, down_ref)):
        total = kept_ref[kind]
        for ref in term_refs:
            total = total + ref[kind].astype(jnp.float32)
        out_ref[...] = total


def shape(dims, dtype=jnp.bfloat16):
    return jax.ShapeDtypeStruct(dims, dtype)


SMEM = pl.BlockSpec(memory_space=pltpu.SMEM)
VMEM = pl.BlockSpec(memory_space=pltpu.VMEM)
HBM = pl.BlockSpec(memory_space=pltpu.HBM)


def call(body, out_shape, specs, scratch=()):
    return pl.pallas_call(
        body,
        out_shape=out_shape,
        in_specs=specs,
        out_specs=jax.tree.map(lambda unused: VMEM, out_shape),
        scratch_shapes=list(scratch),
        compiler_params=pltpu.CompilerParams(vmem_limit_bytes=VMEM_LIMIT),
    )


def local(
    seq_count,
    expert_count,
    rep_count,
    query_rows,
    key_rows,
    value_rows,
    doc_lengths,
    residual,
    out_proj,
    router,
    expert_choice,
    weight_in,
    weight_out,
    grad_out,
):
    tok, width = query_rows.shape[1:]
    hidden = weight_in.shape[2]
    heads = width // HD
    experts = Group(("expert",), (expert_count,))
    reps = Group(("rep",), (rep_count,))
    parts = Group(("seq",), (seq_count,))
    strip = width // (seq_count * rep_count)
    capacity = max(2, (3 * tok + 2 * expert_count - 1) // (2 * expert_count))
    hot_capacity = min(4 * capacity, tok // 2)
    choice = expert_choice.reshape(1, tok)
    router_rows = router.T
    seq_index = lax.axis_index("seq")
    rep_index = lax.axis_index("rep")
    rank = seq_index * rep_count + rep_index
    own = jnp.stack([lax.axis_index("expert")]).astype(jnp.int32)
    part_to = jnp.stack(
        [parts.target(seq_index, k) * rep_count + rep_index for k in range(seq_count)]
    ).astype(jnp.int32)

    def send(array, least_seq, seq_step, rep_step, wrap):
        pairs = []
        for s in range(least_seq, seq_count - seq_step):
            for r in range(rep_count):
                to = r + rep_step
                if wrap or 0 <= to < rep_count:
                    pairs.append(
                        (s * rep_count + r, (s + seq_step) * rep_count + to % rep_count)
                    )
        return lax.ppermute(array, ("seq", "rep"), pairs)

    def block_ids(entries):
        ids = [rank]
        for seq_back, rep, needed in entries:
            block = (seq_index - seq_back) * rep_count + rep
            ids.append(jnp.where(needed & (seq_index >= seq_back), block, -1))
        return jnp.stack(ids).astype(jnp.int32)

    pair = call(
        stack_kernel,
        shape((2 * tok, width)),
        [HBM, HBM],
        [pltpu.SemaphoreType.DMA((2,))],
    )(key_rows[0], value_rows[0])
    always = rep_index >= 0
    reach = (seq_count + 1) // 2
    rounds = [([pair], [(0, rep_index, always)])]
    line = pair
    for step in range(1, reach + 1):
        arrays, entries = [], []
        ahead = send(line, step - 1, 1, 0, False)
        arrays.append(ahead)
        entries.append((step, rep_index, always))
        for d in range(1, rep_count):
            if step == 1:
                arrays.append(send(line, 0, 0, d, False))
                entries.append((0, rep_index - d, rep_index >= d))
            else:
                arrays.append(send(line, step - 1, 0, d, True))
                entries.append((step - 1, (rep_index - d) % rep_count, always))
            if step == reach:
                arrays.append(send(line, step - 1, 1, -d, False))
                entries.append((step, rep_index + d, rep_index + d < rep_count))
        rounds.append((arrays, entries))
        line = ahead

    choices = [choice] + [
        lax.ppermute(choice, "rep", [(i, reps.target(i, k)) for i in range(rep_count)])
        for k in range(1, rep_count)
    ]
    grads = reps.exchange([grad_out[0]] * rep_count)
    sent_grads = call(
        functools.partial(dispatch_kernel, rep_count, hot_capacity),
        [shape((rep_count * hot_capacity, width))] * expert_count,
        [SMEM] + [VMEM] * (2 * rep_count),
    )(own, *choices, *grads)
    got_grads = merged(experts.exchange(sent_grads), MOST_PERMUTES)

    state_shapes = [
        shape((heads, tok), jnp.float32),
        shape((heads, tok), jnp.float32),
        shape((width, tok), jnp.float32),
    ]
    bias = pltpu.VMEM((tok, tok), jnp.float32)
    query = query_rows[0]
    state = ()
    for place, (arrays, entries) in enumerate(rounds[:-1]):
        state = call(
            functools.partial(attend_kernel, len(arrays), place == 0),
            state_shapes,
            [SMEM, SMEM] + [VMEM] * (1 + len(arrays) + len(state)),
            [bias],
        )(block_ids(entries), doc_lengths, query, *arrays, *state)
    arrays, entries = rounds[-1]
    mixed, normed, *sent_rows = call(
        functools.partial(mix_kernel, len(arrays), hot_capacity),
        [shape((tok, width))] * 2 + [shape((hot_capacity, width))] * expert_count,
        [SMEM, SMEM, SMEM] + [VMEM] * (7 + len(arrays)),
        [pltpu.VMEM(one.shape, one.dtype) for one in state_shapes] + [bias],
    )(block_ids(entries), own, doc_lengths, query, choice, residual[0], out_proj, *arrays, *state)

    others = reps.exchange([normed] * rep_count)[1:]
    got_rows = merged(experts.exchange(sent_rows), MOST_PERMUTES)
    more_rows = call(
        functools.partial(dispatch_kernel, rep_count - 1, hot_capacity),
        [shape(((rep_count - 1) * hot_capacity, width))] * expert_count,
        [SMEM] + [VMEM] * (2 * (rep_count - 1)),
    )(own, *choices[1:], *others)
    got_more = merged(experts.exchange(more_rows), MOST_PERMUTES)

    def expert_call(rep_list, rows, out_shape, extra):
        return call(
            functools.partial(
                expert_kernel,
                rep_count,
                rep_list,
                expert_count,
                strip,
                (len(rows), len(got_grads)),
            ),
            out_shape,
            [SMEM, SMEM] + [VMEM] * (3 + len(rows) + len(got_grads) + len(extra)),
            [pltpu.VMEM((2 * len(rep_list), width, expert_count * hot_capacity), jnp.bfloat16)],
        )(own, part_to, weight_in[0], weight_out[0], router_rows, *rows, *got_grads, *extra)

    *back, up_acc, down_acc = expert_call(
        (0,),
        got_rows,
        [shape((2 * hot_capacity, width))] * expert_count
        + [shape((seq_count * strip, hidden), jnp.float32)]
        + [shape((seq_count * strip, width), jnp.float32)],
        [],
    )
    got_back = merged(experts.exchange(back, inverse=True), MOST_PERMUTES)
    *terms, kept = expert_call(
        tuple(range(1, rep_count)),
        got_more,
        [shape((2, strip, hidden))] * (seq_count - 1)
        + [shape((2, strip, hidden), jnp.float32)],
        [up_acc, down_acc],
    )
    got_terms = parts.exchange([None] + terms)[1:]
    layer_out, grad_mixed = call(
        functools.partial(finish_kernel, hot_capacity),
        [shape((tok, width)), shape((tok, width))],
        [SMEM] + [VMEM] * (4 + len(got_back)),
    )(own, choice, router_rows, mixed, grad_out[0], *got_back)
    share_in, share_out = call(
        sum_kernel,
        [shape((strip, hidden), jnp.float32), shape((strip, width), jnp.float32)],
        [VMEM] * seq_count,
    )(kept, *got_terms)
    return (layer_out[None], grad_mixed[None], share_in[None], share_out[None])


def solution(mesh):
    rows = P("expert", ("seq", "rep"), None)
    in_specs = (
        rows,
        rows,
        rows,
        P("expert", None),
        rows,
        P(),
        P(),
        rows,
        P("expert", None, None),
        P("expert", None, None),
        rows,
    )
    body = functools.partial(
        local, mesh.shape["seq"], mesh.shape["expert"], mesh.shape["rep"]
    )
    return jax.shard_map(
        body, mesh=mesh, in_specs=in_specs, out_specs=(rows, rows, rows, rows), check_vma=False
    )
```

```python
import functools
import math

import jax
import jax.numpy as jnp
from jax import lax
from jax.experimental import pallas as pl
from jax.experimental.pallas import tpu as pltpu
from jax.sharding import PartitionSpec as P

HD = 32
norm_eps = 1e-06
masked_score = -1e30
VMEM_LIMIT = 48 * 1024 * 1024
MOST_PERMUTES = 16
NT = (((1,), (1,)), ((), ()))
TN = (((0,), (0,)), ((), ()))


def dot(a, b, dims=None):
    if dims is None:
        return jnp.dot(a, b, preferred_element_type=jnp.float32)
    return lax.dot_general(a, b, dims, preferred_element_type=jnp.float32)


def away(index, offset, size):
    if size & (size - 1) == 0:
        return index ^ offset
    return (index + offset) % size


def back_from(index, offset, size):
    if size & (size - 1) == 0:
        return index ^ offset
    return (index - offset + size) % size


class Group:
    def __init__(self, axes, sizes):
        self.axes, self.sizes = tuple(axes), tuple(sizes)
        self.count = math.prod(sizes)

    def split(self, flat):
        coords = []
        for size in reversed(self.sizes):
            coords.append(flat % size)
            flat = flat // size
        return coords[::-1]

    def moved(self, flat, offset, step):
        place = 0
        for coord, part, size in zip(self.split(flat), self.split(offset), self.sizes):
            place = place * size + step(coord, part, size)
        return place

    def target(self, flat, offset):
        return self.moved(flat, offset, away)

    def source(self, flat, offset):
        return self.moved(flat, offset, back_from)

    def exchange(self, chunks, inverse=False):
        to, start = (self.source, self.target) if inverse else (self.target, self.source)
        if self.count <= MOST_PERMUTES:
            order = sorted(range(1, self.count), key=lambda k: -k)
            got = {0: chunks[0]}
            for k in order:
                pairs = [(i, to(i, k)) for i in range(self.count)]
                got[k] = lax.ppermute(chunks[k], self.axes, pairs)
            return [got[k] for k in range(self.count)]
        me = lax.axis_index(self.axes)
        steps = jnp.arange(self.count, dtype=jnp.int32)
        sent_to = jax.vmap(lambda k: to(me, k))(steps)
        placed = jnp.zeros((self.count,), jnp.int32).at[sent_to].set(steps)
        stacked = jnp.stack(chunks)[placed]
        got = lax.all_to_all(stacked, self.axes, split_axis=0, concat_axis=0, tiled=True)
        came_from = jax.vmap(lambda k: start(me, k))(steps)
        ordered = got[came_from]
        return [ordered[k] for k in range(self.count)]


def merged(chunks, most):
    if len(chunks) <= most:
        return list(chunks)
    return [jnp.concatenate(chunks, axis=0)]


def chunk_rows(refs, count, low, high):
    size = sum(ref.shape[0] for ref in refs) // count
    parts = []
    for chunk in range(count):
        ref, first = (refs[chunk], 0) if len(refs) == count else (refs[0], chunk * size)
        parts.append(ref[first + low : first + high, :])
    return parts[0] if count == 1 else jnp.concatenate(parts, axis=0)


def slot_matrix(choice, own, expert_count, hot_capacity):
    tok = choice.shape[1]
    offset = back_from(choice, own, expert_count)
    one_hot = lax.broadcasted_iota(jnp.int32, (expert_count, tok), 0) == offset
    hits = one_hot.astype(jnp.float32).astype(jnp.bfloat16)
    earlier = lax.broadcasted_iota(jnp.int32, (tok, tok), 0) <= lax.broadcasted_iota(
        jnp.int32, (tok, tok), 1
    )
    counted = dot(hits, earlier.astype(jnp.float32).astype(jnp.bfloat16))
    rank = jnp.sum(jnp.where(one_hot, counted, 0.0), axis=0, keepdims=True) - 1.0
    slots = offset * hot_capacity + rank.astype(jnp.int32)
    rows = lax.broadcasted_iota(jnp.int32, (expert_count * hot_capacity, tok), 0)
    return (rows == slots).astype(jnp.float32).astype(jnp.bfloat16)


def stack_kernel(
    rank_ref,
    choice_ref,
    lengths_ref,
    router_ref,
    key_ref,
    value_ref,
    grad_ref,
    pair_ref,
    extended_ref,
    begin_ref,
    chosen_ref,
    held_router_ref,
    held_lengths_ref,
    sems,
):
    tok, width = key_ref.shape
    targets = (
        (choice_ref, chosen_ref),
        (lengths_ref, held_lengths_ref),
        (key_ref, pair_ref.at[pl.ds(0, tok), :]),
        (value_ref, pair_ref.at[pl.ds(tok, tok), :]),
        (grad_ref, extended_ref.at[pl.ds(0, tok), :]),
        (router_ref, held_router_ref),
    )
    copies = [
        pltpu.make_async_copy(source, target, sems.at[place])
        for place, (source, target) in enumerate(targets)
    ]
    for copy in copies:
        copy.start()
    copies[0].wait()
    chosen = jnp.broadcast_to(chosen_ref[...].astype(jnp.float32), (16, tok))
    extended_ref[tok : tok + 16, 0:tok] = chosen.astype(jnp.bfloat16)
    extended_ref[tok : tok + 16, tok:width] = jnp.zeros((16, width - tok), jnp.bfloat16)
    copies[1].wait()
    position = rank_ref[0] * tok + lax.broadcasted_iota(jnp.int32, (1, tok), 1)
    begin = jnp.zeros((1, tok), jnp.int32)
    bound = jnp.int32(0)
    for doc in range(held_lengths_ref.shape[1] - 1):
        bound = bound + held_lengths_ref[0, doc]
        begin = jnp.maximum(begin, jnp.where(position >= bound, bound, 0))
    begin_ref[...] = begin
    copies[5].wait()
    routed = held_router_ref[...].astype(jnp.float32)
    spare = extended_ref.shape[0] - tok - 16 - routed.shape[0]
    if spare:
        routed = jnp.concatenate([routed, jnp.zeros((spare, width), jnp.float32)], axis=0)
    extended_ref[tok + 16 :, :] = routed.astype(jnp.bfloat16)
    for copy in copies[2:5]:
        copy.wait()


def chosen_of(extended_ref, tok):
    return extended_ref[tok : tok + 16, 0:tok].astype(jnp.float32)[0:1].astype(jnp.int32)


def router_of(extended_ref, tok, expert_count):
    whole = extended_ref[tok + 16 :, :].astype(jnp.float32)
    return whole[0:expert_count].astype(jnp.bfloat16)


def dispatch_kernel(reps, tok, hot_capacity, own_ref, *refs):
    extended_refs, row_refs, sent_refs = refs[:reps], refs[reps : 2 * reps], refs[2 * reps :]
    for rep in range(reps):
        choice = chosen_of(extended_refs[rep], tok)
        placed = slot_matrix(choice, own_ref[0], len(sent_refs), hot_capacity)
        rows = dot(placed, row_refs[rep][0:tok, :]).astype(jnp.bfloat16)
        for k, sent_ref in enumerate(sent_refs):
            sent_ref[rep * hot_capacity : (rep + 1) * hot_capacity] = rows[
                k * hot_capacity : (k + 1) * hot_capacity
            ]


def attend_blocks(block_ref, begin_ref, query_ref, pair_refs, state_refs, bias_ref, first):
    top_ref, total_ref, sum_ref = state_refs
    tok, width = query_ref.shape
    lanes = 128
    per = lanes // HD
    scale = math.log2(math.e) / math.sqrt(HD)
    turned = query_ref[...].T
    head_of_row = lax.broadcasted_iota(jnp.int32, (lanes, tok), 0) // HD
    spread = []
    for group in range(width // lanes):
        part = turned[group * lanes : (group + 1) * lanes]
        spread.append(
            jnp.concatenate(
                [jnp.where(head_of_row == head, part, jnp.zeros_like(part)) for head in range(per)],
                axis=1,
            )
        )
    position = block_ref[0] * tok + lax.broadcasted_iota(jnp.int32, (1, tok), 1)
    begin = begin_ref[...]
    lowest = jnp.min(begin)

    def fold(pair_ref, block, fresh):
        key_position = block * tok + lax.broadcasted_iota(jnp.int32, (tok, tok), 0)
        visible = (key_position >= begin) & (key_position <= position)
        bias_ref[...] = jnp.where(visible, 0.0, masked_score)
        bias = bias_ref[...]
        values = pair_ref[tok : 2 * tok, :].T
        for group in range(width // lanes):
            columns = slice(group * lanes, (group + 1) * lanes)
            scores = dot(pair_ref[0:tok, columns], spread[group])
            weights, factors = [], []
            for head in range(per):
                row = group * per + head
                part = scores[:, head * tok : (head + 1) * tok] + bias
                top = jnp.max(part, axis=0, keepdims=True)
                if not fresh:
                    old = top_ref[row : row + 1, :]
                    top = jnp.maximum(top, old)
                    factors.append(jnp.exp2((old - top) * scale))
                weight = jnp.exp2((part - top) * scale)
                total = jnp.sum(weight, axis=0, keepdims=True)
                if not fresh:
                    total = total + total_ref[row : row + 1, :] * factors[head]
                top_ref[row : row + 1, :] = top
                total_ref[row : row + 1, :] = total
                weights.append(weight.astype(jnp.bfloat16))
            summed = dot(values[columns], jnp.concatenate(weights, axis=1))
            for head in range(per):
                rows = slice((group * per + head) * HD, (group * per + head + 1) * HD)
                piece = summed[head * HD : (head + 1) * HD, head * tok : (head + 1) * tok]
                if not fresh:
                    piece = piece + sum_ref[rows, :] * factors[head]
                sum_ref[rows, :] = piece

    for place, pair_ref in enumerate(pair_refs):
        block = block_ref[1 + place]
        if first and place == 0:
            fold(pair_ref, block, True)
        else:

            @pl.when((block >= 0) & ((block + 1) * tok > lowest))
            def unused(pair_ref=pair_ref, block=block):
                fold(pair_ref, block, False)


def attend_kernel(count, first, block_ref, begin_ref, query_ref, *refs):
    pair_refs, refs = refs[:count], refs[count:]
    if not first:
        for old_ref, new_ref in zip(refs[0:3], refs[3:6]):
            new_ref[...] = old_ref[...]
        refs = refs[3:]
    attend_blocks(block_ref, begin_ref, query_ref, pair_refs, refs[0:3], refs[3], first)


def mix_kernel(count, block_ref, begin_ref, query_ref, residual_ref, proj_ref, *refs):
    pair_refs, refs = refs[:count], refs[count:]
    old_refs, mixed_ref, normed_ref = refs[0:3], refs[3], refs[4]
    state_refs, bias_ref = refs[-4:-1], refs[-1]
    for old_ref, new_ref in zip(old_refs, state_refs):
        new_ref[...] = old_ref[...]
    attend_blocks(block_ref, begin_ref, query_ref, pair_refs, state_refs, bias_ref, False)
    unused_top, total_ref, sum_ref = state_refs
    pieces = [
        (sum_ref[head * HD : (head + 1) * HD, :] / total_ref[head : head + 1, :]).astype(
            jnp.bfloat16
        )
        for head in range(total_ref.shape[0])
    ]
    attended = jnp.concatenate(pieces, axis=0).T
    mixed = (residual_ref[...].astype(jnp.float32) + dot(attended, proj_ref[...])).astype(
        jnp.bfloat16
    )
    mixed_ref[...] = mixed
    mixed_f = mixed.astype(jnp.float32)
    inv_rms = lax.rsqrt(jnp.mean(mixed_f * mixed_f, axis=1, keepdims=True) + norm_eps)
    normed = (mixed_f * inv_rms).astype(jnp.bfloat16)
    normed_ref[...] = normed


def expert_kernel(
    reps,
    rep_list,
    sources,
    tok,
    strip,
    counts,
    own_ref,
    part_ref,
    up_ref,
    down_ref,
    extended_ref,
    *refs,
):
    row_count, grad_count = counts
    row_refs, refs = refs[:row_count], refs[row_count:]
    grad_refs, refs = refs[:grad_count], refs[grad_count:]
    own_rows = rep_list[0] == 0
    held_ref, refs = refs[-1], refs[:-1]
    if own_rows:
        back_refs, (up_acc, down_acc) = refs[:-2], refs[-2:]
    else:
        up_old, down_old = refs[:2]
        term_refs, kept_ref = refs[2:-1], refs[-1]
    total_grads = sum(ref.shape[0] for ref in grad_refs)
    capacity = total_grads // (sources * reps)
    count = sources * capacity
    parts = part_ref.shape[0]
    up = up_ref[...]
    down = down_ref[...]
    router = router_of(extended_ref, tok, sources)
    expert_lane = lax.broadcasted_iota(jnp.int32, (count, router.shape[0]), 1) == own_ref[0]

    def strips(rows, place):
        held_ref[place] = rows.T
        taken = []
        for k in range(parts):
            first = pl.multiple_of(part_ref[k] * strip, strip)
            taken.append(held_ref[place, pl.ds(first, strip), :])
        return jnp.concatenate(taken, axis=0)

    up_term = down_term = None
    for place, rep in enumerate(rep_list):
        rows = chunk_rows(row_refs, sources, place * capacity, (place + 1) * capacity)
        grads = chunk_rows(grad_refs, sources, rep * capacity, (rep + 1) * capacity)
        pre = dot(rows, up)
        sigmoid_pre = jax.nn.sigmoid(pre)
        activated = (pre * sigmoid_pre).astype(jnp.bfloat16)
        logits = dot(rows, router, NT)
        gate = jax.nn.sigmoid(
            jnp.sum(jnp.where(expert_lane, logits, 0.0), axis=1, keepdims=True)
        )
        scaled = (gate * grads.astype(jnp.float32)).astype(jnp.bfloat16)
        act_grad = dot(scaled, down, NT)
        pre_grad = (act_grad * sigmoid_pre * (1.0 + pre * (1.0 - sigmoid_pre))).astype(
            jnp.bfloat16
        )
        if own_rows:
            produced = dot(activated, down).astype(jnp.bfloat16)
            token_grad = dot(pre_grad, up, NT).astype(jnp.bfloat16)
            for k, back_ref in enumerate(back_refs):
                back_ref[0:capacity] = produced[k * capacity : (k + 1) * capacity]
                back_ref[capacity : 2 * capacity] = token_grad[k * capacity : (k + 1) * capacity]
        more_up = dot(strips(rows, 2 * place), pre_grad)
        more_down = dot(strips(activated, 2 * place + 1), scaled)
        up_term = more_up if up_term is None else up_term + more_up
        down_term = more_down if down_term is None else down_term + more_down
    if own_rows:
        up_acc[...] = up_term
        down_acc[...] = down_term
        return
    up_term = up_term + up_old[...]
    down_term = down_term + down_old[...]
    for k in range(parts):
        rows = slice(k * strip, (k + 1) * strip)
        if k == 0:
            kept_ref[0] = up_term[rows]
            kept_ref[1] = down_term[rows]
        else:
            term_refs[k - 1][0] = up_term[rows].astype(jnp.bfloat16)
            term_refs[k - 1][1] = down_term[rows].astype(jnp.bfloat16)


def finish_kernel(
    hot_capacity, expert_count, own_ref, mixed_ref, extended_ref, *refs
):
    back_refs, (layer_ref, grad_mixed_ref) = refs[:-2], refs[-2:]
    tok = mixed_ref.shape[0]
    choice = chosen_of(extended_ref, tok)
    placed = slot_matrix(choice, own_ref[0], expert_count, hot_capacity)
    router = router_of(extended_ref, tok, expert_count)
    mixed_f = mixed_ref[...].astype(jnp.float32)
    inv_rms = lax.rsqrt(jnp.mean(mixed_f * mixed_f, axis=1, keepdims=True) + norm_eps)
    normed = (mixed_f * inv_rms).astype(jnp.bfloat16)
    one_hot = lax.broadcasted_iota(jnp.int32, (expert_count, tok), 0) == choice
    logits = dot(router, normed, NT)
    logit_row = jnp.sum(jnp.where(one_hot, logits, 0.0), axis=0, keepdims=True)
    logit = jnp.broadcast_to(logit_row, (8, tok)).T[:, 0:1]
    gate = jax.nn.sigmoid(logit)
    pair = 2 * hot_capacity
    chunks = [
        ref[first : first + pair] for ref in back_refs for first in range(0, ref.shape[0], pair)
    ]
    results = jnp.concatenate([chunk[:hot_capacity] for chunk in chunks], axis=0)
    grads = jnp.concatenate([chunk[hot_capacity:] for chunk in chunks], axis=0)
    result_f = dot(placed, results, TN)
    normed_grad = dot(placed, grads, TN)
    grad_f = extended_ref[0:tok, :].astype(jnp.float32)
    layer_ref[...] = (mixed_f + gate * result_f).astype(jnp.bfloat16)
    gate_grad = jnp.sum(grad_f * result_f, axis=1, keepdims=True)
    logit_grad = gate_grad * gate * (1.0 - gate)
    router_cols = dot(one_hot.astype(jnp.float32).astype(jnp.bfloat16), router, TN)
    total_grad = normed_grad + logit_grad * router_cols
    mean_term = jnp.mean(total_grad * mixed_f, axis=1, keepdims=True)
    input_grad = inv_rms * total_grad - mixed_f * inv_rms * inv_rms * inv_rms * mean_term
    grad_mixed_ref[...] = (grad_f + input_grad).astype(jnp.bfloat16)


def sum_kernel(kept_ref, *refs):
    term_refs, (up_ref, down_ref) = refs[:-2], refs[-2:]
    for kind, out_ref in enumerate((up_ref, down_ref)):
        total = kept_ref[kind]
        for ref in term_refs:
            total = total + ref[kind].astype(jnp.float32)
        out_ref[...] = total


def shape(dims, dtype=jnp.bfloat16):
    return jax.ShapeDtypeStruct(dims, dtype)


SMEM = pl.BlockSpec(memory_space=pltpu.SMEM)
VMEM = pl.BlockSpec(memory_space=pltpu.VMEM)
HBM = pl.BlockSpec(memory_space=pltpu.HBM)


def call(body, out_shape, specs, scratch=(), cost=0.5):
    return pl.pallas_call(
        body,
        cost_estimate=pl.CostEstimate(
            flops=int(cost * 1e9), bytes_accessed=0, transcendentals=0
        ),
        out_shape=out_shape,
        in_specs=specs,
        out_specs=jax.tree.map(lambda unused: VMEM, out_shape),
        scratch_shapes=list(scratch),
        compiler_params=pltpu.CompilerParams(vmem_limit_bytes=VMEM_LIMIT),
    )


def local(
    seq_count,
    expert_count,
    rep_count,
    query_rows,
    key_rows,
    value_rows,
    doc_lengths,
    residual,
    out_proj,
    router,
    expert_choice,
    weight_in,
    weight_out,
    grad_out,
):
    tok, width = query_rows.shape[1:]
    hidden = weight_in.shape[2]
    heads = width // HD
    experts = Group(("expert",), (expert_count,))
    reps = Group(("rep",), (rep_count,))
    parts = Group(("seq",), (seq_count,))
    strip = width // (seq_count * rep_count)
    capacity = max(2, (3 * tok + 2 * expert_count - 1) // (2 * expert_count))
    hot_capacity = min(4 * capacity, tok // 2)
    choice = expert_choice.reshape(1, tok)
    seq_index = lax.axis_index("seq")
    rep_index = lax.axis_index("rep")
    rank = seq_index * rep_count + rep_index
    own = jnp.stack([lax.axis_index("expert")]).astype(jnp.int32)
    part_to = jnp.stack(
        [parts.target(seq_index, k) * rep_count + rep_index for k in range(seq_count)]
    ).astype(jnp.int32)

    def send(array, least_seq, seq_step, rep_step, wrap):
        pairs = []
        for s in range(least_seq, seq_count - seq_step):
            for r in range(rep_count):
                to = r + rep_step
                if wrap or 0 <= to < rep_count:
                    pairs.append(
                        (s * rep_count + r, (s + seq_step) * rep_count + to % rep_count)
                    )
        return lax.ppermute(array, ("seq", "rep"), pairs)

    def block_ids(entries):
        ids = [rank]
        for seq_back, rep, needed in entries:
            block = (seq_index - seq_back) * rep_count + rep
            ids.append(jnp.where(needed & (seq_index >= seq_back), block, -1))
        return jnp.stack(ids).astype(jnp.int32)

    state_shapes = [
        shape((heads, tok), jnp.float32),
        shape((heads, tok), jnp.float32),
        shape((width, tok), jnp.float32),
    ]
    bias = pltpu.VMEM((tok, tok), jnp.float32)
    query = query_rows[0]

    def attend(blocks, state):
        arrays, entries = blocks
        return call(
            functools.partial(attend_kernel, len(arrays), not state),
            state_shapes,
            [SMEM] + [VMEM] * (2 + len(arrays) + len(state)),
            [bias],
            cost=2.0,
        )(block_ids(entries), begin, query, *arrays, *state)

    pair, extended, begin = pl.pallas_call(
        stack_kernel,
        out_shape=[
            shape((2 * tok, width)),
            shape((tok + 16 + -(-expert_count // 16) * 16, width)),
            shape((1, tok), jnp.int32),
        ],
        in_specs=[SMEM] + [HBM] * 6,
        out_specs=[VMEM] * 3,
        scratch_shapes=[
            pltpu.VMEM((1, tok), jnp.int32),
            pltpu.VMEM((expert_count, width), jnp.bfloat16),
            pltpu.SMEM(doc_lengths.shape, jnp.int32),
            pltpu.SemaphoreType.DMA((6,)),
        ],
        compiler_params=pltpu.CompilerParams(vmem_limit_bytes=60 * 1024 * 1024),
    )(
        jnp.stack([rank]).astype(jnp.int32),
        choice,
        doc_lengths,
        router.T,
        key_rows[0],
        value_rows[0],
        grad_out[0],
    )
    always = rep_index >= 0
    reach = (seq_count + 1) // 2
    rounds = [([pair], [(0, rep_index, always)])]
    line = pair
    extendeds = None
    state = ()
    for step in range(1, reach + 1):
        ahead = send(line, step - 1, 1, 0, False)
        arrays, entries = [ahead], [(step, rep_index, always)]
        for d in range(1, rep_count):
            if step == reach:
                arrays.append(send(line, step - 1, 1, -d, False))
                entries.append((step, rep_index + d, rep_index + d < rep_count))
            if step == 1:
                arrays.append(send(line, 0, 0, d, False))
                entries.append((0, rep_index - d, rep_index >= d))
            else:
                arrays.append(send(line, step - 1, 0, d, True))
                entries.append((step - 1, (rep_index - d) % rep_count, always))
        if step == 1:
            extendeds = reps.exchange([extended] * rep_count)
        state = attend(rounds[-1], state)
        rounds.append((arrays, entries))
        if step < reach:
            line, *held = lax.optimization_barrier((ahead, *state, *extendeds))
            arrays[0], state, extendeds = line, held[:3], held[3:]

    *state, pinned = lax.optimization_barrier((*state, extendeds[0]))
    extendeds = [pinned] + list(extendeds[1:])
    sent_grads = call(
        functools.partial(dispatch_kernel, rep_count, tok, hot_capacity),
        [shape((rep_count * hot_capacity, width))] * expert_count,
        [SMEM] + [VMEM] * (2 * rep_count),
    )(own, *extendeds, *extendeds)
    got_grads = merged(experts.exchange(sent_grads), MOST_PERMUTES)

    arrays, entries = rounds[-1]
    mixed, normed = call(
        functools.partial(mix_kernel, len(arrays)),
        [shape((tok, width))] * 2,
        [SMEM] + [VMEM] * (7 + len(arrays)),
        [pltpu.VMEM(one.shape, one.dtype) for one in state_shapes] + [bias],
        cost=5.0,
    )(block_ids(entries), begin, query, residual[0], out_proj, *arrays, *state)

    normed, got_grads = lax.optimization_barrier((normed, got_grads))

    def dispatch(own_arrays, rows):
        return call(
            functools.partial(dispatch_kernel, len(rows), tok, hot_capacity),
            [shape((len(rows) * hot_capacity, width))] * expert_count,
            [SMEM] + [VMEM] * (2 * len(rows)),
        )(own, *own_arrays, *rows)

    others = reps.exchange([normed] * rep_count)[1:]
    got_rows = merged(experts.exchange(dispatch(extendeds[:1], [normed])), MOST_PERMUTES)
    more_rows = dispatch(extendeds[1:], others)
    more_rows, got_rows = lax.optimization_barrier((more_rows, got_rows))
    got_more = merged(experts.exchange(more_rows), MOST_PERMUTES)

    def expert_call(rep_list, rows, out_shape, extra):
        return call(
            functools.partial(
                expert_kernel,
                rep_count,
                rep_list,
                expert_count,
                tok,
                strip,
                (len(rows), len(got_grads)),
            ),
            out_shape,
            [SMEM, SMEM] + [VMEM] * (3 + len(rows) + len(got_grads) + len(extra)),
            [pltpu.VMEM((2 * len(rep_list), width, expert_count * hot_capacity), jnp.bfloat16)],
            cost=2.0,
        )(own, part_to, weight_in[0], weight_out[0], extendeds[0], *rows, *got_grads, *extra)

    *back, up_acc, down_acc = expert_call(
        (0,),
        got_rows,
        [shape((2 * hot_capacity, width))] * expert_count
        + [shape((seq_count * strip, hidden), jnp.float32)]
        + [shape((seq_count * strip, width), jnp.float32)],
        [],
    )
    got_back = merged(experts.exchange(back, inverse=True), MOST_PERMUTES)
    *terms, kept = expert_call(
        tuple(range(1, rep_count)),
        got_more,
        [shape((2, strip, hidden))] * (seq_count - 1)
        + [shape((2, strip, hidden), jnp.float32)],
        [up_acc, down_acc],
    )
    got_terms = parts.exchange([None] + terms)[1:]
    layer_out, grad_mixed = call(
        functools.partial(finish_kernel, hot_capacity, expert_count),
        [shape((tok, width)), shape((tok, width))],
        [SMEM] + [VMEM] * (2 + len(got_back)),
        cost=1.5,
    )(own, mixed, extended, *got_back)
    share_in, share_out = call(
        sum_kernel,
        [shape((strip, hidden), jnp.float32), shape((strip, width), jnp.float32)],
        [VMEM] * seq_count,
    )(kept, *got_terms)
    return (layer_out[None], grad_mixed[None], share_in[None], share_out[None])


def solution(mesh):
    rows = P("expert", ("seq", "rep"), None)
    in_specs = (
        rows,
        rows,
        rows,
        P("expert", None),
        rows,
        P(),
        P(),
        rows,
        P("expert", None, None),
        P("expert", None, None),
        rows,
    )
    body = functools.partial(
        local, mesh.shape["seq"], mesh.shape["expert"], mesh.shape["rep"]
    )
    return jax.shard_map(
        body, mesh=mesh, in_specs=in_specs, out_specs=(rows, rows, rows, rows), check_vma=False
    )
```

```python
import functools
import math

import jax
import jax.numpy as jnp
from jax import lax
from jax.experimental import pallas as pl
from jax.experimental.pallas import tpu as pltpu
from jax.sharding import PartitionSpec as P

HD = 32
norm_eps = 1e-06
masked_score = -1e30
VMEM_LIMIT = 48 * 1024 * 1024
MOST_PERMUTES = 16
NT = (((1,), (1,)), ((), ()))
TN = (((0,), (0,)), ((), ()))


def dot(a, b, dims=None):
    if dims is None:
        return jnp.dot(a, b, preferred_element_type=jnp.float32)
    return lax.dot_general(a, b, dims, preferred_element_type=jnp.float32)


def away(index, offset, size):
    if size & (size - 1) == 0:
        return index ^ offset
    return (index + offset) % size


def back_from(index, offset, size):
    if size & (size - 1) == 0:
        return index ^ offset
    return (index - offset + size) % size


class Group:
    def __init__(self, axes, sizes):
        self.axes, self.sizes = tuple(axes), tuple(sizes)
        self.count = math.prod(sizes)

    def split(self, flat):
        coords = []
        for size in reversed(self.sizes):
            coords.append(flat % size)
            flat = flat // size
        return coords[::-1]

    def moved(self, flat, offset, step):
        place = 0
        for coord, part, size in zip(self.split(flat), self.split(offset), self.sizes):
            place = place * size + step(coord, part, size)
        return place

    def target(self, flat, offset):
        return self.moved(flat, offset, away)

    def source(self, flat, offset):
        return self.moved(flat, offset, back_from)

    def exchange(self, chunks, inverse=False):
        to, start = (self.source, self.target) if inverse else (self.target, self.source)
        if self.count <= MOST_PERMUTES:
            order = sorted(range(1, self.count), key=lambda k: -k)
            got = {0: chunks[0]}
            for k in order:
                pairs = [(i, to(i, k)) for i in range(self.count)]
                got[k] = lax.ppermute(chunks[k], self.axes, pairs)
            return [got[k] for k in range(self.count)]
        me = lax.axis_index(self.axes)
        steps = jnp.arange(self.count, dtype=jnp.int32)
        sent_to = jax.vmap(lambda k: to(me, k))(steps)
        placed = jnp.zeros((self.count,), jnp.int32).at[sent_to].set(steps)
        stacked = jnp.stack(chunks)[placed]
        got = lax.all_to_all(stacked, self.axes, split_axis=0, concat_axis=0, tiled=True)
        came_from = jax.vmap(lambda k: start(me, k))(steps)
        ordered = got[came_from]
        return [ordered[k] for k in range(self.count)]


def merged(chunks, most):
    if len(chunks) <= most:
        return list(chunks)
    return [jnp.concatenate(chunks, axis=0)]


def chunk_rows(refs, count, low, high):
    size = sum(ref.shape[0] for ref in refs) // count
    parts = []
    for chunk in range(count):
        ref, first = (refs[chunk], 0) if len(refs) == count else (refs[0], chunk * size)
        parts.append(ref[first + low : first + high, :])
    return parts[0] if count == 1 else jnp.concatenate(parts, axis=0)


def slot_matrix(choice, own, expert_count, hot_capacity):
    tok = choice.shape[1]
    offset = back_from(choice, own, expert_count)
    one_hot = lax.broadcasted_iota(jnp.int32, (expert_count, tok), 0) == offset
    hits = one_hot.astype(jnp.float32).astype(jnp.bfloat16)
    earlier = lax.broadcasted_iota(jnp.int32, (tok, tok), 0) <= lax.broadcasted_iota(
        jnp.int32, (tok, tok), 1
    )
    counted = dot(hits, earlier.astype(jnp.float32).astype(jnp.bfloat16))
    rank = jnp.sum(jnp.where(one_hot, counted, 0.0), axis=0, keepdims=True) - 1.0
    slots = offset * hot_capacity + rank.astype(jnp.int32)
    rows = lax.broadcasted_iota(jnp.int32, (expert_count * hot_capacity, tok), 0)
    return (rows == slots).astype(jnp.float32).astype(jnp.bfloat16)


def stack_kernel(
    rank_ref,
    choice_ref,
    lengths_ref,
    router_ref,
    key_ref,
    value_ref,
    grad_ref,
    pair_ref,
    extended_ref,
    begin_ref,
    chosen_ref,
    held_router_ref,
    held_lengths_ref,
    sems,
):
    tok, width = key_ref.shape
    targets = (
        (choice_ref, chosen_ref),
        (lengths_ref, held_lengths_ref),
        (key_ref, pair_ref.at[pl.ds(0, tok), :]),
        (value_ref, pair_ref.at[pl.ds(tok, tok), :]),
        (grad_ref, extended_ref.at[pl.ds(0, tok), :]),
        (router_ref, held_router_ref),
    )
    copies = [
        pltpu.make_async_copy(source, target, sems.at[place])
        for place, (source, target) in enumerate(targets)
    ]
    for copy in copies:
        copy.start()
    copies[0].wait()
    chosen = jnp.broadcast_to(chosen_ref[...].astype(jnp.float32), (16, tok))
    extended_ref[tok : tok + 16, 0:tok] = chosen.astype(jnp.bfloat16)
    extended_ref[tok : tok + 16, tok:width] = jnp.zeros((16, width - tok), jnp.bfloat16)
    copies[1].wait()
    position = rank_ref[0] * tok + lax.broadcasted_iota(jnp.int32, (1, tok), 1)
    begin = jnp.zeros((1, tok), jnp.int32)
    bound = jnp.int32(0)
    for doc in range(held_lengths_ref.shape[1] - 1):
        bound = bound + held_lengths_ref[0, doc]
        begin = jnp.maximum(begin, jnp.where(position >= bound, bound, 0))
    begin_ref[...] = begin
    copies[5].wait()
    routed = held_router_ref[...].astype(jnp.float32)
    spare = extended_ref.shape[0] - tok - 16 - routed.shape[0]
    if spare:
        routed = jnp.concatenate([routed, jnp.zeros((spare, width), jnp.float32)], axis=0)
    extended_ref[tok + 16 :, :] = routed.astype(jnp.bfloat16)
    for copy in copies[2:5]:
        copy.wait()


def chosen_of(extended_ref, tok):
    return extended_ref[tok : tok + 16, 0:tok].astype(jnp.float32)[0:1].astype(jnp.int32)


def router_of(extended_ref, tok, expert_count):
    whole = extended_ref[tok + 16 :, :].astype(jnp.float32)
    return whole[0:expert_count].astype(jnp.bfloat16)


def dispatch_kernel(reps, tok, hot_capacity, own_ref, *refs):
    extended_refs, row_refs, sent_refs = refs[:reps], refs[reps : 2 * reps], refs[2 * reps :]
    for rep in range(reps):
        choice = chosen_of(extended_refs[rep], tok)
        placed = slot_matrix(choice, own_ref[0], len(sent_refs), hot_capacity)
        rows = dot(placed, row_refs[rep][0:tok, :]).astype(jnp.bfloat16)
        for k, sent_ref in enumerate(sent_refs):
            sent_ref[rep * hot_capacity : (rep + 1) * hot_capacity] = rows[
                k * hot_capacity : (k + 1) * hot_capacity
            ]


def attend_blocks(block_ref, begin_ref, query_ref, pair_refs, state_refs, bias_ref, first):
    top_ref, total_ref, sum_ref = state_refs
    tok, width = query_ref.shape
    lanes = 128
    per = lanes // HD
    scale = math.log2(math.e) / math.sqrt(HD)
    turned = query_ref[...].T
    head_of_row = lax.broadcasted_iota(jnp.int32, (lanes, tok), 0) // HD
    spread = []
    for group in range(width // lanes):
        part = turned[group * lanes : (group + 1) * lanes]
        spread.append(
            jnp.concatenate(
                [jnp.where(head_of_row == head, part, jnp.zeros_like(part)) for head in range(per)],
                axis=1,
            )
        )
    position = block_ref[0] * tok + lax.broadcasted_iota(jnp.int32, (1, tok), 1)
    begin = begin_ref[...]
    lowest = jnp.min(begin)

    def fold(pair_ref, block, fresh):
        key_position = block * tok + lax.broadcasted_iota(jnp.int32, (tok, tok), 0)
        visible = (key_position >= begin) & (key_position <= position)
        bias_ref[...] = jnp.where(visible, 0.0, masked_score)
        bias = bias_ref[...]
        values = pair_ref[tok : 2 * tok, :].T
        for group in range(width // lanes):
            columns = slice(group * lanes, (group + 1) * lanes)
            scores = dot(pair_ref[0:tok, columns], spread[group])
            weights, factors = [], []
            for head in range(per):
                row = group * per + head
                part = scores[:, head * tok : (head + 1) * tok] + bias
                top = jnp.max(part, axis=0, keepdims=True)
                if not fresh:
                    old = top_ref[row : row + 1, :]
                    top = jnp.maximum(top, old)
                    factors.append(jnp.exp2((old - top) * scale))
                weight = jnp.exp2((part - top) * scale)
                total = jnp.sum(weight, axis=0, keepdims=True)
                if not fresh:
                    total = total + total_ref[row : row + 1, :] * factors[head]
                top_ref[row : row + 1, :] = top
                total_ref[row : row + 1, :] = total
                weights.append(weight.astype(jnp.bfloat16))
            summed = dot(values[columns], jnp.concatenate(weights, axis=1))
            for head in range(per):
                rows = slice((group * per + head) * HD, (group * per + head + 1) * HD)
                piece = summed[head * HD : (head + 1) * HD, head * tok : (head + 1) * tok]
                if not fresh:
                    piece = piece + sum_ref[rows, :] * factors[head]
                sum_ref[rows, :] = piece

    for place, pair_ref in enumerate(pair_refs):
        block = block_ref[1 + place]
        if first and place == 0:
            fold(pair_ref, block, True)
        else:

            @pl.when((block >= 0) & ((block + 1) * tok > lowest))
            def unused(pair_ref=pair_ref, block=block):
                fold(pair_ref, block, False)


def attend_kernel(count, first, block_ref, begin_ref, query_ref, *refs):
    pair_refs, refs = refs[:count], refs[count:]
    if not first:
        for old_ref, new_ref in zip(refs[0:3], refs[3:6]):
            new_ref[...] = old_ref[...]
        refs = refs[3:]
    attend_blocks(block_ref, begin_ref, query_ref, pair_refs, refs[0:3], refs[3], first)


def mix_kernel(count, block_ref, begin_ref, query_ref, residual_ref, proj_ref, *refs):
    pair_refs, refs = refs[:count], refs[count:]
    old_refs, mixed_ref, normed_ref = refs[0:3], refs[3], refs[4]
    state_refs, bias_ref = refs[-4:-1], refs[-1]
    for old_ref, new_ref in zip(old_refs, state_refs):
        new_ref[...] = old_ref[...]
    attend_blocks(block_ref, begin_ref, query_ref, pair_refs, state_refs, bias_ref, False)
    unused_top, total_ref, sum_ref = state_refs
    pieces = [
        (sum_ref[head * HD : (head + 1) * HD, :] / total_ref[head : head + 1, :]).astype(
            jnp.bfloat16
        )
        for head in range(total_ref.shape[0])
    ]
    attended = jnp.concatenate(pieces, axis=0).T
    mixed = (residual_ref[...].astype(jnp.float32) + dot(attended, proj_ref[...])).astype(
        jnp.bfloat16
    )
    mixed_ref[...] = mixed
    mixed_f = mixed.astype(jnp.float32)
    inv_rms = lax.rsqrt(jnp.mean(mixed_f * mixed_f, axis=1, keepdims=True) + norm_eps)
    normed = (mixed_f * inv_rms).astype(jnp.bfloat16)
    normed_ref[...] = normed


def expert_kernel(
    reps,
    rep_list,
    sources,
    tok,
    strip,
    counts,
    own_ref,
    part_ref,
    up_ref,
    down_ref,
    extended_ref,
    *refs,
):
    row_count, grad_count = counts
    row_refs, refs = refs[:row_count], refs[row_count:]
    grad_refs, refs = refs[:grad_count], refs[grad_count:]
    own_rows = rep_list[0] == 0
    held_ref, refs = refs[-1], refs[:-1]
    if own_rows:
        back_refs, (up_acc, down_acc) = refs[:-2], refs[-2:]
    else:
        up_old, down_old = refs[:2]
        term_refs, kept_ref = refs[2:-1], refs[-1]
    total_grads = sum(ref.shape[0] for ref in grad_refs)
    capacity = total_grads // (sources * reps)
    count = sources * capacity
    parts = part_ref.shape[0]
    up = up_ref[...]
    down = down_ref[...]
    router = router_of(extended_ref, tok, sources)
    expert_lane = lax.broadcasted_iota(jnp.int32, (count, router.shape[0]), 1) == own_ref[0]

    def strips(rows, place):
        held_ref[place] = rows.T
        taken = []
        for k in range(parts):
            first = pl.multiple_of(part_ref[k] * strip, strip)
            taken.append(held_ref[place, pl.ds(first, strip), :])
        return jnp.concatenate(taken, axis=0)

    up_term = down_term = None
    for place, rep in enumerate(rep_list):
        rows = chunk_rows(row_refs, sources, place * capacity, (place + 1) * capacity)
        grads = chunk_rows(grad_refs, sources, rep * capacity, (rep + 1) * capacity)
        pre = dot(rows, up)
        sigmoid_pre = jax.nn.sigmoid(pre)
        activated = (pre * sigmoid_pre).astype(jnp.bfloat16)
        logits = dot(rows, router, NT)
        gate = jax.nn.sigmoid(
            jnp.sum(jnp.where(expert_lane, logits, 0.0), axis=1, keepdims=True)
        )
        scaled = (gate * grads.astype(jnp.float32)).astype(jnp.bfloat16)
        act_grad = dot(scaled, down, NT)
        pre_grad = (act_grad * sigmoid_pre * (1.0 + pre * (1.0 - sigmoid_pre))).astype(
            jnp.bfloat16
        )
        if own_rows:
            produced = dot(activated, down).astype(jnp.bfloat16)
            token_grad = dot(pre_grad, up, NT).astype(jnp.bfloat16)
            for k, back_ref in enumerate(back_refs):
                back_ref[0:capacity] = produced[k * capacity : (k + 1) * capacity]
                back_ref[capacity : 2 * capacity] = token_grad[k * capacity : (k + 1) * capacity]
        more_up = dot(strips(rows, 2 * place), pre_grad)
        more_down = dot(strips(activated, 2 * place + 1), scaled)
        up_term = more_up if up_term is None else up_term + more_up
        down_term = more_down if down_term is None else down_term + more_down
    if own_rows:
        up_acc[...] = up_term
        down_acc[...] = down_term
        return
    up_term = up_term + up_old[...]
    down_term = down_term + down_old[...]
    for k in range(parts):
        rows = slice(k * strip, (k + 1) * strip)
        if k == 0:
            kept_ref[0] = up_term[rows]
            kept_ref[1] = down_term[rows]
        else:
            term_refs[k - 1][0] = up_term[rows].astype(jnp.bfloat16)
            term_refs[k - 1][1] = down_term[rows].astype(jnp.bfloat16)


def finish_kernel(
    hot_capacity, expert_count, own_ref, mixed_ref, extended_ref, *refs
):
    back_refs, (layer_ref, grad_mixed_ref) = refs[:-2], refs[-2:]
    tok = mixed_ref.shape[0]
    choice = chosen_of(extended_ref, tok)
    placed = slot_matrix(choice, own_ref[0], expert_count, hot_capacity)
    router = router_of(extended_ref, tok, expert_count)
    mixed_f = mixed_ref[...].astype(jnp.float32)
    inv_rms = lax.rsqrt(jnp.mean(mixed_f * mixed_f, axis=1, keepdims=True) + norm_eps)
    normed = (mixed_f * inv_rms).astype(jnp.bfloat16)
    one_hot = lax.broadcasted_iota(jnp.int32, (expert_count, tok), 0) == choice
    logits = dot(router, normed, NT)
    logit_row = jnp.sum(jnp.where(one_hot, logits, 0.0), axis=0, keepdims=True)
    logit = jnp.broadcast_to(logit_row, (8, tok)).T[:, 0:1]
    gate = jax.nn.sigmoid(logit)
    pair = 2 * hot_capacity
    chunks = [
        ref[first : first + pair] for ref in back_refs for first in range(0, ref.shape[0], pair)
    ]
    results = jnp.concatenate([chunk[:hot_capacity] for chunk in chunks], axis=0)
    grads = jnp.concatenate([chunk[hot_capacity:] for chunk in chunks], axis=0)
    result_f = dot(placed, results, TN)
    normed_grad = dot(placed, grads, TN)
    grad_f = extended_ref[0:tok, :].astype(jnp.float32)
    layer_ref[...] = (mixed_f + gate * result_f).astype(jnp.bfloat16)
    gate_grad = jnp.sum(grad_f * result_f, axis=1, keepdims=True)
    logit_grad = gate_grad * gate * (1.0 - gate)
    router_cols = dot(one_hot.astype(jnp.float32).astype(jnp.bfloat16), router, TN)
    total_grad = normed_grad + logit_grad * router_cols
    mean_term = jnp.mean(total_grad * mixed_f, axis=1, keepdims=True)
    input_grad = inv_rms * total_grad - mixed_f * inv_rms * inv_rms * inv_rms * mean_term
    grad_mixed_ref[...] = (grad_f + input_grad).astype(jnp.bfloat16)


def sum_kernel(kept_ref, *refs):
    term_refs, (up_ref, down_ref) = refs[:-2], refs[-2:]
    for kind, out_ref in enumerate((up_ref, down_ref)):
        total = kept_ref[kind]
        for ref in term_refs:
            total = total + ref[kind].astype(jnp.float32)
        out_ref[...] = total


def shape(dims, dtype=jnp.bfloat16):
    return jax.ShapeDtypeStruct(dims, dtype)


SMEM = pl.BlockSpec(memory_space=pltpu.SMEM)
VMEM = pl.BlockSpec(memory_space=pltpu.VMEM)
HBM = pl.BlockSpec(memory_space=pltpu.HBM)


def call(body, out_shape, specs, scratch=(), cost=0.5):
    return pl.pallas_call(
        body,
        cost_estimate=pl.CostEstimate(
            flops=int(cost * 1e9), bytes_accessed=0, transcendentals=0
        ),
        out_shape=out_shape,
        in_specs=specs,
        out_specs=jax.tree.map(lambda unused: VMEM, out_shape),
        scratch_shapes=list(scratch),
        compiler_params=pltpu.CompilerParams(vmem_limit_bytes=VMEM_LIMIT),
    )


def local(
    seq_count,
    expert_count,
    rep_count,
    query_rows,
    key_rows,
    value_rows,
    doc_lengths,
    residual,
    out_proj,
    router,
    expert_choice,
    weight_in,
    weight_out,
    grad_out,
):
    tok, width = query_rows.shape[1:]
    hidden = weight_in.shape[2]
    heads = width // HD
    experts = Group(("expert",), (expert_count,))
    reps = Group(("rep",), (rep_count,))
    parts = Group(("seq",), (seq_count,))
    strip = width // (seq_count * rep_count)
    capacity = max(2, (3 * tok + 2 * expert_count - 1) // (2 * expert_count))
    hot_capacity = min(4 * capacity, tok // 2)
    choice = expert_choice.reshape(1, tok)
    seq_index = lax.axis_index("seq")
    rep_index = lax.axis_index("rep")
    rank = seq_index * rep_count + rep_index
    own = jnp.stack([lax.axis_index("expert")]).astype(jnp.int32)
    part_to = jnp.stack(
        [parts.target(seq_index, k) * rep_count + rep_index for k in range(seq_count)]
    ).astype(jnp.int32)

    def send(array, least_seq, seq_step, rep_step, wrap):
        pairs = []
        for s in range(least_seq, seq_count - seq_step):
            for r in range(rep_count):
                to = r + rep_step
                if wrap or 0 <= to < rep_count:
                    pairs.append(
                        (s * rep_count + r, (s + seq_step) * rep_count + to % rep_count)
                    )
        return lax.ppermute(array, ("seq", "rep"), pairs)

    def block_ids(entries):
        ids = [rank]
        for seq_back, rep, needed in entries:
            block = (seq_index - seq_back) * rep_count + rep
            ids.append(jnp.where(needed & (seq_index >= seq_back), block, -1))
        return jnp.stack(ids).astype(jnp.int32)

    state_shapes = [
        shape((heads, tok), jnp.float32),
        shape((heads, tok), jnp.float32),
        shape((width, tok), jnp.float32),
    ]
    bias = pltpu.VMEM((tok, tok), jnp.float32)
    query = query_rows[0]

    def attend(blocks, state):
        arrays, entries = blocks
        return call(
            functools.partial(attend_kernel, len(arrays), not state),
            state_shapes,
            [SMEM] + [VMEM] * (2 + len(arrays) + len(state)),
            [bias],
            cost=2.0,
        )(block_ids(entries), begin, query, *arrays, *state)

    pair, extended, begin = pl.pallas_call(
        stack_kernel,
        out_shape=[
            shape((2 * tok, width)),
            shape((tok + 16 + -(-expert_count // 16) * 16, width)),
            shape((1, tok), jnp.int32),
        ],
        in_specs=[SMEM] + [HBM] * 6,
        out_specs=[VMEM] * 3,
        scratch_shapes=[
            pltpu.VMEM((1, tok), jnp.int32),
            pltpu.VMEM((expert_count, width), jnp.bfloat16),
            pltpu.SMEM(doc_lengths.shape, jnp.int32),
            pltpu.SemaphoreType.DMA((6,)),
        ],
        compiler_params=pltpu.CompilerParams(vmem_limit_bytes=60 * 1024 * 1024),
    )(
        jnp.stack([rank]).astype(jnp.int32),
        choice,
        doc_lengths,
        router.T,
        key_rows[0],
        value_rows[0],
        grad_out[0],
    )
    always = rep_index >= 0
    reach = (seq_count + 1) // 2
    rounds = [([pair], [(0, rep_index, always)])]
    line = pair
    extendeds = None
    state = ()
    for step in range(1, reach + 1):
        ahead = send(line, step - 1, 1, 0, False)
        arrays, entries = [ahead], [(step, rep_index, always)]
        for d in range(1, rep_count):
            if step == reach:
                arrays.append(send(line, step - 1, 1, -d, False))
                entries.append((step, rep_index + d, rep_index + d < rep_count))
            if step == 1:
                arrays.append(send(line, 0, 0, d, False))
                entries.append((0, rep_index - d, rep_index >= d))
            else:
                arrays.append(send(line, step - 1, 0, d, True))
                entries.append((step - 1, (rep_index - d) % rep_count, always))
        if step == 1:
            extendeds = reps.exchange([extended] * rep_count)
        state = attend(rounds[-1], state)
        rounds.append((arrays, entries))
        if step < reach:
            line, *state = lax.optimization_barrier((ahead, *state))
            arrays[0] = line

    *held, pinned = lax.optimization_barrier((*state, extendeds[0]))
    state, extendeds = held, [pinned] + list(extendeds[1:])
    sent_grads = call(
        functools.partial(dispatch_kernel, rep_count, tok, hot_capacity),
        [shape((rep_count * hot_capacity, width))] * expert_count,
        [SMEM] + [VMEM] * (2 * rep_count),
    )(own, *extendeds, *extendeds)
    got_grads = merged(experts.exchange(sent_grads), MOST_PERMUTES)

    arrays, entries = rounds[-1]
    mixed, normed = call(
        functools.partial(mix_kernel, len(arrays)),
        [shape((tok, width))] * 2,
        [SMEM] + [VMEM] * (7 + len(arrays)),
        [pltpu.VMEM(one.shape, one.dtype) for one in state_shapes] + [bias],
        cost=5.0,
    )(block_ids(entries), begin, query, residual[0], out_proj, *arrays, *state)

    normed, got_grads = lax.optimization_barrier((normed, got_grads))

    def dispatch(own_arrays, rows):
        return call(
            functools.partial(dispatch_kernel, len(rows), tok, hot_capacity),
            [shape((len(rows) * hot_capacity, width))] * expert_count,
            [SMEM] + [VMEM] * (2 * len(rows)),
        )(own, *own_arrays, *rows)

    others = reps.exchange([normed] * rep_count)[1:]
    got_rows = merged(experts.exchange(dispatch(extendeds[:1], [normed])), MOST_PERMUTES)
    more_rows = dispatch(extendeds[1:], others)
    more_rows, got_rows = lax.optimization_barrier((more_rows, got_rows))
    got_more = merged(experts.exchange(more_rows), MOST_PERMUTES)

    def expert_call(rep_list, rows, out_shape, extra):
        return call(
            functools.partial(
                expert_kernel,
                rep_count,
                rep_list,
                expert_count,
                tok,
                strip,
                (len(rows), len(got_grads)),
            ),
            out_shape,
            [SMEM, SMEM] + [VMEM] * (3 + len(rows) + len(got_grads) + len(extra)),
            [pltpu.VMEM((2 * len(rep_list), width, expert_count * hot_capacity), jnp.bfloat16)],
            cost=2.0,
        )(own, part_to, weight_in[0], weight_out[0], extendeds[0], *rows, *got_grads, *extra)

    *back, up_acc, down_acc = expert_call(
        (0,),
        got_rows,
        [shape((2 * hot_capacity, width))] * expert_count
        + [shape((seq_count * strip, hidden), jnp.float32)]
        + [shape((seq_count * strip, width), jnp.float32)],
        [],
    )
    got_back = merged(experts.exchange(back, inverse=True), MOST_PERMUTES)
    *terms, kept = expert_call(
        tuple(range(1, rep_count)),
        got_more,
        [shape((2, strip, hidden))] * (seq_count - 1)
        + [shape((2, strip, hidden), jnp.float32)],
        [up_acc, down_acc],
    )
    got_terms = parts.exchange([None] + terms)[1:]
    layer_out, grad_mixed = call(
        functools.partial(finish_kernel, hot_capacity, expert_count),
        [shape((tok, width)), shape((tok, width))],
        [SMEM] + [VMEM] * (2 + len(got_back)),
        cost=1.5,
    )(own, mixed, extended, *got_back)
    kept, layer_out = lax.optimization_barrier((kept, layer_out))
    share_in, share_out = call(
        sum_kernel,
        [shape((strip, hidden), jnp.float32), shape((strip, width), jnp.float32)],
        [VMEM] * seq_count,
    )(kept, *got_terms[::-1])
    return (layer_out[None], grad_mixed[None], share_in[None], share_out[None])


def solution(mesh):
    rows = P("expert", ("seq", "rep"), None)
    in_specs = (
        rows,
        rows,
        rows,
        P("expert", None),
        rows,
        P(),
        P(),
        rows,
        P("expert", None, None),
        P("expert", None, None),
        rows,
    )
    body = functools.partial(
        local, mesh.shape["seq"], mesh.shape["expert"], mesh.shape["rep"]
    )
    return jax.shard_map(
        body, mesh=mesh, in_specs=in_specs, out_specs=(rows, rows, rows, rows), check_vma=False
    )
```

```python
import functools
import math

import jax
import jax.numpy as jnp
from jax import lax
from jax.experimental import pallas as pl
from jax.experimental.pallas import tpu as pltpu
from jax.sharding import PartitionSpec as P

HD = 32
norm_eps = 1e-06
masked_score = -1e30
VMEM_LIMIT = 48 * 1024 * 1024
MOST_PERMUTES = 16
NT = (((1,), (1,)), ((), ()))
TN = (((0,), (0,)), ((), ()))


def dot(a, b, dims=None):
    if dims is None:
        return jnp.dot(a, b, preferred_element_type=jnp.float32)
    return lax.dot_general(a, b, dims, preferred_element_type=jnp.float32)


def away(index, offset, size):
    if size & (size - 1) == 0:
        return index ^ offset
    return (index + offset) % size


def back_from(index, offset, size):
    if size & (size - 1) == 0:
        return index ^ offset
    return (index - offset + size) % size


class Group:
    def __init__(self, axes, sizes):
        self.axes, self.sizes = tuple(axes), tuple(sizes)
        self.count = math.prod(sizes)

    def split(self, flat):
        coords = []
        for size in reversed(self.sizes):
            coords.append(flat % size)
            flat = flat // size
        return coords[::-1]

    def moved(self, flat, offset, step):
        place = 0
        for coord, part, size in zip(self.split(flat), self.split(offset), self.sizes):
            place = place * size + step(coord, part, size)
        return place

    def target(self, flat, offset):
        return self.moved(flat, offset, away)

    def source(self, flat, offset):
        return self.moved(flat, offset, back_from)

    def exchange(self, chunks, inverse=False):
        to, start = (self.source, self.target) if inverse else (self.target, self.source)
        if self.count <= MOST_PERMUTES:
            order = sorted(range(1, self.count), key=lambda k: -k)
            got = {0: chunks[0]}
            for k in order:
                pairs = [(i, to(i, k)) for i in range(self.count)]
                got[k] = lax.ppermute(chunks[k], self.axes, pairs)
            return [got[k] for k in range(self.count)]
        me = lax.axis_index(self.axes)
        steps = jnp.arange(self.count, dtype=jnp.int32)
        sent_to = jax.vmap(lambda k: to(me, k))(steps)
        placed = jnp.zeros((self.count,), jnp.int32).at[sent_to].set(steps)
        stacked = jnp.stack(chunks)[placed]
        got = lax.all_to_all(stacked, self.axes, split_axis=0, concat_axis=0, tiled=True)
        came_from = jax.vmap(lambda k: start(me, k))(steps)
        ordered = got[came_from]
        return [ordered[k] for k in range(self.count)]


def merged(chunks, most):
    if len(chunks) <= most:
        return list(chunks)
    return [jnp.concatenate(chunks, axis=0)]


def chunk_rows(refs, count, low, high):
    size = sum(ref.shape[0] for ref in refs) // count
    parts = []
    for chunk in range(count):
        ref, first = (refs[chunk], 0) if len(refs) == count else (refs[0], chunk * size)
        parts.append(ref[first + low : first + high, :])
    return parts[0] if count == 1 else jnp.concatenate(parts, axis=0)


def slot_matrix(choice, own, expert_count, hot_capacity):
    tok = choice.shape[1]
    offset = back_from(choice, own, expert_count)
    one_hot = lax.broadcasted_iota(jnp.int32, (expert_count, tok), 0) == offset
    hits = one_hot.astype(jnp.float32).astype(jnp.bfloat16)
    earlier = lax.broadcasted_iota(jnp.int32, (tok, tok), 0) <= lax.broadcasted_iota(
        jnp.int32, (tok, tok), 1
    )
    counted = dot(hits, earlier.astype(jnp.float32).astype(jnp.bfloat16))
    rank = jnp.sum(jnp.where(one_hot, counted, 0.0), axis=0, keepdims=True) - 1.0
    slots = offset * hot_capacity + rank.astype(jnp.int32)
    rows = lax.broadcasted_iota(jnp.int32, (expert_count * hot_capacity, tok), 0)
    return (rows == slots).astype(jnp.float32).astype(jnp.bfloat16)


def stack_kernel(
    rank_ref,
    choice_ref,
    lengths_ref,
    router_ref,
    key_ref,
    value_ref,
    grad_ref,
    pair_ref,
    extended_ref,
    begin_ref,
    chosen_ref,
    held_router_ref,
    tail_ref,
    held_lengths_ref,
    sems,
):
    tok, width = key_ref.shape
    rest = tail_ref.shape[0]
    targets = (
        (choice_ref, chosen_ref),
        (router_ref, held_router_ref),
        (lengths_ref, held_lengths_ref),
        (key_ref, pair_ref.at[pl.ds(0, tok), :]),
        (value_ref, pair_ref.at[pl.ds(tok, tok), :]),
        (grad_ref, extended_ref.at[pl.ds(0, tok), :]),
        (tail_ref, extended_ref.at[pl.ds(tok, rest), :]),
    )
    copies = [
        pltpu.make_async_copy(source, target, sems.at[place])
        for place, (source, target) in enumerate(targets)
    ]
    for copy in copies[:-1]:
        copy.start()
    copies[0].wait()
    chosen = jnp.broadcast_to(chosen_ref[...].astype(jnp.float32), (16, tok))
    tail_ref[0:16, 0:tok] = chosen.astype(jnp.bfloat16)
    tail_ref[0:16, tok:width] = jnp.zeros((16, width - tok), jnp.bfloat16)
    copies[1].wait()
    routed = held_router_ref[...].astype(jnp.float32)
    spare = rest - 16 - routed.shape[0]
    if spare:
        routed = jnp.concatenate([routed, jnp.zeros((spare, width), jnp.float32)], axis=0)
    tail_ref[16:rest, :] = routed.astype(jnp.bfloat16)
    copies[-1].start()
    copies[2].wait()
    position = rank_ref[0] * tok + lax.broadcasted_iota(jnp.int32, (1, tok), 1)
    begin = jnp.zeros((1, tok), jnp.int32)
    bound = jnp.int32(0)
    for doc in range(held_lengths_ref.shape[1] - 1):
        bound = bound + held_lengths_ref[0, doc]
        begin = jnp.maximum(begin, jnp.where(position >= bound, bound, 0))
    begin_ref[...] = begin
    for copy in copies[3:]:
        copy.wait()


def chosen_of(extended_ref, tok):
    return extended_ref[tok : tok + 16, 0:tok].astype(jnp.float32)[0:1].astype(jnp.int32)


def router_of(extended_ref, tok, expert_count):
    whole = extended_ref[tok + 16 :, :].astype(jnp.float32)
    return whole[0:expert_count].astype(jnp.bfloat16)


def dispatch_kernel(reps, tok, hot_capacity, own_ref, *refs):
    extended_refs, row_refs, sent_refs = refs[:reps], refs[reps : 2 * reps], refs[2 * reps :]
    for rep in range(reps):
        choice = chosen_of(extended_refs[rep], tok)
        placed = slot_matrix(choice, own_ref[0], len(sent_refs), hot_capacity)
        rows = dot(placed, row_refs[rep][0:tok, :]).astype(jnp.bfloat16)
        for k, sent_ref in enumerate(sent_refs):
            sent_ref[rep * hot_capacity : (rep + 1) * hot_capacity] = rows[
                k * hot_capacity : (k + 1) * hot_capacity
            ]


def attend_blocks(block_ref, begin_ref, query_ref, pair_refs, state_refs, bias_ref, first):
    top_ref, total_ref, sum_ref = state_refs
    tok, width = query_ref.shape
    lanes = 128
    per = lanes // HD
    scale = math.log2(math.e) / math.sqrt(HD)
    turned = query_ref[...].T
    head_of_row = lax.broadcasted_iota(jnp.int32, (lanes, tok), 0) // HD
    spread = []
    for group in range(width // lanes):
        part = turned[group * lanes : (group + 1) * lanes]
        spread.append(
            jnp.concatenate(
                [jnp.where(head_of_row == head, part, jnp.zeros_like(part)) for head in range(per)],
                axis=1,
            )
        )
    position = block_ref[0] * tok + lax.broadcasted_iota(jnp.int32, (1, tok), 1)
    begin = begin_ref[...]
    lowest = jnp.min(begin)

    def fold(pair_ref, block, fresh):
        key_position = block * tok + lax.broadcasted_iota(jnp.int32, (tok, tok), 0)
        visible = (key_position >= begin) & (key_position <= position)
        bias_ref[...] = jnp.where(visible, 0.0, masked_score)
        bias = bias_ref[...]
        values = pair_ref[tok : 2 * tok, :].T
        for group in range(width // lanes):
            columns = slice(group * lanes, (group + 1) * lanes)
            scores = dot(pair_ref[0:tok, columns], spread[group])
            weights, factors = [], []
            for head in range(per):
                row = group * per + head
                part = scores[:, head * tok : (head + 1) * tok] + bias
                top = jnp.max(part, axis=0, keepdims=True)
                if not fresh:
                    old = top_ref[row : row + 1, :]
                    top = jnp.maximum(top, old)
                    factors.append(jnp.exp2((old - top) * scale))
                weight = jnp.exp2((part - top) * scale)
                total = jnp.sum(weight, axis=0, keepdims=True)
                if not fresh:
                    total = total + total_ref[row : row + 1, :] * factors[head]
                top_ref[row : row + 1, :] = top
                total_ref[row : row + 1, :] = total
                weights.append(weight.astype(jnp.bfloat16))
            summed = dot(values[columns], jnp.concatenate(weights, axis=1))
            for head in range(per):
                rows = slice((group * per + head) * HD, (group * per + head + 1) * HD)
                piece = summed[head * HD : (head + 1) * HD, head * tok : (head + 1) * tok]
                if not fresh:
                    piece = piece + sum_ref[rows, :] * factors[head]
                sum_ref[rows, :] = piece

    for place, pair_ref in enumerate(pair_refs):
        block = block_ref[1 + place]
        if first and place == 0:
            fold(pair_ref, block, True)
        else:

            @pl.when((block >= 0) & ((block + 1) * tok > lowest))
            def unused(pair_ref=pair_ref, block=block):
                fold(pair_ref, block, False)


def attend_kernel(count, first, block_ref, begin_ref, query_ref, *refs):
    pair_refs, refs = refs[:count], refs[count:]
    if not first:
        for old_ref, new_ref in zip(refs[0:3], refs[3:6]):
            new_ref[...] = old_ref[...]
        refs = refs[3:]
    attend_blocks(block_ref, begin_ref, query_ref, pair_refs, refs[0:3], refs[3], first)


def mix_kernel(count, block_ref, begin_ref, query_ref, residual_ref, proj_ref, *refs):
    pair_refs, refs = refs[:count], refs[count:]
    old_refs, mixed_ref, normed_ref = refs[0:3], refs[3], refs[4]
    state_refs, bias_ref = refs[-4:-1], refs[-1]
    for old_ref, new_ref in zip(old_refs, state_refs):
        new_ref[...] = old_ref[...]
    attend_blocks(block_ref, begin_ref, query_ref, pair_refs, state_refs, bias_ref, False)
    unused_top, total_ref, sum_ref = state_refs
    pieces = [
        (sum_ref[head * HD : (head + 1) * HD, :] / total_ref[head : head + 1, :]).astype(
            jnp.bfloat16
        )
        for head in range(total_ref.shape[0])
    ]
    attended = jnp.concatenate(pieces, axis=0).T
    mixed = (residual_ref[...].astype(jnp.float32) + dot(attended, proj_ref[...])).astype(
        jnp.bfloat16
    )
    mixed_ref[...] = mixed
    mixed_f = mixed.astype(jnp.float32)
    inv_rms = lax.rsqrt(jnp.mean(mixed_f * mixed_f, axis=1, keepdims=True) + norm_eps)
    normed = (mixed_f * inv_rms).astype(jnp.bfloat16)
    normed_ref[...] = normed


def expert_kernel(
    reps,
    rep_list,
    sources,
    tok,
    strip,
    counts,
    own_ref,
    part_ref,
    up_ref,
    down_ref,
    extended_ref,
    *refs,
):
    row_count, grad_count = counts
    row_refs, refs = refs[:row_count], refs[row_count:]
    grad_refs, refs = refs[:grad_count], refs[grad_count:]
    own_rows = rep_list[0] == 0
    held_ref, refs = refs[-1], refs[:-1]
    if own_rows:
        back_refs, (up_acc, down_acc) = refs[1:-2], refs[-2:]
    else:
        up_old, down_old = refs[:2]
        term_refs, kept_ref = refs[2:-1], refs[-1]
    total_grads = sum(ref.shape[0] for ref in grad_refs)
    capacity = total_grads // (sources * reps)
    count = sources * capacity
    parts = part_ref.shape[0]
    up = up_ref[...]
    down = down_ref[...]
    router = router_of(extended_ref, tok, sources)
    expert_lane = lax.broadcasted_iota(jnp.int32, (count, router.shape[0]), 1) == own_ref[0]

    def strips(rows, place):
        held_ref[place] = rows.T
        taken = []
        for k in range(parts):
            first = pl.multiple_of(part_ref[k] * strip, strip)
            taken.append(held_ref[place, pl.ds(first, strip), :])
        return jnp.concatenate(taken, axis=0)

    up_term = down_term = None
    for place, rep in enumerate(rep_list):
        rows = chunk_rows(row_refs, sources, place * capacity, (place + 1) * capacity)
        grads = chunk_rows(grad_refs, sources, rep * capacity, (rep + 1) * capacity)
        pre = dot(rows, up)
        sigmoid_pre = jax.nn.sigmoid(pre)
        activated = (pre * sigmoid_pre).astype(jnp.bfloat16)
        logits = dot(rows, router, NT)
        gate = jax.nn.sigmoid(
            jnp.sum(jnp.where(expert_lane, logits, 0.0), axis=1, keepdims=True)
        )
        scaled = (gate * grads.astype(jnp.float32)).astype(jnp.bfloat16)
        act_grad = dot(scaled, down, NT)
        pre_grad = (act_grad * sigmoid_pre * (1.0 + pre * (1.0 - sigmoid_pre))).astype(
            jnp.bfloat16
        )
        if own_rows:
            produced = dot(activated, down).astype(jnp.bfloat16)
            token_grad = dot(pre_grad, up, NT).astype(jnp.bfloat16)
            for k, back_ref in enumerate(back_refs):
                back_ref[0:capacity] = produced[k * capacity : (k + 1) * capacity]
                back_ref[capacity : 2 * capacity] = token_grad[k * capacity : (k + 1) * capacity]
        more_up = dot(strips(rows, 2 * place), pre_grad)
        more_down = dot(strips(activated, 2 * place + 1), scaled)
        up_term = more_up if up_term is None else up_term + more_up
        down_term = more_down if down_term is None else down_term + more_down
    if own_rows:
        up_acc[...] = up_term
        down_acc[...] = down_term
        return
    up_term = up_term + up_old[...]
    down_term = down_term + down_old[...]
    for k in range(parts):
        rows = slice(k * strip, (k + 1) * strip)
        if k == 0:
            kept_ref[0] = up_term[rows]
            kept_ref[1] = down_term[rows]
        else:
            term_refs[k - 1][0] = up_term[rows].astype(jnp.bfloat16)
            term_refs[k - 1][1] = down_term[rows].astype(jnp.bfloat16)


def finish_kernel(
    hot_capacity, expert_count, own_ref, mixed_ref, extended_ref, *refs
):
    back_refs, (layer_ref, grad_mixed_ref) = refs[:-2], refs[-2:]
    tok = mixed_ref.shape[0]
    choice = chosen_of(extended_ref, tok)
    placed = slot_matrix(choice, own_ref[0], expert_count, hot_capacity)
    router = router_of(extended_ref, tok, expert_count)
    mixed_f = mixed_ref[...].astype(jnp.float32)
    inv_rms = lax.rsqrt(jnp.mean(mixed_f * mixed_f, axis=1, keepdims=True) + norm_eps)
    normed = (mixed_f * inv_rms).astype(jnp.bfloat16)
    one_hot = lax.broadcasted_iota(jnp.int32, (expert_count, tok), 0) == choice
    logits = dot(router, normed, NT)
    logit_row = jnp.sum(jnp.where(one_hot, logits, 0.0), axis=0, keepdims=True)
    logit = jnp.broadcast_to(logit_row, (8, tok)).T[:, 0:1]
    gate = jax.nn.sigmoid(logit)
    pair = 2 * hot_capacity
    chunks = [
        ref[first : first + pair] for ref in back_refs for first in range(0, ref.shape[0], pair)
    ]
    results = jnp.concatenate([chunk[:hot_capacity] for chunk in chunks], axis=0)
    grads = jnp.concatenate([chunk[hot_capacity:] for chunk in chunks], axis=0)
    result_f = dot(placed, results, TN)
    normed_grad = dot(placed, grads, TN)
    grad_f = extended_ref[0:tok, :].astype(jnp.float32)
    layer_ref[...] = (mixed_f + gate * result_f).astype(jnp.bfloat16)
    gate_grad = jnp.sum(grad_f * result_f, axis=1, keepdims=True)
    logit_grad = gate_grad * gate * (1.0 - gate)
    router_cols = dot(one_hot.astype(jnp.float32).astype(jnp.bfloat16), router, TN)
    total_grad = normed_grad + logit_grad * router_cols
    mean_term = jnp.mean(total_grad * mixed_f, axis=1, keepdims=True)
    input_grad = inv_rms * total_grad - mixed_f * inv_rms * inv_rms * inv_rms * mean_term
    grad_mixed_ref[...] = (grad_f + input_grad).astype(jnp.bfloat16)


def sum_kernel(kept_ref, *refs):
    term_refs, (up_ref, down_ref) = refs[:-2], refs[-2:]
    for kind, out_ref in enumerate((up_ref, down_ref)):
        total = kept_ref[kind]
        for ref in term_refs:
            total = total + ref[kind].astype(jnp.float32)
        out_ref[...] = total


def shape(dims, dtype=jnp.bfloat16):
    return jax.ShapeDtypeStruct(dims, dtype)


SMEM = pl.BlockSpec(memory_space=pltpu.SMEM)
VMEM = pl.BlockSpec(memory_space=pltpu.VMEM)
HBM = pl.BlockSpec(memory_space=pltpu.HBM)


def call(body, out_shape, specs, scratch=(), cost=0.5):
    return pl.pallas_call(
        body,
        cost_estimate=pl.CostEstimate(
            flops=int(cost * 1e9), bytes_accessed=0, transcendentals=0
        ),
        out_shape=out_shape,
        in_specs=specs,
        out_specs=jax.tree.map(lambda unused: VMEM, out_shape),
        scratch_shapes=list(scratch),
        compiler_params=pltpu.CompilerParams(vmem_limit_bytes=VMEM_LIMIT),
    )


def local(
    seq_count,
    expert_count,
    rep_count,
    query_rows,
    key_rows,
    value_rows,
    doc_lengths,
    residual,
    out_proj,
    router,
    expert_choice,
    weight_in,
    weight_out,
    grad_out,
):
    tok, width = query_rows.shape[1:]
    hidden = weight_in.shape[2]
    heads = width // HD
    experts = Group(("expert",), (expert_count,))
    reps = Group(("rep",), (rep_count,))
    parts = Group(("seq",), (seq_count,))
    strip = width // (seq_count * rep_count)
    capacity = max(2, (3 * tok + 2 * expert_count - 1) // (2 * expert_count))
    hot_capacity = min(4 * capacity, tok // 2)
    choice = expert_choice.reshape(1, tok)
    seq_index = lax.axis_index("seq")
    rep_index = lax.axis_index("rep")
    rank = seq_index * rep_count + rep_index
    own = jnp.stack([lax.axis_index("expert")]).astype(jnp.int32)
    part_to = jnp.stack(
        [parts.target(seq_index, k) * rep_count + rep_index for k in range(seq_count)]
    ).astype(jnp.int32)

    def send(array, least_seq, seq_step, rep_step, wrap):
        pairs = []
        for s in range(least_seq, seq_count - seq_step):
            for r in range(rep_count):
                to = r + rep_step
                if wrap or 0 <= to < rep_count:
                    pairs.append(
                        (s * rep_count + r, (s + seq_step) * rep_count + to % rep_count)
                    )
        return lax.ppermute(array, ("seq", "rep"), pairs)

    def block_ids(entries):
        ids = [rank]
        for seq_back, rep, needed in entries:
            block = (seq_index - seq_back) * rep_count + rep
            ids.append(jnp.where(needed & (seq_index >= seq_back), block, -1))
        return jnp.stack(ids).astype(jnp.int32)

    state_shapes = [
        shape((heads, tok), jnp.float32),
        shape((heads, tok), jnp.float32),
        shape((width, tok), jnp.float32),
    ]
    bias = pltpu.VMEM((tok, tok), jnp.float32)
    query = query_rows[0]

    def attend(blocks, state):
        arrays, entries = blocks
        return call(
            functools.partial(attend_kernel, len(arrays), not state),
            state_shapes,
            [SMEM] + [VMEM] * (2 + len(arrays) + len(state)),
            [bias],
            cost=2.0,
        )(block_ids(entries), begin, query, *arrays, *state)

    tail = 16 + -(-expert_count // 16) * 16
    pair, extended, begin = pl.pallas_call(
        stack_kernel,
        out_shape=[
            shape((2 * tok, width)),
            shape((tok + tail, width)),
            shape((1, tok), jnp.int32),
        ],
        in_specs=[SMEM] + [HBM] * 6,
        out_specs=[HBM, HBM, VMEM],
        scratch_shapes=[
            pltpu.VMEM((1, tok), jnp.int32),
            pltpu.VMEM((expert_count, width), jnp.bfloat16),
            pltpu.VMEM((tail, width), jnp.bfloat16),
            pltpu.SMEM(doc_lengths.shape, jnp.int32),
            pltpu.SemaphoreType.DMA((7,)),
        ],
        compiler_params=pltpu.CompilerParams(vmem_limit_bytes=60 * 1024 * 1024),
    )(
        jnp.stack([rank]).astype(jnp.int32),
        choice,
        doc_lengths,
        router.T,
        key_rows[0],
        value_rows[0],
        grad_out[0],
    )
    always = rep_index >= 0
    reach = (seq_count + 1) // 2
    rounds = [([pair], [(0, rep_index, always)])]
    line = pair
    extendeds = None
    state = ()
    for step in range(1, reach + 1):
        arrays, entries = [], []
        if step > 1:
            for d in range(1, rep_count):
                arrays.append(send(line, step - 1, 0, d, True))
                entries.append((step - 1, (rep_index - d) % rep_count, always))
        if step == reach:
            for d in range(1, rep_count):
                arrays.append(send(line, step - 1, 1, -d, False))
                entries.append((step, rep_index + d, rep_index + d < rep_count))
        ahead = send(line, step - 1, 1, 0, False)
        arrays.append(ahead)
        entries.append((step, rep_index, always))
        if step == 1:
            for d in range(1, rep_count):
                arrays.append(send(line, 0, 0, d, False))
                entries.append((0, rep_index - d, rep_index >= d))
            extendeds = reps.exchange([extended] * rep_count)
        if step < reach:
            rounds[-1] = (rounds[-1][0] + arrays, rounds[-1][1] + entries)
        else:
            rounds.append((arrays, entries))
        line = ahead
    state = attend(rounds[0], state)

    *held, pinned = lax.optimization_barrier((*state, extendeds[0]))
    state, extendeds = held, [pinned] + list(extendeds[1:])
    sent_grads = call(
        functools.partial(dispatch_kernel, rep_count, tok, hot_capacity),
        [shape((rep_count * hot_capacity, width))] * expert_count,
        [SMEM] + [VMEM] * (2 * rep_count),
    )(own, *extendeds, *extendeds)
    got_grads = merged(experts.exchange(sent_grads), MOST_PERMUTES)

    arrays, entries = rounds[-1]
    mixed, normed = call(
        functools.partial(mix_kernel, len(arrays)),
        [shape((tok, width))] * 2,
        [SMEM] + [VMEM] * (7 + len(arrays)),
        [pltpu.VMEM(one.shape, one.dtype) for one in state_shapes] + [bias],
        cost=5.0,
    )(block_ids(entries), begin, query, residual[0], out_proj, *arrays, *state)

    normed, got_grads = lax.optimization_barrier((normed, got_grads))

    def dispatch(own_arrays, rows):
        return call(
            functools.partial(dispatch_kernel, len(rows), tok, hot_capacity),
            [shape((len(rows) * hot_capacity, width))] * expert_count,
            [SMEM] + [VMEM] * (2 * len(rows)),
        )(own, *own_arrays, *rows)

    others = reps.exchange([normed] * rep_count)[1:]
    got_rows = merged(experts.exchange(dispatch(extendeds[:1], [normed])), MOST_PERMUTES)
    more_rows = dispatch(extendeds[1:], others)
    got_more = merged(experts.exchange(more_rows), MOST_PERMUTES)

    def expert_call(rep_list, rows, out_shape, extra):
        return call(
            functools.partial(
                expert_kernel,
                rep_count,
                rep_list,
                expert_count,
                tok,
                strip,
                (len(rows), len(got_grads)),
            ),
            out_shape,
            [SMEM, SMEM] + [VMEM] * (3 + len(rows) + len(got_grads) + len(extra)),
            [pltpu.VMEM((2 * len(rep_list), width, expert_count * hot_capacity), jnp.bfloat16)],
            cost=2.0,
        )(own, part_to, weight_in[0], weight_out[0], extendeds[0], *rows, *got_grads, *extra)

    *back, up_acc, down_acc = expert_call(
        (0,),
        got_rows,
        [shape((2 * hot_capacity, width))] * expert_count
        + [shape((seq_count * strip, hidden), jnp.float32)]
        + [shape((seq_count * strip, width), jnp.float32)],
        [more_rows[0]],
    )
    got_back = merged(experts.exchange(back, inverse=True), MOST_PERMUTES)
    *terms, kept = expert_call(
        tuple(range(1, rep_count)),
        got_more,
        [shape((2, strip, hidden))] * (seq_count - 1)
        + [shape((2, strip, hidden), jnp.float32)],
        [up_acc, down_acc],
    )
    got_terms = parts.exchange([None] + terms)[1:]
    layer_out, grad_mixed = call(
        functools.partial(finish_kernel, hot_capacity, expert_count),
        [shape((tok, width)), shape((tok, width))],
        [SMEM] + [VMEM] * (2 + len(got_back)),
        cost=1.5,
    )(own, mixed, extended, *got_back)
    kept, layer_out = lax.optimization_barrier((kept, layer_out))
    share_in, share_out = call(
        sum_kernel,
        [shape((strip, hidden), jnp.float32), shape((strip, width), jnp.float32)],
        [VMEM] * seq_count,
    )(kept, *got_terms[::-1])
    return (layer_out[None], grad_mixed[None], share_in[None], share_out[None])


def solution(mesh):
    rows = P("expert", ("seq", "rep"), None)
    in_specs = (
        rows,
        rows,
        rows,
        P("expert", None),
        rows,
        P(),
        P(),
        rows,
        P("expert", None, None),
        P("expert", None, None),
        rows,
    )
    body = functools.partial(
        local, mesh.shape["seq"], mesh.shape["expert"], mesh.shape["rep"]
    )
    return jax.shard_map(
        body, mesh=mesh, in_specs=in_specs, out_specs=(rows, rows, rows, rows), check_vma=False
    )
```

```python
import functools
import math

import jax
import jax.numpy as jnp
from jax import lax
from jax.experimental import pallas as pl
from jax.experimental.pallas import tpu as pltpu
from jax.sharding import PartitionSpec as P

HD = 32
norm_eps = 1e-06
masked_score = -1e30
VMEM_LIMIT = 48 * 1024 * 1024
MOST_PERMUTES = 16
NT = (((1,), (1,)), ((), ()))
TN = (((0,), (0,)), ((), ()))


def dot(a, b, dims=None):
    if dims is None:
        return jnp.dot(a, b, preferred_element_type=jnp.float32)
    return lax.dot_general(a, b, dims, preferred_element_type=jnp.float32)


def away(index, offset, size):
    if size & (size - 1) == 0:
        return index ^ offset
    return (index + offset) % size


def back_from(index, offset, size):
    if size & (size - 1) == 0:
        return index ^ offset
    return (index - offset + size) % size


class Group:
    def __init__(self, axes, sizes):
        self.axes, self.sizes = tuple(axes), tuple(sizes)
        self.count = math.prod(sizes)

    def split(self, flat):
        coords = []
        for size in reversed(self.sizes):
            coords.append(flat % size)
            flat = flat // size
        return coords[::-1]

    def moved(self, flat, offset, step):
        place = 0
        for coord, part, size in zip(self.split(flat), self.split(offset), self.sizes):
            place = place * size + step(coord, part, size)
        return place

    def target(self, flat, offset):
        return self.moved(flat, offset, away)

    def source(self, flat, offset):
        return self.moved(flat, offset, back_from)

    def exchange(self, chunks, inverse=False):
        to, start = (self.source, self.target) if inverse else (self.target, self.source)
        if self.count <= MOST_PERMUTES:
            order = sorted(range(1, self.count), key=lambda k: -k)
            got = {0: chunks[0]}
            for k in order:
                pairs = [(i, to(i, k)) for i in range(self.count)]
                got[k] = lax.ppermute(chunks[k], self.axes, pairs)
            return [got[k] for k in range(self.count)]
        me = lax.axis_index(self.axes)
        steps = jnp.arange(self.count, dtype=jnp.int32)
        sent_to = jax.vmap(lambda k: to(me, k))(steps)
        placed = jnp.zeros((self.count,), jnp.int32).at[sent_to].set(steps)
        stacked = jnp.stack(chunks)[placed]
        got = lax.all_to_all(stacked, self.axes, split_axis=0, concat_axis=0, tiled=True)
        came_from = jax.vmap(lambda k: start(me, k))(steps)
        ordered = got[came_from]
        return [ordered[k] for k in range(self.count)]


def merged(chunks, most):
    if len(chunks) <= most:
        return list(chunks)
    return [jnp.concatenate(chunks, axis=0)]


def chunk_rows(refs, count, low, high):
    size = sum(ref.shape[0] for ref in refs) // count
    parts = []
    for chunk in range(count):
        ref, first = (refs[chunk], 0) if len(refs) == count else (refs[0], chunk * size)
        parts.append(ref[first + low : first + high, :])
    return parts[0] if count == 1 else jnp.concatenate(parts, axis=0)


def slot_matrix(choice, own, expert_count, hot_capacity):
    tok = choice.shape[1]
    offset = back_from(choice, own, expert_count)
    one_hot = lax.broadcasted_iota(jnp.int32, (expert_count, tok), 0) == offset
    hits = one_hot.astype(jnp.float32).astype(jnp.bfloat16)
    earlier = lax.broadcasted_iota(jnp.int32, (tok, tok), 0) <= lax.broadcasted_iota(
        jnp.int32, (tok, tok), 1
    )
    counted = dot(hits, earlier.astype(jnp.float32).astype(jnp.bfloat16))
    rank = jnp.sum(jnp.where(one_hot, counted, 0.0), axis=0, keepdims=True) - 1.0
    slots = offset * hot_capacity + rank.astype(jnp.int32)
    rows = lax.broadcasted_iota(jnp.int32, (expert_count * hot_capacity, tok), 0)
    return (rows == slots).astype(jnp.float32).astype(jnp.bfloat16)


def stack_kernel(
    rank_ref,
    choice_ref,
    lengths_ref,
    router_ref,
    key_ref,
    value_ref,
    grad_ref,
    pair_ref,
    extended_ref,
    begin_ref,
    chosen_ref,
    held_router_ref,
    held_lengths_ref,
    sems,
):
    tok, width = key_ref.shape
    targets = (
        (choice_ref, chosen_ref),
        (lengths_ref, held_lengths_ref),
        (key_ref, pair_ref.at[pl.ds(0, tok), :]),
        (value_ref, pair_ref.at[pl.ds(tok, tok), :]),
        (grad_ref, extended_ref.at[pl.ds(0, tok), :]),
        (router_ref, held_router_ref),
    )
    copies = [
        pltpu.make_async_copy(source, target, sems.at[place])
        for place, (source, target) in enumerate(targets)
    ]
    for copy in copies:
        copy.start()
    copies[0].wait()
    chosen = jnp.broadcast_to(chosen_ref[...].astype(jnp.float32), (16, tok))
    extended_ref[tok : tok + 16, 0:tok] = chosen.astype(jnp.bfloat16)
    extended_ref[tok : tok + 16, tok:width] = jnp.zeros((16, width - tok), jnp.bfloat16)
    copies[1].wait()
    position = rank_ref[0] * tok + lax.broadcasted_iota(jnp.int32, (1, tok), 1)
    begin = jnp.zeros((1, tok), jnp.int32)
    bound = jnp.int32(0)
    for doc in range(held_lengths_ref.shape[1] - 1):
        bound = bound + held_lengths_ref[0, doc]
        begin = jnp.maximum(begin, jnp.where(position >= bound, bound, 0))
    begin_ref[...] = begin
    copies[5].wait()
    routed = held_router_ref[...].astype(jnp.float32)
    spare = extended_ref.shape[0] - tok - 16 - routed.shape[0]
    if spare:
        routed = jnp.concatenate([routed, jnp.zeros((spare, width), jnp.float32)], axis=0)
    extended_ref[tok + 16 :, :] = routed.astype(jnp.bfloat16)
    for copy in copies[2:5]:
        copy.wait()


def chosen_of(extended_ref, tok):
    return extended_ref[tok : tok + 16, 0:tok].astype(jnp.float32)[0:1].astype(jnp.int32)


def router_of(extended_ref, tok, expert_count):
    whole = extended_ref[tok + 16 :, :].astype(jnp.float32)
    return whole[0:expert_count].astype(jnp.bfloat16)


def dispatch_kernel(reps, tok, hot_capacity, own_ref, *refs):
    extended_refs, row_refs, sent_refs = refs[:reps], refs[reps : 2 * reps], refs[2 * reps :]
    for rep in range(reps):
        choice = chosen_of(extended_refs[rep], tok)
        placed = slot_matrix(choice, own_ref[0], len(sent_refs), hot_capacity)
        rows = dot(placed, row_refs[rep][0:tok, :]).astype(jnp.bfloat16)
        for k, sent_ref in enumerate(sent_refs):
            sent_ref[rep * hot_capacity : (rep + 1) * hot_capacity] = rows[
                k * hot_capacity : (k + 1) * hot_capacity
            ]


def attend_blocks(block_ref, begin_ref, query_ref, pair_refs, state_refs, bias_ref, first):
    top_ref, total_ref, sum_ref = state_refs
    tok, width = query_ref.shape
    lanes = 128
    per = lanes // HD
    scale = math.log2(math.e) / math.sqrt(HD)
    turned = query_ref[...].T
    head_of_row = lax.broadcasted_iota(jnp.int32, (lanes, tok), 0) // HD
    spread = []
    for group in range(width // lanes):
        part = turned[group * lanes : (group + 1) * lanes]
        spread.append(
            jnp.concatenate(
                [jnp.where(head_of_row == head, part, jnp.zeros_like(part)) for head in range(per)],
                axis=1,
            )
        )
    position = block_ref[0] * tok + lax.broadcasted_iota(jnp.int32, (1, tok), 1)
    begin = begin_ref[...]
    lowest = jnp.min(begin)

    def fold(pair_ref, block, fresh):
        key_position = block * tok + lax.broadcasted_iota(jnp.int32, (tok, tok), 0)
        visible = (key_position >= begin) & (key_position <= position)
        bias_ref[...] = jnp.where(visible, 0.0, masked_score)
        bias = bias_ref[...]
        values = pair_ref[tok : 2 * tok, :].T
        for group in range(width // lanes):
            columns = slice(group * lanes, (group + 1) * lanes)
            scores = dot(pair_ref[0:tok, columns], spread[group])
            weights, factors = [], []
            for head in range(per):
                row = group * per + head
                part = scores[:, head * tok : (head + 1) * tok] + bias
                top = jnp.max(part, axis=0, keepdims=True)
                if not fresh:
                    old = top_ref[row : row + 1, :]
                    top = jnp.maximum(top, old)
                    factors.append(jnp.exp2((old - top) * scale))
                weight = jnp.exp2((part - top) * scale)
                total = jnp.sum(weight, axis=0, keepdims=True)
                if not fresh:
                    total = total + total_ref[row : row + 1, :] * factors[head]
                top_ref[row : row + 1, :] = top
                total_ref[row : row + 1, :] = total
                weights.append(weight.astype(jnp.bfloat16))
            summed = dot(values[columns], jnp.concatenate(weights, axis=1))
            for head in range(per):
                rows = slice((group * per + head) * HD, (group * per + head + 1) * HD)
                piece = summed[head * HD : (head + 1) * HD, head * tok : (head + 1) * tok]
                if not fresh:
                    piece = piece + sum_ref[rows, :] * factors[head]
                sum_ref[rows, :] = piece

    for place, pair_ref in enumerate(pair_refs):
        block = block_ref[1 + place]
        if first and place == 0:
            fold(pair_ref, block, True)
        else:

            @pl.when((block >= 0) & ((block + 1) * tok > lowest))
            def unused(pair_ref=pair_ref, block=block):
                fold(pair_ref, block, False)


def attend_kernel(count, first, block_ref, begin_ref, query_ref, *refs):
    pair_refs, refs = refs[:count], refs[count:]
    if not first:
        for old_ref, new_ref in zip(refs[0:3], refs[3:6]):
            new_ref[...] = old_ref[...]
        refs = refs[3:]
    attend_blocks(block_ref, begin_ref, query_ref, pair_refs, refs[0:3], refs[3], first)


def mix_kernel(count, block_ref, begin_ref, query_ref, residual_ref, proj_ref, *refs):
    pair_refs, refs = refs[:count], refs[count:]
    old_refs, mixed_ref, normed_ref = refs[0:3], refs[3], refs[4]
    state_refs, bias_ref = refs[-4:-1], refs[-1]
    for old_ref, new_ref in zip(old_refs, state_refs):
        new_ref[...] = old_ref[...]
    attend_blocks(block_ref, begin_ref, query_ref, pair_refs, state_refs, bias_ref, False)
    unused_top, total_ref, sum_ref = state_refs
    pieces = [
        (sum_ref[head * HD : (head + 1) * HD, :] / total_ref[head : head + 1, :]).astype(
            jnp.bfloat16
        )
        for head in range(total_ref.shape[0])
    ]
    attended = jnp.concatenate(pieces, axis=0).T
    mixed = (residual_ref[...].astype(jnp.float32) + dot(attended, proj_ref[...])).astype(
        jnp.bfloat16
    )
    mixed_ref[...] = mixed
    mixed_f = mixed.astype(jnp.float32)
    inv_rms = lax.rsqrt(jnp.mean(mixed_f * mixed_f, axis=1, keepdims=True) + norm_eps)
    normed = (mixed_f * inv_rms).astype(jnp.bfloat16)
    normed_ref[...] = normed


def expert_kernel(
    reps,
    rep_list,
    sources,
    tok,
    strip,
    counts,
    own_ref,
    part_ref,
    up_ref,
    down_ref,
    extended_ref,
    *refs,
):
    row_count, grad_count = counts
    row_refs, refs = refs[:row_count], refs[row_count:]
    grad_refs, refs = refs[:grad_count][::-1], refs[grad_count:]
    own_rows = rep_list[0] == 0
    held_ref, refs = refs[-1], refs[:-1]
    if own_rows:
        back_refs, (up_acc, down_acc) = refs[1:-2], refs[-2:]
    else:
        up_old, down_old = refs[:2]
        term_refs, kept_ref = refs[2:-1], refs[-1]
    total_grads = sum(ref.shape[0] for ref in grad_refs)
    capacity = total_grads // (sources * reps)
    count = sources * capacity
    parts = part_ref.shape[0]
    up = up_ref[...]
    down = down_ref[...]
    router = router_of(extended_ref, tok, sources)
    expert_lane = lax.broadcasted_iota(jnp.int32, (count, router.shape[0]), 1) == own_ref[0]

    def strips(rows, place):
        held_ref[place] = rows.T
        taken = []
        for k in range(parts):
            first = pl.multiple_of(part_ref[k] * strip, strip)
            taken.append(held_ref[place, pl.ds(first, strip), :])
        return jnp.concatenate(taken, axis=0)

    up_term = down_term = None
    for place, rep in enumerate(rep_list):
        rows = chunk_rows(row_refs, sources, place * capacity, (place + 1) * capacity)
        grads = chunk_rows(grad_refs, sources, rep * capacity, (rep + 1) * capacity)
        pre = dot(rows, up)
        sigmoid_pre = jax.nn.sigmoid(pre)
        activated = (pre * sigmoid_pre).astype(jnp.bfloat16)
        logits = dot(rows, router, NT)
        gate = jax.nn.sigmoid(
            jnp.sum(jnp.where(expert_lane, logits, 0.0), axis=1, keepdims=True)
        )
        scaled = (gate * grads.astype(jnp.float32)).astype(jnp.bfloat16)
        act_grad = dot(scaled, down, NT)
        pre_grad = (act_grad * sigmoid_pre * (1.0 + pre * (1.0 - sigmoid_pre))).astype(
            jnp.bfloat16
        )
        if own_rows:
            produced = dot(activated, down).astype(jnp.bfloat16)
            token_grad = dot(pre_grad, up, NT).astype(jnp.bfloat16)
            for k, back_ref in enumerate(back_refs):
                back_ref[0:capacity] = produced[k * capacity : (k + 1) * capacity]
                back_ref[capacity : 2 * capacity] = token_grad[k * capacity : (k + 1) * capacity]
        more_up = dot(strips(rows, 2 * place), pre_grad)
        more_down = dot(strips(activated, 2 * place + 1), scaled)
        up_term = more_up if up_term is None else up_term + more_up
        down_term = more_down if down_term is None else down_term + more_down
    if own_rows:
        up_acc[...] = up_term
        down_acc[...] = down_term
        return
    up_term = up_term + up_old[...]
    down_term = down_term + down_old[...]
    for k in range(parts):
        rows = slice(k * strip, (k + 1) * strip)
        if k == 0:
            kept_ref[0] = up_term[rows]
            kept_ref[1] = down_term[rows]
        else:
            term_refs[k - 1][0] = up_term[rows].astype(jnp.bfloat16)
            term_refs[k - 1][1] = down_term[rows].astype(jnp.bfloat16)


def finish_kernel(
    hot_capacity, expert_count, own_ref, mixed_ref, extended_ref, *refs
):
    back_refs, (layer_ref, grad_mixed_ref) = refs[:-2], refs[-2:]
    tok = mixed_ref.shape[0]
    choice = chosen_of(extended_ref, tok)
    placed = slot_matrix(choice, own_ref[0], expert_count, hot_capacity)
    router = router_of(extended_ref, tok, expert_count)
    mixed_f = mixed_ref[...].astype(jnp.float32)
    inv_rms = lax.rsqrt(jnp.mean(mixed_f * mixed_f, axis=1, keepdims=True) + norm_eps)
    normed = (mixed_f * inv_rms).astype(jnp.bfloat16)
    one_hot = lax.broadcasted_iota(jnp.int32, (expert_count, tok), 0) == choice
    logits = dot(router, normed, NT)
    logit_row = jnp.sum(jnp.where(one_hot, logits, 0.0), axis=0, keepdims=True)
    logit = jnp.broadcast_to(logit_row, (8, tok)).T[:, 0:1]
    gate = jax.nn.sigmoid(logit)
    pair = 2 * hot_capacity
    chunks = [
        ref[first : first + pair] for ref in back_refs for first in range(0, ref.shape[0], pair)
    ]
    results = jnp.concatenate([chunk[:hot_capacity] for chunk in chunks], axis=0)
    grads = jnp.concatenate([chunk[hot_capacity:] for chunk in chunks], axis=0)
    result_f = dot(placed, results, TN)
    normed_grad = dot(placed, grads, TN)
    grad_f = extended_ref[0:tok, :].astype(jnp.float32)
    layer_ref[...] = (mixed_f + gate * result_f).astype(jnp.bfloat16)
    gate_grad = jnp.sum(grad_f * result_f, axis=1, keepdims=True)
    logit_grad = gate_grad * gate * (1.0 - gate)
    router_cols = dot(one_hot.astype(jnp.float32).astype(jnp.bfloat16), router, TN)
    total_grad = normed_grad + logit_grad * router_cols
    mean_term = jnp.mean(total_grad * mixed_f, axis=1, keepdims=True)
    input_grad = inv_rms * total_grad - mixed_f * inv_rms * inv_rms * inv_rms * mean_term
    grad_mixed_ref[...] = (grad_f + input_grad).astype(jnp.bfloat16)


def sum_kernel(kept_ref, *refs):
    term_refs, (up_ref, down_ref) = refs[:-2], refs[-2:]
    for kind, out_ref in enumerate((up_ref, down_ref)):
        total = kept_ref[kind]
        for ref in term_refs:
            total = total + ref[kind].astype(jnp.float32)
        out_ref[...] = total


def shape(dims, dtype=jnp.bfloat16):
    return jax.ShapeDtypeStruct(dims, dtype)


SMEM = pl.BlockSpec(memory_space=pltpu.SMEM)
VMEM = pl.BlockSpec(memory_space=pltpu.VMEM)
HBM = pl.BlockSpec(memory_space=pltpu.HBM)


def call(body, out_shape, specs, scratch=(), cost=0.5):
    return pl.pallas_call(
        body,
        cost_estimate=pl.CostEstimate(
            flops=int(cost * 1e9), bytes_accessed=0, transcendentals=0
        ),
        out_shape=out_shape,
        in_specs=specs,
        out_specs=jax.tree.map(lambda unused: VMEM, out_shape),
        scratch_shapes=list(scratch),
        compiler_params=pltpu.CompilerParams(vmem_limit_bytes=VMEM_LIMIT),
    )


def local(
    seq_count,
    expert_count,
    rep_count,
    query_rows,
    key_rows,
    value_rows,
    doc_lengths,
    residual,
    out_proj,
    router,
    expert_choice,
    weight_in,
    weight_out,
    grad_out,
):
    tok, width = query_rows.shape[1:]
    hidden = weight_in.shape[2]
    heads = width // HD
    experts = Group(("expert",), (expert_count,))
    reps = Group(("rep",), (rep_count,))
    parts = Group(("seq",), (seq_count,))
    strip = width // (seq_count * rep_count)
    capacity = max(2, (3 * tok + 2 * expert_count - 1) // (2 * expert_count))
    hot_capacity = min(4 * capacity, tok // 2)
    choice = expert_choice.reshape(1, tok)
    seq_index = lax.axis_index("seq")
    rep_index = lax.axis_index("rep")
    rank = seq_index * rep_count + rep_index
    own = jnp.stack([lax.axis_index("expert")]).astype(jnp.int32)
    part_to = jnp.stack(
        [parts.target(seq_index, k) * rep_count + rep_index for k in range(seq_count)]
    ).astype(jnp.int32)

    def send(array, least_seq, seq_step, rep_step, wrap):
        pairs = []
        for s in range(least_seq, seq_count - seq_step):
            for r in range(rep_count):
                to = r + rep_step
                if wrap or 0 <= to < rep_count:
                    pairs.append(
                        (s * rep_count + r, (s + seq_step) * rep_count + to % rep_count)
                    )
        return lax.ppermute(array, ("seq", "rep"), pairs)

    def block_ids(entries):
        ids = [rank]
        for seq_back, rep, needed in entries:
            block = (seq_index - seq_back) * rep_count + rep
            ids.append(jnp.where(needed & (seq_index >= seq_back), block, -1))
        return jnp.stack(ids).astype(jnp.int32)

    state_shapes = [
        shape((heads, tok), jnp.float32),
        shape((heads, tok), jnp.float32),
        shape((width, tok), jnp.float32),
    ]
    bias = pltpu.VMEM((tok, tok), jnp.float32)
    query = query_rows[0]

    def attend(blocks, state):
        arrays, entries = blocks
        return call(
            functools.partial(attend_kernel, len(arrays), not state),
            state_shapes,
            [SMEM] + [VMEM] * (2 + len(arrays) + len(state)),
            [bias],
            cost=2.0,
        )(block_ids(entries), begin, query, *arrays, *state)

    tail = 16 + -(-expert_count // 16) * 16
    pair, extended, begin = pl.pallas_call(
        stack_kernel,
        out_shape=[
            shape((2 * tok, width)),
            shape((tok + tail, width)),
            shape((1, tok), jnp.int32),
        ],
        in_specs=[SMEM] + [HBM] * 6,
        out_specs=[VMEM] * 3,
        scratch_shapes=[
            pltpu.VMEM((1, tok), jnp.int32),
            pltpu.VMEM((expert_count, width), jnp.bfloat16),
            pltpu.SMEM(doc_lengths.shape, jnp.int32),
            pltpu.SemaphoreType.DMA((6,)),
        ],
        compiler_params=pltpu.CompilerParams(vmem_limit_bytes=60 * 1024 * 1024),
    )(
        jnp.stack([rank]).astype(jnp.int32),
        choice,
        doc_lengths,
        router.T,
        key_rows[0],
        value_rows[0],
        grad_out[0],
    )
    always = rep_index >= 0
    reach = (seq_count + 1) // 2
    rounds = [([pair], [(0, rep_index, always)])]
    line = pair
    extendeds = None
    state = ()
    for step in range(1, reach + 1):
        arrays, entries = [], []
        if step > 1:
            for d in range(1, rep_count):
                arrays.append(send(line, step - 1, 0, d, True))
                entries.append((step - 1, (rep_index - d) % rep_count, always))
        if step == reach:
            for d in range(1, rep_count):
                arrays.append(send(line, step - 1, 1, -d, False))
                entries.append((step, rep_index + d, rep_index + d < rep_count))
        ahead = send(line, step - 1, 1, 0, False)
        arrays.append(ahead)
        entries.append((step, rep_index, always))
        if step == 1:
            for d in range(1, rep_count):
                arrays.append(send(line, 0, 0, d, False))
                entries.append((0, rep_index - d, rep_index >= d))
            extendeds = reps.exchange([extended] * rep_count)
        if step < reach:
            rounds[-1] = (rounds[-1][0] + arrays, rounds[-1][1] + entries)
        else:
            rounds.append((arrays, entries))
        line = ahead
    arrays = rounds[0][0]
    arrays[-1], pinned = lax.optimization_barrier((arrays[-1], extendeds[0]))
    extendeds = [pinned] + list(extendeds[1:])
    state = attend(rounds[0], state)

    sent_grads = call(
        functools.partial(dispatch_kernel, rep_count, tok, hot_capacity),
        [shape((rep_count * hot_capacity, width))] * expert_count,
        [SMEM] + [VMEM] * (2 * rep_count),
    )(own, *extendeds, *extendeds)
    got_grads = merged(experts.exchange(sent_grads), MOST_PERMUTES)[::-1]

    arrays, entries = rounds[-1]
    mixed, normed = call(
        functools.partial(mix_kernel, len(arrays)),
        [shape((tok, width))] * 2,
        [SMEM] + [VMEM] * (7 + len(arrays)),
        [pltpu.VMEM(one.shape, one.dtype) for one in state_shapes] + [bias],
        cost=5.0,
    )(block_ids(entries), begin, query, residual[0], out_proj, *arrays, *state)

    normed, got_grads = lax.optimization_barrier((normed, got_grads))

    def dispatch(own_arrays, rows):
        return call(
            functools.partial(dispatch_kernel, len(rows), tok, hot_capacity),
            [shape((len(rows) * hot_capacity, width))] * expert_count,
            [SMEM] + [VMEM] * (2 * len(rows)),
        )(own, *own_arrays, *rows)

    others = reps.exchange([normed] * rep_count)[1:]
    got_rows = merged(experts.exchange(dispatch(extendeds[:1], [normed])), MOST_PERMUTES)
    more_rows = dispatch(extendeds[1:], others)
    got_more = merged(experts.exchange(more_rows), MOST_PERMUTES)

    def expert_call(rep_list, rows, out_shape, extra):
        return call(
            functools.partial(
                expert_kernel,
                rep_count,
                rep_list,
                expert_count,
                tok,
                strip,
                (len(rows), len(got_grads)),
            ),
            out_shape,
            [SMEM, SMEM] + [VMEM] * (3 + len(rows) + len(got_grads) + len(extra)),
            [pltpu.VMEM((2 * len(rep_list), width, expert_count * hot_capacity), jnp.bfloat16)],
            cost=2.0,
        )(own, part_to, weight_in[0], weight_out[0], extendeds[0], *rows, *got_grads, *extra)

    *back, up_acc, down_acc = expert_call(
        (0,),
        got_rows,
        [shape((2 * hot_capacity, width))] * expert_count
        + [shape((seq_count * strip, hidden), jnp.float32)]
        + [shape((seq_count * strip, width), jnp.float32)],
        [more_rows[0]],
    )
    got_back = merged(experts.exchange(back, inverse=True), MOST_PERMUTES)
    *terms, kept = expert_call(
        tuple(range(1, rep_count)),
        got_more,
        [shape((2, strip, hidden))] * (seq_count - 1)
        + [shape((2, strip, hidden), jnp.float32)],
        [up_acc, down_acc],
    )
    got_terms = parts.exchange([None] + terms)[1:]
    layer_out, grad_mixed = call(
        functools.partial(finish_kernel, hot_capacity, expert_count),
        [shape((tok, width)), shape((tok, width))],
        [SMEM] + [VMEM] * (2 + len(got_back)),
        cost=1.5,
    )(own, mixed, extended, *got_back)
    kept, layer_out = lax.optimization_barrier((kept, layer_out))
    share_in, share_out = call(
        sum_kernel,
        [shape((strip, hidden), jnp.float32), shape((strip, width), jnp.float32)],
        [VMEM] * seq_count,
    )(kept, *got_terms[::-1])
    return (layer_out[None], grad_mixed[None], share_in[None], share_out[None])


def solution(mesh):
    rows = P("expert", ("seq", "rep"), None)
    in_specs = (
        rows,
        rows,
        rows,
        P("expert", None),
        rows,
        P(),
        P(),
        rows,
        P("expert", None, None),
        P("expert", None, None),
        rows,
    )
    body = functools.partial(
        local, mesh.shape["seq"], mesh.shape["expert"], mesh.shape["rep"]
    )
    return jax.shard_map(
        body, mesh=mesh, in_specs=in_specs, out_specs=(rows, rows, rows, rows), check_vma=False
    )
```

```python
import functools
import math

import jax
import jax.numpy as jnp
from jax import lax
from jax.experimental import pallas as pl
from jax.experimental.pallas import tpu as pltpu
from jax.sharding import PartitionSpec as P

HD = 32
norm_eps = 1e-06
masked_score = -1e30
VMEM_LIMIT = 48 * 1024 * 1024
MOST_PERMUTES = 16
NT = (((1,), (1,)), ((), ()))
TN = (((0,), (0,)), ((), ()))


def dot(a, b, dims=None):
    if dims is None:
        return jnp.dot(a, b, preferred_element_type=jnp.float32)
    return lax.dot_general(a, b, dims, preferred_element_type=jnp.float32)


def away(index, offset, size):
    if size & (size - 1) == 0:
        return index ^ offset
    return (index + offset) % size


def back_from(index, offset, size):
    if size & (size - 1) == 0:
        return index ^ offset
    return (index - offset + size) % size


class Group:
    def __init__(self, axes, sizes):
        self.axes, self.sizes = tuple(axes), tuple(sizes)
        self.count = math.prod(sizes)

    def split(self, flat):
        coords = []
        for size in reversed(self.sizes):
            coords.append(flat % size)
            flat = flat // size
        return coords[::-1]

    def moved(self, flat, offset, step):
        place = 0
        for coord, part, size in zip(self.split(flat), self.split(offset), self.sizes):
            place = place * size + step(coord, part, size)
        return place

    def target(self, flat, offset):
        return self.moved(flat, offset, away)

    def source(self, flat, offset):
        return self.moved(flat, offset, back_from)

    def exchange(self, chunks, inverse=False):
        to, start = (self.source, self.target) if inverse else (self.target, self.source)
        if self.count <= MOST_PERMUTES:
            order = sorted(range(1, self.count), key=lambda k: -k)
            got = {0: chunks[0]}
            for k in order:
                pairs = [(i, to(i, k)) for i in range(self.count)]
                got[k] = lax.ppermute(chunks[k], self.axes, pairs)
            return [got[k] for k in range(self.count)]
        me = lax.axis_index(self.axes)
        steps = jnp.arange(self.count, dtype=jnp.int32)
        sent_to = jax.vmap(lambda k: to(me, k))(steps)
        placed = jnp.zeros((self.count,), jnp.int32).at[sent_to].set(steps)
        stacked = jnp.stack(chunks)[placed]
        got = lax.all_to_all(stacked, self.axes, split_axis=0, concat_axis=0, tiled=True)
        came_from = jax.vmap(lambda k: start(me, k))(steps)
        ordered = got[came_from]
        return [ordered[k] for k in range(self.count)]


def merged(chunks, most):
    if len(chunks) <= most:
        return list(chunks)
    return [jnp.concatenate(chunks, axis=0)]


def chunk_rows(refs, count, low, high):
    size = sum(ref.shape[0] for ref in refs) // count
    parts = []
    for chunk in range(count):
        ref, first = (refs[chunk], 0) if len(refs) == count else (refs[0], chunk * size)
        parts.append(ref[first + low : first + high, :])
    return parts[0] if count == 1 else jnp.concatenate(parts, axis=0)


def slot_matrix(choice, own, expert_count, hot_capacity):
    tok = choice.shape[1]
    offset = back_from(choice, own, expert_count)
    one_hot = lax.broadcasted_iota(jnp.int32, (expert_count, tok), 0) == offset
    hits = one_hot.astype(jnp.float32).astype(jnp.bfloat16)
    earlier = lax.broadcasted_iota(jnp.int32, (tok, tok), 0) <= lax.broadcasted_iota(
        jnp.int32, (tok, tok), 1
    )
    counted = dot(hits, earlier.astype(jnp.float32).astype(jnp.bfloat16))
    rank = jnp.sum(jnp.where(one_hot, counted, 0.0), axis=0, keepdims=True) - 1.0
    slots = offset * hot_capacity + rank.astype(jnp.int32)
    rows = lax.broadcasted_iota(jnp.int32, (expert_count * hot_capacity, tok), 0)
    return (rows == slots).astype(jnp.float32).astype(jnp.bfloat16)


def stack_kernel(
    ranks_ref,
    choice_ref,
    lengths_ref,
    router_ref,
    key_ref,
    value_ref,
    grad_ref,
    query_ref,
    pair_ref,
    extended_ref,
    begin_ref,
    chosen_ref,
    held_router_ref,
    held_lengths_ref,
    sems,
):
    tok, width = key_ref.shape
    targets = (
        (choice_ref, chosen_ref),
        (lengths_ref, held_lengths_ref),
        (key_ref, pair_ref.at[pl.ds(0, tok), :]),
        (value_ref, pair_ref.at[pl.ds(tok, tok), :]),
        (grad_ref, extended_ref.at[pl.ds(0, tok), :]),
        (query_ref, extended_ref.at[pl.ds(tok, tok), :]),
        (router_ref, held_router_ref),
    )
    copies = [
        pltpu.make_async_copy(source, target, sems.at[place])
        for place, (source, target) in enumerate(targets)
    ]
    for copy in copies:
        copy.start()
    copies[0].wait()
    chosen = jnp.broadcast_to(chosen_ref[...].astype(jnp.float32), (16, tok))
    extended_ref[2 * tok : 2 * tok + 16, 0:tok] = chosen.astype(jnp.bfloat16)
    extended_ref[2 * tok : 2 * tok + 16, tok:width] = jnp.zeros((16, width - tok), jnp.bfloat16)
    copies[1].wait()
    for k in range(begin_ref.shape[0]):
        position = ranks_ref[k] * tok + lax.broadcasted_iota(jnp.int32, (1, tok), 1)
        begin = jnp.zeros((1, tok), jnp.int32)
        bound = jnp.int32(0)
        for doc in range(held_lengths_ref.shape[1] - 1):
            bound = bound + held_lengths_ref[0, doc]
            begin = jnp.maximum(begin, jnp.where(position >= bound, bound, 0))
        begin_ref[k : k + 1, :] = begin
    copies[6].wait()
    routed = held_router_ref[...].astype(jnp.float32)
    spare = extended_ref.shape[0] - 2 * tok - 16 - routed.shape[0]
    if spare:
        routed = jnp.concatenate([routed, jnp.zeros((spare, width), jnp.float32)], axis=0)
    extended_ref[2 * tok + 16 :, :] = routed.astype(jnp.bfloat16)
    for copy in copies[2:6]:
        copy.wait()


def chosen_of(extended_ref, tok):
    return extended_ref[2 * tok : 2 * tok + 16, 0:tok].astype(jnp.float32)[0:1].astype(jnp.int32)


def router_of(extended_ref, tok, expert_count):
    whole = extended_ref[2 * tok + 16 :, :].astype(jnp.float32)
    return whole[0:expert_count].astype(jnp.bfloat16)


def dispatch_kernel(reps, tok, hot_capacity, own_ref, *refs):
    extended_refs, sent_refs = refs[:reps], refs[reps:]
    for rep in range(reps):
        choice = chosen_of(extended_refs[rep], tok)
        placed = slot_matrix(choice, own_ref[0], len(sent_refs), hot_capacity)
        rows = dot(placed, extended_refs[rep][0:tok, :]).astype(jnp.bfloat16)
        for k, sent_ref in enumerate(sent_refs):
            sent_ref[rep * hot_capacity : (rep + 1) * hot_capacity] = rows[
                k * hot_capacity : (k + 1) * hot_capacity
            ]


def fold_blocks(ids_ref, begin_ref, tasks, reps, states, bias_ref):
    lanes = 128
    per = lanes // HD
    scale = math.log2(math.e) / math.sqrt(HD)
    spreads = {}
    for k, extended_ref, unused_pair, unused_first in tasks:
        if k in spreads:
            continue
        tok = begin_ref.shape[1]
        turned = extended_ref[tok : 2 * tok, :].T
        head_of_row = lax.broadcasted_iota(jnp.int32, (lanes, tok), 0) // HD
        spreads[k] = []
        for group in range(turned.shape[0] // lanes):
            part = turned[group * lanes : (group + 1) * lanes]
            spreads[k].append(
                jnp.concatenate(
                    [
                        jnp.where(head_of_row == head, part, jnp.zeros_like(part))
                        for head in range(per)
                    ],
                    axis=1,
                )
            )

    def fold(place, k, pair_ref, block, begin, fresh):
        top_ref, total_ref, sum_ref = states[k]
        tok = begin.shape[1]
        position = ids_ref[k] * tok + lax.broadcasted_iota(jnp.int32, (1, tok), 1)
        key_position = block * tok + lax.broadcasted_iota(jnp.int32, (tok, tok), 0)
        visible = (key_position >= begin) & (key_position <= position)
        bias_ref[place] = jnp.where(visible, 0.0, masked_score)
        bias = bias_ref[place]
        values = pair_ref[tok : 2 * tok, :].T
        for group, spread in enumerate(spreads[k]):
            columns = slice(group * lanes, (group + 1) * lanes)
            scores = dot(pair_ref[0:tok, columns], spread)
            weights, factors = [], []
            for head in range(per):
                row = group * per + head
                part = scores[:, head * tok : (head + 1) * tok] + bias
                top = jnp.max(part, axis=0, keepdims=True)
                if not fresh:
                    old = top_ref[row : row + 1, :]
                    top = jnp.maximum(top, old)
                    factors.append(jnp.exp2((old - top) * scale))
                weight = jnp.exp2((part - top) * scale)
                total = jnp.sum(weight, axis=0, keepdims=True)
                if not fresh:
                    total = total + total_ref[row : row + 1, :] * factors[head]
                top_ref[row : row + 1, :] = top
                total_ref[row : row + 1, :] = total
                weights.append(weight.astype(jnp.bfloat16))
            summed = dot(values[columns], jnp.concatenate(weights, axis=1))
            for head in range(per):
                rows = slice((group * per + head) * HD, (group * per + head + 1) * HD)
                piece = summed[head * HD : (head + 1) * HD, head * tok : (head + 1) * tok]
                if not fresh:
                    piece = piece + sum_ref[rows, :] * factors[head]
                sum_ref[rows, :] = piece

    for place, (k, unused_extended, pair_ref, first) in enumerate(tasks):
        block = ids_ref[reps + place]
        begin = begin_ref[k : k + 1, :]
        tok = begin.shape[1]
        if first and k == 0:
            fold(place, k, pair_ref, block, begin, True)
            continue
        if first:
            top_ref, total_ref, sum_ref = states[k]
            top_ref[...] = jnp.full(top_ref.shape, masked_score, jnp.float32)
            total_ref[...] = jnp.zeros(total_ref.shape, jnp.float32)
            sum_ref[...] = jnp.zeros(sum_ref.shape, jnp.float32)

        @pl.when((block >= 0) & ((block + 1) * tok > jnp.min(begin)))
        def unused(place=place, k=k, pair_ref=pair_ref, block=block, begin=begin):
            fold(place, k, pair_ref, block, begin, False)


def attend_kernel(plan, reps, counts, packed, ids_ref, begin_ref, *refs):
    ks = sorted({k for k, unused_pair, unused_first in plan})
    old_ks = [k for k in ks if not any(first for j, unused_pair, first in plan if j == k)]
    extended_refs, refs = dict(zip(ks, refs)), refs[len(ks) :]
    pair_refs, refs = refs[:counts], refs[counts:]
    old_refs, refs = refs[: 3 * len(old_ks)], refs[3 * len(old_ks) :]
    bias_ref, refs = refs[-1], refs[:-1]
    packed_refs, state_refs = (refs[: len(ks)], refs[len(ks) :]) if packed else ((), refs)
    states = {k: state_refs[3 * place : 3 * place + 3] for place, k in enumerate(ks)}
    for place, k in enumerate(old_ks):
        for old_ref, new_ref in zip(old_refs[3 * place : 3 * place + 3], states[k]):
            new_ref[...] = old_ref[...]
    tasks = [(k, extended_refs[k], pair_refs[pair], first) for k, pair, first in plan]
    fold_blocks(ids_ref, begin_ref, tasks, reps, states, bias_ref)
    for k, packed_ref in zip(ks, packed_refs):
        top_ref, total_ref, sum_ref = states[k]
        heads, width = top_ref.shape[0], sum_ref.shape[0]
        packed_ref[0:width, :] = sum_ref[...].astype(jnp.bfloat16)
        first = width
        for ref, pieces in ((top_ref, 3), (total_ref, 2)):
            rest = ref[...]
            for unused in range(pieces):
                piece = rest.astype(jnp.bfloat16)
                packed_ref[first : first + heads, :] = piece
                rest = rest - piece.astype(jnp.float32)
                first += heads


def mix_kernel(expert_count, hot_capacity, own_ref, extended_ref, residual_ref, proj_ref, *refs):
    top_ref, total_ref, sum_ref = refs[0:3]
    mixed_ref, sent_refs = refs[-1 - expert_count], refs[len(refs) - expert_count :]
    packed_refs = refs[3 : -1 - expert_count]
    tok, width = mixed_ref.shape
    heads = top_ref.shape[0]
    scale = math.log2(math.e) / math.sqrt(HD)
    tops, totals = [top_ref[...]], [total_ref[...]]
    for packed_ref in packed_refs:
        pieces = [
            packed_ref[width + place * heads : width + (place + 1) * heads, :].astype(jnp.float32)
            for place in range(5)
        ]
        tops.append((pieces[0] + pieces[1]) + pieces[2])
        totals.append(pieces[3] + pieces[4])
    top = functools.reduce(jnp.maximum, tops)
    factors = [jnp.exp2((one - top) * scale) for one in tops]
    total = sum(one * factor for one, factor in zip(totals, factors))
    factors = [factor / total for factor in factors]
    pieces = []
    for head in range(heads):
        rows = slice(head * HD, (head + 1) * HD)
        piece = sum_ref[rows, :] * factors[0][head : head + 1, :]
        for packed_ref, factor in zip(packed_refs, factors[1:]):
            piece = piece + packed_ref[rows, :].astype(jnp.float32) * factor[head : head + 1, :]
        pieces.append(piece.astype(jnp.bfloat16))
    attended = jnp.concatenate(pieces, axis=0).T
    mixed = (residual_ref[...].astype(jnp.float32) + dot(attended, proj_ref[...])).astype(
        jnp.bfloat16
    )
    mixed_ref[...] = mixed
    mixed_f = mixed.astype(jnp.float32)
    inv_rms = lax.rsqrt(jnp.mean(mixed_f * mixed_f, axis=1, keepdims=True) + norm_eps)
    normed = (mixed_f * inv_rms).astype(jnp.bfloat16)
    placed = slot_matrix(chosen_of(extended_ref, tok), own_ref[0], len(sent_refs), hot_capacity)
    rows = dot(placed, normed).astype(jnp.bfloat16)
    for k, sent_ref in enumerate(sent_refs):
        sent_ref[...] = rows[k * hot_capacity : (k + 1) * hot_capacity]


def expert_kernel(
    reps,
    rep_list,
    sources,
    tok,
    strip,
    counts,
    own_ref,
    part_ref,
    up_ref,
    down_ref,
    extended_ref,
    *refs,
):
    row_count, grad_count = counts
    row_refs, refs = refs[:row_count], refs[row_count:]
    per_rep = row_count // len(rep_list)
    grad_refs, refs = refs[:grad_count][::-1], refs[grad_count:]
    own_rows = rep_list[0] == 0
    held_ref, refs = refs[-1], refs[:-1]
    if own_rows:
        back_refs, (up_acc, down_acc) = refs[:-2], refs[-2:]
    else:
        up_old, down_old = refs[:2]
        term_refs, kept_ref = refs[2:-1], refs[-1]
    total_grads = sum(ref.shape[0] for ref in grad_refs)
    capacity = total_grads // (sources * reps)
    count = sources * capacity
    parts = part_ref.shape[0]
    up = up_ref[...]
    down = down_ref[...]
    router = router_of(extended_ref, tok, sources)
    expert_lane = lax.broadcasted_iota(jnp.int32, (count, router.shape[0]), 1) == own_ref[0]

    def strips(rows, place):
        held_ref[place] = rows.T
        taken = []
        for k in range(parts):
            first = pl.multiple_of(part_ref[k] * strip, strip)
            taken.append(held_ref[place, pl.ds(first, strip), :])
        return jnp.concatenate(taken, axis=0)

    up_term = down_term = None
    for place, rep in enumerate(rep_list):
        rows = chunk_rows(
            row_refs[place * per_rep : (place + 1) * per_rep], sources, 0, capacity
        )
        grads = chunk_rows(grad_refs, sources, rep * capacity, (rep + 1) * capacity)
        pre = dot(rows, up)
        sigmoid_pre = jax.nn.sigmoid(pre)
        activated = (pre * sigmoid_pre).astype(jnp.bfloat16)
        logits = dot(rows, router, NT)
        gate = jax.nn.sigmoid(
            jnp.sum(jnp.where(expert_lane, logits, 0.0), axis=1, keepdims=True)
        )
        scaled = (gate * grads.astype(jnp.float32)).astype(jnp.bfloat16)
        act_grad = dot(scaled, down, NT)
        pre_grad = (act_grad * sigmoid_pre * (1.0 + pre * (1.0 - sigmoid_pre))).astype(
            jnp.bfloat16
        )
        if own_rows:
            produced = dot(activated, down).astype(jnp.bfloat16)
            token_grad = dot(pre_grad, up, NT).astype(jnp.bfloat16)
            for k, back_ref in enumerate(back_refs):
                back_ref[0:capacity] = produced[k * capacity : (k + 1) * capacity]
                back_ref[capacity : 2 * capacity] = token_grad[k * capacity : (k + 1) * capacity]
        more_up = dot(strips(rows, 2 * place), pre_grad)
        more_down = dot(strips(activated, 2 * place + 1), scaled)
        up_term = more_up if up_term is None else up_term + more_up
        down_term = more_down if down_term is None else down_term + more_down
    if own_rows:
        up_acc[...] = up_term
        down_acc[...] = down_term
        return
    up_term = up_term + up_old[...]
    down_term = down_term + down_old[...]
    for k in range(parts):
        rows = slice(k * strip, (k + 1) * strip)
        if k == 0:
            kept_ref[0] = up_term[rows]
            kept_ref[1] = down_term[rows]
        else:
            term_refs[k - 1][0] = up_term[rows].astype(jnp.bfloat16)
            term_refs[k - 1][1] = down_term[rows].astype(jnp.bfloat16)


def finish_kernel(
    hot_capacity, expert_count, own_ref, mixed_ref, extended_ref, *refs
):
    back_refs, (layer_ref, grad_mixed_ref) = refs[:-2], refs[-2:]
    tok = mixed_ref.shape[0]
    choice = chosen_of(extended_ref, tok)
    placed = slot_matrix(choice, own_ref[0], expert_count, hot_capacity)
    router = router_of(extended_ref, tok, expert_count)
    mixed_f = mixed_ref[...].astype(jnp.float32)
    inv_rms = lax.rsqrt(jnp.mean(mixed_f * mixed_f, axis=1, keepdims=True) + norm_eps)
    normed = (mixed_f * inv_rms).astype(jnp.bfloat16)
    one_hot = lax.broadcasted_iota(jnp.int32, (expert_count, tok), 0) == choice
    logits = dot(router, normed, NT)
    logit_row = jnp.sum(jnp.where(one_hot, logits, 0.0), axis=0, keepdims=True)
    logit = jnp.broadcast_to(logit_row, (8, tok)).T[:, 0:1]
    gate = jax.nn.sigmoid(logit)
    pair = 2 * hot_capacity
    chunks = [
        ref[first : first + pair] for ref in back_refs for first in range(0, ref.shape[0], pair)
    ]
    results = jnp.concatenate([chunk[:hot_capacity] for chunk in chunks], axis=0)
    grads = jnp.concatenate([chunk[hot_capacity:] for chunk in chunks], axis=0)
    result_f = dot(placed, results, TN)
    normed_grad = dot(placed, grads, TN)
    grad_f = extended_ref[0:tok, :].astype(jnp.float32)
    layer_ref[...] = (mixed_f + gate * result_f).astype(jnp.bfloat16)
    gate_grad = jnp.sum(grad_f * result_f, axis=1, keepdims=True)
    logit_grad = gate_grad * gate * (1.0 - gate)
    router_cols = dot(one_hot.astype(jnp.float32).astype(jnp.bfloat16), router, TN)
    total_grad = normed_grad + logit_grad * router_cols
    mean_term = jnp.mean(total_grad * mixed_f, axis=1, keepdims=True)
    input_grad = inv_rms * total_grad - mixed_f * inv_rms * inv_rms * inv_rms * mean_term
    grad_mixed_ref[...] = (grad_f + input_grad).astype(jnp.bfloat16)


def sum_kernel(kept_ref, *refs):
    term_refs, (up_ref, down_ref) = refs[:-2], refs[-2:]
    for kind, out_ref in enumerate((up_ref, down_ref)):
        total = kept_ref[kind]
        for ref in term_refs:
            total = total + ref[kind].astype(jnp.float32)
        out_ref[...] = total


def shape(dims, dtype=jnp.bfloat16):
    return jax.ShapeDtypeStruct(dims, dtype)


SMEM = pl.BlockSpec(memory_space=pltpu.SMEM)
VMEM = pl.BlockSpec(memory_space=pltpu.VMEM)
HBM = pl.BlockSpec(memory_space=pltpu.HBM)


def call(body, out_shape, specs, scratch=(), cost=0.5):
    return pl.pallas_call(
        body,
        cost_estimate=pl.CostEstimate(
            flops=int(cost * 1e9), bytes_accessed=0, transcendentals=0
        ),
        out_shape=out_shape,
        in_specs=specs,
        out_specs=jax.tree.map(lambda unused: VMEM, out_shape),
        scratch_shapes=list(scratch),
        compiler_params=pltpu.CompilerParams(vmem_limit_bytes=VMEM_LIMIT),
    )


def local(
    seq_count,
    expert_count,
    rep_count,
    query_rows,
    key_rows,
    value_rows,
    doc_lengths,
    residual,
    out_proj,
    router,
    expert_choice,
    weight_in,
    weight_out,
    grad_out,
):
    tok, width = query_rows.shape[1:]
    hidden = weight_in.shape[2]
    heads = width // HD
    experts = Group(("expert",), (expert_count,))
    reps = Group(("rep",), (rep_count,))
    owners = Group(("expert", "rep"), (expert_count, rep_count))
    parts = Group(("seq",), (seq_count,))
    strip = width // (seq_count * rep_count)
    capacity = max(2, (3 * tok + 2 * expert_count - 1) // (2 * expert_count))
    hot_capacity = min(4 * capacity, tok // 2)
    choice = expert_choice.reshape(1, tok)
    seq_index = lax.axis_index("seq")
    rep_index = lax.axis_index("rep")
    rank = seq_index * rep_count + rep_index
    own = jnp.stack([lax.axis_index("expert")]).astype(jnp.int32)
    part_to = jnp.stack(
        [parts.target(seq_index, k) * rep_count + rep_index for k in range(seq_count)]
    ).astype(jnp.int32)

    def send(array, least_seq, seq_step, rep_step, wrap):
        pairs = []
        for s in range(least_seq, seq_count - seq_step):
            for r in range(rep_count):
                to = r + rep_step
                if wrap or 0 <= to < rep_count:
                    pairs.append(
                        (s * rep_count + r, (s + seq_step) * rep_count + to % rep_count)
                    )
        return lax.ppermute(array, ("seq", "rep"), pairs)

    reach = (seq_count + 1) // 2
    longest = (seq_count * rep_count + 1) // 2
    query_ranks = [
        seq_index * rep_count + reps.source(rep_index, k) for k in range(rep_count)
    ]

    def task_ids(plan, steps):
        ids = list(query_ranks)
        for k, pair, unused_first in plan:
            block = rank - steps[pair] * rep_count
            behind = query_ranks[k] - block
            ids.append(jnp.where((block >= 0) & (behind >= 0) & (behind <= longest), block, -1))
        return jnp.stack(ids).astype(jnp.int32)

    state_shapes = [
        shape((heads, tok), jnp.float32),
        shape((heads, tok), jnp.float32),
        shape((width, tok), jnp.float32),
    ]
    tail = 16 + -(-expert_count // 16) * 16
    pair, extended, begin = pl.pallas_call(
        stack_kernel,
        out_shape=[
            shape((2 * tok, width)),
            shape((2 * tok + tail, width)),
            shape((rep_count, tok), jnp.int32),
        ],
        in_specs=[SMEM] + [HBM] * 7,
        out_specs=[VMEM] * 3,
        scratch_shapes=[
            pltpu.VMEM((1, tok), jnp.int32),
            pltpu.VMEM((expert_count, width), jnp.bfloat16),
            pltpu.SMEM(doc_lengths.shape, jnp.int32),
            pltpu.SemaphoreType.DMA((7,)),
        ],
        compiler_params=pltpu.CompilerParams(vmem_limit_bytes=60 * 1024 * 1024),
    )(
        jnp.stack(query_ranks).astype(jnp.int32),
        choice,
        doc_lengths,
        router.T,
        key_rows[0],
        value_rows[0],
        grad_out[0],
        query_rows[0],
    )

    def attend(plan, pairs, steps, extendeds, states, packed, cost):
        ks = sorted({k for k, unused_pair, unused_first in plan})
        old = [one for k in ks if k in states for one in states[k]]
        state_out = state_shapes * len(ks)
        if packed:
            out_shape = [shape((width + 5 * heads, tok))] * len(ks)
            scratch = [pltpu.VMEM(one.shape, one.dtype) for one in state_out]
        else:
            out_shape, scratch = state_out, []
        outs = call(
            functools.partial(attend_kernel, plan, rep_count, len(pairs), packed),
            out_shape,
            [SMEM] + [VMEM] * (1 + len(ks) + len(pairs) + len(old)),
            scratch + [pltpu.VMEM((len(plan), tok, tok), jnp.float32)],
            cost=cost,
        )(task_ids(plan, steps), begin, *[extendeds[k] for k in ks], *pairs, *old)
        if packed:
            return dict(zip(ks, outs))
        return {k: list(outs[3 * place : 3 * place + 3]) for place, k in enumerate(ks)}

    others = range(1, rep_count)
    lines = [pair, send(pair, 0, 1, 0, False)]
    extendeds = reps.exchange([extended] * rep_count)
    states = attend(((0, 0, True),), [pair], [0], [extended], {}, False, 2.0)
    lines[1], *states[0] = lax.optimization_barrier((lines[1], *states[0]))
    for step in range(2, reach + 1):
        lines.append(send(lines[-1], step - 1, 1, 0, False))
    middle = tuple((0, step, False) for step in range(1, reach)) + tuple(
        (k, step, step == 0) for k in others for step in range(reach)
    )
    states = attend(middle, lines[:-1], list(range(reach)), extendeds, states, False, 4.0)
    partial = attend(
        tuple((k, 0, False) for k in others), lines[-1:], [reach], extendeds, states, True, 1.5
    )
    partial[1], *extendeds[1:] = lax.optimization_barrier((partial[1], *extendeds[1:]))
    returned = reps.exchange([None] + [partial[k] for k in others], inverse=True)[1:]
    states = attend(((0, 0, False),), lines[-1:], [reach], extendeds, states, False, 1.5)
    sent_grads = call(
        functools.partial(dispatch_kernel, rep_count, tok, hot_capacity),
        [shape((rep_count * hot_capacity, width))] * expert_count,
        [SMEM] + [VMEM] * rep_count,
    )(own, *extendeds)
    got_grads = merged(experts.exchange(sent_grads), MOST_PERMUTES)[::-1]

    mixed, *sent_rows = call(
        functools.partial(mix_kernel, expert_count, hot_capacity),
        [shape((tok, width))] + [shape((hot_capacity, width))] * expert_count,
        [SMEM] + [VMEM] * (6 + len(returned)),
        cost=2.0,
    )(own, extendeds[0], residual[0], out_proj, *states[0], *returned)
    *sent_rows, got_grads = lax.optimization_barrier((*sent_rows, got_grads))
    arrived = owners.exchange([sent_rows[k // rep_count] for k in range(owners.count)])
    got_rows = merged(arrived[0::rep_count], MOST_PERMUTES)
    got_more = [
        one for k in others for one in merged(arrived[k::rep_count], MOST_PERMUTES)
    ]

    def expert_call(rep_list, rows, out_shape, extra):
        return call(
            functools.partial(
                expert_kernel,
                rep_count,
                rep_list,
                expert_count,
                tok,
                strip,
                (len(rows), len(got_grads)),
            ),
            out_shape,
            [SMEM, SMEM] + [VMEM] * (3 + len(rows) + len(got_grads) + len(extra)),
            [pltpu.VMEM((2 * len(rep_list), width, expert_count * hot_capacity), jnp.bfloat16)],
            cost=2.0,
        )(own, part_to, weight_in[0], weight_out[0], extendeds[0], *rows, *got_grads, *extra)

    *back, up_acc, down_acc = expert_call(
        (0,),
        got_rows,
        [shape((2 * hot_capacity, width))] * expert_count
        + [shape((seq_count * strip, hidden), jnp.float32)]
        + [shape((seq_count * strip, width), jnp.float32)],
        [],
    )
    got_back = merged(experts.exchange(back, inverse=True), MOST_PERMUTES)
    *terms, kept = expert_call(
        tuple(range(1, rep_count)),
        got_more,
        [shape((2, strip, hidden))] * (seq_count - 1)
        + [shape((2, strip, hidden), jnp.float32)],
        [up_acc, down_acc],
    )
    got_terms = parts.exchange([None] + terms)[1:]
    layer_out, grad_mixed = call(
        functools.partial(finish_kernel, hot_capacity, expert_count),
        [shape((tok, width)), shape((tok, width))],
        [SMEM] + [VMEM] * (2 + len(got_back)),
        cost=1.5,
    )(own, mixed, extended, *got_back)
    kept, layer_out = lax.optimization_barrier((kept, layer_out))
    share_in, share_out = call(
        sum_kernel,
        [shape((strip, hidden), jnp.float32), shape((strip, width), jnp.float32)],
        [VMEM] * seq_count,
    )(kept, *got_terms[::-1])
    return (layer_out[None], grad_mixed[None], share_in[None], share_out[None])


def solution(mesh):
    rows = P("expert", ("seq", "rep"), None)
    in_specs = (
        rows,
        rows,
        rows,
        P("expert", None),
        rows,
        P(),
        P(),
        rows,
        P("expert", None, None),
        P("expert", None, None),
        rows,
    )
    body = functools.partial(
        local, mesh.shape["seq"], mesh.shape["expert"], mesh.shape["rep"]
    )
    return jax.shard_map(
        body, mesh=mesh, in_specs=in_specs, out_specs=(rows, rows, rows, rows), check_vma=False
    )
```

```python
import functools
import math

import jax
import jax.numpy as jnp
from jax import lax
from jax.experimental import pallas as pl
from jax.experimental.pallas import tpu as pltpu
from jax.sharding import PartitionSpec as P

HD = 32
norm_eps = 1e-06
masked_score = -1e30
VMEM_LIMIT = 48 * 1024 * 1024
MOST_PERMUTES = 16
NT = (((1,), (1,)), ((), ()))
TN = (((0,), (0,)), ((), ()))


def dot(a, b, dims=None):
    if dims is None:
        return jnp.dot(a, b, preferred_element_type=jnp.float32)
    return lax.dot_general(a, b, dims, preferred_element_type=jnp.float32)


def away(index, offset, size):
    if size & (size - 1) == 0:
        return index ^ offset
    return (index + offset) % size


def back_from(index, offset, size):
    if size & (size - 1) == 0:
        return index ^ offset
    return (index - offset + size) % size


class Group:
    def __init__(self, axes, sizes):
        self.axes, self.sizes = tuple(axes), tuple(sizes)
        self.count = math.prod(sizes)

    def split(self, flat):
        coords = []
        for size in reversed(self.sizes):
            coords.append(flat % size)
            flat = flat // size
        return coords[::-1]

    def moved(self, flat, offset, step):
        place = 0
        for coord, part, size in zip(self.split(flat), self.split(offset), self.sizes):
            place = place * size + step(coord, part, size)
        return place

    def target(self, flat, offset):
        return self.moved(flat, offset, away)

    def source(self, flat, offset):
        return self.moved(flat, offset, back_from)

    def exchange(self, chunks, inverse=False):
        to, start = (self.source, self.target) if inverse else (self.target, self.source)
        if self.count <= MOST_PERMUTES:
            order = sorted(range(1, self.count), key=lambda k: -k)
            got = {0: chunks[0]}
            for k in order:
                pairs = [(i, to(i, k)) for i in range(self.count)]
                got[k] = lax.ppermute(chunks[k], self.axes, pairs)
            return [got[k] for k in range(self.count)]
        me = lax.axis_index(self.axes)
        steps = jnp.arange(self.count, dtype=jnp.int32)
        sent_to = jax.vmap(lambda k: to(me, k))(steps)
        placed = jnp.zeros((self.count,), jnp.int32).at[sent_to].set(steps)
        stacked = jnp.stack(chunks)[placed]
        got = lax.all_to_all(stacked, self.axes, split_axis=0, concat_axis=0, tiled=True)
        came_from = jax.vmap(lambda k: start(me, k))(steps)
        ordered = got[came_from]
        return [ordered[k] for k in range(self.count)]


def merged(chunks, most):
    if len(chunks) <= most:
        return list(chunks)
    return [jnp.concatenate(chunks, axis=0)]


def chunk_rows(refs, count, low, high):
    size = sum(ref.shape[0] for ref in refs) // count
    parts = []
    for chunk in range(count):
        ref, first = (refs[chunk], 0) if len(refs) == count else (refs[0], chunk * size)
        parts.append(ref[first + low : first + high, :])
    return parts[0] if count == 1 else jnp.concatenate(parts, axis=0)


def slot_matrix(choice, own, expert_count, hot_capacity):
    tok = choice.shape[1]
    offset = back_from(choice, own, expert_count)
    one_hot = lax.broadcasted_iota(jnp.int32, (expert_count, tok), 0) == offset
    hits = one_hot.astype(jnp.float32).astype(jnp.bfloat16)
    earlier = lax.broadcasted_iota(jnp.int32, (tok, tok), 0) <= lax.broadcasted_iota(
        jnp.int32, (tok, tok), 1
    )
    counted = dot(hits, earlier.astype(jnp.float32).astype(jnp.bfloat16))
    rank = jnp.sum(jnp.where(one_hot, counted, 0.0), axis=0, keepdims=True) - 1.0
    slots = offset * hot_capacity + rank.astype(jnp.int32)
    rows = lax.broadcasted_iota(jnp.int32, (expert_count * hot_capacity, tok), 0)
    return (rows == slots).astype(jnp.float32).astype(jnp.bfloat16)


def stack_kernel(key_ref, value_ref, pair_ref, sems):
    tok = key_ref.shape[0]
    copies = [
        pltpu.make_async_copy(ref, pair_ref.at[pl.ds(place * tok, tok), :], sems.at[place])
        for place, ref in enumerate((key_ref, value_ref))
    ]
    for copy in copies:
        copy.start()
    for copy in copies:
        copy.wait()


def extend_kernel(
    ranks_ref,
    choice_ref,
    lengths_ref,
    router_ref,
    grad_ref,
    query_ref,
    extended_ref,
    begin_ref,
    chosen_ref,
    held_router_ref,
    held_lengths_ref,
    sems,
):
    tok, width = query_ref.shape
    targets = (
        (choice_ref, chosen_ref),
        (lengths_ref, held_lengths_ref),
        (grad_ref, extended_ref.at[pl.ds(0, tok), :]),
        (query_ref, extended_ref.at[pl.ds(tok, tok), :]),
        (router_ref, held_router_ref),
    )
    copies = [
        pltpu.make_async_copy(source, target, sems.at[place])
        for place, (source, target) in enumerate(targets)
    ]
    for copy in copies:
        copy.start()
    copies[0].wait()
    chosen = jnp.broadcast_to(chosen_ref[...].astype(jnp.float32), (16, tok))
    extended_ref[2 * tok : 2 * tok + 16, 0:tok] = chosen.astype(jnp.bfloat16)
    extended_ref[2 * tok : 2 * tok + 16, tok:width] = jnp.zeros((16, width - tok), jnp.bfloat16)
    copies[1].wait()
    for k in range(begin_ref.shape[0]):
        position = ranks_ref[k] * tok + lax.broadcasted_iota(jnp.int32, (1, tok), 1)
        begin = jnp.zeros((1, tok), jnp.int32)
        bound = jnp.int32(0)
        for doc in range(held_lengths_ref.shape[1] - 1):
            bound = bound + held_lengths_ref[0, doc]
            begin = jnp.maximum(begin, jnp.where(position >= bound, bound, 0))
        begin_ref[k : k + 1, :] = begin
    copies[4].wait()
    routed = held_router_ref[...].astype(jnp.float32)
    spare = extended_ref.shape[0] - 2 * tok - 16 - routed.shape[0]
    if spare:
        routed = jnp.concatenate([routed, jnp.zeros((spare, width), jnp.float32)], axis=0)
    extended_ref[2 * tok + 16 :, :] = routed.astype(jnp.bfloat16)
    for copy in copies[2:4]:
        copy.wait()


def chosen_of(extended_ref, tok):
    return extended_ref[2 * tok : 2 * tok + 16, 0:tok].astype(jnp.float32)[0:1].astype(jnp.int32)


def router_of(extended_ref, tok, expert_count):
    whole = extended_ref[2 * tok + 16 :, :].astype(jnp.float32)
    return whole[0:expert_count].astype(jnp.bfloat16)


def dispatch_kernel(reps, tok, hot_capacity, own_ref, *refs):
    extended_refs, sent_refs = refs[:reps], refs[reps:]
    for rep in range(reps):
        choice = chosen_of(extended_refs[rep], tok)
        placed = slot_matrix(choice, own_ref[0], len(sent_refs), hot_capacity)
        rows = dot(placed, extended_refs[rep][0:tok, :]).astype(jnp.bfloat16)
        for k, sent_ref in enumerate(sent_refs):
            sent_ref[rep * hot_capacity : (rep + 1) * hot_capacity] = rows[
                k * hot_capacity : (k + 1) * hot_capacity
            ]


def fold_blocks(ids_ref, begin_ref, tasks, reps, states, bias_ref):
    lanes = 128
    per = lanes // HD
    scale = math.log2(math.e) / math.sqrt(HD)
    spreads = {}
    for k, extended_ref, unused_pair, unused_first in tasks:
        if k in spreads:
            continue
        tok = begin_ref.shape[1]
        first_row = 0 if extended_ref.shape[0] == tok else tok
        turned = extended_ref[first_row : first_row + tok, :].T
        head_of_row = lax.broadcasted_iota(jnp.int32, (lanes, tok), 0) // HD
        spreads[k] = []
        for group in range(turned.shape[0] // lanes):
            part = turned[group * lanes : (group + 1) * lanes]
            spreads[k].append(
                jnp.concatenate(
                    [
                        jnp.where(head_of_row == head, part, jnp.zeros_like(part))
                        for head in range(per)
                    ],
                    axis=1,
                )
            )

    def fold(place, k, pair_ref, block, begin, fresh):
        top_ref, total_ref, sum_ref = states[k]
        tok = begin.shape[1]
        position = ids_ref[k] * tok + lax.broadcasted_iota(jnp.int32, (1, tok), 1)
        key_position = block * tok + lax.broadcasted_iota(jnp.int32, (tok, tok), 0)
        visible = (key_position >= begin) & (key_position <= position)
        bias_ref[place] = jnp.where(visible, 0.0, masked_score)
        bias = bias_ref[place]
        if isinstance(pair_ref, tuple):
            key_ref, value_ref, first_value = pair_ref[0], pair_ref[1], 0
        else:
            key_ref, value_ref, first_value = pair_ref, pair_ref, tok
        values = value_ref[first_value : first_value + tok, :].T
        for group, spread in enumerate(spreads[k]):
            columns = slice(group * lanes, (group + 1) * lanes)
            scores = dot(key_ref[0:tok, columns], spread)
            weights, factors = [], []
            for head in range(per):
                row = group * per + head
                part = scores[:, head * tok : (head + 1) * tok] + bias
                top = jnp.max(part, axis=0, keepdims=True)
                if not fresh:
                    old = top_ref[row : row + 1, :]
                    top = jnp.maximum(top, old)
                    factors.append(jnp.exp2((old - top) * scale))
                weight = jnp.exp2((part - top) * scale)
                total = jnp.sum(weight, axis=0, keepdims=True)
                if not fresh:
                    total = total + total_ref[row : row + 1, :] * factors[head]
                top_ref[row : row + 1, :] = top
                total_ref[row : row + 1, :] = total
                weights.append(weight.astype(jnp.bfloat16))
            summed = dot(values[columns], jnp.concatenate(weights, axis=1))
            for head in range(per):
                rows = slice((group * per + head) * HD, (group * per + head + 1) * HD)
                piece = summed[head * HD : (head + 1) * HD, head * tok : (head + 1) * tok]
                if not fresh:
                    piece = piece + sum_ref[rows, :] * factors[head]
                sum_ref[rows, :] = piece

    for place, (k, unused_extended, pair_ref, first) in enumerate(tasks):
        block = ids_ref[reps + place]
        begin = begin_ref[k : k + 1, :]
        tok = begin.shape[1]
        if first and k == 0:
            fold(place, k, pair_ref, block, begin, True)
            continue
        if first:
            top_ref, total_ref, sum_ref = states[k]
            top_ref[...] = jnp.full(top_ref.shape, masked_score, jnp.float32)
            total_ref[...] = jnp.zeros(total_ref.shape, jnp.float32)
            sum_ref[...] = jnp.zeros(sum_ref.shape, jnp.float32)

        @pl.when((block >= 0) & ((block + 1) * tok > jnp.min(begin)))
        def unused(place=place, k=k, pair_ref=pair_ref, block=block, begin=begin):
            fold(place, k, pair_ref, block, begin, False)


def attend_kernel(plan, reps, counts, packed, ids_ref, begin_ref, *refs):
    ks = sorted({k for k, unused_pair, unused_first in plan})
    old_ks = [k for k in ks if not any(first for j, unused_pair, first in plan if j == k)]
    extended_refs, refs = dict(zip(ks, refs)), refs[len(ks) :]
    if counts == 0:
        pair_refs, refs = [tuple(refs[:2])], refs[2:]
    else:
        pair_refs, refs = refs[:counts], refs[counts:]
    old_refs, refs = refs[: 3 * len(old_ks)], refs[3 * len(old_ks) :]
    bias_ref, refs = refs[-1], refs[:-1]
    packed_refs, state_refs = (refs[: len(ks)], refs[len(ks) :]) if packed else ((), refs)
    states = {k: state_refs[3 * place : 3 * place + 3] for place, k in enumerate(ks)}
    for place, k in enumerate(old_ks):
        for old_ref, new_ref in zip(old_refs[3 * place : 3 * place + 3], states[k]):
            new_ref[...] = old_ref[...]
    tasks = [(k, extended_refs[k], pair_refs[pair], first) for k, pair, first in plan]
    fold_blocks(ids_ref, begin_ref, tasks, reps, states, bias_ref)
    for k, packed_ref in zip(ks, packed_refs):
        top_ref, total_ref, sum_ref = states[k]
        heads, width = top_ref.shape[0], sum_ref.shape[0]
        packed_ref[0:width, :] = sum_ref[...].astype(jnp.bfloat16)
        first = width
        for ref, pieces in ((top_ref, 3), (total_ref, 2)):
            rest = ref[...]
            for unused in range(pieces):
                piece = rest.astype(jnp.bfloat16)
                packed_ref[first : first + heads, :] = piece
                rest = rest - piece.astype(jnp.float32)
                first += heads


def mix_kernel(expert_count, hot_capacity, own_ref, extended_ref, residual_ref, proj_ref, *refs):
    top_ref, total_ref, sum_ref = refs[0:3]
    mixed_ref, sent_refs = refs[-1 - expert_count], refs[len(refs) - expert_count :]
    packed_refs = refs[3 : -1 - expert_count]
    tok, width = mixed_ref.shape
    heads = top_ref.shape[0]
    scale = math.log2(math.e) / math.sqrt(HD)
    tops, totals = [top_ref[...]], [total_ref[...]]
    for packed_ref in packed_refs:
        pieces = [
            packed_ref[width + place * heads : width + (place + 1) * heads, :].astype(jnp.float32)
            for place in range(5)
        ]
        tops.append((pieces[0] + pieces[1]) + pieces[2])
        totals.append(pieces[3] + pieces[4])
    top = functools.reduce(jnp.maximum, tops)
    factors = [jnp.exp2((one - top) * scale) for one in tops]
    total = sum(one * factor for one, factor in zip(totals, factors))
    factors = [factor / total for factor in factors]
    pieces = []
    for head in range(heads):
        rows = slice(head * HD, (head + 1) * HD)
        piece = sum_ref[rows, :] * factors[0][head : head + 1, :]
        for packed_ref, factor in zip(packed_refs, factors[1:]):
            piece = piece + packed_ref[rows, :].astype(jnp.float32) * factor[head : head + 1, :]
        pieces.append(piece.astype(jnp.bfloat16))
    attended = jnp.concatenate(pieces, axis=0).T
    mixed = (residual_ref[...].astype(jnp.float32) + dot(attended, proj_ref[...])).astype(
        jnp.bfloat16
    )
    mixed_ref[...] = mixed
    mixed_f = mixed.astype(jnp.float32)
    inv_rms = lax.rsqrt(jnp.mean(mixed_f * mixed_f, axis=1, keepdims=True) + norm_eps)
    normed = (mixed_f * inv_rms).astype(jnp.bfloat16)
    placed = slot_matrix(chosen_of(extended_ref, tok), own_ref[0], len(sent_refs), hot_capacity)
    rows = dot(placed, normed).astype(jnp.bfloat16)
    for k, sent_ref in enumerate(sent_refs):
        sent_ref[...] = rows[k * hot_capacity : (k + 1) * hot_capacity]


def expert_kernel(
    reps,
    rep_list,
    sources,
    tok,
    strip,
    counts,
    own_ref,
    part_ref,
    up_ref,
    down_ref,
    extended_ref,
    *refs,
):
    row_count, grad_count = counts
    row_refs, refs = refs[:row_count], refs[row_count:]
    per_rep = row_count // len(rep_list)
    grad_refs, refs = refs[:grad_count][::-1], refs[grad_count:]
    own_rows = rep_list[0] == 0
    held_ref, refs = refs[-1], refs[:-1]
    if own_rows:
        back_refs, (up_acc, down_acc) = refs[:-2], refs[-2:]
    else:
        up_old, down_old = refs[:2]
        term_refs, kept_ref = refs[2:-1], refs[-1]
    total_grads = sum(ref.shape[0] for ref in grad_refs)
    capacity = total_grads // (sources * reps)
    count = sources * capacity
    parts = part_ref.shape[0]
    up = up_ref[...]
    down = down_ref[...]
    router = router_of(extended_ref, tok, sources)
    expert_lane = lax.broadcasted_iota(jnp.int32, (count, router.shape[0]), 1) == own_ref[0]

    def strips(rows, place):
        held_ref[place] = rows.T
        taken = []
        for k in range(parts):
            first = pl.multiple_of(part_ref[k] * strip, strip)
            taken.append(held_ref[place, pl.ds(first, strip), :])
        return jnp.concatenate(taken, axis=0)

    up_term = down_term = None
    for place, rep in enumerate(rep_list):
        rows = chunk_rows(
            row_refs[place * per_rep : (place + 1) * per_rep], sources, 0, capacity
        )
        grads = chunk_rows(grad_refs, sources, rep * capacity, (rep + 1) * capacity)
        pre = dot(rows, up)
        sigmoid_pre = jax.nn.sigmoid(pre)
        activated = (pre * sigmoid_pre).astype(jnp.bfloat16)
        logits = dot(rows, router, NT)
        gate = jax.nn.sigmoid(
            jnp.sum(jnp.where(expert_lane, logits, 0.0), axis=1, keepdims=True)
        )
        scaled = (gate * grads.astype(jnp.float32)).astype(jnp.bfloat16)
        act_grad = dot(scaled, down, NT)
        pre_grad = (act_grad * sigmoid_pre * (1.0 + pre * (1.0 - sigmoid_pre))).astype(
            jnp.bfloat16
        )
        if own_rows:
            produced = dot(activated, down).astype(jnp.bfloat16)
            token_grad = dot(pre_grad, up, NT).astype(jnp.bfloat16)
            for k, back_ref in enumerate(back_refs):
                back_ref[0:capacity] = produced[k * capacity : (k + 1) * capacity]
                back_ref[capacity : 2 * capacity] = token_grad[k * capacity : (k + 1) * capacity]
        more_up = dot(strips(rows, 2 * place), pre_grad)
        more_down = dot(strips(activated, 2 * place + 1), scaled)
        up_term = more_up if up_term is None else up_term + more_up
        down_term = more_down if down_term is None else down_term + more_down
    if own_rows:
        up_acc[...] = up_term
        down_acc[...] = down_term
        return
    up_term = up_term + up_old[...]
    down_term = down_term + down_old[...]
    for k in range(parts):
        rows = slice(k * strip, (k + 1) * strip)
        if k == 0:
            kept_ref[0] = up_term[rows]
            kept_ref[1] = down_term[rows]
        else:
            term_refs[k - 1][0] = up_term[rows].astype(jnp.bfloat16)
            term_refs[k - 1][1] = down_term[rows].astype(jnp.bfloat16)


def finish_kernel(
    hot_capacity, expert_count, own_ref, mixed_ref, extended_ref, *refs
):
    back_refs, (layer_ref, grad_mixed_ref) = refs[:-2], refs[-2:]
    tok = mixed_ref.shape[0]
    choice = chosen_of(extended_ref, tok)
    placed = slot_matrix(choice, own_ref[0], expert_count, hot_capacity)
    router = router_of(extended_ref, tok, expert_count)
    mixed_f = mixed_ref[...].astype(jnp.float32)
    inv_rms = lax.rsqrt(jnp.mean(mixed_f * mixed_f, axis=1, keepdims=True) + norm_eps)
    normed = (mixed_f * inv_rms).astype(jnp.bfloat16)
    one_hot = lax.broadcasted_iota(jnp.int32, (expert_count, tok), 0) == choice
    logits = dot(router, normed, NT)
    logit_row = jnp.sum(jnp.where(one_hot, logits, 0.0), axis=0, keepdims=True)
    logit = jnp.broadcast_to(logit_row, (8, tok)).T[:, 0:1]
    gate = jax.nn.sigmoid(logit)
    pair = 2 * hot_capacity
    chunks = [
        ref[first : first + pair] for ref in back_refs for first in range(0, ref.shape[0], pair)
    ]
    results = jnp.concatenate([chunk[:hot_capacity] for chunk in chunks], axis=0)
    grads = jnp.concatenate([chunk[hot_capacity:] for chunk in chunks], axis=0)
    result_f = dot(placed, results, TN)
    normed_grad = dot(placed, grads, TN)
    grad_f = extended_ref[0:tok, :].astype(jnp.float32)
    layer_ref[...] = (mixed_f + gate * result_f).astype(jnp.bfloat16)
    gate_grad = jnp.sum(grad_f * result_f, axis=1, keepdims=True)
    logit_grad = gate_grad * gate * (1.0 - gate)
    router_cols = dot(one_hot.astype(jnp.float32).astype(jnp.bfloat16), router, TN)
    total_grad = normed_grad + logit_grad * router_cols
    mean_term = jnp.mean(total_grad * mixed_f, axis=1, keepdims=True)
    input_grad = inv_rms * total_grad - mixed_f * inv_rms * inv_rms * inv_rms * mean_term
    grad_mixed_ref[...] = (grad_f + input_grad).astype(jnp.bfloat16)


def sum_kernel(kept_ref, *refs):
    term_refs, (up_ref, down_ref) = refs[:-2], refs[-2:]
    for kind, out_ref in enumerate((up_ref, down_ref)):
        total = kept_ref[kind]
        for ref in term_refs:
            total = total + ref[kind].astype(jnp.float32)
        out_ref[...] = total


def shape(dims, dtype=jnp.bfloat16):
    return jax.ShapeDtypeStruct(dims, dtype)


SMEM = pl.BlockSpec(memory_space=pltpu.SMEM)
VMEM = pl.BlockSpec(memory_space=pltpu.VMEM)
HBM = pl.BlockSpec(memory_space=pltpu.HBM)


def call(body, out_shape, specs, scratch=(), cost=0.5):
    return pl.pallas_call(
        body,
        cost_estimate=pl.CostEstimate(
            flops=int(cost * 1e9), bytes_accessed=0, transcendentals=0
        ),
        out_shape=out_shape,
        in_specs=specs,
        out_specs=jax.tree.map(lambda unused: VMEM, out_shape),
        scratch_shapes=list(scratch),
        compiler_params=pltpu.CompilerParams(vmem_limit_bytes=VMEM_LIMIT),
    )


def local(
    seq_count,
    expert_count,
    rep_count,
    query_rows,
    key_rows,
    value_rows,
    doc_lengths,
    residual,
    out_proj,
    router,
    expert_choice,
    weight_in,
    weight_out,
    grad_out,
):
    tok, width = query_rows.shape[1:]
    hidden = weight_in.shape[2]
    heads = width // HD
    experts = Group(("expert",), (expert_count,))
    reps = Group(("rep",), (rep_count,))
    owners = Group(("expert", "rep"), (expert_count, rep_count))
    parts = Group(("seq",), (seq_count,))
    strip = width // (seq_count * rep_count)
    capacity = max(2, (3 * tok + 2 * expert_count - 1) // (2 * expert_count))
    hot_capacity = min(4 * capacity, tok // 2)
    choice = expert_choice.reshape(1, tok)
    seq_index = lax.axis_index("seq")
    rep_index = lax.axis_index("rep")
    rank = seq_index * rep_count + rep_index
    own = jnp.stack([lax.axis_index("expert")]).astype(jnp.int32)
    part_to = jnp.stack(
        [parts.target(seq_index, k) * rep_count + rep_index for k in range(seq_count)]
    ).astype(jnp.int32)

    def forward(array):
        return lax.ppermute(array, "seq", [(i, (i + 1) % seq_count) for i in range(seq_count)])

    reach = (seq_count + 1) // 2
    longest = (seq_count * rep_count + 1) // 2
    query_ranks = [
        seq_index * rep_count + reps.source(rep_index, k) for k in range(rep_count)
    ]

    def task_ids(plan, steps):
        ids = list(query_ranks)
        for k, pair, unused_first in plan:
            block = rank - steps[pair] * rep_count
            behind = query_ranks[k] - block
            ids.append(jnp.where((block >= 0) & (behind >= 0) & (behind <= longest), block, -1))
        return jnp.stack(ids).astype(jnp.int32)

    state_shapes = [
        shape((heads, tok), jnp.float32),
        shape((heads, tok), jnp.float32),
        shape((width, tok), jnp.float32),
    ]
    tail = 16 + -(-expert_count // 16) * 16
    def early(body, out_shape, specs, scratch):
        return pl.pallas_call(
            body,
            out_shape=out_shape,
            in_specs=specs,
            out_specs=jax.tree.map(lambda unused: VMEM, out_shape),
            scratch_shapes=scratch,
            compiler_params=pltpu.CompilerParams(vmem_limit_bytes=60 * 1024 * 1024),
        )

    pair = early(
        stack_kernel, shape((2 * tok, width)), [HBM, HBM], [pltpu.SemaphoreType.DMA((2,))]
    )(key_rows[0], value_rows[0])
    extended, begin = early(
        extend_kernel,
        [shape((2 * tok + tail, width)), shape((rep_count, tok), jnp.int32)],
        [SMEM] + [HBM] * 5,
        [
            pltpu.VMEM((1, tok), jnp.int32),
            pltpu.VMEM((expert_count, width), jnp.bfloat16),
            pltpu.SMEM(doc_lengths.shape, jnp.int32),
            pltpu.SemaphoreType.DMA((5,)),
        ],
    )(
        jnp.stack(query_ranks).astype(jnp.int32),
        choice,
        doc_lengths,
        router.T,
        grad_out[0],
        query_rows[0],
    )

    def attend(plan, pairs, steps, extendeds, states, packed, cost, raw=False):
        ks = sorted({k for k, unused_pair, unused_first in plan})
        old = [one for k in ks if k in states for one in states[k]]
        state_out = state_shapes * len(ks)
        if packed:
            out_shape = [shape((width + 5 * heads, tok))] * len(ks)
            scratch = [pltpu.VMEM(one.shape, one.dtype) for one in state_out]
        else:
            out_shape, scratch = state_out, []
        outs = call(
            functools.partial(
                attend_kernel, plan, rep_count, 0 if raw else len(pairs), packed
            ),
            out_shape,
            [SMEM] + [VMEM] * (1 + len(ks) + len(pairs) + len(old)),
            scratch + [pltpu.VMEM((len(plan), tok, tok), jnp.float32)],
            cost=cost,
        )(task_ids(plan, steps), begin, *[extendeds[k] for k in ks], *pairs, *old)
        if packed:
            return dict(zip(ks, outs))
        return {k: list(outs[3 * place : 3 * place + 3]) for place, k in enumerate(ks)}

    others = range(1, rep_count)
    lines = [pair, forward(pair)]
    extendeds = reps.exchange([extended] * rep_count)
    states = attend(
        ((0, 0, True),), [key_rows[0], value_rows[0]], [0], [query_rows[0]], {}, False, 2.0, True
    )
    lines[1], *states[0] = lax.optimization_barrier((lines[1], *states[0]))
    for step in range(2, reach + 1):
        lines.append(forward(lines[-1]))
    middle = tuple((0, step, False) for step in range(1, reach)) + tuple(
        (k, step, step == 0) for k in others for step in range(reach)
    )
    states = attend(middle, lines[:-1], list(range(reach)), extendeds, states, False, 4.0)
    partial = attend(
        tuple((k, 0, False) for k in others), lines[-1:], [reach], extendeds, states, True, 1.5
    )
    partial[1], *extendeds[1:] = lax.optimization_barrier((partial[1], *extendeds[1:]))
    returned = reps.exchange([None] + [partial[k] for k in others], inverse=True)[1:]
    states = attend(((0, 0, False),), lines[-1:], [reach], extendeds, states, False, 1.5)
    sent_grads = call(
        functools.partial(dispatch_kernel, rep_count, tok, hot_capacity),
        [shape((rep_count * hot_capacity, width))] * expert_count,
        [SMEM] + [VMEM] * rep_count,
    )(own, *extendeds)
    got_grads = merged(experts.exchange(sent_grads), MOST_PERMUTES)[::-1]

    mixed, *sent_rows = call(
        functools.partial(mix_kernel, expert_count, hot_capacity),
        [shape((tok, width))] + [shape((hot_capacity, width))] * expert_count,
        [SMEM] + [VMEM] * (6 + len(returned)),
        cost=2.0,
    )(own, extendeds[0], residual[0], out_proj, *states[0], *returned)
    arrived = owners.exchange([sent_rows[k // rep_count] for k in range(owners.count)])
    got_rows = merged(arrived[0::rep_count], MOST_PERMUTES)
    got_more = [
        one for k in others for one in merged(arrived[k::rep_count], MOST_PERMUTES)
    ]

    def expert_call(rep_list, rows, out_shape, extra):
        return call(
            functools.partial(
                expert_kernel,
                rep_count,
                rep_list,
                expert_count,
                tok,
                strip,
                (len(rows), len(got_grads)),
            ),
            out_shape,
            [SMEM, SMEM] + [VMEM] * (3 + len(rows) + len(got_grads) + len(extra)),
            [pltpu.VMEM((2 * len(rep_list), width, expert_count * hot_capacity), jnp.bfloat16)],
            cost=2.0,
        )(own, part_to, weight_in[0], weight_out[0], extendeds[0], *rows, *got_grads, *extra)

    *back, up_acc, down_acc = expert_call(
        (0,),
        got_rows,
        [shape((2 * hot_capacity, width))] * expert_count
        + [shape((seq_count * strip, hidden), jnp.float32)]
        + [shape((seq_count * strip, width), jnp.float32)],
        [],
    )
    got_back = merged(experts.exchange(back, inverse=True), MOST_PERMUTES)
    *terms, kept = expert_call(
        tuple(range(1, rep_count)),
        got_more,
        [shape((2, strip, hidden))] * (seq_count - 1)
        + [shape((2, strip, hidden), jnp.float32)],
        [up_acc, down_acc],
    )
    got_terms = parts.exchange([None] + terms)[1:]
    layer_out, grad_mixed = call(
        functools.partial(finish_kernel, hot_capacity, expert_count),
        [shape((tok, width)), shape((tok, width))],
        [SMEM] + [VMEM] * (2 + len(got_back)),
        cost=1.5,
    )(own, mixed, extended, *got_back)
    kept, layer_out = lax.optimization_barrier((kept, layer_out))
    share_in, share_out = call(
        sum_kernel,
        [shape((strip, hidden), jnp.float32), shape((strip, width), jnp.float32)],
        [VMEM] * seq_count,
    )(kept, *got_terms[::-1])
    return (layer_out[None], grad_mixed[None], share_in[None], share_out[None])


def solution(mesh):
    rows = P("expert", ("seq", "rep"), None)
    in_specs = (
        rows,
        rows,
        rows,
        P("expert", None),
        rows,
        P(),
        P(),
        rows,
        P("expert", None, None),
        P("expert", None, None),
        rows,
    )
    body = functools.partial(
        local, mesh.shape["seq"], mesh.shape["expert"], mesh.shape["rep"]
    )
    return jax.shard_map(
        body, mesh=mesh, in_specs=in_specs, out_specs=(rows, rows, rows, rows), check_vma=False
    )
```

```python
import functools
import math

import jax
import jax.numpy as jnp
from jax import lax
from jax.experimental import pallas as pl
from jax.experimental.pallas import tpu as pltpu
from jax.sharding import PartitionSpec as P

HD = 32
norm_eps = 1e-06
masked_score = -1e30
VMEM_LIMIT = 48 * 1024 * 1024
MOST_PERMUTES = 16
NT = (((1,), (1,)), ((), ()))
TN = (((0,), (0,)), ((), ()))


def dot(a, b, dims=None):
    if dims is None:
        return jnp.dot(a, b, preferred_element_type=jnp.float32)
    return lax.dot_general(a, b, dims, preferred_element_type=jnp.float32)


def away(index, offset, size):
    if size & (size - 1) == 0:
        return index ^ offset
    return (index + offset) % size


def back_from(index, offset, size):
    if size & (size - 1) == 0:
        return index ^ offset
    return (index - offset + size) % size


class Group:
    def __init__(self, axes, sizes):
        self.axes, self.sizes = tuple(axes), tuple(sizes)
        self.count = math.prod(sizes)

    def split(self, flat):
        coords = []
        for size in reversed(self.sizes):
            coords.append(flat % size)
            flat = flat // size
        return coords[::-1]

    def moved(self, flat, offset, step):
        place = 0
        for coord, part, size in zip(self.split(flat), self.split(offset), self.sizes):
            place = place * size + step(coord, part, size)
        return place

    def target(self, flat, offset):
        return self.moved(flat, offset, away)

    def source(self, flat, offset):
        return self.moved(flat, offset, back_from)

    def exchange(self, chunks, inverse=False):
        to, start = (self.source, self.target) if inverse else (self.target, self.source)
        if self.count <= MOST_PERMUTES:
            order = sorted(range(1, self.count), key=lambda k: -k)
            got = {0: chunks[0]}
            for k in order:
                pairs = [(i, to(i, k)) for i in range(self.count)]
                got[k] = lax.ppermute(chunks[k], self.axes, pairs)
            return [got[k] for k in range(self.count)]
        me = lax.axis_index(self.axes)
        steps = jnp.arange(self.count, dtype=jnp.int32)
        sent_to = jax.vmap(lambda k: to(me, k))(steps)
        placed = jnp.zeros((self.count,), jnp.int32).at[sent_to].set(steps)
        stacked = jnp.stack(chunks)[placed]
        got = lax.all_to_all(stacked, self.axes, split_axis=0, concat_axis=0, tiled=True)
        came_from = jax.vmap(lambda k: start(me, k))(steps)
        ordered = got[came_from]
        return [ordered[k] for k in range(self.count)]


def merged(chunks, most):
    if len(chunks) <= most:
        return list(chunks)
    return [jnp.concatenate(chunks, axis=0)]


def chunk_rows(refs, count, low, high):
    size = sum(ref.shape[0] for ref in refs) // count
    parts = []
    for chunk in range(count):
        ref, first = (refs[chunk], 0) if len(refs) == count else (refs[0], chunk * size)
        parts.append(ref[first + low : first + high, :])
    return parts[0] if count == 1 else jnp.concatenate(parts, axis=0)


def slot_matrix(choice, own, expert_count, hot_capacity):
    tok = choice.shape[1]
    offset = back_from(choice, own, expert_count)
    one_hot = lax.broadcasted_iota(jnp.int32, (expert_count, tok), 0) == offset
    hits = one_hot.astype(jnp.float32).astype(jnp.bfloat16)
    earlier = lax.broadcasted_iota(jnp.int32, (tok, tok), 0) <= lax.broadcasted_iota(
        jnp.int32, (tok, tok), 1
    )
    counted = dot(hits, earlier.astype(jnp.float32).astype(jnp.bfloat16))
    rank = jnp.sum(jnp.where(one_hot, counted, 0.0), axis=0, keepdims=True) - 1.0
    slots = offset * hot_capacity + rank.astype(jnp.int32)
    rows = lax.broadcasted_iota(jnp.int32, (expert_count * hot_capacity, tok), 0)
    return (rows == slots).astype(jnp.float32).astype(jnp.bfloat16)


def stack_kernel(key_ref, value_ref, pair_ref, sems):
    tok = key_ref.shape[0]
    copies = [
        pltpu.make_async_copy(ref, pair_ref.at[pl.ds(place * tok, tok), :], sems.at[place])
        for place, ref in enumerate((key_ref, value_ref))
    ]
    for copy in copies:
        copy.start()
    for copy in copies:
        copy.wait()


def extend_kernel(
    ranks_ref,
    choice_ref,
    lengths_ref,
    router_ref,
    grad_ref,
    extended_ref,
    begin_ref,
    chosen_ref,
    held_router_ref,
    held_lengths_ref,
    sems,
):
    tok, width = grad_ref.shape
    targets = (
        (choice_ref, chosen_ref),
        (lengths_ref, held_lengths_ref),
        (grad_ref, extended_ref.at[pl.ds(0, tok), :]),
        (router_ref, held_router_ref),
    )
    copies = [
        pltpu.make_async_copy(source, target, sems.at[place])
        for place, (source, target) in enumerate(targets)
    ]
    for copy in copies:
        copy.start()
    copies[0].wait()
    chosen = jnp.broadcast_to(chosen_ref[...].astype(jnp.float32), (16, tok))
    extended_ref[tok : tok + 16, 0:tok] = chosen.astype(jnp.bfloat16)
    extended_ref[tok : tok + 16, tok:width] = jnp.zeros((16, width - tok), jnp.bfloat16)
    copies[1].wait()
    for k in range(begin_ref.shape[0]):
        position = ranks_ref[k] * tok + lax.broadcasted_iota(jnp.int32, (1, tok), 1)
        begin = jnp.zeros((1, tok), jnp.int32)
        bound = jnp.int32(0)
        for doc in range(held_lengths_ref.shape[1] - 1):
            bound = bound + held_lengths_ref[0, doc]
            begin = jnp.maximum(begin, jnp.where(position >= bound, bound, 0))
        begin_ref[k : k + 1, :] = begin
    copies[3].wait()
    routed = held_router_ref[...].astype(jnp.float32)
    spare = extended_ref.shape[0] - tok - 16 - routed.shape[0]
    if spare:
        routed = jnp.concatenate([routed, jnp.zeros((spare, width), jnp.float32)], axis=0)
    extended_ref[tok + 16 :, :] = routed.astype(jnp.bfloat16)
    copies[2].wait()


def chosen_of(extended_ref, tok):
    return extended_ref[tok : tok + 16, 0:tok].astype(jnp.float32)[0:1].astype(jnp.int32)


def router_of(extended_ref, tok, expert_count):
    whole = extended_ref[tok + 16 :, :].astype(jnp.float32)
    return whole[0:expert_count].astype(jnp.bfloat16)


def dispatch_kernel(reps, tok, hot_capacity, own_ref, *refs):
    extended_refs, sent_refs = refs[:reps], refs[reps:]
    for rep in range(reps):
        choice = chosen_of(extended_refs[rep], tok)
        placed = slot_matrix(choice, own_ref[0], len(sent_refs), hot_capacity)
        rows = dot(placed, extended_refs[rep][0:tok, :]).astype(jnp.bfloat16)
        for k, sent_ref in enumerate(sent_refs):
            sent_ref[rep * hot_capacity : (rep + 1) * hot_capacity] = rows[
                k * hot_capacity : (k + 1) * hot_capacity
            ]


def fold_blocks(ids_ref, begin_ref, tasks, reps, states, bias_ref):
    lanes = 128
    per = lanes // HD
    scale = math.log2(math.e) / math.sqrt(HD)
    spreads = {}
    lowest = {}
    for k, query_ref, unused_pair, unused_first in tasks:
        if k in spreads:
            continue
        lowest[k] = jnp.min(begin_ref[k : k + 1, :])
        tok = begin_ref.shape[1]
        turned = query_ref[...].T
        head_of_row = lax.broadcasted_iota(jnp.int32, (lanes, tok), 0) // HD
        spreads[k] = []
        for group in range(turned.shape[0] // lanes):
            part = turned[group * lanes : (group + 1) * lanes]
            spreads[k].append(
                jnp.concatenate(
                    [
                        jnp.where(head_of_row == head, part, jnp.zeros_like(part))
                        for head in range(per)
                    ],
                    axis=1,
                )
            )

    def fold(place, k, pair_ref, block, begin, fresh):
        top_ref, total_ref, sum_ref = states[k]
        tok = begin.shape[1]
        position = ids_ref[k] * tok + lax.broadcasted_iota(jnp.int32, (1, tok), 1)
        key_position = block * tok + lax.broadcasted_iota(jnp.int32, (tok, tok), 0)
        visible = (key_position >= begin) & (key_position <= position)
        bias_ref[place] = jnp.where(visible, 0.0, masked_score)
        bias = bias_ref[place]
        if isinstance(pair_ref, tuple):
            key_ref, value_ref, first_value = pair_ref[0], pair_ref[1], 0
        else:
            key_ref, value_ref, first_value = pair_ref, pair_ref, tok
        values = value_ref[first_value : first_value + tok, :].T
        for group, spread in enumerate(spreads[k]):
            columns = slice(group * lanes, (group + 1) * lanes)
            scores = dot(key_ref[0:tok, columns], spread)
            weights, factors = [], []
            for head in range(per):
                row = group * per + head
                part = scores[:, head * tok : (head + 1) * tok] + bias
                top = jnp.max(part, axis=0, keepdims=True)
                if not fresh:
                    old = top_ref[row : row + 1, :]
                    top = jnp.maximum(top, old)
                    factors.append(jnp.exp2((old - top) * scale))
                weight = jnp.exp2((part - top) * scale)
                total = jnp.sum(weight, axis=0, keepdims=True)
                if not fresh:
                    total = total + total_ref[row : row + 1, :] * factors[head]
                top_ref[row : row + 1, :] = top
                total_ref[row : row + 1, :] = total
                weights.append(weight.astype(jnp.bfloat16))
            summed = dot(values[columns], jnp.concatenate(weights, axis=1))
            for head in range(per):
                rows = slice((group * per + head) * HD, (group * per + head + 1) * HD)
                piece = summed[head * HD : (head + 1) * HD, head * tok : (head + 1) * tok]
                if not fresh:
                    piece = piece + sum_ref[rows, :] * factors[head]
                sum_ref[rows, :] = piece

    for place, (k, unused_query, pair_ref, first) in enumerate(tasks):
        block = ids_ref[reps + place]
        begin = begin_ref[k : k + 1, :]
        tok = begin.shape[1]
        if first and k == 0:
            fold(place, k, pair_ref, block, begin, True)
            continue
        if first:
            top_ref, total_ref, sum_ref = states[k]
            top_ref[...] = jnp.full(top_ref.shape, masked_score, jnp.float32)
            total_ref[...] = jnp.zeros(total_ref.shape, jnp.float32)
            sum_ref[...] = jnp.zeros(sum_ref.shape, jnp.float32)

        @pl.when((block >= 0) & ((block + 1) * tok > lowest[k]))
        def unused(place=place, k=k, pair_ref=pair_ref, block=block, begin=begin):
            fold(place, k, pair_ref, block, begin, False)


def attend_kernel(plan, reps, counts, packed, ahead, ids_ref, begin_ref, *refs):
    ks = sorted({k for k, unused_pair, unused_first in plan})
    old_ks = [k for k in ks if not any(first for j, unused_pair, first in plan if j == k)]
    query_refs, refs = dict(zip(ks, refs)), refs[len(ks) + ahead :]
    if counts == 0:
        pair_refs, refs = [tuple(refs[:2])], refs[2:]
    else:
        pair_refs, refs = refs[:counts], refs[counts:]
    old_refs, refs = refs[: 3 * len(old_ks)], refs[3 * len(old_ks) :]
    bias_ref, refs = refs[-1], refs[:-1]
    packed_refs, state_refs = (refs[: len(ks)], refs[len(ks) :]) if packed else ((), refs)
    states = {k: state_refs[3 * place : 3 * place + 3] for place, k in enumerate(ks)}
    for place, k in enumerate(old_ks):
        for old_ref, new_ref in zip(old_refs[3 * place : 3 * place + 3], states[k]):
            new_ref[...] = old_ref[...]
    tasks = [(k, query_refs[k], pair_refs[pair], first) for k, pair, first in plan]
    fold_blocks(ids_ref, begin_ref, tasks, reps, states, bias_ref)
    for k, packed_ref in zip(ks, packed_refs):
        top_ref, total_ref, sum_ref = states[k]
        heads, width = top_ref.shape[0], sum_ref.shape[0]
        packed_ref[0:width, :] = sum_ref[...].astype(jnp.bfloat16)
        first = width
        for ref, pieces in ((top_ref, 3), (total_ref, 2)):
            rest = ref[...]
            for unused in range(pieces):
                piece = rest.astype(jnp.bfloat16)
                packed_ref[first : first + heads, :] = piece
                rest = rest - piece.astype(jnp.float32)
                first += heads


def mix_kernel(expert_count, hot_capacity, own_ref, extended_ref, residual_ref, proj_ref, *refs):
    top_ref, total_ref, sum_ref = refs[0:3]
    mixed_ref, sent_refs = refs[-1 - expert_count], refs[len(refs) - expert_count :]
    packed_refs = refs[3 : -1 - expert_count]
    tok, width = mixed_ref.shape
    heads = top_ref.shape[0]
    scale = math.log2(math.e) / math.sqrt(HD)
    tops, totals = [top_ref[...]], [total_ref[...]]
    for packed_ref in packed_refs:
        pieces = [
            packed_ref[width + place * heads : width + (place + 1) * heads, :].astype(jnp.float32)
            for place in range(5)
        ]
        tops.append((pieces[0] + pieces[1]) + pieces[2])
        totals.append(pieces[3] + pieces[4])
    top = functools.reduce(jnp.maximum, tops)
    factors = [jnp.exp2((one - top) * scale) for one in tops]
    total = sum(one * factor for one, factor in zip(totals, factors))
    factors = [factor / total for factor in factors]
    pieces = []
    for head in range(heads):
        rows = slice(head * HD, (head + 1) * HD)
        piece = sum_ref[rows, :] * factors[0][head : head + 1, :]
        for packed_ref, factor in zip(packed_refs, factors[1:]):
            piece = piece + packed_ref[rows, :].astype(jnp.float32) * factor[head : head + 1, :]
        pieces.append(piece.astype(jnp.bfloat16))
    attended = jnp.concatenate(pieces, axis=0).T
    mixed = (residual_ref[...].astype(jnp.float32) + dot(attended, proj_ref[...])).astype(
        jnp.bfloat16
    )
    mixed_ref[...] = mixed
    mixed_f = mixed.astype(jnp.float32)
    inv_rms = lax.rsqrt(jnp.mean(mixed_f * mixed_f, axis=1, keepdims=True) + norm_eps)
    normed = (mixed_f * inv_rms).astype(jnp.bfloat16)
    placed = slot_matrix(chosen_of(extended_ref, tok), own_ref[0], len(sent_refs), hot_capacity)
    rows = dot(placed, normed).astype(jnp.bfloat16)
    for k, sent_ref in enumerate(sent_refs):
        sent_ref[...] = rows[k * hot_capacity : (k + 1) * hot_capacity]


def expert_kernel(
    reps,
    rep_list,
    sources,
    tok,
    strip,
    counts,
    own_ref,
    part_ref,
    up_ref,
    down_ref,
    extended_ref,
    *refs,
):
    row_count, grad_count = counts
    row_refs, refs = refs[:row_count], refs[row_count:]
    per_rep = row_count // len(rep_list)
    grad_refs, refs = refs[:grad_count][::-1], refs[grad_count:]
    own_rows = rep_list[0] == 0
    held_ref, refs = refs[-1], refs[:-1]
    if own_rows:
        back_refs, (up_acc, down_acc) = refs[:-2], refs[-2:]
    else:
        up_old, down_old = refs[:2]
        term_refs, kept_ref = refs[2:-1], refs[-1]
    total_grads = sum(ref.shape[0] for ref in grad_refs)
    capacity = total_grads // (sources * reps)
    count = sources * capacity
    parts = part_ref.shape[0]
    up = up_ref[...]
    down = down_ref[...]
    router = router_of(extended_ref, tok, sources)
    expert_lane = lax.broadcasted_iota(jnp.int32, (count, router.shape[0]), 1) == own_ref[0]

    def strips(rows, place):
        held_ref[place] = rows.T
        taken = []
        for k in range(parts):
            first = pl.multiple_of(part_ref[k] * strip, strip)
            taken.append(held_ref[place, pl.ds(first, strip), :])
        return jnp.concatenate(taken, axis=0)

    up_term = down_term = None
    for place, rep in enumerate(rep_list):
        rows = chunk_rows(
            row_refs[place * per_rep : (place + 1) * per_rep], sources, 0, capacity
        )
        grads = chunk_rows(grad_refs, sources, rep * capacity, (rep + 1) * capacity)
        pre = dot(rows, up)
        sigmoid_pre = jax.nn.sigmoid(pre)
        activated = (pre * sigmoid_pre).astype(jnp.bfloat16)
        logits = dot(rows, router, NT)
        gate = jax.nn.sigmoid(
            jnp.sum(jnp.where(expert_lane, logits, 0.0), axis=1, keepdims=True)
        )
        scaled = (gate * grads.astype(jnp.float32)).astype(jnp.bfloat16)
        act_grad = dot(scaled, down, NT)
        pre_grad = (act_grad * sigmoid_pre * (1.0 + pre * (1.0 - sigmoid_pre))).astype(
            jnp.bfloat16
        )
        if own_rows:
            produced = dot(activated, down).astype(jnp.bfloat16)
            token_grad = dot(pre_grad, up, NT).astype(jnp.bfloat16)
            for k, back_ref in enumerate(back_refs):
                back_ref[0:capacity] = produced[k * capacity : (k + 1) * capacity]
                back_ref[capacity : 2 * capacity] = token_grad[k * capacity : (k + 1) * capacity]
        more_up = dot(strips(rows, 2 * place), pre_grad)
        more_down = dot(strips(activated, 2 * place + 1), scaled)
        up_term = more_up if up_term is None else up_term + more_up
        down_term = more_down if down_term is None else down_term + more_down
    if own_rows:
        up_acc[...] = up_term
        down_acc[...] = down_term
        return
    up_term = up_term + up_old[...]
    down_term = down_term + down_old[...]
    for k in range(parts):
        rows = slice(k * strip, (k + 1) * strip)
        if k == 0:
            kept_ref[0] = up_term[rows]
            kept_ref[1] = down_term[rows]
        else:
            term_refs[k - 1][0] = up_term[rows].astype(jnp.bfloat16)
            term_refs[k - 1][1] = down_term[rows].astype(jnp.bfloat16)


def finish_kernel(
    hot_capacity, expert_count, own_ref, mixed_ref, extended_ref, *refs
):
    back_refs, (layer_ref, grad_mixed_ref) = refs[:-2], refs[-2:]
    tok = mixed_ref.shape[0]
    choice = chosen_of(extended_ref, tok)
    placed = slot_matrix(choice, own_ref[0], expert_count, hot_capacity)
    router = router_of(extended_ref, tok, expert_count)
    mixed_f = mixed_ref[...].astype(jnp.float32)
    inv_rms = lax.rsqrt(jnp.mean(mixed_f * mixed_f, axis=1, keepdims=True) + norm_eps)
    normed = (mixed_f * inv_rms).astype(jnp.bfloat16)
    one_hot = lax.broadcasted_iota(jnp.int32, (expert_count, tok), 0) == choice
    logits = dot(router, normed, NT)
    logit_row = jnp.sum(jnp.where(one_hot, logits, 0.0), axis=0, keepdims=True)
    logit = jnp.broadcast_to(logit_row, (8, tok)).T[:, 0:1]
    gate = jax.nn.sigmoid(logit)
    pair = 2 * hot_capacity
    chunks = [
        ref[first : first + pair] for ref in back_refs for first in range(0, ref.shape[0], pair)
    ]
    results = jnp.concatenate([chunk[:hot_capacity] for chunk in chunks], axis=0)
    grads = jnp.concatenate([chunk[hot_capacity:] for chunk in chunks], axis=0)
    result_f = dot(placed, results, TN)
    normed_grad = dot(placed, grads, TN)
    grad_f = extended_ref[0:tok, :].astype(jnp.float32)
    layer_ref[...] = (mixed_f + gate * result_f).astype(jnp.bfloat16)
    gate_grad = jnp.sum(grad_f * result_f, axis=1, keepdims=True)
    logit_grad = gate_grad * gate * (1.0 - gate)
    router_cols = dot(one_hot.astype(jnp.float32).astype(jnp.bfloat16), router, TN)
    total_grad = normed_grad + logit_grad * router_cols
    mean_term = jnp.mean(total_grad * mixed_f, axis=1, keepdims=True)
    input_grad = inv_rms * total_grad - mixed_f * inv_rms * inv_rms * inv_rms * mean_term
    grad_mixed_ref[...] = (grad_f + input_grad).astype(jnp.bfloat16)


def sum_kernel(kept_ref, *refs):
    term_refs, (up_ref, down_ref) = refs[:-2], refs[-2:]
    for kind, out_ref in enumerate((up_ref, down_ref)):
        total = kept_ref[kind]
        for ref in term_refs:
            total = total + ref[kind].astype(jnp.float32)
        out_ref[...] = total


def shape(dims, dtype=jnp.bfloat16):
    return jax.ShapeDtypeStruct(dims, dtype)


SMEM = pl.BlockSpec(memory_space=pltpu.SMEM)
VMEM = pl.BlockSpec(memory_space=pltpu.VMEM)
HBM = pl.BlockSpec(memory_space=pltpu.HBM)


def call(body, out_shape, specs, scratch=(), cost=0.5):
    return pl.pallas_call(
        body,
        cost_estimate=pl.CostEstimate(
            flops=int(cost * 1e9), bytes_accessed=0, transcendentals=0
        ),
        out_shape=out_shape,
        in_specs=specs,
        out_specs=jax.tree.map(lambda unused: VMEM, out_shape),
        scratch_shapes=list(scratch),
        compiler_params=pltpu.CompilerParams(vmem_limit_bytes=VMEM_LIMIT),
    )


def local(
    seq_count,
    expert_count,
    rep_count,
    query_rows,
    key_rows,
    value_rows,
    doc_lengths,
    residual,
    out_proj,
    router,
    expert_choice,
    weight_in,
    weight_out,
    grad_out,
):
    tok, width = query_rows.shape[1:]
    hidden = weight_in.shape[2]
    heads = width // HD
    experts = Group(("expert",), (expert_count,))
    reps = Group(("rep",), (rep_count,))
    owners = Group(("expert", "rep"), (expert_count, rep_count))
    parts = Group(("seq",), (seq_count,))
    strip = width // (seq_count * rep_count)
    capacity = max(2, (3 * tok + 2 * expert_count - 1) // (2 * expert_count))
    hot_capacity = min(4 * capacity, tok // 2)
    choice = expert_choice.reshape(1, tok)
    seq_index = lax.axis_index("seq")
    rep_index = lax.axis_index("rep")
    rank = seq_index * rep_count + rep_index
    own = jnp.stack([lax.axis_index("expert")]).astype(jnp.int32)
    part_to = jnp.stack(
        [parts.target(seq_index, k) * rep_count + rep_index for k in range(seq_count)]
    ).astype(jnp.int32)

    def forward(array):
        return lax.ppermute(array, "seq", [(i, (i + 1) % seq_count) for i in range(seq_count)])

    reach = (seq_count + 1) // 2
    longest = (seq_count * rep_count + 1) // 2
    query_ranks = [
        seq_index * rep_count + reps.source(rep_index, k) for k in range(rep_count)
    ]

    def task_ids(plan, steps):
        ids = list(query_ranks)
        for k, pair, unused_first in plan:
            block = rank - steps[pair] * rep_count
            behind = query_ranks[k] - block
            ids.append(jnp.where((block >= 0) & (behind >= 0) & (behind <= longest), block, -1))
        return jnp.stack(ids).astype(jnp.int32)

    state_shapes = [
        shape((heads, tok), jnp.float32),
        shape((heads, tok), jnp.float32),
        shape((width, tok), jnp.float32),
    ]
    tail = 16 + -(-expert_count // 16) * 16
    def early(body, out_shape, specs, scratch):
        return pl.pallas_call(
            body,
            out_shape=out_shape,
            in_specs=specs,
            out_specs=jax.tree.map(lambda unused: VMEM, out_shape),
            scratch_shapes=scratch,
            compiler_params=pltpu.CompilerParams(vmem_limit_bytes=60 * 1024 * 1024),
        )

    pair = early(
        stack_kernel, shape((2 * tok, width)), [HBM, HBM], [pltpu.SemaphoreType.DMA((2,))]
    )(key_rows[0], value_rows[0])
    extended, begin = early(
        extend_kernel,
        [shape((tok + tail, width)), shape((rep_count, tok), jnp.int32)],
        [SMEM] + [HBM] * 4,
        [
            pltpu.VMEM((1, tok), jnp.int32),
            pltpu.VMEM((expert_count, width), jnp.bfloat16),
            pltpu.SMEM(doc_lengths.shape, jnp.int32),
            pltpu.SemaphoreType.DMA((4,)),
        ],
    )(
        jnp.stack(query_ranks).astype(jnp.int32),
        choice,
        doc_lengths,
        router.T,
        grad_out[0],
    )

    def attend(plan, pairs, steps, queries, states, packed, cost, raw=False, ahead=()):
        ks = sorted({k for k, unused_pair, unused_first in plan})
        old = [one for k in ks if k in states for one in states[k]]
        state_out = state_shapes * len(ks)
        if packed:
            out_shape = [shape((width + 5 * heads, tok))] * len(ks)
            scratch = [pltpu.VMEM(one.shape, one.dtype) for one in state_out]
        else:
            out_shape, scratch = state_out, []
        outs = call(
            functools.partial(
                attend_kernel, plan, rep_count, 0 if raw else len(pairs), packed, len(ahead)
            ),
            out_shape,
            [SMEM] + [VMEM] * (1 + len(ks) + len(ahead) + len(pairs) + len(old)),
            scratch + [pltpu.VMEM((len(plan), tok, tok), jnp.float32)],
            cost=cost,
        )(task_ids(plan, steps), begin, *[queries[k] for k in ks], *ahead, *pairs, *old)
        if packed:
            return dict(zip(ks, outs))
        return {k: list(outs[3 * place : 3 * place + 3]) for place, k in enumerate(ks)}

    others = range(1, rep_count)
    lines = [pair, forward(pair)]
    queries = reps.exchange([query_rows[0]] * rep_count)
    extendeds = reps.exchange([extended] * rep_count)
    states = attend(
        ((0, 0, True),), [key_rows[0], value_rows[0]], [0], queries, {}, False, 2.0, True
    )
    lines[1], *states[0] = lax.optimization_barrier((lines[1], *states[0]))
    for step in range(2, reach + 1):
        lines.append(forward(lines[-1]))
    middle = tuple((0, step, False) for step in range(1, reach)) + tuple(
        (k, step, step == 0) for k in others for step in range(reach)
    )
    states = attend(middle, lines[:-1], list(range(reach)), queries, states, False, 4.0)
    states[1][0], *extendeds[1:] = lax.optimization_barrier((states[1][0], *extendeds[1:]))
    sent_grads = call(
        functools.partial(dispatch_kernel, rep_count, tok, hot_capacity),
        [shape((rep_count * hot_capacity, width))] * expert_count,
        [SMEM] + [VMEM] * rep_count,
    )(own, *extendeds)
    partial = attend(
        tuple((k, 0, False) for k in others),
        lines[-1:],
        [reach],
        queries,
        states,
        True,
        1.5,
        ahead=sent_grads[:1],
    )
    returned = reps.exchange([None] + [partial[k] for k in others], inverse=True)[1:]
    states = attend(((0, 0, False),), lines[-1:], [reach], queries, states, False, 1.5)
    got_grads = merged(experts.exchange(sent_grads), MOST_PERMUTES)[::-1]

    mixed, *sent_rows = call(
        functools.partial(mix_kernel, expert_count, hot_capacity),
        [shape((tok, width))] + [shape((hot_capacity, width))] * expert_count,
        [SMEM] + [VMEM] * (6 + len(returned)),
        cost=2.0,
    )(own, extendeds[0], residual[0], out_proj, *states[0], *returned)
    arrived = owners.exchange([sent_rows[k // rep_count] for k in range(owners.count)])
    got_rows = merged(arrived[0::rep_count], MOST_PERMUTES)
    got_more = [
        one for k in others for one in merged(arrived[k::rep_count], MOST_PERMUTES)
    ]

    def expert_call(rep_list, rows, out_shape, extra):
        return call(
            functools.partial(
                expert_kernel,
                rep_count,
                rep_list,
                expert_count,
                tok,
                strip,
                (len(rows), len(got_grads)),
            ),
            out_shape,
            [SMEM, SMEM] + [VMEM] * (3 + len(rows) + len(got_grads) + len(extra)),
            [pltpu.VMEM((2 * len(rep_list), width, expert_count * hot_capacity), jnp.bfloat16)],
            cost=2.0,
        )(own, part_to, weight_in[0], weight_out[0], extendeds[0], *rows, *got_grads, *extra)

    *back, up_acc, down_acc = expert_call(
        (0,),
        got_rows,
        [shape((2 * hot_capacity, width))] * expert_count
        + [shape((seq_count * strip, hidden), jnp.float32)]
        + [shape((seq_count * strip, width), jnp.float32)],
        [],
    )
    got_back = merged(experts.exchange(back, inverse=True), MOST_PERMUTES)
    *terms, kept = expert_call(
        tuple(range(1, rep_count)),
        got_more,
        [shape((2, strip, hidden))] * (seq_count - 1)
        + [shape((2, strip, hidden), jnp.float32)],
        [up_acc, down_acc],
    )
    got_terms = parts.exchange([None] + terms)[1:]
    layer_out, grad_mixed = call(
        functools.partial(finish_kernel, hot_capacity, expert_count),
        [shape((tok, width)), shape((tok, width))],
        [SMEM] + [VMEM] * (2 + len(got_back)),
        cost=1.5,
    )(own, mixed, extended, *got_back)
    kept, layer_out = lax.optimization_barrier((kept, layer_out))
    share_in, share_out = call(
        sum_kernel,
        [shape((strip, hidden), jnp.float32), shape((strip, width), jnp.float32)],
        [VMEM] * seq_count,
    )(kept, *got_terms[::-1])
    return (layer_out[None], grad_mixed[None], share_in[None], share_out[None])


def solution(mesh):
    rows = P("expert", ("seq", "rep"), None)
    in_specs = (
        rows,
        rows,
        rows,
        P("expert", None),
        rows,
        P(),
        P(),
        rows,
        P("expert", None, None),
        P("expert", None, None),
        rows,
    )
    body = functools.partial(
        local, mesh.shape["seq"], mesh.shape["expert"], mesh.shape["rep"]
    )
    return jax.shard_map(
        body, mesh=mesh, in_specs=in_specs, out_specs=(rows, rows, rows, rows), check_vma=False
    )
```

```python
import functools
import math

import jax
import jax.numpy as jnp
from jax import lax
from jax.experimental import pallas as pl
from jax.experimental.pallas import tpu as pltpu
from jax.sharding import PartitionSpec as P

HD = 32
norm_eps = 1e-06
masked_score = -1e30
VMEM_LIMIT = 48 * 1024 * 1024
MOST_PERMUTES = 16
NT = (((1,), (1,)), ((), ()))
TN = (((0,), (0,)), ((), ()))


def dot(a, b, dims=None):
    if dims is None:
        return jnp.dot(a, b, preferred_element_type=jnp.float32)
    return lax.dot_general(a, b, dims, preferred_element_type=jnp.float32)


def away(index, offset, size):
    if size & (size - 1) == 0:
        return index ^ offset
    return (index + offset) % size


def back_from(index, offset, size):
    if size & (size - 1) == 0:
        return index ^ offset
    return (index - offset + size) % size


class Group:
    def __init__(self, axes, sizes):
        self.axes, self.sizes = tuple(axes), tuple(sizes)
        self.count = math.prod(sizes)

    def split(self, flat):
        coords = []
        for size in reversed(self.sizes):
            coords.append(flat % size)
            flat = flat // size
        return coords[::-1]

    def moved(self, flat, offset, step):
        place = 0
        for coord, part, size in zip(self.split(flat), self.split(offset), self.sizes):
            place = place * size + step(coord, part, size)
        return place

    def target(self, flat, offset):
        return self.moved(flat, offset, away)

    def source(self, flat, offset):
        return self.moved(flat, offset, back_from)

    def exchange(self, chunks, inverse=False):
        to, start = (self.source, self.target) if inverse else (self.target, self.source)
        if self.count <= MOST_PERMUTES:
            order = sorted(range(1, self.count), key=lambda k: -k)
            got = {0: chunks[0]}
            for k in order:
                pairs = [(i, to(i, k)) for i in range(self.count)]
                got[k] = lax.ppermute(chunks[k], self.axes, pairs)
            return [got[k] for k in range(self.count)]
        me = lax.axis_index(self.axes)
        steps = jnp.arange(self.count, dtype=jnp.int32)
        sent_to = jax.vmap(lambda k: to(me, k))(steps)
        placed = jnp.zeros((self.count,), jnp.int32).at[sent_to].set(steps)
        stacked = jnp.stack(chunks)[placed]
        got = lax.all_to_all(stacked, self.axes, split_axis=0, concat_axis=0, tiled=True)
        came_from = jax.vmap(lambda k: start(me, k))(steps)
        ordered = got[came_from]
        return [ordered[k] for k in range(self.count)]


def merged(chunks, most):
    if len(chunks) <= most:
        return list(chunks)
    return [jnp.concatenate(chunks, axis=0)]


def chunk_rows(refs, count, low, high):
    size = sum(ref.shape[0] for ref in refs) // count
    parts = []
    for chunk in range(count):
        ref, first = (refs[chunk], 0) if len(refs) == count else (refs[0], chunk * size)
        parts.append(ref[first + low : first + high, :])
    return parts[0] if count == 1 else jnp.concatenate(parts, axis=0)


def slot_matrix(choice, own, expert_count, hot_capacity):
    tok = choice.shape[1]
    offset = back_from(choice, own, expert_count)
    one_hot = lax.broadcasted_iota(jnp.int32, (expert_count, tok), 0) == offset
    hits = one_hot.astype(jnp.float32).astype(jnp.bfloat16)
    earlier = lax.broadcasted_iota(jnp.int32, (tok, tok), 0) <= lax.broadcasted_iota(
        jnp.int32, (tok, tok), 1
    )
    counted = dot(hits, earlier.astype(jnp.float32).astype(jnp.bfloat16))
    rank = jnp.sum(jnp.where(one_hot, counted, 0.0), axis=0, keepdims=True) - 1.0
    slots = offset * hot_capacity + rank.astype(jnp.int32)
    rows = lax.broadcasted_iota(jnp.int32, (expert_count * hot_capacity, tok), 0)
    return (rows == slots).astype(jnp.float32).astype(jnp.bfloat16)


def extend_kernel(
    ranks_ref, lengths_ref, choice_ref, router_ref, grad_ref, extended_ref, begin_ref
):
    tok, width = grad_ref.shape
    extended_ref[0:tok, :] = grad_ref[...]
    chosen = jnp.broadcast_to(choice_ref[...].astype(jnp.float32), (16, tok))
    extended_ref[tok : tok + 16, 0:tok] = chosen.astype(jnp.bfloat16)
    extended_ref[tok : tok + 16, tok:width] = jnp.zeros((16, width - tok), jnp.bfloat16)
    routed = router_ref[...].astype(jnp.float32)
    spare = extended_ref.shape[0] - tok - 16 - routed.shape[0]
    if spare:
        routed = jnp.concatenate([routed, jnp.zeros((spare, width), jnp.float32)], axis=0)
    extended_ref[tok + 16 :, :] = routed.astype(jnp.bfloat16)
    for k in range(begin_ref.shape[0]):
        position = ranks_ref[k] * tok + lax.broadcasted_iota(jnp.int32, (1, tok), 1)
        begin = jnp.zeros((1, tok), jnp.int32)
        bound = jnp.int32(0)
        for doc in range(lengths_ref.shape[1] - 1):
            bound = bound + lengths_ref[0, doc]
            begin = jnp.maximum(begin, jnp.where(position >= bound, bound, 0))
        begin_ref[k : k + 1, :] = begin


def chosen_of(extended_ref, tok):
    return extended_ref[tok : tok + 16, 0:tok].astype(jnp.float32)[0:1].astype(jnp.int32)


def router_of(extended_ref, tok, expert_count):
    whole = extended_ref[tok + 16 :, :].astype(jnp.float32)
    return whole[0:expert_count].astype(jnp.bfloat16)


def dispatch_kernel(reps, tok, hot_capacity, own_ref, *refs):
    extended_refs, sent_refs = refs[:reps], refs[reps:]
    for rep in range(reps):
        choice = chosen_of(extended_refs[rep], tok)
        placed = slot_matrix(choice, own_ref[0], len(sent_refs), hot_capacity)
        rows = dot(placed, extended_refs[rep][0:tok, :]).astype(jnp.bfloat16)
        for k, sent_ref in enumerate(sent_refs):
            sent_ref[rep * hot_capacity : (rep + 1) * hot_capacity] = rows[
                k * hot_capacity : (k + 1) * hot_capacity
            ]


def fold_blocks(ids_ref, begin_ref, tasks, reps, states, bias_ref):
    lanes = 128
    per = lanes // HD
    scale = math.log2(math.e) / math.sqrt(HD)
    spreads = {}
    lowest = {}
    for k, query_ref, unused_pair, unused_first in tasks:
        if k in spreads:
            continue
        lowest[k] = jnp.min(begin_ref[k : k + 1, :])
        tok = begin_ref.shape[1]
        turned = query_ref[...].T
        head_of_row = lax.broadcasted_iota(jnp.int32, (lanes, tok), 0) // HD
        spreads[k] = []
        for group in range(turned.shape[0] // lanes):
            part = turned[group * lanes : (group + 1) * lanes]
            spreads[k].append(
                jnp.concatenate(
                    [
                        jnp.where(head_of_row == head, part, jnp.zeros_like(part))
                        for head in range(per)
                    ],
                    axis=1,
                )
            )

    def fold(place, k, pair_ref, block, begin, fresh):
        top_ref, total_ref, sum_ref = states[k]
        tok = begin.shape[1]
        position = ids_ref[k] * tok + lax.broadcasted_iota(jnp.int32, (1, tok), 1)
        key_position = block * tok + lax.broadcasted_iota(jnp.int32, (tok, tok), 0)
        visible = (key_position >= begin) & (key_position <= position)
        bias_ref[place] = jnp.where(visible, 0.0, masked_score)
        bias = bias_ref[place]
        key_ref, value_ref = pair_ref
        values = value_ref[...].T
        for group, spread in enumerate(spreads[k]):
            columns = slice(group * lanes, (group + 1) * lanes)
            scores = dot(key_ref[:, columns], spread)
            weights, factors = [], []
            for head in range(per):
                row = group * per + head
                part = scores[:, head * tok : (head + 1) * tok] + bias
                top = jnp.max(part, axis=0, keepdims=True)
                if not fresh:
                    old = top_ref[row : row + 1, :]
                    top = jnp.maximum(top, old)
                    factors.append(jnp.exp2((old - top) * scale))
                weight = jnp.exp2((part - top) * scale)
                total = jnp.sum(weight, axis=0, keepdims=True)
                if not fresh:
                    total = total + total_ref[row : row + 1, :] * factors[head]
                top_ref[row : row + 1, :] = top
                total_ref[row : row + 1, :] = total
                weights.append(weight.astype(jnp.bfloat16))
            summed = dot(values[columns], jnp.concatenate(weights, axis=1))
            for head in range(per):
                rows = slice((group * per + head) * HD, (group * per + head + 1) * HD)
                piece = summed[head * HD : (head + 1) * HD, head * tok : (head + 1) * tok]
                if not fresh:
                    piece = piece + sum_ref[rows, :] * factors[head]
                sum_ref[rows, :] = piece

    for place, (k, unused_query, pair_ref, first) in enumerate(tasks):
        block = ids_ref[reps + place]
        begin = begin_ref[k : k + 1, :]
        tok = begin.shape[1]
        if first and k == 0:
            fold(place, k, pair_ref, block, begin, True)
            continue
        if first:
            top_ref, total_ref, sum_ref = states[k]
            top_ref[...] = jnp.full(top_ref.shape, masked_score, jnp.float32)
            total_ref[...] = jnp.zeros(total_ref.shape, jnp.float32)
            sum_ref[...] = jnp.zeros(sum_ref.shape, jnp.float32)

        @pl.when((block >= 0) & ((block + 1) * tok > lowest[k]))
        def unused(place=place, k=k, pair_ref=pair_ref, block=block, begin=begin):
            fold(place, k, pair_ref, block, begin, False)


def attend_kernel(plan, reps, counts, packed, ahead, ids_ref, begin_ref, *refs):
    ks = sorted({k for k, unused_pair, unused_first in plan})
    old_ks = [k for k in ks if not any(first for j, unused_pair, first in plan if j == k)]
    query_refs, refs = dict(zip(ks, refs)), refs[len(ks) + ahead :]
    pair_refs = [refs[2 * place : 2 * place + 2] for place in range(counts)]
    refs = refs[2 * counts :]
    old_refs, refs = refs[: 3 * len(old_ks)], refs[3 * len(old_ks) :]
    bias_ref, refs = refs[-1], refs[:-1]
    packed_refs, state_refs = (refs[: len(ks)], refs[len(ks) :]) if packed else ((), refs)
    states = {k: state_refs[3 * place : 3 * place + 3] for place, k in enumerate(ks)}
    for place, k in enumerate(old_ks):
        for old_ref, new_ref in zip(old_refs[3 * place : 3 * place + 3], states[k]):
            new_ref[...] = old_ref[...]
    tasks = [(k, query_refs[k], pair_refs[pair], first) for k, pair, first in plan]
    fold_blocks(ids_ref, begin_ref, tasks, reps, states, bias_ref)
    for k, packed_ref in zip(ks, packed_refs):
        top_ref, total_ref, sum_ref = states[k]
        heads, width = top_ref.shape[0], sum_ref.shape[0]
        packed_ref[0:width, :] = sum_ref[...].astype(jnp.bfloat16)
        first = width
        for ref, pieces in ((top_ref, 3), (total_ref, 2)):
            rest = ref[...]
            for unused in range(pieces):
                piece = rest.astype(jnp.bfloat16)
                packed_ref[first : first + heads, :] = piece
                rest = rest - piece.astype(jnp.float32)
                first += heads


def mix_kernel(expert_count, hot_capacity, own_ref, extended_ref, residual_ref, proj_ref, *refs):
    top_ref, total_ref, sum_ref = refs[0:3]
    mixed_ref, sent_refs = refs[-1 - expert_count], refs[len(refs) - expert_count :]
    packed_refs = refs[3 : -1 - expert_count]
    tok, width = mixed_ref.shape
    heads = top_ref.shape[0]
    scale = math.log2(math.e) / math.sqrt(HD)
    tops, totals = [top_ref[...]], [total_ref[...]]
    for packed_ref in packed_refs:
        pieces = [
            packed_ref[width + place * heads : width + (place + 1) * heads, :].astype(jnp.float32)
            for place in range(5)
        ]
        tops.append((pieces[0] + pieces[1]) + pieces[2])
        totals.append(pieces[3] + pieces[4])
    top = functools.reduce(jnp.maximum, tops)
    factors = [jnp.exp2((one - top) * scale) for one in tops]
    total = sum(one * factor for one, factor in zip(totals, factors))
    factors = [factor / total for factor in factors]
    pieces = []
    for head in range(heads):
        rows = slice(head * HD, (head + 1) * HD)
        piece = sum_ref[rows, :] * factors[0][head : head + 1, :]
        for packed_ref, factor in zip(packed_refs, factors[1:]):
            piece = piece + packed_ref[rows, :].astype(jnp.float32) * factor[head : head + 1, :]
        pieces.append(piece.astype(jnp.bfloat16))
    attended = jnp.concatenate(pieces, axis=0).T
    mixed = (residual_ref[...].astype(jnp.float32) + dot(attended, proj_ref[...])).astype(
        jnp.bfloat16
    )
    mixed_ref[...] = mixed
    mixed_f = mixed.astype(jnp.float32)
    inv_rms = lax.rsqrt(jnp.mean(mixed_f * mixed_f, axis=1, keepdims=True) + norm_eps)
    normed = (mixed_f * inv_rms).astype(jnp.bfloat16)
    placed = slot_matrix(chosen_of(extended_ref, tok), own_ref[0], len(sent_refs), hot_capacity)
    rows = dot(placed, normed).astype(jnp.bfloat16)
    for k, sent_ref in enumerate(sent_refs):
        sent_ref[...] = rows[k * hot_capacity : (k + 1) * hot_capacity]


def expert_kernel(
    reps,
    rep_list,
    sources,
    tok,
    strip,
    counts,
    own_ref,
    part_ref,
    up_ref,
    down_ref,
    extended_ref,
    *refs,
):
    row_count, grad_count = counts
    row_refs, refs = refs[:row_count], refs[row_count:]
    per_rep = row_count // len(rep_list)
    grad_refs, refs = refs[:grad_count][::-1], refs[grad_count:]
    own_rows = rep_list[0] == 0
    held_ref, refs = refs[-1], refs[:-1]
    if own_rows:
        back_refs, (up_acc, down_acc) = refs[:-2], refs[-2:]
    else:
        up_old, down_old = refs[:2]
        term_refs, kept_ref = refs[2:-1], refs[-1]
    total_grads = sum(ref.shape[0] for ref in grad_refs)
    capacity = total_grads // (sources * reps)
    count = sources * capacity
    parts = part_ref.shape[0]
    up = up_ref[...]
    down = down_ref[...]
    router = router_of(extended_ref, tok, sources)
    expert_lane = lax.broadcasted_iota(jnp.int32, (count, router.shape[0]), 1) == own_ref[0]

    def strips(rows, place):
        held_ref[place] = rows.T
        taken = []
        for k in range(parts):
            first = pl.multiple_of(part_ref[k] * strip, strip)
            taken.append(held_ref[place, pl.ds(first, strip), :])
        return jnp.concatenate(taken, axis=0)

    up_term = down_term = None
    for place, rep in enumerate(rep_list):
        rows = chunk_rows(
            row_refs[place * per_rep : (place + 1) * per_rep], sources, 0, capacity
        )
        grads = chunk_rows(grad_refs, sources, rep * capacity, (rep + 1) * capacity)
        pre = dot(rows, up)
        sigmoid_pre = jax.nn.sigmoid(pre)
        activated = (pre * sigmoid_pre).astype(jnp.bfloat16)
        logits = dot(rows, router, NT)
        gate = jax.nn.sigmoid(
            jnp.sum(jnp.where(expert_lane, logits, 0.0), axis=1, keepdims=True)
        )
        scaled = (gate * grads.astype(jnp.float32)).astype(jnp.bfloat16)
        act_grad = dot(scaled, down, NT)
        pre_grad = (act_grad * sigmoid_pre * (1.0 + pre * (1.0 - sigmoid_pre))).astype(
            jnp.bfloat16
        )
        if own_rows:
            produced = dot(activated, down).astype(jnp.bfloat16)
            token_grad = dot(pre_grad, up, NT).astype(jnp.bfloat16)
            for k, back_ref in enumerate(back_refs):
                back_ref[0:capacity] = produced[k * capacity : (k + 1) * capacity]
                back_ref[capacity : 2 * capacity] = token_grad[k * capacity : (k + 1) * capacity]
        more_up = dot(strips(rows, 2 * place), pre_grad)
        more_down = dot(strips(activated, 2 * place + 1), scaled)
        up_term = more_up if up_term is None else up_term + more_up
        down_term = more_down if down_term is None else down_term + more_down
    if own_rows:
        up_acc[...] = up_term
        down_acc[...] = down_term
        return
    up_term = up_term + up_old[...]
    down_term = down_term + down_old[...]
    for k in range(parts):
        rows = slice(k * strip, (k + 1) * strip)
        if k == 0:
            kept_ref[0] = up_term[rows]
            kept_ref[1] = down_term[rows]
        else:
            term_refs[k - 1][0] = up_term[rows].astype(jnp.bfloat16)
            term_refs[k - 1][1] = down_term[rows].astype(jnp.bfloat16)


def finish_kernel(
    hot_capacity, expert_count, own_ref, mixed_ref, extended_ref, *refs
):
    back_refs, (layer_ref, grad_mixed_ref) = refs[:-2], refs[-2:]
    tok = mixed_ref.shape[0]
    choice = chosen_of(extended_ref, tok)
    placed = slot_matrix(choice, own_ref[0], expert_count, hot_capacity)
    router = router_of(extended_ref, tok, expert_count)
    mixed_f = mixed_ref[...].astype(jnp.float32)
    inv_rms = lax.rsqrt(jnp.mean(mixed_f * mixed_f, axis=1, keepdims=True) + norm_eps)
    normed = (mixed_f * inv_rms).astype(jnp.bfloat16)
    one_hot = lax.broadcasted_iota(jnp.int32, (expert_count, tok), 0) == choice
    logits = dot(router, normed, NT)
    logit_row = jnp.sum(jnp.where(one_hot, logits, 0.0), axis=0, keepdims=True)
    logit = jnp.broadcast_to(logit_row, (8, tok)).T[:, 0:1]
    gate = jax.nn.sigmoid(logit)
    pair = 2 * hot_capacity
    chunks = [
        ref[first : first + pair] for ref in back_refs for first in range(0, ref.shape[0], pair)
    ]
    results = jnp.concatenate([chunk[:hot_capacity] for chunk in chunks], axis=0)
    grads = jnp.concatenate([chunk[hot_capacity:] for chunk in chunks], axis=0)
    result_f = dot(placed, results, TN)
    normed_grad = dot(placed, grads, TN)
    grad_f = extended_ref[0:tok, :].astype(jnp.float32)
    layer_ref[...] = (mixed_f + gate * result_f).astype(jnp.bfloat16)
    gate_grad = jnp.sum(grad_f * result_f, axis=1, keepdims=True)
    logit_grad = gate_grad * gate * (1.0 - gate)
    router_cols = dot(one_hot.astype(jnp.float32).astype(jnp.bfloat16), router, TN)
    total_grad = normed_grad + logit_grad * router_cols
    mean_term = jnp.mean(total_grad * mixed_f, axis=1, keepdims=True)
    input_grad = inv_rms * total_grad - mixed_f * inv_rms * inv_rms * inv_rms * mean_term
    grad_mixed_ref[...] = (grad_f + input_grad).astype(jnp.bfloat16)


def sum_kernel(kept_ref, *refs):
    term_refs, (up_ref, down_ref) = refs[:-2], refs[-2:]
    for kind, out_ref in enumerate((up_ref, down_ref)):
        total = kept_ref[kind]
        for ref in term_refs:
            total = total + ref[kind].astype(jnp.float32)
        out_ref[...] = total


def shape(dims, dtype=jnp.bfloat16):
    return jax.ShapeDtypeStruct(dims, dtype)


SMEM = pl.BlockSpec(memory_space=pltpu.SMEM)
VMEM = pl.BlockSpec(memory_space=pltpu.VMEM)
HBM = pl.BlockSpec(memory_space=pltpu.HBM)


def call(body, out_shape, specs, scratch=(), cost=0.5):
    return pl.pallas_call(
        body,
        cost_estimate=pl.CostEstimate(
            flops=int(cost * 1e9), bytes_accessed=0, transcendentals=0
        ),
        out_shape=out_shape,
        in_specs=specs,
        out_specs=jax.tree.map(lambda unused: VMEM, out_shape),
        scratch_shapes=list(scratch),
        compiler_params=pltpu.CompilerParams(vmem_limit_bytes=VMEM_LIMIT),
    )


def local(
    seq_count,
    expert_count,
    rep_count,
    query_rows,
    key_rows,
    value_rows,
    doc_lengths,
    residual,
    out_proj,
    router,
    expert_choice,
    weight_in,
    weight_out,
    grad_out,
):
    tok, width = query_rows.shape[1:]
    hidden = weight_in.shape[2]
    heads = width // HD
    experts = Group(("expert",), (expert_count,))
    reps = Group(("rep",), (rep_count,))
    owners = Group(("expert", "rep"), (expert_count, rep_count))
    parts = Group(("seq",), (seq_count,))
    strip = width // (seq_count * rep_count)
    capacity = max(2, (3 * tok + 2 * expert_count - 1) // (2 * expert_count))
    hot_capacity = min(4 * capacity, tok // 2)
    choice = expert_choice.reshape(1, tok)
    seq_index = lax.axis_index("seq")
    rep_index = lax.axis_index("rep")
    rank = seq_index * rep_count + rep_index
    own = jnp.stack([lax.axis_index("expert")]).astype(jnp.int32)
    part_to = jnp.stack(
        [parts.target(seq_index, k) * rep_count + rep_index for k in range(seq_count)]
    ).astype(jnp.int32)

    def forward(array):
        return lax.ppermute(array, "seq", [(i, (i + 1) % seq_count) for i in range(seq_count)])

    reach = (seq_count + 1) // 2
    longest = (seq_count * rep_count + 1) // 2
    query_ranks = [
        seq_index * rep_count + reps.source(rep_index, k) for k in range(rep_count)
    ]

    def task_ids(plan, steps):
        ids = list(query_ranks)
        for k, pair, unused_first in plan:
            block = rank - steps[pair] * rep_count
            behind = query_ranks[k] - block
            ids.append(jnp.where((block >= 0) & (behind >= 0) & (behind <= longest), block, -1))
        return jnp.stack(ids).astype(jnp.int32)

    state_shapes = [
        shape((heads, tok), jnp.float32),
        shape((heads, tok), jnp.float32),
        shape((width, tok), jnp.float32),
    ]
    tail = 16 + -(-expert_count // 16) * 16
    extended, begin = call(
        extend_kernel,
        [shape((tok + tail, width)), shape((rep_count, tok), jnp.int32)],
        [SMEM, SMEM] + [VMEM] * 3,
    )(
        jnp.stack(query_ranks).astype(jnp.int32), doc_lengths, choice, router.T, grad_out[0]
    )

    def attend(plan, pairs, steps, queries, states, packed, cost, ahead=()):
        ks = sorted({k for k, unused_pair, unused_first in plan})
        old = [one for k in ks if k in states for one in states[k]]
        state_out = state_shapes * len(ks)
        if packed:
            out_shape = [shape((width + 5 * heads, tok))] * len(ks)
            scratch = [pltpu.VMEM(one.shape, one.dtype) for one in state_out]
        else:
            out_shape, scratch = state_out, []
        outs = call(
            functools.partial(
                attend_kernel, plan, rep_count, len(pairs), packed, len(ahead)
            ),
            out_shape,
            [SMEM] + [VMEM] * (1 + len(ks) + len(ahead) + 2 * len(pairs) + len(old)),
            scratch + [pltpu.VMEM((len(plan), tok, tok), jnp.float32)],
            cost=cost,
        )(task_ids(plan, steps), begin, *[queries[k] for k in ks], *ahead, *[one for both in pairs for one in both], *old)
        if packed:
            return dict(zip(ks, outs))
        return {k: list(outs[3 * place : 3 * place + 3]) for place, k in enumerate(ks)}

    others = range(1, rep_count)
    lines = [(key_rows[0], value_rows[0])]
    for unused in range(reach):
        lines.append(tuple(forward(one) for one in lines[-1]))
    queries = reps.exchange([query_rows[0]] * rep_count)
    extendeds = reps.exchange([extended] * rep_count)
    middle = tuple((0, step, step == 0) for step in range(reach)) + tuple(
        (k, step, step == 0) for k in others for step in range(reach)
    )
    states = attend(middle, lines[:-1], list(range(reach)), queries, {}, False, 5.0)
    states[1][0], *extendeds[1:] = lax.optimization_barrier((states[1][0], *extendeds[1:]))
    sent_grads = call(
        functools.partial(dispatch_kernel, rep_count, tok, hot_capacity),
        [shape((rep_count * hot_capacity, width))] * expert_count,
        [SMEM] + [VMEM] * rep_count,
    )(own, *extendeds)
    partial = attend(
        tuple((k, 0, False) for k in others),
        lines[-1:],
        [reach],
        queries,
        states,
        True,
        1.5,
        ahead=sent_grads[:1],
    )
    returned = reps.exchange([None] + [partial[k] for k in others], inverse=True)[1:]
    states = attend(((0, 0, False),), lines[-1:], [reach], queries, states, False, 1.5)
    got_grads = merged(experts.exchange(sent_grads), MOST_PERMUTES)[::-1]

    mixed, *sent_rows = call(
        functools.partial(mix_kernel, expert_count, hot_capacity),
        [shape((tok, width))] + [shape((hot_capacity, width))] * expert_count,
        [SMEM] + [VMEM] * (6 + len(returned)),
        cost=2.0,
    )(own, extendeds[0], residual[0], out_proj, *states[0], *returned)
    arrived = owners.exchange([sent_rows[k // rep_count] for k in range(owners.count)])
    got_rows = merged(arrived[0::rep_count], MOST_PERMUTES)
    got_more = [
        one for k in others for one in merged(arrived[k::rep_count], MOST_PERMUTES)
    ]

    def expert_call(rep_list, rows, out_shape, extra):
        return call(
            functools.partial(
                expert_kernel,
                rep_count,
                rep_list,
                expert_count,
                tok,
                strip,
                (len(rows), len(got_grads)),
            ),
            out_shape,
            [SMEM, SMEM] + [VMEM] * (3 + len(rows) + len(got_grads) + len(extra)),
            [pltpu.VMEM((2 * len(rep_list), width, expert_count * hot_capacity), jnp.bfloat16)],
            cost=2.0,
        )(own, part_to, weight_in[0], weight_out[0], extendeds[0], *rows, *got_grads, *extra)

    *back, up_acc, down_acc = expert_call(
        (0,),
        got_rows,
        [shape((2 * hot_capacity, width))] * expert_count
        + [shape((seq_count * strip, hidden), jnp.float32)]
        + [shape((seq_count * strip, width), jnp.float32)],
        [],
    )
    got_back = merged(experts.exchange(back, inverse=True), MOST_PERMUTES)
    *terms, kept = expert_call(
        tuple(range(1, rep_count)),
        got_more,
        [shape((2, strip, hidden))] * (seq_count - 1)
        + [shape((2, strip, hidden), jnp.float32)],
        [up_acc, down_acc],
    )
    got_terms = parts.exchange([None] + terms)[1:]
    layer_out, grad_mixed = call(
        functools.partial(finish_kernel, hot_capacity, expert_count),
        [shape((tok, width)), shape((tok, width))],
        [SMEM] + [VMEM] * (2 + len(got_back)),
        cost=1.5,
    )(own, mixed, extended, *got_back)
    kept, layer_out = lax.optimization_barrier((kept, layer_out))
    share_in, share_out = call(
        sum_kernel,
        [shape((strip, hidden), jnp.float32), shape((strip, width), jnp.float32)],
        [VMEM] * seq_count,
    )(kept, *got_terms[::-1])
    return (layer_out[None], grad_mixed[None], share_in[None], share_out[None])


def solution(mesh):
    rows = P("expert", ("seq", "rep"), None)
    in_specs = (
        rows,
        rows,
        rows,
        P("expert", None),
        rows,
        P(),
        P(),
        rows,
        P("expert", None, None),
        P("expert", None, None),
        rows,
    )
    body = functools.partial(
        local, mesh.shape["seq"], mesh.shape["expert"], mesh.shape["rep"]
    )
    return jax.shard_map(
        body, mesh=mesh, in_specs=in_specs, out_specs=(rows, rows, rows, rows), check_vma=False
    )
```

```python
import functools
import math

import jax
import jax.numpy as jnp
from jax import lax
from jax.experimental import pallas as pl
from jax.experimental.pallas import tpu as pltpu
from jax.sharding import PartitionSpec as P

HD = 32
norm_eps = 1e-06
masked_score = -1e30
VMEM_LIMIT = 48 * 1024 * 1024
MOST_PERMUTES = 16
NT = (((1,), (1,)), ((), ()))
TN = (((0,), (0,)), ((), ()))


def dot(a, b, dims=None):
    if dims is None:
        return jnp.dot(a, b, preferred_element_type=jnp.float32)
    return lax.dot_general(a, b, dims, preferred_element_type=jnp.float32)


def away(index, offset, size):
    if size & (size - 1) == 0:
        return index ^ offset
    return (index + offset) % size


def back_from(index, offset, size):
    if size & (size - 1) == 0:
        return index ^ offset
    return (index - offset + size) % size


class Group:
    def __init__(self, axes, sizes):
        self.axes, self.sizes = tuple(axes), tuple(sizes)
        self.count = math.prod(sizes)

    def split(self, flat):
        coords = []
        for size in reversed(self.sizes):
            coords.append(flat % size)
            flat = flat // size
        return coords[::-1]

    def moved(self, flat, offset, step):
        place = 0
        for coord, part, size in zip(self.split(flat), self.split(offset), self.sizes):
            place = place * size + step(coord, part, size)
        return place

    def target(self, flat, offset):
        return self.moved(flat, offset, away)

    def source(self, flat, offset):
        return self.moved(flat, offset, back_from)

    def exchange(self, chunks, inverse=False):
        to, start = (self.source, self.target) if inverse else (self.target, self.source)
        if self.count <= MOST_PERMUTES:
            order = sorted(range(1, self.count), key=lambda k: -k)
            got = {0: chunks[0]}
            for k in order:
                pairs = [(i, to(i, k)) for i in range(self.count)]
                got[k] = lax.ppermute(chunks[k], self.axes, pairs)
            return [got[k] for k in range(self.count)]
        me = lax.axis_index(self.axes)
        steps = jnp.arange(self.count, dtype=jnp.int32)
        sent_to = jax.vmap(lambda k: to(me, k))(steps)
        placed = jnp.zeros((self.count,), jnp.int32).at[sent_to].set(steps)
        stacked = jnp.stack(chunks)[placed]
        got = lax.all_to_all(stacked, self.axes, split_axis=0, concat_axis=0, tiled=True)
        came_from = jax.vmap(lambda k: start(me, k))(steps)
        ordered = got[came_from]
        return [ordered[k] for k in range(self.count)]


def merged(chunks, most):
    if len(chunks) <= most:
        return list(chunks)
    return [jnp.concatenate(chunks, axis=0)]


def chunk_rows(refs, count, low, high):
    size = sum(ref.shape[0] for ref in refs) // count
    parts = []
    for chunk in range(count):
        ref, first = (refs[chunk], 0) if len(refs) == count else (refs[0], chunk * size)
        parts.append(ref[first + low : first + high, :])
    return parts[0] if count == 1 else jnp.concatenate(parts, axis=0)


def slot_matrix(choice, own, expert_count, hot_capacity):
    tok = choice.shape[1]
    offset = back_from(choice, own, expert_count)
    one_hot = lax.broadcasted_iota(jnp.int32, (expert_count, tok), 0) == offset
    hits = one_hot.astype(jnp.float32).astype(jnp.bfloat16)
    earlier = lax.broadcasted_iota(jnp.int32, (tok, tok), 0) <= lax.broadcasted_iota(
        jnp.int32, (tok, tok), 1
    )
    counted = dot(hits, earlier.astype(jnp.float32).astype(jnp.bfloat16))
    rank = jnp.sum(jnp.where(one_hot, counted, 0.0), axis=0, keepdims=True) - 1.0
    slots = offset * hot_capacity + rank.astype(jnp.int32)
    rows = lax.broadcasted_iota(jnp.int32, (expert_count * hot_capacity, tok), 0)
    return (rows == slots).astype(jnp.float32).astype(jnp.bfloat16)


def extend_kernel(
    ranks_ref, lengths_ref, choice_ref, router_ref, grad_ref, extended_ref, begin_ref
):
    tok, width = grad_ref.shape
    extended_ref[0:tok, :] = grad_ref[...]
    chosen = jnp.broadcast_to(choice_ref[...].astype(jnp.float32), (16, tok))
    extended_ref[tok : tok + 16, 0:tok] = chosen.astype(jnp.bfloat16)
    extended_ref[tok : tok + 16, tok:width] = jnp.zeros((16, width - tok), jnp.bfloat16)
    routed = router_ref[...].astype(jnp.float32)
    spare = extended_ref.shape[0] - tok - 16 - routed.shape[0]
    if spare:
        routed = jnp.concatenate([routed, jnp.zeros((spare, width), jnp.float32)], axis=0)
    extended_ref[tok + 16 :, :] = routed.astype(jnp.bfloat16)
    for k in range(begin_ref.shape[0]):
        position = ranks_ref[k] * tok + lax.broadcasted_iota(jnp.int32, (1, tok), 1)
        begin = jnp.zeros((1, tok), jnp.int32)
        bound = jnp.int32(0)
        for doc in range(lengths_ref.shape[1] - 1):
            bound = bound + lengths_ref[0, doc]
            begin = jnp.maximum(begin, jnp.where(position >= bound, bound, 0))
        begin_ref[k : k + 1, :] = begin


def chosen_of(extended_ref, tok):
    return extended_ref[tok : tok + 16, 0:tok].astype(jnp.float32)[0:1].astype(jnp.int32)


def router_of(extended_ref, tok, expert_count):
    whole = extended_ref[tok + 16 :, :].astype(jnp.float32)
    return whole[0:expert_count].astype(jnp.bfloat16)


def dispatch_kernel(reps, tok, hot_capacity, own_ref, *refs):
    extended_refs, sent_refs = refs[:reps], refs[reps:]
    for rep in range(reps):
        choice = chosen_of(extended_refs[rep], tok)
        placed = slot_matrix(choice, own_ref[0], len(sent_refs), hot_capacity)
        rows = dot(placed, extended_refs[rep][0:tok, :]).astype(jnp.bfloat16)
        for k, sent_ref in enumerate(sent_refs):
            sent_ref[rep * hot_capacity : (rep + 1) * hot_capacity] = rows[
                k * hot_capacity : (k + 1) * hot_capacity
            ]


def fold_blocks(ids_ref, begin_ref, tasks, reps, states, bias_ref):
    lanes = 128
    per = lanes // HD
    scale = math.log2(math.e) / math.sqrt(HD)
    spreads = {}
    lowest = {}
    for k, query_ref, unused_pair, unused_first in tasks:
        if k in spreads:
            continue
        lowest[k] = jnp.min(begin_ref[k : k + 1, :])
        tok = begin_ref.shape[1]
        turned = query_ref[...].T
        head_of_row = lax.broadcasted_iota(jnp.int32, (lanes, tok), 0) // HD
        spreads[k] = []
        for group in range(turned.shape[0] // lanes):
            part = turned[group * lanes : (group + 1) * lanes]
            spreads[k].append(
                jnp.concatenate(
                    [
                        jnp.where(head_of_row == head, part, jnp.zeros_like(part))
                        for head in range(per)
                    ],
                    axis=1,
                )
            )

    def fold(place, k, pair_ref, block, begin, fresh):
        top_ref, total_ref, sum_ref = states[k]
        tok = begin.shape[1]
        position = ids_ref[k] * tok + lax.broadcasted_iota(jnp.int32, (1, tok), 1)
        key_position = block * tok + lax.broadcasted_iota(jnp.int32, (tok, tok), 0)
        visible = (key_position >= begin) & (key_position <= position)
        bias_ref[place] = jnp.where(visible, 0.0, masked_score)
        bias = bias_ref[place]
        key_ref, value_ref = pair_ref
        values = value_ref[...].T
        for group, spread in enumerate(spreads[k]):
            columns = slice(group * lanes, (group + 1) * lanes)
            scores = dot(key_ref[:, columns], spread)
            weights, factors = [], []
            for head in range(per):
                row = group * per + head
                part = scores[:, head * tok : (head + 1) * tok] + bias
                top = jnp.max(part, axis=0, keepdims=True)
                if not fresh:
                    old = top_ref[row : row + 1, :]
                    top = jnp.maximum(top, old)
                    factors.append(jnp.exp2((old - top) * scale))
                weight = jnp.exp2((part - top) * scale)
                total = jnp.sum(weight, axis=0, keepdims=True)
                if not fresh:
                    total = total + total_ref[row : row + 1, :] * factors[head]
                top_ref[row : row + 1, :] = top
                total_ref[row : row + 1, :] = total
                weights.append(weight.astype(jnp.bfloat16))
            summed = dot(values[columns], jnp.concatenate(weights, axis=1))
            for head in range(per):
                rows = slice((group * per + head) * HD, (group * per + head + 1) * HD)
                piece = summed[head * HD : (head + 1) * HD, head * tok : (head + 1) * tok]
                if not fresh:
                    piece = piece + sum_ref[rows, :] * factors[head]
                sum_ref[rows, :] = piece

    for place, (k, unused_query, pair_ref, first) in enumerate(tasks):
        block = ids_ref[reps + place]
        begin = begin_ref[k : k + 1, :]
        tok = begin.shape[1]
        if first and k == 0:
            fold(place, k, pair_ref, block, begin, True)
            continue
        if first:
            top_ref, total_ref, sum_ref = states[k]
            top_ref[...] = jnp.full(top_ref.shape, masked_score, jnp.float32)
            total_ref[...] = jnp.zeros(total_ref.shape, jnp.float32)
            sum_ref[...] = jnp.zeros(sum_ref.shape, jnp.float32)

        @pl.when((block >= 0) & ((block + 1) * tok > lowest[k]))
        def unused(place=place, k=k, pair_ref=pair_ref, block=block, begin=begin):
            fold(place, k, pair_ref, block, begin, False)


def attend_kernel(plan, reps, counts, packed, ids_ref, begin_ref, *refs):
    ks = sorted({k for k, unused_pair, unused_first in plan})
    old_ks = [k for k in ks if not any(first for j, unused_pair, first in plan if j == k)]
    query_refs, refs = dict(zip(ks, refs)), refs[len(ks) :]
    pair_refs = [refs[2 * place : 2 * place + 2] for place in range(counts)]
    refs = refs[2 * counts :]
    old_refs, refs = refs[: 3 * len(old_ks)], refs[3 * len(old_ks) :]
    bias_ref, refs = refs[-1], refs[:-1]
    packed_refs, state_refs = (refs[: len(ks)], refs[len(ks) :]) if packed else ((), refs)
    states = {k: state_refs[3 * place : 3 * place + 3] for place, k in enumerate(ks)}
    for place, k in enumerate(old_ks):
        for old_ref, new_ref in zip(old_refs[3 * place : 3 * place + 3], states[k]):
            new_ref[...] = old_ref[...]
    tasks = [(k, query_refs[k], pair_refs[pair], first) for k, pair, first in plan]
    fold_blocks(ids_ref, begin_ref, tasks, reps, states, bias_ref)
    for k, packed_ref in zip(ks, packed_refs):
        top_ref, total_ref, sum_ref = states[k]
        heads, width = top_ref.shape[0], sum_ref.shape[0]
        packed_ref[0:width, :] = sum_ref[...].astype(jnp.bfloat16)
        first = width
        for ref, pieces in ((top_ref, 3), (total_ref, 2)):
            rest = ref[...]
            for unused in range(pieces):
                piece = rest.astype(jnp.bfloat16)
                packed_ref[first : first + heads, :] = piece
                rest = rest - piece.astype(jnp.float32)
                first += heads


def mix_kernel(expert_count, hot_capacity, own_ref, extended_ref, residual_ref, proj_ref, *refs):
    top_ref, total_ref, sum_ref = refs[0:3]
    mixed_ref, sent_refs = refs[-1 - expert_count], refs[len(refs) - expert_count :]
    packed_refs = refs[3 : -1 - expert_count]
    tok, width = mixed_ref.shape
    heads = top_ref.shape[0]
    scale = math.log2(math.e) / math.sqrt(HD)
    tops, totals = [top_ref[...]], [total_ref[...]]
    for packed_ref in packed_refs:
        pieces = [
            packed_ref[width + place * heads : width + (place + 1) * heads, :].astype(jnp.float32)
            for place in range(5)
        ]
        tops.append((pieces[0] + pieces[1]) + pieces[2])
        totals.append(pieces[3] + pieces[4])
    top = functools.reduce(jnp.maximum, tops)
    factors = [jnp.exp2((one - top) * scale) for one in tops]
    total = sum(one * factor for one, factor in zip(totals, factors))
    factors = [factor / total for factor in factors]
    pieces = []
    for head in range(heads):
        rows = slice(head * HD, (head + 1) * HD)
        piece = sum_ref[rows, :] * factors[0][head : head + 1, :]
        for packed_ref, factor in zip(packed_refs, factors[1:]):
            piece = piece + packed_ref[rows, :].astype(jnp.float32) * factor[head : head + 1, :]
        pieces.append(piece.astype(jnp.bfloat16))
    attended = jnp.concatenate(pieces, axis=0).T
    mixed = (residual_ref[...].astype(jnp.float32) + dot(attended, proj_ref[...])).astype(
        jnp.bfloat16
    )
    mixed_ref[...] = mixed
    mixed_f = mixed.astype(jnp.float32)
    inv_rms = lax.rsqrt(jnp.mean(mixed_f * mixed_f, axis=1, keepdims=True) + norm_eps)
    normed = (mixed_f * inv_rms).astype(jnp.bfloat16)
    placed = slot_matrix(chosen_of(extended_ref, tok), own_ref[0], len(sent_refs), hot_capacity)
    rows = dot(placed, normed).astype(jnp.bfloat16)
    for k, sent_ref in enumerate(sent_refs):
        sent_ref[...] = rows[k * hot_capacity : (k + 1) * hot_capacity]


def grad_plan(parts):
    if parts == 4:
        return [[(0, 0), (1, 0), (1, 2)], [(0, 1), (1, 1), (1, 3)], [(0, 2)], [(0, 3)]]
    return [[(0, 0), (1, 0)]] + [[(0, k), (1, k)] for k in range(1, parts)]


def pair_kernel(kept_ref, near_ref, sent_ref):
    sent_ref[0] = (kept_ref[2] + near_ref[2].astype(jnp.float32)).astype(jnp.bfloat16)


def expert_kernel(
    reps,
    rep_list,
    sources,
    tok,
    strip,
    counts,
    own_ref,
    part_ref,
    up_ref,
    down_ref,
    extended_ref,
    *refs,
):
    row_count, grad_count = counts
    row_refs, refs = refs[:row_count], refs[row_count:]
    per_rep = row_count // len(rep_list)
    grad_refs, refs = refs[:grad_count][::-1], refs[grad_count:]
    own_rows = rep_list[0] == 0
    held_ref, refs = refs[-1], refs[:-1]
    if own_rows:
        back_refs, (up_acc, down_acc) = refs[:-2], refs[-2:]
    else:
        up_old, down_old = refs[:2]
        term_refs, kept_ref = refs[2:-1], refs[-1]
    total_grads = sum(ref.shape[0] for ref in grad_refs)
    capacity = total_grads // (sources * reps)
    count = sources * capacity
    parts = part_ref.shape[0]
    up = up_ref[...]
    down = down_ref[...]
    router = router_of(extended_ref, tok, sources)
    expert_lane = lax.broadcasted_iota(jnp.int32, (count, router.shape[0]), 1) == own_ref[0]

    def strips(rows, place):
        held_ref[place] = rows.T
        taken = []
        for k in range(parts):
            first = pl.multiple_of(part_ref[k] * strip, strip)
            taken.append(held_ref[place, pl.ds(first, strip), :])
        return jnp.concatenate(taken, axis=0)

    up_term = down_term = None
    for place, rep in enumerate(rep_list):
        rows = chunk_rows(
            row_refs[place * per_rep : (place + 1) * per_rep], sources, 0, capacity
        )
        grads = chunk_rows(grad_refs, sources, rep * capacity, (rep + 1) * capacity)
        pre = dot(rows, up)
        sigmoid_pre = jax.nn.sigmoid(pre)
        activated = (pre * sigmoid_pre).astype(jnp.bfloat16)
        logits = dot(rows, router, NT)
        gate = jax.nn.sigmoid(
            jnp.sum(jnp.where(expert_lane, logits, 0.0), axis=1, keepdims=True)
        )
        scaled = (gate * grads.astype(jnp.float32)).astype(jnp.bfloat16)
        act_grad = dot(scaled, down, NT)
        pre_grad = (act_grad * sigmoid_pre * (1.0 + pre * (1.0 - sigmoid_pre))).astype(
            jnp.bfloat16
        )
        if own_rows:
            produced = dot(activated, down).astype(jnp.bfloat16)
            token_grad = dot(pre_grad, up, NT).astype(jnp.bfloat16)
            for k, back_ref in enumerate(back_refs):
                back_ref[0:capacity] = produced[k * capacity : (k + 1) * capacity]
                back_ref[capacity : 2 * capacity] = token_grad[k * capacity : (k + 1) * capacity]
        more_up = dot(strips(rows, 2 * place), pre_grad)
        more_down = dot(strips(activated, 2 * place + 1), scaled)
        up_term = more_up if up_term is None else up_term + more_up
        down_term = more_down if down_term is None else down_term + more_down
    if own_rows:
        up_acc[...] = up_term
        down_acc[...] = down_term
        return
    up_term = up_term + up_old[...]
    down_term = down_term + down_old[...]
    for ref, entries in zip((kept_ref, *term_refs), grad_plan(parts)):
        for place, (kind, k) in enumerate(entries):
            term = (up_term, down_term)[kind][k * strip : (k + 1) * strip]
            ref[place] = term.astype(ref.dtype)


def finish_kernel(
    hot_capacity, expert_count, own_ref, mixed_ref, extended_ref, *refs
):
    back_refs, (layer_ref, grad_mixed_ref) = refs[:-2], refs[-2:]
    tok = mixed_ref.shape[0]
    choice = chosen_of(extended_ref, tok)
    placed = slot_matrix(choice, own_ref[0], expert_count, hot_capacity)
    router = router_of(extended_ref, tok, expert_count)
    mixed_f = mixed_ref[...].astype(jnp.float32)
    inv_rms = lax.rsqrt(jnp.mean(mixed_f * mixed_f, axis=1, keepdims=True) + norm_eps)
    normed = (mixed_f * inv_rms).astype(jnp.bfloat16)
    one_hot = lax.broadcasted_iota(jnp.int32, (expert_count, tok), 0) == choice
    logits = dot(router, normed, NT)
    logit_row = jnp.sum(jnp.where(one_hot, logits, 0.0), axis=0, keepdims=True)
    logit = jnp.broadcast_to(logit_row, (8, tok)).T[:, 0:1]
    gate = jax.nn.sigmoid(logit)
    pair = 2 * hot_capacity
    chunks = [
        ref[first : first + pair] for ref in back_refs for first in range(0, ref.shape[0], pair)
    ]
    results = jnp.concatenate([chunk[:hot_capacity] for chunk in chunks], axis=0)
    grads = jnp.concatenate([chunk[hot_capacity:] for chunk in chunks], axis=0)
    result_f = dot(placed, results, TN)
    normed_grad = dot(placed, grads, TN)
    grad_f = extended_ref[0:tok, :].astype(jnp.float32)
    layer_ref[...] = (mixed_f + gate * result_f).astype(jnp.bfloat16)
    gate_grad = jnp.sum(grad_f * result_f, axis=1, keepdims=True)
    logit_grad = gate_grad * gate * (1.0 - gate)
    router_cols = dot(one_hot.astype(jnp.float32).astype(jnp.bfloat16), router, TN)
    total_grad = normed_grad + logit_grad * router_cols
    mean_term = jnp.mean(total_grad * mixed_f, axis=1, keepdims=True)
    input_grad = inv_rms * total_grad - mixed_f * inv_rms * inv_rms * inv_rms * mean_term
    grad_mixed_ref[...] = (grad_f + input_grad).astype(jnp.bfloat16)


def sum_kernel(plan, kept_ref, *refs):
    term_refs, out_refs = refs[:-2], refs[-2:]
    totals = [kept_ref[0], kept_ref[1]]
    for kinds, ref in zip(plan, term_refs):
        for place, kind in enumerate(kinds):
            totals[kind] = totals[kind] + ref[place].astype(jnp.float32)
    for total, out_ref in zip(totals, out_refs):
        out_ref[...] = total


def shape(dims, dtype=jnp.bfloat16):
    return jax.ShapeDtypeStruct(dims, dtype)


SMEM = pl.BlockSpec(memory_space=pltpu.SMEM)
VMEM = pl.BlockSpec(memory_space=pltpu.VMEM)
HBM = pl.BlockSpec(memory_space=pltpu.HBM)


def call(body, out_shape, specs, scratch=(), cost=0.5):
    return pl.pallas_call(
        body,
        cost_estimate=pl.CostEstimate(
            flops=int(cost * 1e9), bytes_accessed=0, transcendentals=0
        ),
        out_shape=out_shape,
        in_specs=specs,
        out_specs=jax.tree.map(lambda unused: VMEM, out_shape),
        scratch_shapes=list(scratch),
        compiler_params=pltpu.CompilerParams(vmem_limit_bytes=VMEM_LIMIT),
    )


def local(
    seq_count,
    expert_count,
    rep_count,
    query_rows,
    key_rows,
    value_rows,
    doc_lengths,
    residual,
    out_proj,
    router,
    expert_choice,
    weight_in,
    weight_out,
    grad_out,
):
    tok, width = query_rows.shape[1:]
    hidden = weight_in.shape[2]
    heads = width // HD
    experts = Group(("expert",), (expert_count,))
    reps = Group(("rep",), (rep_count,))
    owners = Group(("expert", "rep"), (expert_count, rep_count))
    parts = Group(("seq",), (seq_count,))
    strip = width // (seq_count * rep_count)
    capacity = max(2, (3 * tok + 2 * expert_count - 1) // (2 * expert_count))
    hot_capacity = min(4 * capacity, tok // 2)
    choice = expert_choice.reshape(1, tok)
    seq_index = lax.axis_index("seq")
    rep_index = lax.axis_index("rep")
    rank = seq_index * rep_count + rep_index
    own = jnp.stack([lax.axis_index("expert")]).astype(jnp.int32)
    part_to = jnp.stack(
        [parts.target(seq_index, k) * rep_count + rep_index for k in range(seq_count)]
    ).astype(jnp.int32)

    def forward(array):
        return lax.ppermute(array, "seq", [(i, (i + 1) % seq_count) for i in range(seq_count)])

    reach = (seq_count + 1) // 2
    longest = (seq_count * rep_count + 1) // 2
    query_ranks = [
        seq_index * rep_count + reps.source(rep_index, k) for k in range(rep_count)
    ]

    def task_ids(plan, steps):
        ids = list(query_ranks)
        for k, pair, unused_first in plan:
            block = rank - steps[pair] * rep_count
            behind = query_ranks[k] - block
            ids.append(jnp.where((block >= 0) & (behind >= 0) & (behind <= longest), block, -1))
        return jnp.stack(ids).astype(jnp.int32)

    state_shapes = [
        shape((heads, tok), jnp.float32),
        shape((heads, tok), jnp.float32),
        shape((width, tok), jnp.float32),
    ]
    tail = 16 + -(-expert_count // 16) * 16
    extended, begin = call(
        extend_kernel,
        [shape((tok + tail, width)), shape((rep_count, tok), jnp.int32)],
        [SMEM, SMEM] + [VMEM] * 3,
    )(
        jnp.stack(query_ranks).astype(jnp.int32), doc_lengths, choice, router.T, grad_out[0]
    )

    def attend(plan, pairs, steps, queries, states, packed, cost):
        ks = sorted({k for k, unused_pair, unused_first in plan})
        old = [one for k in ks if k in states for one in states[k]]
        state_out = state_shapes * len(ks)
        if packed:
            out_shape = [shape((width + 5 * heads, tok))] * len(ks)
            scratch = [pltpu.VMEM(one.shape, one.dtype) for one in state_out]
        else:
            out_shape, scratch = state_out, []
        outs = call(
            functools.partial(
                attend_kernel, plan, rep_count, len(pairs), packed
            ),
            out_shape,
            [SMEM] + [VMEM] * (1 + len(ks) + 2 * len(pairs) + len(old)),
            scratch + [pltpu.VMEM((len(plan), tok, tok), jnp.float32)],
            cost=cost,
        )(task_ids(plan, steps), begin, *[queries[k] for k in ks], *[one for both in pairs for one in both], *old)
        if packed:
            return dict(zip(ks, outs))
        return {k: list(outs[3 * place : 3 * place + 3]) for place, k in enumerate(ks)}

    others = range(1, rep_count)
    lines = [(key_rows[0], value_rows[0])]
    lines.append(tuple(forward(one) for one in lines[0]))
    queries = reps.exchange([query_rows[0]] * rep_count)
    extendeds = reps.exchange([extended] * rep_count)
    states = attend(((0, 0, True),), lines[:1], [0], queries, {}, False, 2.0)
    ahead, *states[0] = lax.optimization_barrier((lines[1][0], *states[0]))
    lines[1] = (ahead, lines[1][1])
    for unused in range(1, reach):
        lines.append(tuple(forward(one) for one in lines[-1]))
    middle = tuple((0, step, False) for step in range(1, reach)) + tuple(
        (k, step, step == 0) for k in others for step in range(reach)
    )
    states = attend(middle, lines[:-1], list(range(reach)), queries, states, False, 4.0)
    partial = attend(
        tuple((k, 0, False) for k in others), lines[-1:], [reach], queries, states, True, 1.5
    )
    partial[1], *extendeds[1:] = lax.optimization_barrier((partial[1], *extendeds[1:]))
    returned = reps.exchange([None] + [partial[k] for k in others], inverse=True)[1:]
    states = attend(((0, 0, False),), lines[-1:], [reach], queries, states, False, 1.5)
    sent_grads = call(
        functools.partial(dispatch_kernel, rep_count, tok, hot_capacity),
        [shape((rep_count * hot_capacity, width))] * expert_count,
        [SMEM] + [VMEM] * rep_count,
    )(own, *extendeds)
    got_grads = merged(experts.exchange(sent_grads), MOST_PERMUTES)[::-1]

    mixed, *sent_rows = call(
        functools.partial(mix_kernel, expert_count, hot_capacity),
        [shape((tok, width))] + [shape((hot_capacity, width))] * expert_count,
        [SMEM] + [VMEM] * (6 + len(returned)),
        cost=2.0,
    )(own, extendeds[0], residual[0], out_proj, *states[0], *returned)
    arrived = owners.exchange([sent_rows[k // rep_count] for k in range(owners.count)])
    got_rows = merged(arrived[0::rep_count], MOST_PERMUTES)
    got_more = [
        one for k in others for one in merged(arrived[k::rep_count], MOST_PERMUTES)
    ]

    def expert_call(rep_list, rows, out_shape, extra):
        return call(
            functools.partial(
                expert_kernel,
                rep_count,
                rep_list,
                expert_count,
                tok,
                strip,
                (len(rows), len(got_grads)),
            ),
            out_shape,
            [SMEM, SMEM] + [VMEM] * (3 + len(rows) + len(got_grads) + len(extra)),
            [pltpu.VMEM((2 * len(rep_list), width, expert_count * hot_capacity), jnp.bfloat16)],
            cost=2.0,
        )(own, part_to, weight_in[0], weight_out[0], extendeds[0], *rows, *got_grads, *extra)

    *back, up_acc, down_acc = expert_call(
        (0,),
        got_rows,
        [shape((2 * hot_capacity, width))] * expert_count
        + [shape((seq_count * strip, hidden), jnp.float32)]
        + [shape((seq_count * strip, width), jnp.float32)],
        [],
    )
    got_back = merged(experts.exchange(back, inverse=True), MOST_PERMUTES)
    *terms, kept = expert_call(
        tuple(range(1, rep_count)),
        got_more,
        [shape((len(entries), strip, hidden)) for entries in grad_plan(seq_count)[1:]]
        + [shape((len(grad_plan(seq_count)[0]), strip, hidden), jnp.float32)],
        [up_acc, down_acc],
    )
    if seq_count == 4:
        near, *direct = parts.exchange([None] + terms)[1:]
        crossing = call(pair_kernel, shape((1, strip, hidden)), [VMEM, VMEM])(kept, near)
        crossed = lax.ppermute(crossing, "seq", [(i, parts.target(i, 2)) for i in range(4)])
        got_terms = [near, *direct, crossed]
        plan = ((0, 1), (0,), (0,), (1,))
    else:
        got_terms = parts.exchange([None] + terms)[1:]
        plan = ((0, 1),) * len(got_terms)
    layer_out, grad_mixed = call(
        functools.partial(finish_kernel, hot_capacity, expert_count),
        [shape((tok, width)), shape((tok, width))],
        [SMEM] + [VMEM] * (2 + len(got_back)),
        cost=1.5,
    )(own, mixed, extended, *got_back)
    kept, layer_out = lax.optimization_barrier((kept, layer_out))
    share_in, share_out = call(
        functools.partial(sum_kernel, plan),
        [shape((strip, hidden), jnp.float32), shape((strip, width), jnp.float32)],
        [VMEM] * (1 + len(got_terms)),
    )(kept, *got_terms)
    return (layer_out[None], grad_mixed[None], share_in[None], share_out[None])


def solution(mesh):
    rows = P("expert", ("seq", "rep"), None)
    in_specs = (
        rows,
        rows,
        rows,
        P("expert", None),
        rows,
        P(),
        P(),
        rows,
        P("expert", None, None),
        P("expert", None, None),
        rows,
    )
    body = functools.partial(
        local, mesh.shape["seq"], mesh.shape["expert"], mesh.shape["rep"]
    )
    return jax.shard_map(
        body, mesh=mesh, in_specs=in_specs, out_specs=(rows, rows, rows, rows), check_vma=False
    )
```

```python
import functools
import math

import jax
import jax.numpy as jnp
from jax import lax
from jax.experimental import pallas as pl
from jax.experimental.pallas import tpu as pltpu
from jax.sharding import PartitionSpec as P

HD = 32
norm_eps = 1e-06
masked_score = -1e30
VMEM_LIMIT = 48 * 1024 * 1024
MOST_PERMUTES = 16
NT = (((1,), (1,)), ((), ()))
TN = (((0,), (0,)), ((), ()))


def dot(a, b, dims=None):
    if dims is None:
        return jnp.dot(a, b, preferred_element_type=jnp.float32)
    return lax.dot_general(a, b, dims, preferred_element_type=jnp.float32)


def away(index, offset, size):
    if size & (size - 1) == 0:
        return index ^ offset
    return (index + offset) % size


def back_from(index, offset, size):
    if size & (size - 1) == 0:
        return index ^ offset
    return (index - offset + size) % size


class Group:
    def __init__(self, axes, sizes):
        self.axes, self.sizes = tuple(axes), tuple(sizes)
        self.count = math.prod(sizes)

    def split(self, flat):
        coords = []
        for size in reversed(self.sizes):
            coords.append(flat % size)
            flat = flat // size
        return coords[::-1]

    def moved(self, flat, offset, step):
        place = 0
        for coord, part, size in zip(self.split(flat), self.split(offset), self.sizes):
            place = place * size + step(coord, part, size)
        return place

    def target(self, flat, offset):
        return self.moved(flat, offset, away)

    def source(self, flat, offset):
        return self.moved(flat, offset, back_from)

    def exchange(self, chunks, inverse=False):
        to, start = (self.source, self.target) if inverse else (self.target, self.source)
        if self.count <= MOST_PERMUTES:
            order = sorted(range(1, self.count), key=lambda k: -k)
            got = {0: chunks[0]}
            for k in order:
                pairs = [(i, to(i, k)) for i in range(self.count)]
                got[k] = lax.ppermute(chunks[k], self.axes, pairs)
            return [got[k] for k in range(self.count)]
        me = lax.axis_index(self.axes)
        steps = jnp.arange(self.count, dtype=jnp.int32)
        sent_to = jax.vmap(lambda k: to(me, k))(steps)
        placed = jnp.zeros((self.count,), jnp.int32).at[sent_to].set(steps)
        stacked = jnp.stack(chunks)[placed]
        got = lax.all_to_all(stacked, self.axes, split_axis=0, concat_axis=0, tiled=True)
        came_from = jax.vmap(lambda k: start(me, k))(steps)
        ordered = got[came_from]
        return [ordered[k] for k in range(self.count)]


def merged(chunks, most):
    if len(chunks) <= most:
        return list(chunks)
    return [jnp.concatenate(chunks, axis=0)]


def chunk_rows(refs, count, low, high):
    size = sum(ref.shape[0] for ref in refs) // count
    parts = []
    for chunk in range(count):
        ref, first = (refs[chunk], 0) if len(refs) == count else (refs[0], chunk * size)
        parts.append(ref[first + low : first + high, :])
    return parts[0] if count == 1 else jnp.concatenate(parts, axis=0)


def slot_matrix(choice, own, expert_count, hot_capacity):
    tok = choice.shape[1]
    offset = back_from(choice, own, expert_count)
    one_hot = lax.broadcasted_iota(jnp.int32, (expert_count, tok), 0) == offset
    hits = one_hot.astype(jnp.float32).astype(jnp.bfloat16)
    earlier = lax.broadcasted_iota(jnp.int32, (tok, tok), 0) <= lax.broadcasted_iota(
        jnp.int32, (tok, tok), 1
    )
    counted = dot(hits, earlier.astype(jnp.float32).astype(jnp.bfloat16))
    rank = jnp.sum(jnp.where(one_hot, counted, 0.0), axis=0, keepdims=True) - 1.0
    slots = offset * hot_capacity + rank.astype(jnp.int32)
    rows = lax.broadcasted_iota(jnp.int32, (expert_count * hot_capacity, tok), 0)
    return (rows == slots).astype(jnp.float32).astype(jnp.bfloat16)


def extend_kernel(
    ranks_ref, lengths_ref, choice_ref, router_ref, grad_ref, extended_ref, begin_ref
):
    tok, width = grad_ref.shape
    extended_ref[0:tok, :] = grad_ref[...]
    chosen = jnp.broadcast_to(choice_ref[...].astype(jnp.float32), (16, tok))
    extended_ref[tok : tok + 16, 0:tok] = chosen.astype(jnp.bfloat16)
    extended_ref[tok : tok + 16, tok:width] = jnp.zeros((16, width - tok), jnp.bfloat16)
    routed = router_ref[...].astype(jnp.float32)
    spare = extended_ref.shape[0] - tok - 16 - routed.shape[0]
    if spare:
        routed = jnp.concatenate([routed, jnp.zeros((spare, width), jnp.float32)], axis=0)
    extended_ref[tok + 16 :, :] = routed.astype(jnp.bfloat16)
    for k in range(begin_ref.shape[0]):
        position = ranks_ref[k] * tok + lax.broadcasted_iota(jnp.int32, (1, tok), 1)
        begin = jnp.zeros((1, tok), jnp.int32)
        bound = jnp.int32(0)
        for doc in range(lengths_ref.shape[1] - 1):
            bound = bound + lengths_ref[0, doc]
            begin = jnp.maximum(begin, jnp.where(position >= bound, bound, 0))
        begin_ref[k : k + 1, :] = begin


def chosen_of(extended_ref, tok):
    return extended_ref[tok : tok + 16, 0:tok].astype(jnp.float32)[0:1].astype(jnp.int32)


def router_of(extended_ref, tok, expert_count):
    whole = extended_ref[tok + 16 :, :].astype(jnp.float32)
    return whole[0:expert_count].astype(jnp.bfloat16)


def dispatch_kernel(reps, tok, hot_capacity, own_ref, *refs):
    extended_refs, sent_refs = refs[:reps], refs[reps:]
    for rep in range(reps):
        choice = chosen_of(extended_refs[rep], tok)
        placed = slot_matrix(choice, own_ref[0], len(sent_refs), hot_capacity)
        rows = dot(placed, extended_refs[rep][0:tok, :]).astype(jnp.bfloat16)
        for k, sent_ref in enumerate(sent_refs):
            sent_ref[rep * hot_capacity : (rep + 1) * hot_capacity] = rows[
                k * hot_capacity : (k + 1) * hot_capacity
            ]


def fold_blocks(ids_ref, begin_ref, tasks, reps, states, bias_ref):
    lanes = 128
    per = lanes // HD
    scale = math.log2(math.e) / math.sqrt(HD)
    spreads = {}
    lowest = {}
    for k, query_ref, unused_pair, unused_first in tasks:
        if k in spreads:
            continue
        lowest[k] = jnp.min(begin_ref[k : k + 1, :])
        tok = begin_ref.shape[1]
        turned = query_ref[...].T
        head_of_row = lax.broadcasted_iota(jnp.int32, (lanes, tok), 0) // HD
        spreads[k] = []
        for group in range(turned.shape[0] // lanes):
            part = turned[group * lanes : (group + 1) * lanes]
            spreads[k].append(
                jnp.concatenate(
                    [
                        jnp.where(head_of_row == head, part, jnp.zeros_like(part))
                        for head in range(per)
                    ],
                    axis=1,
                )
            )

    def fold(place, k, pair_ref, block, begin, fresh):
        top_ref, total_ref, sum_ref = states[k]
        tok = begin.shape[1]
        position = ids_ref[k] * tok + lax.broadcasted_iota(jnp.int32, (1, tok), 1)
        key_position = block * tok + lax.broadcasted_iota(jnp.int32, (tok, tok), 0)
        visible = (key_position >= begin) & (key_position <= position)
        bias_ref[place] = jnp.where(visible, 0.0, masked_score)
        bias = bias_ref[place]
        key_ref, value_ref = pair_ref
        values = value_ref[...].T
        for group, spread in enumerate(spreads[k]):
            columns = slice(group * lanes, (group + 1) * lanes)
            scores = dot(key_ref[:, columns], spread)
            weights, factors = [], []
            for head in range(per):
                row = group * per + head
                part = scores[:, head * tok : (head + 1) * tok] + bias
                top = jnp.max(part, axis=0, keepdims=True)
                if not fresh:
                    old = top_ref[row : row + 1, :]
                    top = jnp.maximum(top, old)
                    factors.append(jnp.exp2((old - top) * scale))
                weight = jnp.exp2((part - top) * scale)
                total = jnp.sum(weight, axis=0, keepdims=True)
                if not fresh:
                    total = total + total_ref[row : row + 1, :] * factors[head]
                top_ref[row : row + 1, :] = top
                total_ref[row : row + 1, :] = total
                weights.append(weight.astype(jnp.bfloat16))
            summed = dot(values[columns], jnp.concatenate(weights, axis=1))
            for head in range(per):
                rows = slice((group * per + head) * HD, (group * per + head + 1) * HD)
                piece = summed[head * HD : (head + 1) * HD, head * tok : (head + 1) * tok]
                if not fresh:
                    piece = piece + sum_ref[rows, :] * factors[head]
                sum_ref[rows, :] = piece

    for place, (k, unused_query, pair_ref, first) in enumerate(tasks):
        block = ids_ref[reps + place]
        begin = begin_ref[k : k + 1, :]
        tok = begin.shape[1]
        if first and k == 0:
            fold(place, k, pair_ref, block, begin, True)
            continue
        if first:
            top_ref, total_ref, sum_ref = states[k]
            top_ref[...] = jnp.full(top_ref.shape, masked_score, jnp.float32)
            total_ref[...] = jnp.zeros(total_ref.shape, jnp.float32)
            sum_ref[...] = jnp.zeros(sum_ref.shape, jnp.float32)

        @pl.when((block >= 0) & ((block + 1) * tok > lowest[k]))
        def unused(place=place, k=k, pair_ref=pair_ref, block=block, begin=begin):
            fold(place, k, pair_ref, block, begin, False)


def attend_kernel(plan, reps, counts, packed, ids_ref, begin_ref, *refs):
    ks = sorted({k for k, unused_pair, unused_first in plan})
    old_ks = [k for k in ks if not any(first for j, unused_pair, first in plan if j == k)]
    query_refs, refs = dict(zip(ks, refs)), refs[len(ks) :]
    pair_refs = [refs[2 * place : 2 * place + 2] for place in range(counts)]
    refs = refs[2 * counts :]
    old_refs, refs = refs[: 3 * len(old_ks)], refs[3 * len(old_ks) :]
    bias_ref, refs = refs[-1], refs[:-1]
    packed_refs, state_refs = (refs[: len(ks)], refs[len(ks) :]) if packed else ((), refs)
    states = {k: state_refs[3 * place : 3 * place + 3] for place, k in enumerate(ks)}
    for place, k in enumerate(old_ks):
        for old_ref, new_ref in zip(old_refs[3 * place : 3 * place + 3], states[k]):
            new_ref[...] = old_ref[...]
    tasks = [(k, query_refs[k], pair_refs[pair], first) for k, pair, first in plan]
    fold_blocks(ids_ref, begin_ref, tasks, reps, states, bias_ref)
    for k, packed_ref in zip(ks, packed_refs):
        top_ref, total_ref, sum_ref = states[k]
        heads, width = top_ref.shape[0], sum_ref.shape[0]
        packed_ref[0:width, :] = sum_ref[...].astype(jnp.bfloat16)
        first = width
        for ref, pieces in ((top_ref, 3), (total_ref, 2)):
            rest = ref[...]
            for unused in range(pieces):
                piece = rest.astype(jnp.bfloat16)
                packed_ref[first : first + heads, :] = piece
                rest = rest - piece.astype(jnp.float32)
                first += heads


def mix_kernel(expert_count, hot_capacity, own_ref, extended_ref, residual_ref, proj_ref, *refs):
    top_ref, total_ref, sum_ref = refs[0:3]
    mixed_ref, sent_refs = refs[-1 - expert_count], refs[len(refs) - expert_count :]
    packed_refs = refs[3 : -1 - expert_count]
    tok, width = mixed_ref.shape
    heads = top_ref.shape[0]
    scale = math.log2(math.e) / math.sqrt(HD)
    tops, totals = [top_ref[...]], [total_ref[...]]
    for packed_ref in packed_refs:
        pieces = [
            packed_ref[width + place * heads : width + (place + 1) * heads, :].astype(jnp.float32)
            for place in range(5)
        ]
        tops.append((pieces[0] + pieces[1]) + pieces[2])
        totals.append(pieces[3] + pieces[4])
    top = functools.reduce(jnp.maximum, tops)
    factors = [jnp.exp2((one - top) * scale) for one in tops]
    total = sum(one * factor for one, factor in zip(totals, factors))
    factors = [factor / total for factor in factors]
    pieces = []
    for head in range(heads):
        rows = slice(head * HD, (head + 1) * HD)
        piece = sum_ref[rows, :] * factors[0][head : head + 1, :]
        for packed_ref, factor in zip(packed_refs, factors[1:]):
            piece = piece + packed_ref[rows, :].astype(jnp.float32) * factor[head : head + 1, :]
        pieces.append(piece.astype(jnp.bfloat16))
    attended = jnp.concatenate(pieces, axis=0).T
    mixed = (residual_ref[...].astype(jnp.float32) + dot(attended, proj_ref[...])).astype(
        jnp.bfloat16
    )
    mixed_ref[...] = mixed
    mixed_f = mixed.astype(jnp.float32)
    inv_rms = lax.rsqrt(jnp.mean(mixed_f * mixed_f, axis=1, keepdims=True) + norm_eps)
    normed = (mixed_f * inv_rms).astype(jnp.bfloat16)
    placed = slot_matrix(chosen_of(extended_ref, tok), own_ref[0], len(sent_refs), hot_capacity)
    rows = dot(placed, normed).astype(jnp.bfloat16)
    for k, sent_ref in enumerate(sent_refs):
        sent_ref[...] = rows[k * hot_capacity : (k + 1) * hot_capacity]


def expert_kernel(
    reps,
    rep_list,
    sources,
    tok,
    strip,
    counts,
    own_ref,
    part_ref,
    up_ref,
    down_ref,
    extended_ref,
    *refs,
):
    row_count, grad_count = counts
    row_refs, refs = refs[:row_count], refs[row_count:]
    per_rep = row_count // len(rep_list)
    grad_refs, refs = refs[:grad_count], refs[grad_count:]
    own_rows = rep_list[0] == 0
    held_ref, refs = refs[-1], refs[:-1]
    if own_rows:
        back_refs, (up_acc, down_acc) = refs[:-2], refs[-2:]
    else:
        up_old, down_old = refs[:2]
        term_refs, kept_ref = refs[2:-1], refs[-1]
    total_grads = sum(ref.shape[0] for ref in grad_refs)
    capacity = total_grads // (sources * reps)
    count = sources * capacity
    parts = part_ref.shape[0]
    up = up_ref[...]
    down = down_ref[...]
    router = router_of(extended_ref, tok, sources)
    expert_lane = lax.broadcasted_iota(jnp.int32, (count, router.shape[0]), 1) == own_ref[0]

    def strips(rows, place):
        held_ref[place] = rows.T
        taken = []
        for k in range(parts):
            first = pl.multiple_of(part_ref[k] * strip, strip)
            taken.append(held_ref[place, pl.ds(first, strip), :])
        return jnp.concatenate(taken, axis=0)

    up_term = down_term = None
    for place, rep in enumerate(rep_list):
        rows = chunk_rows(
            row_refs[place * per_rep : (place + 1) * per_rep], sources, 0, capacity
        )
        grads = chunk_rows(grad_refs, sources, rep * capacity, (rep + 1) * capacity)
        pre = dot(rows, up)
        sigmoid_pre = jax.nn.sigmoid(pre)
        activated = (pre * sigmoid_pre).astype(jnp.bfloat16)
        logits = dot(rows, router, NT)
        gate = jax.nn.sigmoid(
            jnp.sum(jnp.where(expert_lane, logits, 0.0), axis=1, keepdims=True)
        )
        scaled = (gate * grads.astype(jnp.float32)).astype(jnp.bfloat16)
        act_grad = dot(scaled, down, NT)
        pre_grad = (act_grad * sigmoid_pre * (1.0 + pre * (1.0 - sigmoid_pre))).astype(
            jnp.bfloat16
        )
        if own_rows:
            produced = dot(activated, down).astype(jnp.bfloat16)
            token_grad = dot(pre_grad, up, NT).astype(jnp.bfloat16)
            for k, back_ref in enumerate(back_refs):
                back_ref[0:capacity] = produced[k * capacity : (k + 1) * capacity]
                back_ref[capacity : 2 * capacity] = token_grad[k * capacity : (k + 1) * capacity]
        more_up = dot(strips(rows, 2 * place), pre_grad)
        more_down = dot(strips(activated, 2 * place + 1), scaled)
        up_term = more_up if up_term is None else up_term + more_up
        down_term = more_down if down_term is None else down_term + more_down
    if own_rows:
        up_acc[...] = up_term
        down_acc[...] = down_term
        return
    up_term = up_term + up_old[...]
    down_term = down_term + down_old[...]
    for k, ref in enumerate((kept_ref, *term_refs)):
        rows = slice(k * strip, (k + 1) * strip)
        ref[0] = up_term[rows].astype(ref.dtype)
        ref[1] = down_term[rows].astype(ref.dtype)


def finish_kernel(
    hot_capacity, expert_count, own_ref, mixed_ref, extended_ref, *refs
):
    back_refs, (layer_ref, grad_mixed_ref) = refs[:-2], refs[-2:]
    tok = mixed_ref.shape[0]
    choice = chosen_of(extended_ref, tok)
    placed = slot_matrix(choice, own_ref[0], expert_count, hot_capacity)
    router = router_of(extended_ref, tok, expert_count)
    mixed_f = mixed_ref[...].astype(jnp.float32)
    inv_rms = lax.rsqrt(jnp.mean(mixed_f * mixed_f, axis=1, keepdims=True) + norm_eps)
    normed = (mixed_f * inv_rms).astype(jnp.bfloat16)
    one_hot = lax.broadcasted_iota(jnp.int32, (expert_count, tok), 0) == choice
    logits = dot(router, normed, NT)
    logit_row = jnp.sum(jnp.where(one_hot, logits, 0.0), axis=0, keepdims=True)
    logit = jnp.broadcast_to(logit_row, (8, tok)).T[:, 0:1]
    gate = jax.nn.sigmoid(logit)
    pair = 2 * hot_capacity
    chunks = [
        ref[first : first + pair] for ref in back_refs for first in range(0, ref.shape[0], pair)
    ]
    results = jnp.concatenate([chunk[:hot_capacity] for chunk in chunks], axis=0)
    grads = jnp.concatenate([chunk[hot_capacity:] for chunk in chunks], axis=0)
    result_f = dot(placed, results, TN)
    normed_grad = dot(placed, grads, TN)
    grad_f = extended_ref[0:tok, :].astype(jnp.float32)
    layer_ref[...] = (mixed_f + gate * result_f).astype(jnp.bfloat16)
    gate_grad = jnp.sum(grad_f * result_f, axis=1, keepdims=True)
    logit_grad = gate_grad * gate * (1.0 - gate)
    router_cols = dot(one_hot.astype(jnp.float32).astype(jnp.bfloat16), router, TN)
    total_grad = normed_grad + logit_grad * router_cols
    mean_term = jnp.mean(total_grad * mixed_f, axis=1, keepdims=True)
    input_grad = inv_rms * total_grad - mixed_f * inv_rms * inv_rms * inv_rms * mean_term
    grad_mixed_ref[...] = (grad_f + input_grad).astype(jnp.bfloat16)


def sum_kernel(kept_ref, *refs):
    term_refs, (up_ref, down_ref) = refs[:-2], refs[-2:]
    for kind, out_ref in enumerate((up_ref, down_ref)):
        total = kept_ref[kind]
        for ref in term_refs:
            total = total + ref[kind].astype(jnp.float32)
        out_ref[...] = total


def shape(dims, dtype=jnp.bfloat16):
    return jax.ShapeDtypeStruct(dims, dtype)


SMEM = pl.BlockSpec(memory_space=pltpu.SMEM)
VMEM = pl.BlockSpec(memory_space=pltpu.VMEM)
HBM = pl.BlockSpec(memory_space=pltpu.HBM)


def call(body, out_shape, specs, scratch=(), cost=0.5):
    return pl.pallas_call(
        body,
        cost_estimate=pl.CostEstimate(
            flops=int(cost * 1e9), bytes_accessed=0, transcendentals=0
        ),
        out_shape=out_shape,
        in_specs=specs,
        out_specs=jax.tree.map(lambda unused: VMEM, out_shape),
        scratch_shapes=list(scratch),
        compiler_params=pltpu.CompilerParams(vmem_limit_bytes=VMEM_LIMIT),
    )


def local(
    seq_count,
    expert_count,
    rep_count,
    query_rows,
    key_rows,
    value_rows,
    doc_lengths,
    residual,
    out_proj,
    router,
    expert_choice,
    weight_in,
    weight_out,
    grad_out,
):
    tok, width = query_rows.shape[1:]
    hidden = weight_in.shape[2]
    heads = width // HD
    experts = Group(("expert",), (expert_count,))
    reps = Group(("rep",), (rep_count,))
    owners = Group(("expert", "rep"), (expert_count, rep_count))
    parts = Group(("seq",), (seq_count,))
    strip = width // (seq_count * rep_count)
    capacity = max(2, (3 * tok + 2 * expert_count - 1) // (2 * expert_count))
    hot_capacity = min(4 * capacity, tok // 2)
    choice = expert_choice.reshape(1, tok)
    seq_index = lax.axis_index("seq")
    rep_index = lax.axis_index("rep")
    rank = seq_index * rep_count + rep_index
    own = jnp.stack([lax.axis_index("expert")]).astype(jnp.int32)
    part_to = jnp.stack(
        [parts.target(seq_index, k) * rep_count + rep_index for k in range(seq_count)]
    ).astype(jnp.int32)

    def forward(array):
        return lax.ppermute(array, "seq", [(i, (i + 1) % seq_count) for i in range(seq_count)])

    reach = (seq_count + 1) // 2
    longest = (seq_count * rep_count + 1) // 2
    query_ranks = [
        seq_index * rep_count + reps.source(rep_index, k) for k in range(rep_count)
    ]

    def task_ids(plan, steps):
        ids = list(query_ranks)
        for k, pair, unused_first in plan:
            block = rank - steps[pair] * rep_count
            behind = query_ranks[k] - block
            ids.append(jnp.where((block >= 0) & (behind >= 0) & (behind <= longest), block, -1))
        return jnp.stack(ids).astype(jnp.int32)

    state_shapes = [
        shape((heads, tok), jnp.float32),
        shape((heads, tok), jnp.float32),
        shape((width, tok), jnp.float32),
    ]
    tail = 16 + -(-expert_count // 16) * 16
    extended, begin = call(
        extend_kernel,
        [shape((tok + tail, width)), shape((rep_count, tok), jnp.int32)],
        [SMEM, SMEM] + [VMEM] * 3,
    )(
        jnp.stack(query_ranks).astype(jnp.int32), doc_lengths, choice, router.T, grad_out[0]
    )

    def attend(plan, pairs, steps, queries, states, packed, cost):
        ks = sorted({k for k, unused_pair, unused_first in plan})
        old = [one for k in ks if k in states for one in states[k]]
        state_out = state_shapes * len(ks)
        if packed:
            out_shape = [shape((width + 5 * heads, tok))] * len(ks)
            scratch = [pltpu.VMEM(one.shape, one.dtype) for one in state_out]
        else:
            out_shape, scratch = state_out, []
        outs = call(
            functools.partial(
                attend_kernel, plan, rep_count, len(pairs), packed
            ),
            out_shape,
            [SMEM] + [VMEM] * (1 + len(ks) + 2 * len(pairs) + len(old)),
            scratch + [pltpu.VMEM((len(plan), tok, tok), jnp.float32)],
            cost=cost,
        )(task_ids(plan, steps), begin, *[queries[k] for k in ks], *[one for both in pairs for one in both], *old)
        if packed:
            return dict(zip(ks, outs))
        return {k: list(outs[3 * place : 3 * place + 3]) for place, k in enumerate(ks)}

    others = range(1, rep_count)
    lines = [(key_rows[0], value_rows[0])]
    lines.append(tuple(forward(one) for one in lines[0]))
    queries = reps.exchange([query_rows[0]] * rep_count)
    extendeds = reps.exchange([extended] * rep_count)
    states = attend(((0, 0, True),), lines[:1], [0], queries, {}, False, 2.0)
    ahead, *states[0] = lax.optimization_barrier((lines[1][0], *states[0]))
    lines[1] = (ahead, lines[1][1])
    for unused in range(1, reach):
        lines.append(tuple(forward(one) for one in lines[-1]))
    middle = tuple((0, step, False) for step in range(1, reach)) + tuple(
        (k, step, step == 0) for k in others for step in range(reach)
    )
    states = attend(middle, lines[:-1], list(range(reach)), queries, states, False, 4.0)
    partial = attend(
        tuple((k, 0, False) for k in others), lines[-1:], [reach], queries, states, True, 1.5
    )
    partial[1], *extendeds[1:] = lax.optimization_barrier((partial[1], *extendeds[1:]))
    returned = reps.exchange([None] + [partial[k] for k in others], inverse=True)[1:]
    states = attend(((0, 0, False),), lines[-1:], [reach], queries, states, False, 1.5)
    sent_grads = call(
        functools.partial(dispatch_kernel, rep_count, tok, hot_capacity),
        [shape((rep_count * hot_capacity, width))] * expert_count,
        [SMEM] + [VMEM] * rep_count,
    )(own, *extendeds)
    got_grads = merged(experts.exchange(sent_grads), MOST_PERMUTES)

    mixed, *sent_rows = call(
        functools.partial(mix_kernel, expert_count, hot_capacity),
        [shape((tok, width))] + [shape((hot_capacity, width))] * expert_count,
        [SMEM] + [VMEM] * (6 + len(returned)),
        cost=2.0,
    )(own, extendeds[0], residual[0], out_proj, *states[0], *returned)
    arrived = owners.exchange([sent_rows[k // rep_count] for k in range(owners.count)])
    got_rows = merged(arrived[0::rep_count], MOST_PERMUTES)
    got_more = [
        one for k in others for one in merged(arrived[k::rep_count], MOST_PERMUTES)
    ]

    def expert_call(rep_list, rows, out_shape, extra):
        return call(
            functools.partial(
                expert_kernel,
                rep_count,
                rep_list,
                expert_count,
                tok,
                strip,
                (len(rows), len(got_grads)),
            ),
            out_shape,
            [SMEM, SMEM] + [VMEM] * (3 + len(rows) + len(got_grads) + len(extra)),
            [pltpu.VMEM((2 * len(rep_list), width, expert_count * hot_capacity), jnp.bfloat16)],
            cost=2.0,
        )(own, part_to, weight_in[0], weight_out[0], extendeds[0], *rows, *got_grads, *extra)

    *back, up_acc, down_acc = expert_call(
        (0,),
        got_rows,
        [shape((2 * hot_capacity, width))] * expert_count
        + [shape((seq_count * strip, hidden), jnp.float32)]
        + [shape((seq_count * strip, width), jnp.float32)],
        [],
    )
    got_back = merged(experts.exchange(back, inverse=True), MOST_PERMUTES)
    *terms, kept = expert_call(
        tuple(range(1, rep_count)),
        got_more,
        [shape((2, strip, hidden))] * (seq_count - 1)
        + [shape((2, strip, hidden), jnp.float32)],
        [up_acc, down_acc],
    )
    got_terms = parts.exchange([None] + terms)[1:]
    layer_out, grad_mixed = call(
        functools.partial(finish_kernel, hot_capacity, expert_count),
        [shape((tok, width)), shape((tok, width))],
        [SMEM] + [VMEM] * (2 + len(got_back)),
        cost=1.5,
    )(own, mixed, extended, *got_back)
    kept, layer_out = lax.optimization_barrier((kept, layer_out))
    share_in, share_out = call(
        sum_kernel,
        [shape((strip, hidden), jnp.float32), shape((strip, width), jnp.float32)],
        [VMEM] * seq_count,
    )(kept, *got_terms[::-1])
    return (layer_out[None], grad_mixed[None], share_in[None], share_out[None])


def solution(mesh):
    rows = P("expert", ("seq", "rep"), None)
    in_specs = (
        rows,
        rows,
        rows,
        P("expert", None),
        rows,
        P(),
        P(),
        rows,
        P("expert", None, None),
        P("expert", None, None),
        rows,
    )
    body = functools.partial(
        local, mesh.shape["seq"], mesh.shape["expert"], mesh.shape["rep"]
    )
    return jax.shard_map(
        body, mesh=mesh, in_specs=in_specs, out_specs=(rows, rows, rows, rows), check_vma=False
    )
```

```python
import functools
import math

import jax
import jax.numpy as jnp
from jax import lax
from jax.experimental import pallas as pl
from jax.experimental.pallas import tpu as pltpu
from jax.sharding import PartitionSpec as P

HD = 32
norm_eps = 1e-06
masked_score = -1e30
VMEM_LIMIT = 48 * 1024 * 1024
MOST_PERMUTES = 16
NT = (((1,), (1,)), ((), ()))
TN = (((0,), (0,)), ((), ()))


def dot(a, b, dims=None):
    if dims is None:
        return jnp.dot(a, b, preferred_element_type=jnp.float32)
    return lax.dot_general(a, b, dims, preferred_element_type=jnp.float32)


def away(index, offset, size):
    if size & (size - 1) == 0:
        return index ^ offset
    return (index + offset) % size


def back_from(index, offset, size):
    if size & (size - 1) == 0:
        return index ^ offset
    return (index - offset + size) % size


class Group:
    def __init__(self, axes, sizes):
        self.axes, self.sizes = tuple(axes), tuple(sizes)
        self.count = math.prod(sizes)

    def split(self, flat):
        coords = []
        for size in reversed(self.sizes):
            coords.append(flat % size)
            flat = flat // size
        return coords[::-1]

    def moved(self, flat, offset, step):
        place = 0
        for coord, part, size in zip(self.split(flat), self.split(offset), self.sizes):
            place = place * size + step(coord, part, size)
        return place

    def target(self, flat, offset):
        return self.moved(flat, offset, away)

    def source(self, flat, offset):
        return self.moved(flat, offset, back_from)

    def exchange(self, chunks, inverse=False):
        to, start = (self.source, self.target) if inverse else (self.target, self.source)
        if self.count <= MOST_PERMUTES:
            order = sorted(range(1, self.count), key=lambda k: -k)
            got = {0: chunks[0]}
            for k in order:
                pairs = [(i, to(i, k)) for i in range(self.count)]
                got[k] = lax.ppermute(chunks[k], self.axes, pairs)
            return [got[k] for k in range(self.count)]
        me = lax.axis_index(self.axes)
        steps = jnp.arange(self.count, dtype=jnp.int32)
        sent_to = jax.vmap(lambda k: to(me, k))(steps)
        placed = jnp.zeros((self.count,), jnp.int32).at[sent_to].set(steps)
        stacked = jnp.stack(chunks)[placed]
        got = lax.all_to_all(stacked, self.axes, split_axis=0, concat_axis=0, tiled=True)
        came_from = jax.vmap(lambda k: start(me, k))(steps)
        ordered = got[came_from]
        return [ordered[k] for k in range(self.count)]


def merged(chunks, most):
    if len(chunks) <= most:
        return list(chunks)
    return [jnp.concatenate(chunks, axis=0)]


def chunk_rows(refs, count, low, high):
    size = sum(ref.shape[0] for ref in refs) // count
    parts = []
    for chunk in range(count):
        ref, first = (refs[chunk], 0) if len(refs) == count else (refs[0], chunk * size)
        parts.append(ref[first + low : first + high, :])
    return parts[0] if count == 1 else jnp.concatenate(parts, axis=0)


def slot_matrix(choice, own, expert_count, hot_capacity):
    tok = choice.shape[1]
    offset = back_from(choice, own, expert_count)
    one_hot = lax.broadcasted_iota(jnp.int32, (expert_count, tok), 0) == offset
    hits = one_hot.astype(jnp.float32).astype(jnp.bfloat16)
    earlier = lax.broadcasted_iota(jnp.int32, (tok, tok), 0) <= lax.broadcasted_iota(
        jnp.int32, (tok, tok), 1
    )
    counted = dot(hits, earlier.astype(jnp.float32).astype(jnp.bfloat16))
    rank = jnp.sum(jnp.where(one_hot, counted, 0.0), axis=0, keepdims=True) - 1.0
    slots = offset * hot_capacity + rank.astype(jnp.int32)
    rows = lax.broadcasted_iota(jnp.int32, (expert_count * hot_capacity, tok), 0)
    return (rows == slots).astype(jnp.float32).astype(jnp.bfloat16)


def extend_kernel(
    ranks_ref, lengths_ref, choice_ref, router_ref, grad_ref, extended_ref, begin_ref
):
    tok, width = grad_ref.shape
    extended_ref[0:tok, :] = grad_ref[...]
    chosen = jnp.broadcast_to(choice_ref[...].astype(jnp.float32), (16, tok))
    extended_ref[tok : tok + 16, 0:tok] = chosen.astype(jnp.bfloat16)
    extended_ref[tok : tok + 16, tok:width] = jnp.zeros((16, width - tok), jnp.bfloat16)
    routed = router_ref[...].astype(jnp.float32)
    spare = extended_ref.shape[0] - tok - 16 - routed.shape[0]
    if spare:
        routed = jnp.concatenate([routed, jnp.zeros((spare, width), jnp.float32)], axis=0)
    extended_ref[tok + 16 :, :] = routed.astype(jnp.bfloat16)
    for k in range(begin_ref.shape[0]):
        position = ranks_ref[k] * tok + lax.broadcasted_iota(jnp.int32, (1, tok), 1)
        begin = jnp.zeros((1, tok), jnp.int32)
        bound = jnp.int32(0)
        for doc in range(lengths_ref.shape[1] - 1):
            bound = bound + lengths_ref[0, doc]
            begin = jnp.maximum(begin, jnp.where(position >= bound, bound, 0))
        begin_ref[k : k + 1, :] = begin


def chosen_of(extended_ref, tok):
    return extended_ref[tok : tok + 16, 0:tok].astype(jnp.float32)[0:1].astype(jnp.int32)


def router_of(extended_ref, tok, expert_count):
    whole = extended_ref[tok + 16 :, :].astype(jnp.float32)
    return whole[0:expert_count].astype(jnp.bfloat16)


def fold_blocks(ids_ref, begin_ref, tasks, reps, states, bias_ref):
    lanes = 128
    per = lanes // HD
    scale = math.log2(math.e) / math.sqrt(HD)
    spreads = {}
    lowest = {}
    for k, query_ref, unused_pair, unused_first in tasks:
        if k in spreads:
            continue
        lowest[k] = jnp.min(begin_ref[k : k + 1, :])
        tok = begin_ref.shape[1]
        turned = query_ref[...].T
        head_of_row = lax.broadcasted_iota(jnp.int32, (lanes, tok), 0) // HD
        spreads[k] = []
        for group in range(turned.shape[0] // lanes):
            part = turned[group * lanes : (group + 1) * lanes]
            spreads[k].append(
                jnp.concatenate(
                    [
                        jnp.where(head_of_row == head, part, jnp.zeros_like(part))
                        for head in range(per)
                    ],
                    axis=1,
                )
            )

    def fold(place, k, pair_ref, block, begin, fresh):
        top_ref, total_ref, sum_ref = states[k]
        tok = begin.shape[1]
        position = ids_ref[k] * tok + lax.broadcasted_iota(jnp.int32, (1, tok), 1)
        key_position = block * tok + lax.broadcasted_iota(jnp.int32, (tok, tok), 0)
        visible = (key_position >= begin) & (key_position <= position)
        bias_ref[place] = jnp.where(visible, 0.0, masked_score)
        bias = bias_ref[place]
        key_ref, value_ref = pair_ref
        values = value_ref[...].T
        for group, spread in enumerate(spreads[k]):
            columns = slice(group * lanes, (group + 1) * lanes)
            scores = dot(key_ref[:, columns], spread)
            weights, factors = [], []
            for head in range(per):
                row = group * per + head
                part = scores[:, head * tok : (head + 1) * tok] + bias
                top = jnp.max(part, axis=0, keepdims=True)
                if not fresh:
                    old = top_ref[row : row + 1, :]
                    top = jnp.maximum(top, old)
                    factors.append(jnp.exp2((old - top) * scale))
                weight = jnp.exp2((part - top) * scale)
                total = jnp.sum(weight, axis=0, keepdims=True)
                if not fresh:
                    total = total + total_ref[row : row + 1, :] * factors[head]
                top_ref[row : row + 1, :] = top
                total_ref[row : row + 1, :] = total
                weights.append(weight.astype(jnp.bfloat16))
            summed = dot(values[columns], jnp.concatenate(weights, axis=1))
            for head in range(per):
                rows = slice((group * per + head) * HD, (group * per + head + 1) * HD)
                piece = summed[head * HD : (head + 1) * HD, head * tok : (head + 1) * tok]
                if not fresh:
                    piece = piece + sum_ref[rows, :] * factors[head]
                sum_ref[rows, :] = piece

    for place, (k, unused_query, pair_ref, first) in enumerate(tasks):
        block = ids_ref[reps + place]
        begin = begin_ref[k : k + 1, :]
        tok = begin.shape[1]
        if first and k == 0:
            fold(place, k, pair_ref, block, begin, True)
            continue
        if first:
            top_ref, total_ref, sum_ref = states[k]
            top_ref[...] = jnp.full(top_ref.shape, masked_score, jnp.float32)
            total_ref[...] = jnp.zeros(total_ref.shape, jnp.float32)
            sum_ref[...] = jnp.zeros(sum_ref.shape, jnp.float32)

        @pl.when((block >= 0) & ((block + 1) * tok > lowest[k]))
        def unused(place=place, k=k, pair_ref=pair_ref, block=block, begin=begin):
            fold(place, k, pair_ref, block, begin, False)


def attend_kernel(plan, reps, counts, packed, ids_ref, begin_ref, *refs):
    ks = sorted({k for k, unused_pair, unused_first in plan})
    old_ks = [k for k in ks if not any(first for j, unused_pair, first in plan if j == k)]
    query_refs, refs = dict(zip(ks, refs)), refs[len(ks) :]
    pair_refs = [refs[2 * place : 2 * place + 2] for place in range(counts)]
    refs = refs[2 * counts :]
    old_refs, refs = refs[: 3 * len(old_ks)], refs[3 * len(old_ks) :]
    bias_ref, refs = refs[-1], refs[:-1]
    packed_refs, state_refs = (refs[: len(ks)], refs[len(ks) :]) if packed else ((), refs)
    states = {k: state_refs[3 * place : 3 * place + 3] for place, k in enumerate(ks)}
    for place, k in enumerate(old_ks):
        for old_ref, new_ref in zip(old_refs[3 * place : 3 * place + 3], states[k]):
            new_ref[...] = old_ref[...]
    tasks = [(k, query_refs[k], pair_refs[pair], first) for k, pair, first in plan]
    fold_blocks(ids_ref, begin_ref, tasks, reps, states, bias_ref)
    for k, packed_ref in zip(ks, packed_refs):
        top_ref, total_ref, sum_ref = states[k]
        heads, width = top_ref.shape[0], sum_ref.shape[0]
        packed_ref[0:width, :] = sum_ref[...].astype(jnp.bfloat16)
        first = width
        for ref, pieces in ((top_ref, 3), (total_ref, 2)):
            rest = ref[...]
            for unused in range(pieces):
                piece = rest.astype(jnp.bfloat16)
                packed_ref[first : first + heads, :] = piece
                rest = rest - piece.astype(jnp.float32)
                first += heads


def mix_kernel(expert_count, hot_capacity, own_ref, extended_ref, residual_ref, proj_ref, *refs):
    top_ref, total_ref, sum_ref = refs[0:3]
    mixed_ref, sent_refs = refs[-1 - expert_count], refs[len(refs) - expert_count :]
    packed_refs = refs[3 : -1 - expert_count]
    tok, width = mixed_ref.shape
    heads = top_ref.shape[0]
    scale = math.log2(math.e) / math.sqrt(HD)
    tops, totals = [top_ref[...]], [total_ref[...]]
    for packed_ref in packed_refs:
        pieces = [
            packed_ref[width + place * heads : width + (place + 1) * heads, :].astype(jnp.float32)
            for place in range(5)
        ]
        tops.append((pieces[0] + pieces[1]) + pieces[2])
        totals.append(pieces[3] + pieces[4])
    top = functools.reduce(jnp.maximum, tops)
    factors = [jnp.exp2((one - top) * scale) for one in tops]
    total = sum(one * factor for one, factor in zip(totals, factors))
    factors = [factor / total for factor in factors]
    pieces = []
    for head in range(heads):
        rows = slice(head * HD, (head + 1) * HD)
        piece = sum_ref[rows, :] * factors[0][head : head + 1, :]
        for packed_ref, factor in zip(packed_refs, factors[1:]):
            piece = piece + packed_ref[rows, :].astype(jnp.float32) * factor[head : head + 1, :]
        pieces.append(piece.astype(jnp.bfloat16))
    attended = jnp.concatenate(pieces, axis=0).T
    mixed = (residual_ref[...].astype(jnp.float32) + dot(attended, proj_ref[...])).astype(
        jnp.bfloat16
    )
    mixed_ref[...] = mixed
    mixed_f = mixed.astype(jnp.float32)
    inv_rms = lax.rsqrt(jnp.mean(mixed_f * mixed_f, axis=1, keepdims=True) + norm_eps)
    normed = (mixed_f * inv_rms).astype(jnp.bfloat16)
    placed = slot_matrix(chosen_of(extended_ref, tok), own_ref[0], len(sent_refs), hot_capacity)
    rows = dot(placed, normed).astype(jnp.bfloat16)
    grads = dot(placed, extended_ref[0:tok, :]).astype(jnp.bfloat16)
    for k, sent_ref in enumerate(sent_refs):
        sent_ref[0:hot_capacity] = rows[k * hot_capacity : (k + 1) * hot_capacity]
        sent_ref[hot_capacity:] = grads[k * hot_capacity : (k + 1) * hot_capacity]


def expert_kernel(
    rep_list,
    sources,
    tok,
    strip,
    row_count,
    own_ref,
    part_ref,
    up_ref,
    down_ref,
    extended_ref,
    *refs,
):
    row_refs, refs = refs[:row_count], refs[row_count:]
    per_rep = row_count // len(rep_list)
    own_rows = rep_list[0] == 0
    held_ref, refs = refs[-1], refs[:-1]
    if own_rows:
        back_refs, (up_acc, down_acc) = refs[:-2], refs[-2:]
    else:
        up_old, down_old = refs[:2]
        term_refs, kept_ref = refs[2:-1], refs[-1]
    capacity = sum(ref.shape[0] for ref in row_refs[:per_rep]) // (2 * sources)
    count = sources * capacity
    parts = part_ref.shape[0]
    up = up_ref[...]
    down = down_ref[...]
    router = router_of(extended_ref, tok, sources)
    expert_lane = lax.broadcasted_iota(jnp.int32, (count, router.shape[0]), 1) == own_ref[0]

    def strips(rows, place):
        held_ref[place] = rows.T
        taken = []
        for k in range(parts):
            first = pl.multiple_of(part_ref[k] * strip, strip)
            taken.append(held_ref[place, pl.ds(first, strip), :])
        return jnp.concatenate(taken, axis=0)

    up_term = down_term = None
    for place in range(len(rep_list)):
        chunks = row_refs[place * per_rep : (place + 1) * per_rep]
        rows = chunk_rows(chunks, sources, 0, capacity)
        grads = chunk_rows(chunks, sources, capacity, 2 * capacity)
        pre = dot(rows, up)
        sigmoid_pre = jax.nn.sigmoid(pre)
        activated = (pre * sigmoid_pre).astype(jnp.bfloat16)
        logits = dot(rows, router, NT)
        gate = jax.nn.sigmoid(
            jnp.sum(jnp.where(expert_lane, logits, 0.0), axis=1, keepdims=True)
        )
        scaled = (gate * grads.astype(jnp.float32)).astype(jnp.bfloat16)
        act_grad = dot(scaled, down, NT)
        pre_grad = (act_grad * sigmoid_pre * (1.0 + pre * (1.0 - sigmoid_pre))).astype(
            jnp.bfloat16
        )
        if own_rows:
            produced = dot(activated, down).astype(jnp.bfloat16)
            token_grad = dot(pre_grad, up, NT).astype(jnp.bfloat16)
            for k, back_ref in enumerate(back_refs):
                back_ref[0:capacity] = produced[k * capacity : (k + 1) * capacity]
                back_ref[capacity : 2 * capacity] = token_grad[k * capacity : (k + 1) * capacity]
        more_up = dot(strips(rows, 2 * place), pre_grad)
        more_down = dot(strips(activated, 2 * place + 1), scaled)
        up_term = more_up if up_term is None else up_term + more_up
        down_term = more_down if down_term is None else down_term + more_down
    if own_rows:
        up_acc[...] = up_term
        down_acc[...] = down_term
        return
    up_term = up_term + up_old[...]
    down_term = down_term + down_old[...]
    for k, ref in enumerate((kept_ref, *term_refs)):
        rows = slice(k * strip, (k + 1) * strip)
        ref[0] = up_term[rows].astype(ref.dtype)
        ref[1] = down_term[rows].astype(ref.dtype)


def finish_kernel(
    hot_capacity, expert_count, own_ref, mixed_ref, extended_ref, *refs
):
    back_refs, (layer_ref, grad_mixed_ref) = refs[:-2], refs[-2:]
    tok = mixed_ref.shape[0]
    choice = chosen_of(extended_ref, tok)
    placed = slot_matrix(choice, own_ref[0], expert_count, hot_capacity)
    router = router_of(extended_ref, tok, expert_count)
    mixed_f = mixed_ref[...].astype(jnp.float32)
    inv_rms = lax.rsqrt(jnp.mean(mixed_f * mixed_f, axis=1, keepdims=True) + norm_eps)
    normed = (mixed_f * inv_rms).astype(jnp.bfloat16)
    one_hot = lax.broadcasted_iota(jnp.int32, (expert_count, tok), 0) == choice
    logits = dot(router, normed, NT)
    logit_row = jnp.sum(jnp.where(one_hot, logits, 0.0), axis=0, keepdims=True)
    logit = jnp.broadcast_to(logit_row, (8, tok)).T[:, 0:1]
    gate = jax.nn.sigmoid(logit)
    pair = 2 * hot_capacity
    chunks = [
        ref[first : first + pair] for ref in back_refs for first in range(0, ref.shape[0], pair)
    ]
    results = jnp.concatenate([chunk[:hot_capacity] for chunk in chunks], axis=0)
    grads = jnp.concatenate([chunk[hot_capacity:] for chunk in chunks], axis=0)
    result_f = dot(placed, results, TN)
    normed_grad = dot(placed, grads, TN)
    grad_f = extended_ref[0:tok, :].astype(jnp.float32)
    layer_ref[...] = (mixed_f + gate * result_f).astype(jnp.bfloat16)
    gate_grad = jnp.sum(grad_f * result_f, axis=1, keepdims=True)
    logit_grad = gate_grad * gate * (1.0 - gate)
    router_cols = dot(one_hot.astype(jnp.float32).astype(jnp.bfloat16), router, TN)
    total_grad = normed_grad + logit_grad * router_cols
    mean_term = jnp.mean(total_grad * mixed_f, axis=1, keepdims=True)
    input_grad = inv_rms * total_grad - mixed_f * inv_rms * inv_rms * inv_rms * mean_term
    grad_mixed_ref[...] = (grad_f + input_grad).astype(jnp.bfloat16)


def sum_kernel(kept_ref, *refs):
    term_refs, (up_ref, down_ref) = refs[:-2], refs[-2:]
    for kind, out_ref in enumerate((up_ref, down_ref)):
        total = kept_ref[kind]
        for ref in term_refs:
            total = total + ref[kind].astype(jnp.float32)
        out_ref[...] = total


def shape(dims, dtype=jnp.bfloat16):
    return jax.ShapeDtypeStruct(dims, dtype)


SMEM = pl.BlockSpec(memory_space=pltpu.SMEM)
VMEM = pl.BlockSpec(memory_space=pltpu.VMEM)
HBM = pl.BlockSpec(memory_space=pltpu.HBM)


def call(body, out_shape, specs, scratch=(), cost=0.5):
    return pl.pallas_call(
        body,
        cost_estimate=pl.CostEstimate(
            flops=int(cost * 1e9), bytes_accessed=0, transcendentals=0
        ),
        out_shape=out_shape,
        in_specs=specs,
        out_specs=jax.tree.map(lambda unused: VMEM, out_shape),
        scratch_shapes=list(scratch),
        compiler_params=pltpu.CompilerParams(vmem_limit_bytes=VMEM_LIMIT),
    )


def local(
    seq_count,
    expert_count,
    rep_count,
    query_rows,
    key_rows,
    value_rows,
    doc_lengths,
    residual,
    out_proj,
    router,
    expert_choice,
    weight_in,
    weight_out,
    grad_out,
):
    tok, width = query_rows.shape[1:]
    hidden = weight_in.shape[2]
    heads = width // HD
    experts = Group(("expert",), (expert_count,))
    reps = Group(("rep",), (rep_count,))
    owners = Group(("expert", "rep"), (expert_count, rep_count))
    parts = Group(("seq",), (seq_count,))
    strip = width // (seq_count * rep_count)
    capacity = max(2, (3 * tok + 2 * expert_count - 1) // (2 * expert_count))
    hot_capacity = min(4 * capacity, tok // 2)
    choice = expert_choice.reshape(1, tok)
    seq_index = lax.axis_index("seq")
    rep_index = lax.axis_index("rep")
    rank = seq_index * rep_count + rep_index
    own = jnp.stack([lax.axis_index("expert")]).astype(jnp.int32)
    part_to = jnp.stack(
        [parts.target(seq_index, k) * rep_count + rep_index for k in range(seq_count)]
    ).astype(jnp.int32)

    def forward(array):
        return lax.ppermute(array, "seq", [(i, (i + 1) % seq_count) for i in range(seq_count)])

    reach = (seq_count + 1) // 2
    longest = (seq_count * rep_count + 1) // 2
    query_ranks = [
        seq_index * rep_count + reps.source(rep_index, k) for k in range(rep_count)
    ]

    def task_ids(plan, steps):
        ids = list(query_ranks)
        for k, pair, unused_first in plan:
            block = rank - steps[pair] * rep_count
            behind = query_ranks[k] - block
            ids.append(jnp.where((block >= 0) & (behind >= 0) & (behind <= longest), block, -1))
        return jnp.stack(ids).astype(jnp.int32)

    state_shapes = [
        shape((heads, tok), jnp.float32),
        shape((heads, tok), jnp.float32),
        shape((width, tok), jnp.float32),
    ]
    tail = 16 + -(-expert_count // 16) * 16
    extended, begin = call(
        extend_kernel,
        [shape((tok + tail, width)), shape((rep_count, tok), jnp.int32)],
        [SMEM, SMEM] + [VMEM] * 3,
    )(
        jnp.stack(query_ranks).astype(jnp.int32), doc_lengths, choice, router.T, grad_out[0]
    )

    def attend(plan, pairs, steps, queries, states, packed, cost):
        ks = sorted({k for k, unused_pair, unused_first in plan})
        old = [one for k in ks if k in states for one in states[k]]
        state_out = state_shapes * len(ks)
        if packed:
            out_shape = [shape((width + 5 * heads, tok))] * len(ks)
            scratch = [pltpu.VMEM(one.shape, one.dtype) for one in state_out]
        else:
            out_shape, scratch = state_out, []
        outs = call(
            functools.partial(
                attend_kernel, plan, rep_count, len(pairs), packed
            ),
            out_shape,
            [SMEM] + [VMEM] * (1 + len(ks) + 2 * len(pairs) + len(old)),
            scratch + [pltpu.VMEM((len(plan), tok, tok), jnp.float32)],
            cost=cost,
        )(task_ids(plan, steps), begin, *[queries[k] for k in ks], *[one for both in pairs for one in both], *old)
        if packed:
            return dict(zip(ks, outs))
        return {k: list(outs[3 * place : 3 * place + 3]) for place, k in enumerate(ks)}

    others = range(1, rep_count)
    lines = [(key_rows[0], value_rows[0])]
    lines.append(tuple(forward(one) for one in lines[0]))
    queries = reps.exchange([query_rows[0]] * rep_count)
    states = attend(((0, 0, True),), lines[:1], [0], queries, {}, False, 2.0)
    ahead, *states[0] = lax.optimization_barrier((lines[1][0], *states[0]))
    lines[1] = (ahead, lines[1][1])
    for unused in range(1, reach):
        lines.append(tuple(forward(one) for one in lines[-1]))
    middle = tuple((0, step, False) for step in range(1, reach)) + tuple(
        (k, step, step == 0) for k in others for step in range(reach)
    )
    states = attend(middle, lines[:-1], list(range(reach)), queries, states, False, 4.0)
    partial = attend(
        tuple((k, 0, False) for k in others), lines[-1:], [reach], queries, states, True, 1.5
    )
    returned = reps.exchange([None] + [partial[k] for k in others], inverse=True)[1:]
    states = attend(((0, 0, False),), lines[-1:], [reach], queries, states, False, 1.5)
    mixed, *sent_rows = call(
        functools.partial(mix_kernel, expert_count, hot_capacity),
        [shape((tok, width))] + [shape((2 * hot_capacity, width))] * expert_count,
        [SMEM] + [VMEM] * (6 + len(returned)),
        cost=2.0,
    )(own, extended, residual[0], out_proj, *states[0], *returned)
    arrived = owners.exchange([sent_rows[k // rep_count] for k in range(owners.count)])
    got_rows = merged(arrived[0::rep_count], MOST_PERMUTES)
    got_more = [
        one for k in others for one in merged(arrived[k::rep_count], MOST_PERMUTES)
    ]

    def expert_call(rep_list, rows, out_shape, extra):
        return call(
            functools.partial(
                expert_kernel,
                rep_list,
                expert_count,
                tok,
                strip,
                len(rows),
            ),
            out_shape,
            [SMEM, SMEM] + [VMEM] * (3 + len(rows) + len(extra)),
            [pltpu.VMEM((2 * len(rep_list), width, expert_count * hot_capacity), jnp.bfloat16)],
            cost=2.0,
        )(own, part_to, weight_in[0], weight_out[0], extended, *rows, *extra)

    *back, up_acc, down_acc = expert_call(
        (0,),
        got_rows,
        [shape((2 * hot_capacity, width))] * expert_count
        + [shape((seq_count * strip, hidden), jnp.float32)]
        + [shape((seq_count * strip, width), jnp.float32)],
        [],
    )
    got_back = merged(experts.exchange(back, inverse=True), MOST_PERMUTES)
    *terms, kept = expert_call(
        tuple(range(1, rep_count)),
        got_more,
        [shape((2, strip, hidden))] * (seq_count - 1)
        + [shape((2, strip, hidden), jnp.float32)],
        [up_acc, down_acc],
    )
    got_terms = parts.exchange([None] + terms)[1:]
    layer_out, grad_mixed = call(
        functools.partial(finish_kernel, hot_capacity, expert_count),
        [shape((tok, width)), shape((tok, width))],
        [SMEM] + [VMEM] * (2 + len(got_back)),
        cost=1.5,
    )(own, mixed, extended, *got_back)
    kept, layer_out = lax.optimization_barrier((kept, layer_out))
    share_in, share_out = call(
        sum_kernel,
        [shape((strip, hidden), jnp.float32), shape((strip, width), jnp.float32)],
        [VMEM] * seq_count,
    )(kept, *got_terms[::-1])
    return (layer_out[None], grad_mixed[None], share_in[None], share_out[None])


def solution(mesh):
    rows = P("expert", ("seq", "rep"), None)
    in_specs = (
        rows,
        rows,
        rows,
        P("expert", None),
        rows,
        P(),
        P(),
        rows,
        P("expert", None, None),
        P("expert", None, None),
        rows,
    )
    body = functools.partial(
        local, mesh.shape["seq"], mesh.shape["expert"], mesh.shape["rep"]
    )
    return jax.shard_map(
        body, mesh=mesh, in_specs=in_specs, out_specs=(rows, rows, rows, rows), check_vma=False
    )
```

```python
import functools
import math

import jax
import jax.numpy as jnp
from jax import lax
from jax.experimental import pallas as pl
from jax.experimental.pallas import tpu as pltpu
from jax.sharding import PartitionSpec as P

HD = 32
norm_eps = 1e-06
masked_score = -1e30
VMEM_LIMIT = 48 * 1024 * 1024
MOST_PERMUTES = 16
NT = (((1,), (1,)), ((), ()))
TN = (((0,), (0,)), ((), ()))


def dot(a, b, dims=None):
    if dims is None:
        return jnp.dot(a, b, preferred_element_type=jnp.float32)
    return lax.dot_general(a, b, dims, preferred_element_type=jnp.float32)


def away(index, offset, size):
    if size & (size - 1) == 0:
        return index ^ offset
    return (index + offset) % size


def back_from(index, offset, size):
    if size & (size - 1) == 0:
        return index ^ offset
    return (index - offset + size) % size


class Group:
    def __init__(self, axes, sizes):
        self.axes, self.sizes = tuple(axes), tuple(sizes)
        self.count = math.prod(sizes)

    def split(self, flat):
        coords = []
        for size in reversed(self.sizes):
            coords.append(flat % size)
            flat = flat // size
        return coords[::-1]

    def moved(self, flat, offset, step):
        place = 0
        for coord, part, size in zip(self.split(flat), self.split(offset), self.sizes):
            place = place * size + step(coord, part, size)
        return place

    def target(self, flat, offset):
        return self.moved(flat, offset, away)

    def source(self, flat, offset):
        return self.moved(flat, offset, back_from)

    def exchange(self, chunks, inverse=False):
        to, start = (self.source, self.target) if inverse else (self.target, self.source)
        if self.count <= MOST_PERMUTES:
            order = sorted(range(1, self.count), key=lambda k: -k)
            got = {0: chunks[0]}
            for k in order:
                pairs = [(i, to(i, k)) for i in range(self.count)]
                got[k] = lax.ppermute(chunks[k], self.axes, pairs)
            return [got[k] for k in range(self.count)]
        me = lax.axis_index(self.axes)
        steps = jnp.arange(self.count, dtype=jnp.int32)
        sent_to = jax.vmap(lambda k: to(me, k))(steps)
        placed = jnp.zeros((self.count,), jnp.int32).at[sent_to].set(steps)
        stacked = jnp.stack(chunks)[placed]
        got = lax.all_to_all(stacked, self.axes, split_axis=0, concat_axis=0, tiled=True)
        came_from = jax.vmap(lambda k: start(me, k))(steps)
        ordered = got[came_from]
        return [ordered[k] for k in range(self.count)]


def merged(chunks, most):
    if len(chunks) <= most:
        return list(chunks)
    return [jnp.concatenate(chunks, axis=0)]


def chunk_rows(refs, count, low, high):
    size = sum(ref.shape[0] for ref in refs) // count
    parts = []
    for chunk in range(count):
        ref, first = (refs[chunk], 0) if len(refs) == count else (refs[0], chunk * size)
        parts.append(ref[first + low : first + high, :])
    return parts[0] if count == 1 else jnp.concatenate(parts, axis=0)


def slot_matrix(choice, own, expert_count, hot_capacity):
    tok = choice.shape[1]
    offset = back_from(choice, own, expert_count)
    one_hot = lax.broadcasted_iota(jnp.int32, (expert_count, tok), 0) == offset
    hits = one_hot.astype(jnp.float32).astype(jnp.bfloat16)
    earlier = lax.broadcasted_iota(jnp.int32, (tok, tok), 0) <= lax.broadcasted_iota(
        jnp.int32, (tok, tok), 1
    )
    counted = dot(hits, earlier.astype(jnp.float32).astype(jnp.bfloat16))
    rank = jnp.sum(jnp.where(one_hot, counted, 0.0), axis=0, keepdims=True) - 1.0
    slots = offset * hot_capacity + rank.astype(jnp.int32)
    rows = lax.broadcasted_iota(jnp.int32, (expert_count * hot_capacity, tok), 0)
    return (rows == slots).astype(jnp.float32).astype(jnp.bfloat16)


def extend_kernel(
    ranks_ref, lengths_ref, choice_ref, router_ref, grad_ref, extended_ref, begin_ref
):
    tok, width = grad_ref.shape
    extended_ref[0:tok, :] = grad_ref[...]
    chosen = jnp.broadcast_to(choice_ref[...].astype(jnp.float32), (16, tok))
    extended_ref[tok : tok + 16, 0:tok] = chosen.astype(jnp.bfloat16)
    extended_ref[tok : tok + 16, tok:width] = jnp.zeros((16, width - tok), jnp.bfloat16)
    routed = router_ref[...].astype(jnp.float32)
    spare = extended_ref.shape[0] - tok - 16 - routed.shape[0]
    if spare:
        routed = jnp.concatenate([routed, jnp.zeros((spare, width), jnp.float32)], axis=0)
    extended_ref[tok + 16 :, :] = routed.astype(jnp.bfloat16)
    for k in range(begin_ref.shape[0]):
        position = ranks_ref[k] * tok + lax.broadcasted_iota(jnp.int32, (1, tok), 1)
        begin = jnp.zeros((1, tok), jnp.int32)
        bound = jnp.int32(0)
        for doc in range(lengths_ref.shape[1] - 1):
            bound = bound + lengths_ref[0, doc]
            begin = jnp.maximum(begin, jnp.where(position >= bound, bound, 0))
        begin_ref[k : k + 1, :] = begin


def chosen_of(extended_ref, tok):
    return extended_ref[tok : tok + 16, 0:tok].astype(jnp.float32)[0:1].astype(jnp.int32)


def router_of(extended_ref, tok, expert_count):
    whole = extended_ref[tok + 16 :, :].astype(jnp.float32)
    return whole[0:expert_count].astype(jnp.bfloat16)


def dispatch_kernel(reps, tok, hot_capacity, own_ref, *refs):
    extended_refs, sent_refs = refs[:reps], refs[reps:]
    for rep in range(reps):
        choice = chosen_of(extended_refs[rep], tok)
        placed = slot_matrix(choice, own_ref[0], len(sent_refs), hot_capacity)
        rows = dot(placed, extended_refs[rep][0:tok, :]).astype(jnp.bfloat16)
        for k, sent_ref in enumerate(sent_refs):
            sent_ref[rep * hot_capacity : (rep + 1) * hot_capacity] = rows[
                k * hot_capacity : (k + 1) * hot_capacity
            ]


def fold_blocks(ids_ref, begin_ref, tasks, reps, states, bias_ref):
    lanes = 128
    per = lanes // HD
    scale = math.log2(math.e) / math.sqrt(HD)
    spreads = {}
    lowest = {}
    for k, query_ref, unused_pair, unused_first in tasks:
        if k in spreads:
            continue
        lowest[k] = jnp.min(begin_ref[k : k + 1, :])
        tok = begin_ref.shape[1]
        turned = query_ref[...].T
        head_of_row = lax.broadcasted_iota(jnp.int32, (lanes, tok), 0) // HD
        spreads[k] = []
        for group in range(turned.shape[0] // lanes):
            part = turned[group * lanes : (group + 1) * lanes]
            spreads[k].append(
                jnp.concatenate(
                    [
                        jnp.where(head_of_row == head, part, jnp.zeros_like(part))
                        for head in range(per)
                    ],
                    axis=1,
                )
            )

    def fold(place, k, pair_ref, block, begin, fresh):
        top_ref, total_ref, sum_ref = states[k]
        tok = begin.shape[1]
        position = ids_ref[k] * tok + lax.broadcasted_iota(jnp.int32, (1, tok), 1)
        key_position = block * tok + lax.broadcasted_iota(jnp.int32, (tok, tok), 0)
        visible = (key_position >= begin) & (key_position <= position)
        bias_ref[place] = jnp.where(visible, 0.0, masked_score)
        bias = bias_ref[place]
        key_ref, value_ref = pair_ref
        values = value_ref[...].T
        for group, spread in enumerate(spreads[k]):
            columns = slice(group * lanes, (group + 1) * lanes)
            scores = dot(key_ref[:, columns], spread)
            weights, factors = [], []
            for head in range(per):
                row = group * per + head
                part = scores[:, head * tok : (head + 1) * tok] + bias
                top = jnp.max(part, axis=0, keepdims=True)
                if not fresh:
                    old = top_ref[row : row + 1, :]
                    top = jnp.maximum(top, old)
                    factors.append(jnp.exp2((old - top) * scale))
                weight = jnp.exp2((part - top) * scale)
                total = jnp.sum(weight, axis=0, keepdims=True)
                if not fresh:
                    total = total + total_ref[row : row + 1, :] * factors[head]
                top_ref[row : row + 1, :] = top
                total_ref[row : row + 1, :] = total
                weights.append(weight.astype(jnp.bfloat16))
            summed = dot(values[columns], jnp.concatenate(weights, axis=1))
            for head in range(per):
                rows = slice((group * per + head) * HD, (group * per + head + 1) * HD)
                piece = summed[head * HD : (head + 1) * HD, head * tok : (head + 1) * tok]
                if not fresh:
                    piece = piece + sum_ref[rows, :] * factors[head]
                sum_ref[rows, :] = piece

    for place, (k, unused_query, pair_ref, first) in enumerate(tasks):
        block = ids_ref[reps + place]
        begin = begin_ref[k : k + 1, :]
        tok = begin.shape[1]
        if first and k == 0:
            fold(place, k, pair_ref, block, begin, True)
            continue
        if first:
            top_ref, total_ref, sum_ref = states[k]
            top_ref[...] = jnp.full(top_ref.shape, masked_score, jnp.float32)
            total_ref[...] = jnp.zeros(total_ref.shape, jnp.float32)
            sum_ref[...] = jnp.zeros(sum_ref.shape, jnp.float32)

        @pl.when((block >= 0) & ((block + 1) * tok > lowest[k]))
        def unused(place=place, k=k, pair_ref=pair_ref, block=block, begin=begin):
            fold(place, k, pair_ref, block, begin, False)


def attend_kernel(plan, reps, counts, packed, ids_ref, begin_ref, *refs):
    ks = sorted({k for k, unused_pair, unused_first in plan})
    old_ks = [k for k in ks if not any(first for j, unused_pair, first in plan if j == k)]
    query_refs, refs = dict(zip(ks, refs)), refs[len(ks) :]
    pair_refs = [refs[2 * place : 2 * place + 2] for place in range(counts)]
    refs = refs[2 * counts :]
    old_refs, refs = refs[: 3 * len(old_ks)], refs[3 * len(old_ks) :]
    bias_ref, refs = refs[-1], refs[:-1]
    packed_refs, state_refs = (refs[: len(ks)], refs[len(ks) :]) if packed else ((), refs)
    states = {k: state_refs[3 * place : 3 * place + 3] for place, k in enumerate(ks)}
    for place, k in enumerate(old_ks):
        for old_ref, new_ref in zip(old_refs[3 * place : 3 * place + 3], states[k]):
            new_ref[...] = old_ref[...]
    tasks = [(k, query_refs[k], pair_refs[pair], first) for k, pair, first in plan]
    fold_blocks(ids_ref, begin_ref, tasks, reps, states, bias_ref)
    for k, packed_ref in zip(ks, packed_refs):
        top_ref, total_ref, sum_ref = states[k]
        heads, width = top_ref.shape[0], sum_ref.shape[0]
        packed_ref[0:width, :] = sum_ref[...].astype(jnp.bfloat16)
        first = width
        for ref, pieces in ((top_ref, 3), (total_ref, 2)):
            rest = ref[...]
            for unused in range(pieces):
                piece = rest.astype(jnp.bfloat16)
                packed_ref[first : first + heads, :] = piece
                rest = rest - piece.astype(jnp.float32)
                first += heads


def mix_kernel(expert_count, hot_capacity, own_ref, extended_ref, residual_ref, proj_ref, *refs):
    top_ref, total_ref, sum_ref = refs[0:3]
    mixed_ref, sent_refs = refs[-1 - expert_count], refs[len(refs) - expert_count :]
    packed_refs = refs[3 : -1 - expert_count]
    tok, width = mixed_ref.shape
    heads = top_ref.shape[0]
    scale = math.log2(math.e) / math.sqrt(HD)
    tops, totals = [top_ref[...]], [total_ref[...]]
    for packed_ref in packed_refs:
        pieces = [
            packed_ref[width + place * heads : width + (place + 1) * heads, :].astype(jnp.float32)
            for place in range(5)
        ]
        tops.append((pieces[0] + pieces[1]) + pieces[2])
        totals.append(pieces[3] + pieces[4])
    top = functools.reduce(jnp.maximum, tops)
    factors = [jnp.exp2((one - top) * scale) for one in tops]
    total = sum(one * factor for one, factor in zip(totals, factors))
    factors = [factor / total for factor in factors]
    pieces = []
    for head in range(heads):
        rows = slice(head * HD, (head + 1) * HD)
        piece = sum_ref[rows, :] * factors[0][head : head + 1, :]
        for packed_ref, factor in zip(packed_refs, factors[1:]):
            piece = piece + packed_ref[rows, :].astype(jnp.float32) * factor[head : head + 1, :]
        pieces.append(piece.astype(jnp.bfloat16))
    attended = jnp.concatenate(pieces, axis=0).T
    mixed = (residual_ref[...].astype(jnp.float32) + dot(attended, proj_ref[...])).astype(
        jnp.bfloat16
    )
    mixed_ref[...] = mixed
    mixed_f = mixed.astype(jnp.float32)
    inv_rms = lax.rsqrt(jnp.mean(mixed_f * mixed_f, axis=1, keepdims=True) + norm_eps)
    normed = (mixed_f * inv_rms).astype(jnp.bfloat16)
    placed = slot_matrix(chosen_of(extended_ref, tok), own_ref[0], len(sent_refs), hot_capacity)
    rows = dot(placed, normed).astype(jnp.bfloat16)
    for k, sent_ref in enumerate(sent_refs):
        sent_ref[...] = rows[k * hot_capacity : (k + 1) * hot_capacity]


def expert_kernel(
    reps,
    rep_list,
    sources,
    tok,
    strip,
    counts,
    own_ref,
    part_ref,
    up_ref,
    down_ref,
    extended_ref,
    *refs,
):
    row_count, grad_count = counts
    row_refs, refs = refs[:row_count], refs[row_count:]
    per_rep = row_count // len(rep_list)
    grad_refs, refs = refs[:grad_count], refs[grad_count:]
    own_rows = rep_list[0] == 0
    held_ref, refs = refs[-1], refs[:-1]
    if own_rows:
        activated_ref, pre_grad_ref, up_acc, down_acc = refs
    else:
        up_old, down_old = refs[:2]
        term_refs, kept_ref = refs[2:-1], refs[-1]
    total_grads = sum(ref.shape[0] for ref in grad_refs)
    capacity = total_grads // (sources * reps)
    count = sources * capacity
    parts = part_ref.shape[0]
    up = up_ref[...]
    down = down_ref[...]
    router = router_of(extended_ref, tok, sources)
    expert_lane = lax.broadcasted_iota(jnp.int32, (count, router.shape[0]), 1) == own_ref[0]

    def strips(rows, place):
        held_ref[place] = rows.T
        taken = []
        for k in range(parts):
            first = pl.multiple_of(part_ref[k] * strip, strip)
            taken.append(held_ref[place, pl.ds(first, strip), :])
        return jnp.concatenate(taken, axis=0)

    up_term = down_term = None
    for place, rep in enumerate(rep_list):
        rows = chunk_rows(
            row_refs[place * per_rep : (place + 1) * per_rep], sources, 0, capacity
        )
        grads = chunk_rows(grad_refs, sources, rep * capacity, (rep + 1) * capacity)
        pre = dot(rows, up)
        sigmoid_pre = jax.nn.sigmoid(pre)
        activated = (pre * sigmoid_pre).astype(jnp.bfloat16)
        logits = dot(rows, router, NT)
        gate = jax.nn.sigmoid(
            jnp.sum(jnp.where(expert_lane, logits, 0.0), axis=1, keepdims=True)
        )
        scaled = (gate * grads.astype(jnp.float32)).astype(jnp.bfloat16)
        act_grad = dot(scaled, down, NT)
        pre_grad = (act_grad * sigmoid_pre * (1.0 + pre * (1.0 - sigmoid_pre))).astype(
            jnp.bfloat16
        )
        if own_rows:
            activated_ref[...] = activated
            pre_grad_ref[...] = pre_grad
        more_up = dot(strips(rows, 2 * place), pre_grad)
        more_down = dot(strips(activated, 2 * place + 1), scaled)
        up_term = more_up if up_term is None else up_term + more_up
        down_term = more_down if down_term is None else down_term + more_down
    if own_rows:
        up_acc[...] = up_term
        down_acc[...] = down_term
        return
    up_term = up_term + up_old[...]
    down_term = down_term + down_old[...]
    for k, ref in enumerate((kept_ref, *term_refs)):
        rows = slice(k * strip, (k + 1) * strip)
        ref[0] = up_term[rows].astype(ref.dtype)
        ref[1] = down_term[rows].astype(ref.dtype)


def back_kernel(sources, up_ref, down_ref, activated_ref, pre_grad_ref, *back_refs):
    capacity = activated_ref.shape[0] // sources
    produced = dot(activated_ref[...], down_ref[...]).astype(jnp.bfloat16)
    token_grad = dot(pre_grad_ref[...], up_ref[...], NT).astype(jnp.bfloat16)
    for k, back_ref in enumerate(back_refs):
        rows = slice(k * capacity, (k + 1) * capacity)
        back_ref[0:capacity] = produced[rows]
        back_ref[capacity : 2 * capacity] = token_grad[rows]


def prepare_kernel(
    hot_capacity,
    expert_count,
    own_ref,
    mixed_ref,
    extended_ref,
    placed_ref,
    factors_ref,
    router_cols_ref,
):
    tok = mixed_ref.shape[0]
    choice = chosen_of(extended_ref, tok)
    placed = slot_matrix(choice, own_ref[0], expert_count, hot_capacity)
    placed_ref[...] = placed.T
    router = router_of(extended_ref, tok, expert_count)
    mixed_f = mixed_ref[...].astype(jnp.float32)
    inv_rms = lax.rsqrt(jnp.mean(mixed_f * mixed_f, axis=1, keepdims=True) + norm_eps)
    normed = (mixed_f * inv_rms).astype(jnp.bfloat16)
    one_hot = lax.broadcasted_iota(jnp.int32, (expert_count, tok), 0) == choice
    logits = dot(router, normed, NT)
    logit_row = jnp.sum(jnp.where(one_hot, logits, 0.0), axis=0, keepdims=True)
    gate = jax.nn.sigmoid(jnp.broadcast_to(logit_row, (8, tok)).T[:, 0:1])
    lane = lax.broadcasted_iota(jnp.int32, factors_ref.shape, 1)
    factors_ref[...] = jnp.where(lane == 0, inv_rms, gate)
    router_cols_ref[...] = dot(one_hot.astype(jnp.float32).astype(jnp.bfloat16), router, TN)


def finish_kernel(
    hot_capacity,
    placed_ref,
    factors_ref,
    router_cols_ref,
    mixed_ref,
    extended_ref,
    *refs,
):
    back_refs, (layer_ref, grad_mixed_ref) = refs[:-2][::-1], refs[-2:]
    tok = mixed_ref.shape[0]
    mixed_f = mixed_ref[...].astype(jnp.float32)
    inv_rms = factors_ref[:, 0:1]
    gate = factors_ref[:, 1:2]
    pair = 2 * hot_capacity
    chunks = [
        ref[first : first + pair] for ref in back_refs for first in range(0, ref.shape[0], pair)
    ]
    results = jnp.concatenate([chunk[:hot_capacity] for chunk in chunks], axis=0)
    grads = jnp.concatenate([chunk[hot_capacity:] for chunk in chunks], axis=0)
    placed = placed_ref[...]
    result_f = dot(placed, results)
    normed_grad = dot(placed, grads)
    grad_f = extended_ref[0:tok, :].astype(jnp.float32)
    layer_ref[...] = (mixed_f + gate * result_f).astype(jnp.bfloat16)
    gate_grad = jnp.sum(grad_f * result_f, axis=1, keepdims=True)
    logit_grad = gate_grad * gate * (1.0 - gate)
    total_grad = normed_grad + logit_grad * router_cols_ref[...]
    mean_term = jnp.mean(total_grad * mixed_f, axis=1, keepdims=True)
    input_grad = inv_rms * total_grad - mixed_f * inv_rms * inv_rms * inv_rms * mean_term
    grad_mixed_ref[...] = (grad_f + input_grad).astype(jnp.bfloat16)


def sum_kernel(kept_ref, *refs):
    term_refs, (up_ref, down_ref) = refs[:-2], refs[-2:]
    for kind, out_ref in enumerate((up_ref, down_ref)):
        total = kept_ref[kind]
        for ref in term_refs:
            total = total + ref[kind].astype(jnp.float32)
        out_ref[...] = total


def shape(dims, dtype=jnp.bfloat16):
    return jax.ShapeDtypeStruct(dims, dtype)


SMEM = pl.BlockSpec(memory_space=pltpu.SMEM)
VMEM = pl.BlockSpec(memory_space=pltpu.VMEM)
HBM = pl.BlockSpec(memory_space=pltpu.HBM)


def call(body, out_shape, specs, scratch=(), cost=0.5):
    return pl.pallas_call(
        body,
        cost_estimate=pl.CostEstimate(
            flops=int(cost * 1e9), bytes_accessed=0, transcendentals=0
        ),
        out_shape=out_shape,
        in_specs=specs,
        out_specs=jax.tree.map(lambda unused: VMEM, out_shape),
        scratch_shapes=list(scratch),
        compiler_params=pltpu.CompilerParams(vmem_limit_bytes=VMEM_LIMIT),
    )


def local(
    seq_count,
    expert_count,
    rep_count,
    query_rows,
    key_rows,
    value_rows,
    doc_lengths,
    residual,
    out_proj,
    router,
    expert_choice,
    weight_in,
    weight_out,
    grad_out,
):
    tok, width = query_rows.shape[1:]
    hidden = weight_in.shape[2]
    heads = width // HD
    experts = Group(("expert",), (expert_count,))
    reps = Group(("rep",), (rep_count,))
    owners = Group(("expert", "rep"), (expert_count, rep_count))
    parts = Group(("seq",), (seq_count,))
    strip = width // (seq_count * rep_count)
    capacity = max(2, (3 * tok + 2 * expert_count - 1) // (2 * expert_count))
    hot_capacity = min(4 * capacity, tok // 2)
    choice = expert_choice.reshape(1, tok)
    seq_index = lax.axis_index("seq")
    rep_index = lax.axis_index("rep")
    rank = seq_index * rep_count + rep_index
    own = jnp.stack([lax.axis_index("expert")]).astype(jnp.int32)
    part_to = jnp.stack(
        [parts.target(seq_index, k) * rep_count + rep_index for k in range(seq_count)]
    ).astype(jnp.int32)

    def forward(array):
        return lax.ppermute(array, "seq", [(i, (i + 1) % seq_count) for i in range(seq_count)])

    reach = (seq_count + 1) // 2
    longest = (seq_count * rep_count + 1) // 2
    query_ranks = [
        seq_index * rep_count + reps.source(rep_index, k) for k in range(rep_count)
    ]

    def task_ids(plan, steps):
        ids = list(query_ranks)
        for k, pair, unused_first in plan:
            block = rank - steps[pair] * rep_count
            behind = query_ranks[k] - block
            ids.append(jnp.where((block >= 0) & (behind >= 0) & (behind <= longest), block, -1))
        return jnp.stack(ids).astype(jnp.int32)

    state_shapes = [
        shape((heads, tok), jnp.float32),
        shape((heads, tok), jnp.float32),
        shape((width, tok), jnp.float32),
    ]
    tail = 16 + -(-expert_count // 16) * 16
    extended, begin = call(
        extend_kernel,
        [shape((tok + tail, width)), shape((rep_count, tok), jnp.int32)],
        [SMEM, SMEM] + [VMEM] * 3,
    )(
        jnp.stack(query_ranks).astype(jnp.int32), doc_lengths, choice, router.T, grad_out[0]
    )

    def attend(plan, pairs, steps, queries, states, packed, cost):
        ks = sorted({k for k, unused_pair, unused_first in plan})
        old = [one for k in ks if k in states for one in states[k]]
        state_out = state_shapes * len(ks)
        if packed:
            out_shape = [shape((width + 5 * heads, tok))] * len(ks)
            scratch = [pltpu.VMEM(one.shape, one.dtype) for one in state_out]
        else:
            out_shape, scratch = state_out, []
        outs = call(
            functools.partial(
                attend_kernel, plan, rep_count, len(pairs), packed
            ),
            out_shape,
            [SMEM] + [VMEM] * (1 + len(ks) + 2 * len(pairs) + len(old)),
            scratch + [pltpu.VMEM((len(plan), tok, tok), jnp.float32)],
            cost=cost,
        )(task_ids(plan, steps), begin, *[queries[k] for k in ks], *[one for both in pairs for one in both], *old)
        if packed:
            return dict(zip(ks, outs))
        return {k: list(outs[3 * place : 3 * place + 3]) for place, k in enumerate(ks)}

    others = range(1, rep_count)
    lines = [(key_rows[0], value_rows[0])]
    lines.append(tuple(forward(one) for one in lines[0]))
    queries = reps.exchange([query_rows[0]] * rep_count)
    extendeds = reps.exchange([extended] * rep_count)
    states = attend(((0, 0, True),), lines[:1], [0], queries, {}, False, 2.0)
    ahead, *states[0] = lax.optimization_barrier((lines[1][0], *states[0]))
    lines[1] = (ahead, lines[1][1])
    for unused in range(1, reach):
        lines.append(tuple(forward(one) for one in lines[-1]))
    middle = tuple((0, step, False) for step in range(1, reach)) + tuple(
        (k, step, step == 0) for k in others for step in range(reach)
    )
    states = attend(middle, lines[:-1], list(range(reach)), queries, states, False, 4.0)
    partial = attend(
        tuple((k, 0, False) for k in others), lines[-1:], [reach], queries, states, True, 1.5
    )
    partial[1], *extendeds[1:] = lax.optimization_barrier((partial[1], *extendeds[1:]))
    returned = reps.exchange([None] + [partial[k] for k in others], inverse=True)[1:]
    states = attend(((0, 0, False),), lines[-1:], [reach], queries, states, False, 1.5)
    sent_grads = call(
        functools.partial(dispatch_kernel, rep_count, tok, hot_capacity),
        [shape((rep_count * hot_capacity, width))] * expert_count,
        [SMEM] + [VMEM] * rep_count,
    )(own, *extendeds)
    got_grads = merged(experts.exchange(sent_grads), MOST_PERMUTES)

    mixed, *sent_rows = call(
        functools.partial(mix_kernel, expert_count, hot_capacity),
        [shape((tok, width))] + [shape((hot_capacity, width))] * expert_count,
        [SMEM] + [VMEM] * (6 + len(returned)),
        cost=2.0,
    )(own, extendeds[0], residual[0], out_proj, *states[0], *returned)
    arrived = owners.exchange([sent_rows[k // rep_count] for k in range(owners.count)])
    got_rows = merged(arrived[0::rep_count], MOST_PERMUTES)
    got_more = [
        one for k in others for one in merged(arrived[k::rep_count], MOST_PERMUTES)
    ]

    def expert_call(rep_list, rows, out_shape, extra):
        return call(
            functools.partial(
                expert_kernel,
                rep_count,
                rep_list,
                expert_count,
                tok,
                strip,
                (len(rows), len(got_grads)),
            ),
            out_shape,
            [SMEM, SMEM] + [VMEM] * (3 + len(rows) + len(got_grads) + len(extra)),
            [pltpu.VMEM((2 * len(rep_list), width, expert_count * hot_capacity), jnp.bfloat16)],
            cost=2.0,
        )(own, part_to, weight_in[0], weight_out[0], extendeds[0], *rows, *got_grads, *extra)

    slots = expert_count * hot_capacity
    activated, pre_grad, up_acc, down_acc = expert_call(
        (0,),
        got_rows,
        [
            shape((slots, hidden)),
            shape((slots, hidden)),
            shape((seq_count * strip, hidden), jnp.float32),
            shape((seq_count * strip, width), jnp.float32),
        ],
        [],
    )
    *terms, kept = expert_call(
        tuple(range(1, rep_count)),
        got_more,
        [shape((2, strip, hidden))] * (seq_count - 1)
        + [shape((2, strip, hidden), jnp.float32)],
        [up_acc, down_acc],
    )
    got_terms = parts.exchange([None] + terms)[1:]
    activated, mixed, kept = lax.optimization_barrier((activated, mixed, kept))
    back = call(
        functools.partial(back_kernel, expert_count),
        [shape((2 * hot_capacity, width))] * expert_count,
        [VMEM] * 4,
        cost=1.0,
    )(weight_in[0], weight_out[0], activated, pre_grad)
    got_back = merged(experts.exchange(back, inverse=True), MOST_PERMUTES)
    prepared = call(
        functools.partial(prepare_kernel, hot_capacity, expert_count),
        [
            shape((tok, slots)),
            shape((tok, 128), jnp.float32),
            shape((tok, width), jnp.float32),
        ],
        [SMEM, VMEM, VMEM],
        cost=1.0,
    )(own, mixed, extended)
    layer_out, grad_mixed = call(
        functools.partial(finish_kernel, hot_capacity),
        [shape((tok, width)), shape((tok, width))],
        [VMEM] * (5 + len(got_back)),
        cost=1.0,
    )(*prepared, mixed, extended, *got_back[::-1])
    share_in, share_out = call(
        sum_kernel,
        [shape((strip, hidden), jnp.float32), shape((strip, width), jnp.float32)],
        [VMEM] * seq_count,
    )(kept, *got_terms[::-1])
    return (layer_out[None], grad_mixed[None], share_in[None], share_out[None])


def solution(mesh):
    rows = P("expert", ("seq", "rep"), None)
    in_specs = (
        rows,
        rows,
        rows,
        P("expert", None),
        rows,
        P(),
        P(),
        rows,
        P("expert", None, None),
        P("expert", None, None),
        rows,
    )
    body = functools.partial(
        local, mesh.shape["seq"], mesh.shape["expert"], mesh.shape["rep"]
    )
    return jax.shard_map(
        body, mesh=mesh, in_specs=in_specs, out_specs=(rows, rows, rows, rows), check_vma=False
    )
```

```python
import functools
import math

import jax
import jax.numpy as jnp
from jax import lax
from jax.experimental import pallas as pl
from jax.experimental.pallas import tpu as pltpu
from jax.sharding import PartitionSpec as P

HD = 32
norm_eps = 1e-06
masked_score = -1e30
VMEM_LIMIT = 48 * 1024 * 1024
MOST_PERMUTES = 16
NT = (((1,), (1,)), ((), ()))
TN = (((0,), (0,)), ((), ()))


def dot(a, b, dims=None):
    if dims is None:
        return jnp.dot(a, b, preferred_element_type=jnp.float32)
    return lax.dot_general(a, b, dims, preferred_element_type=jnp.float32)


def away(index, offset, size):
    if size & (size - 1) == 0:
        return index ^ offset
    return (index + offset) % size


def back_from(index, offset, size):
    if size & (size - 1) == 0:
        return index ^ offset
    return (index - offset + size) % size


class Group:
    def __init__(self, axes, sizes):
        self.axes, self.sizes = tuple(axes), tuple(sizes)
        self.count = math.prod(sizes)

    def split(self, flat):
        coords = []
        for size in reversed(self.sizes):
            coords.append(flat % size)
            flat = flat // size
        return coords[::-1]

    def moved(self, flat, offset, step):
        place = 0
        for coord, part, size in zip(self.split(flat), self.split(offset), self.sizes):
            place = place * size + step(coord, part, size)
        return place

    def target(self, flat, offset):
        return self.moved(flat, offset, away)

    def source(self, flat, offset):
        return self.moved(flat, offset, back_from)

    def exchange(self, chunks, inverse=False):
        to, start = (self.source, self.target) if inverse else (self.target, self.source)
        if self.count <= MOST_PERMUTES:
            order = sorted(range(1, self.count), key=lambda k: -k)
            got = {0: chunks[0]}
            for k in order:
                pairs = [(i, to(i, k)) for i in range(self.count)]
                got[k] = lax.ppermute(chunks[k], self.axes, pairs)
            return [got[k] for k in range(self.count)]
        me = lax.axis_index(self.axes)
        steps = jnp.arange(self.count, dtype=jnp.int32)
        sent_to = jax.vmap(lambda k: to(me, k))(steps)
        placed = jnp.zeros((self.count,), jnp.int32).at[sent_to].set(steps)
        stacked = jnp.stack(chunks)[placed]
        got = lax.all_to_all(stacked, self.axes, split_axis=0, concat_axis=0, tiled=True)
        came_from = jax.vmap(lambda k: start(me, k))(steps)
        ordered = got[came_from]
        return [ordered[k] for k in range(self.count)]


def merged(chunks, most):
    if len(chunks) <= most:
        return list(chunks)
    return [jnp.concatenate(chunks, axis=0)]


def chunk_rows(refs, count, low, high):
    size = sum(ref.shape[0] for ref in refs) // count
    parts = []
    for chunk in range(count):
        ref, first = (refs[chunk], 0) if len(refs) == count else (refs[0], chunk * size)
        parts.append(ref[first + low : first + high, :])
    return parts[0] if count == 1 else jnp.concatenate(parts, axis=0)


def slot_matrix(choice, own, expert_count, hot_capacity):
    tok = choice.shape[1]
    offset = back_from(choice, own, expert_count)
    one_hot = lax.broadcasted_iota(jnp.int32, (expert_count, tok), 0) == offset
    hits = one_hot.astype(jnp.float32).astype(jnp.bfloat16)
    earlier = lax.broadcasted_iota(jnp.int32, (tok, tok), 0) <= lax.broadcasted_iota(
        jnp.int32, (tok, tok), 1
    )
    counted = dot(hits, earlier.astype(jnp.float32).astype(jnp.bfloat16))
    rank = jnp.sum(jnp.where(one_hot, counted, 0.0), axis=0, keepdims=True) - 1.0
    slots = offset * hot_capacity + rank.astype(jnp.int32)
    rows = lax.broadcasted_iota(jnp.int32, (expert_count * hot_capacity, tok), 0)
    return (rows == slots).astype(jnp.float32).astype(jnp.bfloat16)


def extend_kernel(
    ranks_ref, lengths_ref, choice_ref, router_ref, grad_ref, extended_ref, begin_ref
):
    tok, width = grad_ref.shape
    extended_ref[0:tok, :] = grad_ref[...]
    chosen = jnp.broadcast_to(choice_ref[...].astype(jnp.float32), (16, tok))
    extended_ref[tok : tok + 16, 0:tok] = chosen.astype(jnp.bfloat16)
    extended_ref[tok : tok + 16, tok:width] = jnp.zeros((16, width - tok), jnp.bfloat16)
    routed = router_ref[...].astype(jnp.float32)
    spare = extended_ref.shape[0] - tok - 16 - routed.shape[0]
    if spare:
        routed = jnp.concatenate([routed, jnp.zeros((spare, width), jnp.float32)], axis=0)
    extended_ref[tok + 16 :, :] = routed.astype(jnp.bfloat16)
    for k in range(begin_ref.shape[0]):
        position = ranks_ref[k] * tok + lax.broadcasted_iota(jnp.int32, (1, tok), 1)
        begin = jnp.zeros((1, tok), jnp.int32)
        bound = jnp.int32(0)
        for doc in range(lengths_ref.shape[1] - 1):
            bound = bound + lengths_ref[0, doc]
            begin = jnp.maximum(begin, jnp.where(position >= bound, bound, 0))
        begin_ref[k : k + 1, :] = begin


def chosen_of(extended_ref, tok):
    return extended_ref[tok : tok + 16, 0:tok].astype(jnp.float32)[0:1].astype(jnp.int32)


def router_of(extended_ref, tok, expert_count):
    whole = extended_ref[tok + 16 :, :].astype(jnp.float32)
    return whole[0:expert_count].astype(jnp.bfloat16)


def dispatch_kernel(reps, tok, hot_capacity, own_ref, *refs):
    extended_refs, sent_refs = refs[:reps], refs[reps:]
    for rep in range(reps):
        choice = chosen_of(extended_refs[rep], tok)
        placed = slot_matrix(choice, own_ref[0], len(sent_refs), hot_capacity)
        rows = dot(placed, extended_refs[rep][0:tok, :]).astype(jnp.bfloat16)
        for k, sent_ref in enumerate(sent_refs):
            sent_ref[rep * hot_capacity : (rep + 1) * hot_capacity] = rows[
                k * hot_capacity : (k + 1) * hot_capacity
            ]


def fold_blocks(ids_ref, begin_ref, tasks, reps, states, bias_ref):
    lanes = 128
    per = lanes // HD
    scale = math.log2(math.e) / math.sqrt(HD)
    spreads = {}
    lowest = {}
    for k, query_ref, unused_pair, unused_first in tasks:
        if k in spreads:
            continue
        lowest[k] = jnp.min(begin_ref[k : k + 1, :])
        tok = begin_ref.shape[1]
        turned = query_ref[...].T
        head_of_row = lax.broadcasted_iota(jnp.int32, (lanes, tok), 0) // HD
        spreads[k] = []
        for group in range(turned.shape[0] // lanes):
            part = turned[group * lanes : (group + 1) * lanes]
            spreads[k].append(
                jnp.concatenate(
                    [
                        jnp.where(head_of_row == head, part, jnp.zeros_like(part))
                        for head in range(per)
                    ],
                    axis=1,
                )
            )

    def fold(place, k, pair_ref, block, begin, fresh):
        top_ref, total_ref, sum_ref = states[k]
        tok = begin.shape[1]
        position = ids_ref[k] * tok + lax.broadcasted_iota(jnp.int32, (1, tok), 1)
        key_position = block * tok + lax.broadcasted_iota(jnp.int32, (tok, tok), 0)
        visible = (key_position >= begin) & (key_position <= position)
        bias_ref[place] = jnp.where(visible, 0.0, masked_score)
        bias = bias_ref[place]
        key_ref, value_ref = pair_ref
        values = value_ref[...].T
        for group, spread in enumerate(spreads[k]):
            columns = slice(group * lanes, (group + 1) * lanes)
            scores = dot(key_ref[:, columns], spread)
            weights, factors = [], []
            for head in range(per):
                row = group * per + head
                part = scores[:, head * tok : (head + 1) * tok] + bias
                top = jnp.max(part, axis=0, keepdims=True)
                if not fresh:
                    old = top_ref[row : row + 1, :]
                    top = jnp.maximum(top, old)
                    factors.append(jnp.exp2((old - top) * scale))
                weight = jnp.exp2((part - top) * scale)
                total = jnp.sum(weight, axis=0, keepdims=True)
                if not fresh:
                    total = total + total_ref[row : row + 1, :] * factors[head]
                top_ref[row : row + 1, :] = top
                total_ref[row : row + 1, :] = total
                weights.append(weight.astype(jnp.bfloat16))
            summed = dot(values[columns], jnp.concatenate(weights, axis=1))
            for head in range(per):
                rows = slice((group * per + head) * HD, (group * per + head + 1) * HD)
                piece = summed[head * HD : (head + 1) * HD, head * tok : (head + 1) * tok]
                if not fresh:
                    piece = piece + sum_ref[rows, :] * factors[head]
                sum_ref[rows, :] = piece

    for place, (k, unused_query, pair_ref, first) in enumerate(tasks):
        block = ids_ref[reps + place]
        begin = begin_ref[k : k + 1, :]
        tok = begin.shape[1]
        if first and k == 0:
            fold(place, k, pair_ref, block, begin, True)
            continue
        if first:
            top_ref, total_ref, sum_ref = states[k]
            top_ref[...] = jnp.full(top_ref.shape, masked_score, jnp.float32)
            total_ref[...] = jnp.zeros(total_ref.shape, jnp.float32)
            sum_ref[...] = jnp.zeros(sum_ref.shape, jnp.float32)

        @pl.when((block >= 0) & ((block + 1) * tok > lowest[k]))
        def unused(place=place, k=k, pair_ref=pair_ref, block=block, begin=begin):
            fold(place, k, pair_ref, block, begin, False)


def attend_kernel(plan, reps, counts, packed, ids_ref, begin_ref, *refs):
    ks = sorted({k for k, unused_pair, unused_first in plan})
    old_ks = [k for k in ks if not any(first for j, unused_pair, first in plan if j == k)]
    query_refs, refs = dict(zip(ks, refs)), refs[len(ks) :]
    pair_refs = [refs[2 * place : 2 * place + 2] for place in range(counts)]
    refs = refs[2 * counts :]
    old_refs, refs = refs[: 3 * len(old_ks)], refs[3 * len(old_ks) :]
    bias_ref, refs = refs[-1], refs[:-1]
    packed_refs, state_refs = (refs[: len(ks)], refs[len(ks) :]) if packed else ((), refs)
    states = {k: state_refs[3 * place : 3 * place + 3] for place, k in enumerate(ks)}
    for place, k in enumerate(old_ks):
        for old_ref, new_ref in zip(old_refs[3 * place : 3 * place + 3], states[k]):
            new_ref[...] = old_ref[...]
    tasks = [(k, query_refs[k], pair_refs[pair], first) for k, pair, first in plan]
    fold_blocks(ids_ref, begin_ref, tasks, reps, states, bias_ref)
    for k, packed_ref in zip(ks, packed_refs):
        top_ref, total_ref, sum_ref = states[k]
        heads, width = top_ref.shape[0], sum_ref.shape[0]
        packed_ref[0:width, :] = sum_ref[...].astype(jnp.bfloat16)
        first = width
        for ref, pieces in ((top_ref, 3), (total_ref, 2)):
            rest = ref[...]
            for unused in range(pieces):
                piece = rest.astype(jnp.bfloat16)
                packed_ref[first : first + heads, :] = piece
                rest = rest - piece.astype(jnp.float32)
                first += heads


def mix_kernel(expert_count, hot_capacity, own_ref, extended_ref, residual_ref, proj_ref, *refs):
    top_ref, total_ref, sum_ref = refs[0:3]
    mixed_ref, sent_refs = refs[-1 - expert_count], refs[len(refs) - expert_count :]
    packed_refs = refs[3 : -1 - expert_count]
    tok, width = mixed_ref.shape
    heads = top_ref.shape[0]
    scale = math.log2(math.e) / math.sqrt(HD)
    tops, totals = [top_ref[...]], [total_ref[...]]
    for packed_ref in packed_refs:
        pieces = [
            packed_ref[width + place * heads : width + (place + 1) * heads, :].astype(jnp.float32)
            for place in range(5)
        ]
        tops.append((pieces[0] + pieces[1]) + pieces[2])
        totals.append(pieces[3] + pieces[4])
    top = functools.reduce(jnp.maximum, tops)
    factors = [jnp.exp2((one - top) * scale) for one in tops]
    total = sum(one * factor for one, factor in zip(totals, factors))
    factors = [factor / total for factor in factors]
    pieces = []
    for head in range(heads):
        rows = slice(head * HD, (head + 1) * HD)
        piece = sum_ref[rows, :] * factors[0][head : head + 1, :]
        for packed_ref, factor in zip(packed_refs, factors[1:]):
            piece = piece + packed_ref[rows, :].astype(jnp.float32) * factor[head : head + 1, :]
        pieces.append(piece.astype(jnp.bfloat16))
    attended = jnp.concatenate(pieces, axis=0).T
    mixed = (residual_ref[...].astype(jnp.float32) + dot(attended, proj_ref[...])).astype(
        jnp.bfloat16
    )
    mixed_ref[...] = mixed
    mixed_f = mixed.astype(jnp.float32)
    inv_rms = lax.rsqrt(jnp.mean(mixed_f * mixed_f, axis=1, keepdims=True) + norm_eps)
    normed = (mixed_f * inv_rms).astype(jnp.bfloat16)
    placed = slot_matrix(chosen_of(extended_ref, tok), own_ref[0], len(sent_refs), hot_capacity)
    rows = dot(placed, normed).astype(jnp.bfloat16)
    for k, sent_ref in enumerate(sent_refs):
        sent_ref[...] = rows[k * hot_capacity : (k + 1) * hot_capacity]


def expert_kernel(
    reps,
    rep_list,
    sources,
    tok,
    strip,
    counts,
    own_ref,
    part_ref,
    up_ref,
    down_ref,
    extended_ref,
    *refs,
):
    row_count, grad_count = counts
    row_refs, refs = refs[:row_count], refs[row_count:]
    per_rep = row_count // len(rep_list)
    grad_refs, refs = refs[:grad_count], refs[grad_count:]
    own_rows = rep_list[0] == 0
    held_ref, refs = refs[-1], refs[:-1]
    if own_rows:
        up_old, down_old, activated_ref, pre_grad_ref = refs[:4]
        term_refs, kept_ref = refs[4:-1], refs[-1]
    else:
        up_acc, down_acc = refs
    total_grads = sum(ref.shape[0] for ref in grad_refs)
    capacity = total_grads // (sources * reps)
    count = sources * capacity
    parts = part_ref.shape[0]
    up = up_ref[...]
    down = down_ref[...]
    router = router_of(extended_ref, tok, sources)
    expert_lane = lax.broadcasted_iota(jnp.int32, (count, router.shape[0]), 1) == own_ref[0]

    def strips(rows, place):
        held_ref[place] = rows.T
        taken = []
        for k in range(parts):
            first = pl.multiple_of(part_ref[k] * strip, strip)
            taken.append(held_ref[place, pl.ds(first, strip), :])
        return jnp.concatenate(taken, axis=0)

    up_term = down_term = None
    for place, rep in enumerate(rep_list):
        rows = chunk_rows(
            row_refs[place * per_rep : (place + 1) * per_rep], sources, 0, capacity
        )
        grads = chunk_rows(grad_refs, sources, rep * capacity, (rep + 1) * capacity)
        pre = dot(rows, up)
        sigmoid_pre = jax.nn.sigmoid(pre)
        activated = (pre * sigmoid_pre).astype(jnp.bfloat16)
        logits = dot(rows, router, NT)
        gate = jax.nn.sigmoid(
            jnp.sum(jnp.where(expert_lane, logits, 0.0), axis=1, keepdims=True)
        )
        scaled = (gate * grads.astype(jnp.float32)).astype(jnp.bfloat16)
        act_grad = dot(scaled, down, NT)
        pre_grad = (act_grad * sigmoid_pre * (1.0 + pre * (1.0 - sigmoid_pre))).astype(
            jnp.bfloat16
        )
        if own_rows:
            activated_ref[...] = activated
            pre_grad_ref[...] = pre_grad
        more_up = dot(strips(rows, 2 * place), pre_grad)
        more_down = dot(strips(activated, 2 * place + 1), scaled)
        up_term = more_up if up_term is None else up_term + more_up
        down_term = more_down if down_term is None else down_term + more_down
    if not own_rows:
        up_acc[...] = up_term
        down_acc[...] = down_term
        return
    up_term = up_term + up_old[...]
    down_term = down_term + down_old[...]
    for k, ref in enumerate((kept_ref, *term_refs)):
        rows = slice(k * strip, (k + 1) * strip)
        ref[0] = up_term[rows].astype(ref.dtype)
        ref[1] = down_term[rows].astype(ref.dtype)


def back_kernel(sources, up_ref, down_ref, activated_ref, pre_grad_ref, *back_refs):
    capacity = activated_ref.shape[0] // sources
    produced = dot(activated_ref[...], down_ref[...]).astype(jnp.bfloat16)
    token_grad = dot(pre_grad_ref[...], up_ref[...], NT).astype(jnp.bfloat16)
    for k, back_ref in enumerate(back_refs):
        rows = slice(k * capacity, (k + 1) * capacity)
        back_ref[0:capacity] = produced[rows]
        back_ref[capacity : 2 * capacity] = token_grad[rows]


def prepare_kernel(
    hot_capacity,
    expert_count,
    own_ref,
    mixed_ref,
    extended_ref,
    placed_ref,
    factors_ref,
    router_cols_ref,
):
    tok = mixed_ref.shape[0]
    choice = chosen_of(extended_ref, tok)
    placed = slot_matrix(choice, own_ref[0], expert_count, hot_capacity)
    placed_ref[...] = placed.T
    router = router_of(extended_ref, tok, expert_count)
    mixed_f = mixed_ref[...].astype(jnp.float32)
    inv_rms = lax.rsqrt(jnp.mean(mixed_f * mixed_f, axis=1, keepdims=True) + norm_eps)
    normed = (mixed_f * inv_rms).astype(jnp.bfloat16)
    one_hot = lax.broadcasted_iota(jnp.int32, (expert_count, tok), 0) == choice
    logits = dot(router, normed, NT)
    logit_row = jnp.sum(jnp.where(one_hot, logits, 0.0), axis=0, keepdims=True)
    gate = jax.nn.sigmoid(jnp.broadcast_to(logit_row, (8, tok)).T[:, 0:1])
    lane = lax.broadcasted_iota(jnp.int32, factors_ref.shape, 1)
    factors_ref[...] = jnp.where(lane == 0, inv_rms, gate)
    router_cols_ref[...] = dot(one_hot.astype(jnp.float32).astype(jnp.bfloat16), router, TN)


def finish_kernel(
    hot_capacity,
    parts,
    placed_ref,
    factors_ref,
    router_cols_ref,
    mixed_ref,
    extended_ref,
    *refs,
):
    refs, (layer_ref, grad_mixed_ref, *share_refs) = refs[:-4], refs[-4:]
    (kept_ref, *term_refs), back_refs = refs[:parts], refs[parts:][::-1]
    for kind, share_ref in enumerate(share_refs):
        total = kept_ref[kind]
        for ref in term_refs:
            total = total + ref[kind].astype(jnp.float32)
        share_ref[...] = total
    tok = mixed_ref.shape[0]
    mixed_f = mixed_ref[...].astype(jnp.float32)
    inv_rms = factors_ref[:, 0:1]
    gate = factors_ref[:, 1:2]
    pair = 2 * hot_capacity
    chunks = [
        ref[first : first + pair] for ref in back_refs for first in range(0, ref.shape[0], pair)
    ]
    results = jnp.concatenate([chunk[:hot_capacity] for chunk in chunks], axis=0)
    grads = jnp.concatenate([chunk[hot_capacity:] for chunk in chunks], axis=0)
    placed = placed_ref[...]
    result_f = dot(placed, results)
    normed_grad = dot(placed, grads)
    grad_f = extended_ref[0:tok, :].astype(jnp.float32)
    layer_ref[...] = (mixed_f + gate * result_f).astype(jnp.bfloat16)
    gate_grad = jnp.sum(grad_f * result_f, axis=1, keepdims=True)
    logit_grad = gate_grad * gate * (1.0 - gate)
    total_grad = normed_grad + logit_grad * router_cols_ref[...]
    mean_term = jnp.mean(total_grad * mixed_f, axis=1, keepdims=True)
    input_grad = inv_rms * total_grad - mixed_f * inv_rms * inv_rms * inv_rms * mean_term
    grad_mixed_ref[...] = (grad_f + input_grad).astype(jnp.bfloat16)


def shape(dims, dtype=jnp.bfloat16):
    return jax.ShapeDtypeStruct(dims, dtype)


SMEM = pl.BlockSpec(memory_space=pltpu.SMEM)
VMEM = pl.BlockSpec(memory_space=pltpu.VMEM)
HBM = pl.BlockSpec(memory_space=pltpu.HBM)


def call(body, out_shape, specs, scratch=(), cost=0.5):
    return pl.pallas_call(
        body,
        cost_estimate=pl.CostEstimate(
            flops=int(cost * 1e9), bytes_accessed=0, transcendentals=0
        ),
        out_shape=out_shape,
        in_specs=specs,
        out_specs=jax.tree.map(lambda unused: VMEM, out_shape),
        scratch_shapes=list(scratch),
        compiler_params=pltpu.CompilerParams(vmem_limit_bytes=VMEM_LIMIT),
    )


def local(
    seq_count,
    expert_count,
    rep_count,
    query_rows,
    key_rows,
    value_rows,
    doc_lengths,
    residual,
    out_proj,
    router,
    expert_choice,
    weight_in,
    weight_out,
    grad_out,
):
    tok, width = query_rows.shape[1:]
    hidden = weight_in.shape[2]
    heads = width // HD
    experts = Group(("expert",), (expert_count,))
    reps = Group(("rep",), (rep_count,))
    owners = Group(("expert", "rep"), (expert_count, rep_count))
    parts = Group(("seq",), (seq_count,))
    strip = width // (seq_count * rep_count)
    capacity = max(2, (3 * tok + 2 * expert_count - 1) // (2 * expert_count))
    hot_capacity = min(4 * capacity, tok // 2)
    choice = expert_choice.reshape(1, tok)
    seq_index = lax.axis_index("seq")
    rep_index = lax.axis_index("rep")
    rank = seq_index * rep_count + rep_index
    own = jnp.stack([lax.axis_index("expert")]).astype(jnp.int32)
    part_to = jnp.stack(
        [parts.target(seq_index, k) * rep_count + rep_index for k in range(seq_count)]
    ).astype(jnp.int32)

    def forward(array):
        return lax.ppermute(array, "seq", [(i, (i + 1) % seq_count) for i in range(seq_count)])

    reach = (seq_count + 1) // 2
    longest = (seq_count * rep_count + 1) // 2
    query_ranks = [
        seq_index * rep_count + reps.source(rep_index, k) for k in range(rep_count)
    ]

    def task_ids(plan, steps):
        ids = list(query_ranks)
        for k, pair, unused_first in plan:
            block = rank - steps[pair] * rep_count
            behind = query_ranks[k] - block
            ids.append(jnp.where((block >= 0) & (behind >= 0) & (behind <= longest), block, -1))
        return jnp.stack(ids).astype(jnp.int32)

    state_shapes = [
        shape((heads, tok), jnp.float32),
        shape((heads, tok), jnp.float32),
        shape((width, tok), jnp.float32),
    ]
    tail = 16 + -(-expert_count // 16) * 16
    extended, begin = call(
        extend_kernel,
        [shape((tok + tail, width)), shape((rep_count, tok), jnp.int32)],
        [SMEM, SMEM] + [VMEM] * 3,
    )(
        jnp.stack(query_ranks).astype(jnp.int32), doc_lengths, choice, router.T, grad_out[0]
    )

    def attend(plan, pairs, steps, queries, states, packed, cost):
        ks = sorted({k for k, unused_pair, unused_first in plan})
        old = [one for k in ks if k in states for one in states[k]]
        state_out = state_shapes * len(ks)
        if packed:
            out_shape = [shape((width + 5 * heads, tok))] * len(ks)
            scratch = [pltpu.VMEM(one.shape, one.dtype) for one in state_out]
        else:
            out_shape, scratch = state_out, []
        outs = call(
            functools.partial(
                attend_kernel, plan, rep_count, len(pairs), packed
            ),
            out_shape,
            [SMEM] + [VMEM] * (1 + len(ks) + 2 * len(pairs) + len(old)),
            scratch + [pltpu.VMEM((len(plan), tok, tok), jnp.float32)],
            cost=cost,
        )(task_ids(plan, steps), begin, *[queries[k] for k in ks], *[one for both in pairs for one in both], *old)
        if packed:
            return dict(zip(ks, outs))
        return {k: list(outs[3 * place : 3 * place + 3]) for place, k in enumerate(ks)}

    others = range(1, rep_count)
    lines = [(key_rows[0], value_rows[0])]
    lines.append(tuple(forward(one) for one in lines[0]))
    queries = reps.exchange([query_rows[0]] * rep_count)
    extendeds = reps.exchange([extended] * rep_count)
    states = attend(((0, 0, True),), lines[:1], [0], queries, {}, False, 2.0)
    ahead, *states[0] = lax.optimization_barrier((lines[1][0], *states[0]))
    lines[1] = (ahead, lines[1][1])
    for unused in range(1, reach):
        lines.append(tuple(forward(one) for one in lines[-1]))
    middle = tuple((0, step, False) for step in range(1, reach)) + tuple(
        (k, step, step == 0) for k in others for step in range(reach)
    )
    states = attend(middle, lines[:-1], list(range(reach)), queries, states, False, 4.0)
    partial = attend(
        tuple((k, 0, False) for k in others), lines[-1:], [reach], queries, states, True, 1.5
    )
    partial[1], *extendeds[1:] = lax.optimization_barrier((partial[1], *extendeds[1:]))
    returned = reps.exchange([None] + [partial[k] for k in others], inverse=True)[1:]
    states = attend(((0, 0, False),), lines[-1:], [reach], queries, states, False, 1.5)
    sent_grads = call(
        functools.partial(dispatch_kernel, rep_count, tok, hot_capacity),
        [shape((rep_count * hot_capacity, width))] * expert_count,
        [SMEM] + [VMEM] * rep_count,
    )(own, *extendeds)
    got_grads = merged(experts.exchange(sent_grads), MOST_PERMUTES)

    mixed, *sent_rows = call(
        functools.partial(mix_kernel, expert_count, hot_capacity),
        [shape((tok, width))] + [shape((hot_capacity, width))] * expert_count,
        [SMEM] + [VMEM] * (6 + len(returned)),
        cost=2.0,
    )(own, extendeds[0], residual[0], out_proj, *states[0], *returned)
    arrived = owners.exchange([sent_rows[k // rep_count] for k in range(owners.count)])
    got_rows = merged(arrived[0::rep_count], MOST_PERMUTES)
    got_more = [
        one for k in others for one in merged(arrived[k::rep_count], MOST_PERMUTES)
    ]

    def expert_call(rep_list, rows, out_shape, extra):
        return call(
            functools.partial(
                expert_kernel,
                rep_count,
                rep_list,
                expert_count,
                tok,
                strip,
                (len(rows), len(got_grads)),
            ),
            out_shape,
            [SMEM, SMEM] + [VMEM] * (3 + len(rows) + len(got_grads) + len(extra)),
            [pltpu.VMEM((2 * len(rep_list), width, expert_count * hot_capacity), jnp.bfloat16)],
            cost=2.0,
        )(own, part_to, weight_in[0], weight_out[0], extendeds[0], *rows, *got_grads, *extra)

    slots = expert_count * hot_capacity
    sums = expert_call(
        tuple(others),
        got_more,
        [
            shape((seq_count * strip, hidden), jnp.float32),
            shape((seq_count * strip, width), jnp.float32),
        ],
        [],
    )
    activated, pre_grad, *terms, kept = expert_call(
        (0,),
        got_rows,
        [shape((slots, hidden))] * 2
        + [shape((2, strip, hidden))] * (seq_count - 1)
        + [shape((2, strip, hidden), jnp.float32)],
        list(sums),
    )
    got_terms = parts.exchange([None] + terms)[1:]
    activated, mixed, kept = lax.optimization_barrier((activated, mixed, kept))
    back = call(
        functools.partial(back_kernel, expert_count),
        [shape((2 * hot_capacity, width))] * expert_count,
        [VMEM] * 4,
        cost=1.0,
    )(weight_in[0], weight_out[0], activated, pre_grad)
    got_back = merged(experts.exchange(back, inverse=True), MOST_PERMUTES)
    prepared = call(
        functools.partial(prepare_kernel, hot_capacity, expert_count),
        [
            shape((tok, slots)),
            shape((tok, 128), jnp.float32),
            shape((tok, width), jnp.float32),
        ],
        [SMEM, VMEM, VMEM],
        cost=1.0,
    )(own, mixed, extended)
    layer_out, grad_mixed, share_in, share_out = call(
        functools.partial(finish_kernel, hot_capacity, seq_count),
        [
            shape((tok, width)),
            shape((tok, width)),
            shape((strip, hidden), jnp.float32),
            shape((strip, width), jnp.float32),
        ],
        [VMEM] * (5 + seq_count + len(got_back)),
        cost=1.0,
    )(*prepared, mixed, extended, kept, *got_terms[::-1], *got_back[::-1])
    return (layer_out[None], grad_mixed[None], share_in[None], share_out[None])


def solution(mesh):
    rows = P("expert", ("seq", "rep"), None)
    in_specs = (
        rows,
        rows,
        rows,
        P("expert", None),
        rows,
        P(),
        P(),
        rows,
        P("expert", None, None),
        P("expert", None, None),
        rows,
    )
    body = functools.partial(
        local, mesh.shape["seq"], mesh.shape["expert"], mesh.shape["rep"]
    )
    return jax.shard_map(
        body, mesh=mesh, in_specs=in_specs, out_specs=(rows, rows, rows, rows), check_vma=False
    )
```

```python
import functools
import math

import jax
import jax.numpy as jnp
from jax import lax
from jax.experimental import pallas as pl
from jax.experimental.pallas import tpu as pltpu
from jax.sharding import PartitionSpec as P

HD = 32
norm_eps = 1e-06
masked_score = -1e30
VMEM_LIMIT = 48 * 1024 * 1024
MOST_PERMUTES = 16
NT = (((1,), (1,)), ((), ()))
TN = (((0,), (0,)), ((), ()))


def dot(a, b, dims=None):
    if dims is None:
        return jnp.dot(a, b, preferred_element_type=jnp.float32)
    return lax.dot_general(a, b, dims, preferred_element_type=jnp.float32)


def away(index, offset, size):
    if size & (size - 1) == 0:
        return index ^ offset
    return (index + offset) % size


def back_from(index, offset, size):
    if size & (size - 1) == 0:
        return index ^ offset
    return (index - offset + size) % size


class Group:
    def __init__(self, axes, sizes):
        self.axes, self.sizes = tuple(axes), tuple(sizes)
        self.count = math.prod(sizes)

    def split(self, flat):
        coords = []
        for size in reversed(self.sizes):
            coords.append(flat % size)
            flat = flat // size
        return coords[::-1]

    def moved(self, flat, offset, step):
        place = 0
        for coord, part, size in zip(self.split(flat), self.split(offset), self.sizes):
            place = place * size + step(coord, part, size)
        return place

    def target(self, flat, offset):
        return self.moved(flat, offset, away)

    def source(self, flat, offset):
        return self.moved(flat, offset, back_from)

    def exchange(self, chunks, inverse=False):
        to, start = (self.source, self.target) if inverse else (self.target, self.source)
        if self.count <= MOST_PERMUTES:
            order = sorted(range(1, self.count), key=lambda k: -k)
            got = {0: chunks[0]}
            for k in order:
                pairs = [(i, to(i, k)) for i in range(self.count)]
                got[k] = lax.ppermute(chunks[k], self.axes, pairs)
            return [got[k] for k in range(self.count)]
        me = lax.axis_index(self.axes)
        steps = jnp.arange(self.count, dtype=jnp.int32)
        sent_to = jax.vmap(lambda k: to(me, k))(steps)
        placed = jnp.zeros((self.count,), jnp.int32).at[sent_to].set(steps)
        stacked = jnp.stack(chunks)[placed]
        got = lax.all_to_all(stacked, self.axes, split_axis=0, concat_axis=0, tiled=True)
        came_from = jax.vmap(lambda k: start(me, k))(steps)
        ordered = got[came_from]
        return [ordered[k] for k in range(self.count)]


def merged(chunks, most):
    if len(chunks) <= most:
        return list(chunks)
    return [jnp.concatenate(chunks, axis=0)]


def chunk_rows(refs, count, low, high):
    size = sum(ref.shape[0] for ref in refs) // count
    parts = []
    for chunk in range(count):
        ref, first = (refs[chunk], 0) if len(refs) == count else (refs[0], chunk * size)
        parts.append(ref[first + low : first + high, :])
    return parts[0] if count == 1 else jnp.concatenate(parts, axis=0)


def slot_matrix(choice, own, expert_count, hot_capacity):
    tok = choice.shape[1]
    offset = back_from(choice, own, expert_count)
    one_hot = lax.broadcasted_iota(jnp.int32, (expert_count, tok), 0) == offset
    hits = one_hot.astype(jnp.float32).astype(jnp.bfloat16)
    earlier = lax.broadcasted_iota(jnp.int32, (tok, tok), 0) <= lax.broadcasted_iota(
        jnp.int32, (tok, tok), 1
    )
    counted = dot(hits, earlier.astype(jnp.float32).astype(jnp.bfloat16))
    rank = jnp.sum(jnp.where(one_hot, counted, 0.0), axis=0, keepdims=True) - 1.0
    slots = offset * hot_capacity + rank.astype(jnp.int32)
    rows = lax.broadcasted_iota(jnp.int32, (expert_count * hot_capacity, tok), 0)
    return (rows == slots).astype(jnp.float32).astype(jnp.bfloat16)


def extend_kernel(
    ranks_ref, lengths_ref, choice_ref, router_ref, grad_ref, extended_ref, begin_ref
):
    tok, width = grad_ref.shape
    extended_ref[0:tok, :] = grad_ref[...]
    chosen = jnp.broadcast_to(choice_ref[...].astype(jnp.float32), (16, tok))
    extended_ref[tok : tok + 16, 0:tok] = chosen.astype(jnp.bfloat16)
    extended_ref[tok : tok + 16, tok:width] = jnp.zeros((16, width - tok), jnp.bfloat16)
    routed = router_ref[...].astype(jnp.float32)
    spare = extended_ref.shape[0] - tok - 16 - routed.shape[0]
    if spare:
        routed = jnp.concatenate([routed, jnp.zeros((spare, width), jnp.float32)], axis=0)
    extended_ref[tok + 16 :, :] = routed.astype(jnp.bfloat16)
    for k in range(begin_ref.shape[0]):
        position = ranks_ref[k] * tok + lax.broadcasted_iota(jnp.int32, (1, tok), 1)
        begin = jnp.zeros((1, tok), jnp.int32)
        bound = jnp.int32(0)
        for doc in range(lengths_ref.shape[1] - 1):
            bound = bound + lengths_ref[0, doc]
            begin = jnp.maximum(begin, jnp.where(position >= bound, bound, 0))
        begin_ref[k : k + 1, :] = begin


def chosen_of(extended_ref, tok):
    return extended_ref[tok : tok + 16, 0:tok].astype(jnp.float32)[0:1].astype(jnp.int32)


def router_of(extended_ref, tok, expert_count):
    whole = extended_ref[tok + 16 :, :].astype(jnp.float32)
    return whole[0:expert_count].astype(jnp.bfloat16)


def dispatch_kernel(reps, tok, hot_capacity, own_ref, *refs):
    extended_refs, sent_refs = refs[:reps], refs[reps:]
    for rep in range(reps):
        choice = chosen_of(extended_refs[rep], tok)
        placed = slot_matrix(choice, own_ref[0], len(sent_refs), hot_capacity)
        rows = dot(placed, extended_refs[rep][0:tok, :]).astype(jnp.bfloat16)
        for k, sent_ref in enumerate(sent_refs):
            sent_ref[rep * hot_capacity : (rep + 1) * hot_capacity] = rows[
                k * hot_capacity : (k + 1) * hot_capacity
            ]


def fold_blocks(ids_ref, begin_ref, tasks, reps, states, bias_ref):
    lanes = 128
    per = lanes // HD
    scale = math.log2(math.e) / math.sqrt(HD)
    spreads = {}
    lowest = {}
    for k, query_ref, unused_pair, unused_first in tasks:
        if k in spreads:
            continue
        lowest[k] = jnp.min(begin_ref[k : k + 1, :])
        tok = begin_ref.shape[1]
        turned = query_ref[...].T
        head_of_row = lax.broadcasted_iota(jnp.int32, (lanes, tok), 0) // HD
        spreads[k] = []
        for group in range(turned.shape[0] // lanes):
            part = turned[group * lanes : (group + 1) * lanes]
            spreads[k].append(
                jnp.concatenate(
                    [
                        jnp.where(head_of_row == head, part, jnp.zeros_like(part))
                        for head in range(per)
                    ],
                    axis=1,
                )
            )

    def fold(place, k, pair_ref, block, begin, fresh):
        top_ref, total_ref, sum_ref = states[k]
        tok = begin.shape[1]
        position = ids_ref[k] * tok + lax.broadcasted_iota(jnp.int32, (1, tok), 1)
        key_position = block * tok + lax.broadcasted_iota(jnp.int32, (tok, tok), 0)
        visible = (key_position >= begin) & (key_position <= position)
        bias_ref[place] = jnp.where(visible, 0.0, masked_score)
        bias = bias_ref[place]
        key_ref, value_ref = pair_ref
        values = value_ref[...].T
        for group, spread in enumerate(spreads[k]):
            columns = slice(group * lanes, (group + 1) * lanes)
            scores = dot(key_ref[:, columns], spread)
            weights, factors = [], []
            for head in range(per):
                row = group * per + head
                part = scores[:, head * tok : (head + 1) * tok] + bias
                top = jnp.max(part, axis=0, keepdims=True)
                if not fresh:
                    old = top_ref[row : row + 1, :]
                    top = jnp.maximum(top, old)
                    factors.append(jnp.exp2((old - top) * scale))
                weight = jnp.exp2((part - top) * scale)
                total = jnp.sum(weight, axis=0, keepdims=True)
                if not fresh:
                    total = total + total_ref[row : row + 1, :] * factors[head]
                top_ref[row : row + 1, :] = top
                total_ref[row : row + 1, :] = total
                weights.append(weight.astype(jnp.bfloat16))
            summed = dot(values[columns], jnp.concatenate(weights, axis=1))
            for head in range(per):
                rows = slice((group * per + head) * HD, (group * per + head + 1) * HD)
                piece = summed[head * HD : (head + 1) * HD, head * tok : (head + 1) * tok]
                if not fresh:
                    piece = piece + sum_ref[rows, :] * factors[head]
                sum_ref[rows, :] = piece

    for place, (k, unused_query, pair_ref, first) in enumerate(tasks):
        block = ids_ref[reps + place]
        begin = begin_ref[k : k + 1, :]
        tok = begin.shape[1]
        if first and k == 0:
            fold(place, k, pair_ref, block, begin, True)
            continue
        if first:
            top_ref, total_ref, sum_ref = states[k]
            top_ref[...] = jnp.full(top_ref.shape, masked_score, jnp.float32)
            total_ref[...] = jnp.zeros(total_ref.shape, jnp.float32)
            sum_ref[...] = jnp.zeros(sum_ref.shape, jnp.float32)

        @pl.when((block >= 0) & ((block + 1) * tok > lowest[k]))
        def unused(place=place, k=k, pair_ref=pair_ref, block=block, begin=begin):
            fold(place, k, pair_ref, block, begin, False)


def attend_kernel(plan, reps, counts, packed, ids_ref, begin_ref, *refs):
    ks = sorted({k for k, unused_pair, unused_first in plan})
    old_ks = [k for k in ks if not any(first for j, unused_pair, first in plan if j == k)]
    query_refs, refs = dict(zip(ks, refs)), refs[len(ks) :]
    pair_refs = [refs[2 * place : 2 * place + 2] for place in range(counts)]
    refs = refs[2 * counts :]
    old_refs, refs = refs[: 3 * len(old_ks)], refs[3 * len(old_ks) :]
    bias_ref, refs = refs[-1], refs[:-1]
    packed_refs, state_refs = (refs[: len(ks)], refs[len(ks) :]) if packed else ((), refs)
    states = {k: state_refs[3 * place : 3 * place + 3] for place, k in enumerate(ks)}
    for place, k in enumerate(old_ks):
        for old_ref, new_ref in zip(old_refs[3 * place : 3 * place + 3], states[k]):
            new_ref[...] = old_ref[...]
    tasks = [(k, query_refs[k], pair_refs[pair], first) for k, pair, first in plan]
    fold_blocks(ids_ref, begin_ref, tasks, reps, states, bias_ref)
    for k, packed_ref in zip(ks, packed_refs):
        top_ref, total_ref, sum_ref = states[k]
        heads, width = top_ref.shape[0], sum_ref.shape[0]
        packed_ref[0:width, :] = sum_ref[...].astype(jnp.bfloat16)
        first = width
        for ref, pieces in ((top_ref, 3), (total_ref, 2)):
            rest = ref[...]
            for unused in range(pieces):
                piece = rest.astype(jnp.bfloat16)
                packed_ref[first : first + heads, :] = piece
                rest = rest - piece.astype(jnp.float32)
                first += heads


def mix_kernel(expert_count, hot_capacity, own_ref, extended_ref, residual_ref, proj_ref, *refs):
    top_ref, total_ref, sum_ref = refs[0:3]
    mixed_ref, sent_refs = refs[-1 - expert_count], refs[len(refs) - expert_count :]
    packed_refs = refs[3 : -1 - expert_count]
    tok, width = mixed_ref.shape
    heads = top_ref.shape[0]
    scale = math.log2(math.e) / math.sqrt(HD)
    tops, totals = [top_ref[...]], [total_ref[...]]
    for packed_ref in packed_refs:
        pieces = [
            packed_ref[width + place * heads : width + (place + 1) * heads, :].astype(jnp.float32)
            for place in range(5)
        ]
        tops.append((pieces[0] + pieces[1]) + pieces[2])
        totals.append(pieces[3] + pieces[4])
    top = functools.reduce(jnp.maximum, tops)
    factors = [jnp.exp2((one - top) * scale) for one in tops]
    total = sum(one * factor for one, factor in zip(totals, factors))
    factors = [factor / total for factor in factors]
    pieces = []
    for head in range(heads):
        rows = slice(head * HD, (head + 1) * HD)
        piece = sum_ref[rows, :] * factors[0][head : head + 1, :]
        for packed_ref, factor in zip(packed_refs, factors[1:]):
            piece = piece + packed_ref[rows, :].astype(jnp.float32) * factor[head : head + 1, :]
        pieces.append(piece.astype(jnp.bfloat16))
    attended = jnp.concatenate(pieces, axis=0).T
    mixed = (residual_ref[...].astype(jnp.float32) + dot(attended, proj_ref[...])).astype(
        jnp.bfloat16
    )
    mixed_ref[...] = mixed
    mixed_f = mixed.astype(jnp.float32)
    inv_rms = lax.rsqrt(jnp.mean(mixed_f * mixed_f, axis=1, keepdims=True) + norm_eps)
    normed = (mixed_f * inv_rms).astype(jnp.bfloat16)
    placed = slot_matrix(chosen_of(extended_ref, tok), own_ref[0], len(sent_refs), hot_capacity)
    rows = dot(placed, normed).astype(jnp.bfloat16)
    for k, sent_ref in enumerate(sent_refs):
        sent_ref[...] = rows[k * hot_capacity : (k + 1) * hot_capacity]


def grad_plan(parts):
    if parts == 4:
        return [[(0, 0), (1, 0), (1, 2)], [(0, 1), (1, 1), (1, 3)], [(0, 2)], [(0, 3)]]
    return [[(0, 0), (1, 0)]] + [[(0, k), (1, k)] for k in range(1, parts)]


def pair_kernel(kept_ref, near_ref, sent_ref):
    sent_ref[0] = (kept_ref[2] + near_ref[2].astype(jnp.float32)).astype(jnp.bfloat16)


def expert_kernel(
    reps,
    rep_list,
    sources,
    tok,
    strip,
    counts,
    own_ref,
    part_ref,
    up_ref,
    down_ref,
    extended_ref,
    *refs,
):
    row_count, grad_count = counts
    row_refs, refs = refs[:row_count], refs[row_count:]
    per_rep = row_count // len(rep_list)
    grad_refs, refs = refs[:grad_count], refs[grad_count:]
    own_rows = rep_list[0] == 0
    held_ref, refs = refs[-1], refs[:-1]
    if own_rows:
        up_old, down_old, activated_ref, pre_grad_ref = refs[:4]
        term_refs, kept_ref = refs[4:-1], refs[-1]
    else:
        up_acc, down_acc = refs
    total_grads = sum(ref.shape[0] for ref in grad_refs)
    capacity = total_grads // (sources * reps)
    count = sources * capacity
    parts = part_ref.shape[0]
    up = up_ref[...]
    down = down_ref[...]
    router = router_of(extended_ref, tok, sources)
    expert_lane = lax.broadcasted_iota(jnp.int32, (count, router.shape[0]), 1) == own_ref[0]

    def strips(rows, place):
        held_ref[place] = rows.T
        taken = []
        for k in range(parts):
            first = pl.multiple_of(part_ref[k] * strip, strip)
            taken.append(held_ref[place, pl.ds(first, strip), :])
        return jnp.concatenate(taken, axis=0)

    up_term = down_term = None
    for place, rep in enumerate(rep_list):
        rows = chunk_rows(
            row_refs[place * per_rep : (place + 1) * per_rep], sources, 0, capacity
        )
        grads = chunk_rows(grad_refs, sources, rep * capacity, (rep + 1) * capacity)
        pre = dot(rows, up)
        sigmoid_pre = jax.nn.sigmoid(pre)
        activated = (pre * sigmoid_pre).astype(jnp.bfloat16)
        logits = dot(rows, router, NT)
        gate = jax.nn.sigmoid(
            jnp.sum(jnp.where(expert_lane, logits, 0.0), axis=1, keepdims=True)
        )
        scaled = (gate * grads.astype(jnp.float32)).astype(jnp.bfloat16)
        act_grad = dot(scaled, down, NT)
        pre_grad = (act_grad * sigmoid_pre * (1.0 + pre * (1.0 - sigmoid_pre))).astype(
            jnp.bfloat16
        )
        if own_rows:
            activated_ref[...] = activated
            pre_grad_ref[...] = pre_grad
        more_up = dot(strips(rows, 2 * place), pre_grad)
        more_down = dot(strips(activated, 2 * place + 1), scaled)
        up_term = more_up if up_term is None else up_term + more_up
        down_term = more_down if down_term is None else down_term + more_down
    if not own_rows:
        up_acc[...] = up_term
        down_acc[...] = down_term
        return
    up_term = up_term + up_old[...]
    down_term = down_term + down_old[...]
    for ref, entries in zip((kept_ref, *term_refs), grad_plan(parts)):
        for place, (kind, k) in enumerate(entries):
            term = (up_term, down_term)[kind][k * strip : (k + 1) * strip]
            ref[place] = term.astype(ref.dtype)


def back_kernel(sources, up_ref, down_ref, activated_ref, pre_grad_ref, *back_refs):
    capacity = activated_ref.shape[0] // sources
    produced = dot(activated_ref[...], down_ref[...]).astype(jnp.bfloat16)
    token_grad = dot(pre_grad_ref[...], up_ref[...], NT).astype(jnp.bfloat16)
    for k, back_ref in enumerate(back_refs):
        rows = slice(k * capacity, (k + 1) * capacity)
        back_ref[0:capacity] = produced[rows]
        back_ref[capacity : 2 * capacity] = token_grad[rows]


def prepare_kernel(
    hot_capacity,
    expert_count,
    own_ref,
    mixed_ref,
    extended_ref,
    placed_ref,
    factors_ref,
    router_cols_ref,
):
    tok = mixed_ref.shape[0]
    choice = chosen_of(extended_ref, tok)
    placed = slot_matrix(choice, own_ref[0], expert_count, hot_capacity)
    placed_ref[...] = placed.T
    router = router_of(extended_ref, tok, expert_count)
    mixed_f = mixed_ref[...].astype(jnp.float32)
    inv_rms = lax.rsqrt(jnp.mean(mixed_f * mixed_f, axis=1, keepdims=True) + norm_eps)
    normed = (mixed_f * inv_rms).astype(jnp.bfloat16)
    one_hot = lax.broadcasted_iota(jnp.int32, (expert_count, tok), 0) == choice
    logits = dot(router, normed, NT)
    logit_row = jnp.sum(jnp.where(one_hot, logits, 0.0), axis=0, keepdims=True)
    gate = jax.nn.sigmoid(jnp.broadcast_to(logit_row, (8, tok)).T[:, 0:1])
    lane = lax.broadcasted_iota(jnp.int32, factors_ref.shape, 1)
    factors_ref[...] = jnp.where(lane == 0, inv_rms, gate)
    router_cols_ref[...] = dot(one_hot.astype(jnp.float32).astype(jnp.bfloat16), router, TN)


def finish_kernel(
    hot_capacity,
    plan,
    placed_ref,
    factors_ref,
    router_cols_ref,
    mixed_ref,
    extended_ref,
    *refs,
):
    refs, (layer_ref, grad_mixed_ref, *share_refs) = refs[:-4], refs[-4:]
    kept_ref, *refs = refs
    term_refs, back_refs = refs[: len(plan)], refs[len(plan) :][::-1]
    totals = [kept_ref[0], kept_ref[1]]
    for kinds, ref in zip(plan, term_refs):
        for place, kind in enumerate(kinds):
            totals[kind] = totals[kind] + ref[place].astype(jnp.float32)
    for total, share_ref in zip(totals, share_refs):
        share_ref[...] = total
    tok = mixed_ref.shape[0]
    mixed_f = mixed_ref[...].astype(jnp.float32)
    inv_rms = factors_ref[:, 0:1]
    gate = factors_ref[:, 1:2]
    pair = 2 * hot_capacity
    chunks = [
        ref[first : first + pair] for ref in back_refs for first in range(0, ref.shape[0], pair)
    ]
    results = jnp.concatenate([chunk[:hot_capacity] for chunk in chunks], axis=0)
    grads = jnp.concatenate([chunk[hot_capacity:] for chunk in chunks], axis=0)
    placed = placed_ref[...]
    result_f = dot(placed, results)
    normed_grad = dot(placed, grads)
    grad_f = extended_ref[0:tok, :].astype(jnp.float32)
    layer_ref[...] = (mixed_f + gate * result_f).astype(jnp.bfloat16)
    gate_grad = jnp.sum(grad_f * result_f, axis=1, keepdims=True)
    logit_grad = gate_grad * gate * (1.0 - gate)
    total_grad = normed_grad + logit_grad * router_cols_ref[...]
    mean_term = jnp.mean(total_grad * mixed_f, axis=1, keepdims=True)
    input_grad = inv_rms * total_grad - mixed_f * inv_rms * inv_rms * inv_rms * mean_term
    grad_mixed_ref[...] = (grad_f + input_grad).astype(jnp.bfloat16)


def shape(dims, dtype=jnp.bfloat16):
    return jax.ShapeDtypeStruct(dims, dtype)


SMEM = pl.BlockSpec(memory_space=pltpu.SMEM)
VMEM = pl.BlockSpec(memory_space=pltpu.VMEM)
HBM = pl.BlockSpec(memory_space=pltpu.HBM)


def call(body, out_shape, specs, scratch=(), cost=0.5):
    return pl.pallas_call(
        body,
        cost_estimate=pl.CostEstimate(
            flops=int(cost * 1e9), bytes_accessed=0, transcendentals=0
        ),
        out_shape=out_shape,
        in_specs=specs,
        out_specs=jax.tree.map(lambda unused: VMEM, out_shape),
        scratch_shapes=list(scratch),
        compiler_params=pltpu.CompilerParams(vmem_limit_bytes=VMEM_LIMIT),
    )


def local(
    seq_count,
    expert_count,
    rep_count,
    query_rows,
    key_rows,
    value_rows,
    doc_lengths,
    residual,
    out_proj,
    router,
    expert_choice,
    weight_in,
    weight_out,
    grad_out,
):
    tok, width = query_rows.shape[1:]
    hidden = weight_in.shape[2]
    heads = width // HD
    experts = Group(("expert",), (expert_count,))
    reps = Group(("rep",), (rep_count,))
    owners = Group(("expert", "rep"), (expert_count, rep_count))
    parts = Group(("seq",), (seq_count,))
    strip = width // (seq_count * rep_count)
    capacity = max(2, (3 * tok + 2 * expert_count - 1) // (2 * expert_count))
    hot_capacity = min(4 * capacity, tok // 2)
    choice = expert_choice.reshape(1, tok)
    seq_index = lax.axis_index("seq")
    rep_index = lax.axis_index("rep")
    rank = seq_index * rep_count + rep_index
    own = jnp.stack([lax.axis_index("expert")]).astype(jnp.int32)
    part_to = jnp.stack(
        [parts.target(seq_index, k) * rep_count + rep_index for k in range(seq_count)]
    ).astype(jnp.int32)

    def forward(array):
        return lax.ppermute(array, "seq", [(i, (i + 1) % seq_count) for i in range(seq_count)])

    reach = (seq_count + 1) // 2
    longest = (seq_count * rep_count + 1) // 2
    query_ranks = [
        seq_index * rep_count + reps.source(rep_index, k) for k in range(rep_count)
    ]

    def task_ids(plan, steps):
        ids = list(query_ranks)
        for k, pair, unused_first in plan:
            block = rank - steps[pair] * rep_count
            behind = query_ranks[k] - block
            ids.append(jnp.where((block >= 0) & (behind >= 0) & (behind <= longest), block, -1))
        return jnp.stack(ids).astype(jnp.int32)

    state_shapes = [
        shape((heads, tok), jnp.float32),
        shape((heads, tok), jnp.float32),
        shape((width, tok), jnp.float32),
    ]
    tail = 16 + -(-expert_count // 16) * 16
    extended, begin = call(
        extend_kernel,
        [shape((tok + tail, width)), shape((rep_count, tok), jnp.int32)],
        [SMEM, SMEM] + [VMEM] * 3,
    )(
        jnp.stack(query_ranks).astype(jnp.int32), doc_lengths, choice, router.T, grad_out[0]
    )

    def attend(plan, pairs, steps, queries, states, packed, cost):
        ks = sorted({k for k, unused_pair, unused_first in plan})
        old = [one for k in ks if k in states for one in states[k]]
        state_out = state_shapes * len(ks)
        if packed:
            out_shape = [shape((width + 5 * heads, tok))] * len(ks)
            scratch = [pltpu.VMEM(one.shape, one.dtype) for one in state_out]
        else:
            out_shape, scratch = state_out, []
        outs = call(
            functools.partial(
                attend_kernel, plan, rep_count, len(pairs), packed
            ),
            out_shape,
            [SMEM] + [VMEM] * (1 + len(ks) + 2 * len(pairs) + len(old)),
            scratch + [pltpu.VMEM((len(plan), tok, tok), jnp.float32)],
            cost=cost,
        )(task_ids(plan, steps), begin, *[queries[k] for k in ks], *[one for both in pairs for one in both], *old)
        if packed:
            return dict(zip(ks, outs))
        return {k: list(outs[3 * place : 3 * place + 3]) for place, k in enumerate(ks)}

    others = range(1, rep_count)
    lines = [(key_rows[0], value_rows[0])]
    lines.append(tuple(forward(one) for one in lines[0]))
    queries = reps.exchange([query_rows[0]] * rep_count)
    extendeds = reps.exchange([extended] * rep_count)
    states = attend(((0, 0, True),), lines[:1], [0], queries, {}, False, 2.0)
    ahead, *states[0] = lax.optimization_barrier((lines[1][0], *states[0]))
    lines[1] = (ahead, lines[1][1])
    for unused in range(1, reach):
        lines.append(tuple(forward(one) for one in lines[-1]))
    middle = tuple((0, step, False) for step in range(1, reach)) + tuple(
        (k, step, step == 0) for k in others for step in range(reach)
    )
    states = attend(middle, lines[:-1], list(range(reach)), queries, states, False, 4.0)
    partial = attend(
        tuple((k, 0, False) for k in others), lines[-1:], [reach], queries, states, True, 1.5
    )
    partial[1], *extendeds[1:] = lax.optimization_barrier((partial[1], *extendeds[1:]))
    returned = reps.exchange([None] + [partial[k] for k in others], inverse=True)[1:]
    states = attend(((0, 0, False),), lines[-1:], [reach], queries, states, False, 1.5)
    sent_grads = call(
        functools.partial(dispatch_kernel, rep_count, tok, hot_capacity),
        [shape((rep_count * hot_capacity, width))] * expert_count,
        [SMEM] + [VMEM] * rep_count,
    )(own, *extendeds)
    got_grads = merged(experts.exchange(sent_grads), MOST_PERMUTES)

    mixed, *sent_rows = call(
        functools.partial(mix_kernel, expert_count, hot_capacity),
        [shape((tok, width))] + [shape((hot_capacity, width))] * expert_count,
        [SMEM] + [VMEM] * (6 + len(returned)),
        cost=2.0,
    )(own, extendeds[0], residual[0], out_proj, *states[0], *returned)
    arrived = owners.exchange([sent_rows[k // rep_count] for k in range(owners.count)])
    got_rows = merged(arrived[0::rep_count], MOST_PERMUTES)
    got_more = [
        one for k in others for one in merged(arrived[k::rep_count], MOST_PERMUTES)
    ]

    def expert_call(rep_list, rows, out_shape, extra):
        return call(
            functools.partial(
                expert_kernel,
                rep_count,
                rep_list,
                expert_count,
                tok,
                strip,
                (len(rows), len(got_grads)),
            ),
            out_shape,
            [SMEM, SMEM] + [VMEM] * (3 + len(rows) + len(got_grads) + len(extra)),
            [pltpu.VMEM((2 * len(rep_list), width, expert_count * hot_capacity), jnp.bfloat16)],
            cost=2.0,
        )(own, part_to, weight_in[0], weight_out[0], extendeds[0], *rows, *got_grads, *extra)

    slots = expert_count * hot_capacity
    sums = expert_call(
        tuple(others),
        got_more,
        [
            shape((seq_count * strip, hidden), jnp.float32),
            shape((seq_count * strip, width), jnp.float32),
        ],
        [],
    )
    activated, pre_grad, *terms, kept = expert_call(
        (0,),
        got_rows,
        [shape((slots, hidden))] * 2
        + [shape((len(entries), strip, hidden)) for entries in grad_plan(seq_count)[1:]]
        + [shape((len(grad_plan(seq_count)[0]), strip, hidden), jnp.float32)],
        list(sums),
    )
    if seq_count == 4:
        near, *direct = parts.exchange([None] + terms)[1:]
        crossing = call(pair_kernel, shape((1, strip, hidden)), [VMEM, VMEM])(kept, near)
        crossed = lax.ppermute(crossing, "seq", [(i, parts.target(i, 2)) for i in range(4)])
        got_terms = [near, *direct, crossed]
        plan = ((0, 1), (0,), (0,), (1,))
    else:
        got_terms = parts.exchange([None] + terms)[1:]
        plan = ((0, 1),) * len(got_terms)
    activated, mixed, kept = lax.optimization_barrier((activated, mixed, kept))
    back = call(
        functools.partial(back_kernel, expert_count),
        [shape((2 * hot_capacity, width))] * expert_count,
        [VMEM] * 4,
        cost=1.0,
    )(weight_in[0], weight_out[0], activated, pre_grad)
    got_back = merged(experts.exchange(back, inverse=True), MOST_PERMUTES)
    prepared = call(
        functools.partial(prepare_kernel, hot_capacity, expert_count),
        [
            shape((tok, slots)),
            shape((tok, 128), jnp.float32),
            shape((tok, width), jnp.float32),
        ],
        [SMEM, VMEM, VMEM],
        cost=1.0,
    )(own, mixed, extended)
    layer_out, grad_mixed, share_in, share_out = call(
        functools.partial(finish_kernel, hot_capacity, plan),
        [
            shape((tok, width)),
            shape((tok, width)),
            shape((strip, hidden), jnp.float32),
            shape((strip, width), jnp.float32),
        ],
        [VMEM] * (6 + len(got_terms) + len(got_back)),
        cost=1.0,
    )(*prepared, mixed, extended, kept, *got_terms, *got_back[::-1])
    return (layer_out[None], grad_mixed[None], share_in[None], share_out[None])


def solution(mesh):
    rows = P("expert", ("seq", "rep"), None)
    in_specs = (
        rows,
        rows,
        rows,
        P("expert", None),
        rows,
        P(),
        P(),
        rows,
        P("expert", None, None),
        P("expert", None, None),
        rows,
    )
    body = functools.partial(
        local, mesh.shape["seq"], mesh.shape["expert"], mesh.shape["rep"]
    )
    return jax.shard_map(
        body, mesh=mesh, in_specs=in_specs, out_specs=(rows, rows, rows, rows), check_vma=False
    )
```

```python
import functools
import math

import jax
import jax.numpy as jnp
from jax import lax
from jax.experimental import pallas as pl
from jax.experimental.pallas import tpu as pltpu
from jax.sharding import PartitionSpec as P

HD = 32
norm_eps = 1e-06
masked_score = -1e30
VMEM_LIMIT = 48 * 1024 * 1024
MOST_PERMUTES = 16
NT = (((1,), (1,)), ((), ()))
TN = (((0,), (0,)), ((), ()))


def dot(a, b, dims=None):
    if dims is None:
        return jnp.dot(a, b, preferred_element_type=jnp.float32)
    return lax.dot_general(a, b, dims, preferred_element_type=jnp.float32)


def away(index, offset, size):
    if size & (size - 1) == 0:
        return index ^ offset
    return (index + offset) % size


def back_from(index, offset, size):
    if size & (size - 1) == 0:
        return index ^ offset
    return (index - offset + size) % size


class Group:
    def __init__(self, axes, sizes):
        self.axes, self.sizes = tuple(axes), tuple(sizes)
        self.count = math.prod(sizes)

    def split(self, flat):
        coords = []
        for size in reversed(self.sizes):
            coords.append(flat % size)
            flat = flat // size
        return coords[::-1]

    def moved(self, flat, offset, step):
        place = 0
        for coord, part, size in zip(self.split(flat), self.split(offset), self.sizes):
            place = place * size + step(coord, part, size)
        return place

    def target(self, flat, offset):
        return self.moved(flat, offset, away)

    def source(self, flat, offset):
        return self.moved(flat, offset, back_from)

    def exchange(self, chunks, inverse=False):
        to, start = (self.source, self.target) if inverse else (self.target, self.source)
        if self.count <= MOST_PERMUTES:
            order = sorted(range(1, self.count), key=lambda k: -k)
            got = {0: chunks[0]}
            for k in order:
                pairs = [(i, to(i, k)) for i in range(self.count)]
                got[k] = lax.ppermute(chunks[k], self.axes, pairs)
            return [got[k] for k in range(self.count)]
        me = lax.axis_index(self.axes)
        steps = jnp.arange(self.count, dtype=jnp.int32)
        sent_to = jax.vmap(lambda k: to(me, k))(steps)
        placed = jnp.zeros((self.count,), jnp.int32).at[sent_to].set(steps)
        stacked = jnp.stack(chunks)[placed]
        got = lax.all_to_all(stacked, self.axes, split_axis=0, concat_axis=0, tiled=True)
        came_from = jax.vmap(lambda k: start(me, k))(steps)
        ordered = got[came_from]
        return [ordered[k] for k in range(self.count)]


def merged(chunks, most):
    if len(chunks) <= most:
        return list(chunks)
    return [jnp.concatenate(chunks, axis=0)]


def chunk_rows(refs, count, low, high):
    size = sum(ref.shape[0] for ref in refs) // count
    parts = []
    for chunk in range(count):
        ref, first = (refs[chunk], 0) if len(refs) == count else (refs[0], chunk * size)
        parts.append(ref[first + low : first + high, :])
    return parts[0] if count == 1 else jnp.concatenate(parts, axis=0)


def slot_matrix(choice, own, expert_count, hot_capacity):
    tok = choice.shape[1]
    offset = back_from(choice, own, expert_count)
    one_hot = lax.broadcasted_iota(jnp.int32, (expert_count, tok), 0) == offset
    hits = one_hot.astype(jnp.float32).astype(jnp.bfloat16)
    earlier = lax.broadcasted_iota(jnp.int32, (tok, tok), 0) <= lax.broadcasted_iota(
        jnp.int32, (tok, tok), 1
    )
    counted = dot(hits, earlier.astype(jnp.float32).astype(jnp.bfloat16))
    rank = jnp.sum(jnp.where(one_hot, counted, 0.0), axis=0, keepdims=True) - 1.0
    slots = offset * hot_capacity + rank.astype(jnp.int32)
    rows = lax.broadcasted_iota(jnp.int32, (expert_count * hot_capacity, tok), 0)
    return (rows == slots).astype(jnp.float32).astype(jnp.bfloat16)


def extend_kernel(
    ranks_ref, lengths_ref, choice_ref, router_ref, grad_ref, extended_ref, begin_ref
):
    tok, width = grad_ref.shape
    extended_ref[0:tok, :] = grad_ref[...]
    chosen = jnp.broadcast_to(choice_ref[...].astype(jnp.float32), (16, tok))
    extended_ref[tok : tok + 16, 0:tok] = chosen.astype(jnp.bfloat16)
    extended_ref[tok : tok + 16, tok:width] = jnp.zeros((16, width - tok), jnp.bfloat16)
    routed = router_ref[...].astype(jnp.float32)
    spare = extended_ref.shape[0] - tok - 16 - routed.shape[0]
    if spare:
        routed = jnp.concatenate([routed, jnp.zeros((spare, width), jnp.float32)], axis=0)
    extended_ref[tok + 16 :, :] = routed.astype(jnp.bfloat16)
    for k in range(begin_ref.shape[0]):
        position = ranks_ref[k] * tok + lax.broadcasted_iota(jnp.int32, (1, tok), 1)
        begin = jnp.zeros((1, tok), jnp.int32)
        bound = jnp.int32(0)
        for doc in range(lengths_ref.shape[1] - 1):
            bound = bound + lengths_ref[0, doc]
            begin = jnp.maximum(begin, jnp.where(position >= bound, bound, 0))
        begin_ref[k : k + 1, :] = begin


def chosen_of(extended_ref, tok):
    return extended_ref[tok : tok + 16, 0:tok].astype(jnp.float32)[0:1].astype(jnp.int32)


def router_of(extended_ref, tok, expert_count):
    whole = extended_ref[tok + 16 :, :].astype(jnp.float32)
    return whole[0:expert_count].astype(jnp.bfloat16)


def dispatch_kernel(reps, tok, hot_capacity, own_ref, *refs):
    extended_refs, sent_refs = refs[:reps], refs[reps:]
    for rep in range(reps):
        choice = chosen_of(extended_refs[rep], tok)
        placed = slot_matrix(choice, own_ref[0], len(sent_refs), hot_capacity)
        rows = dot(placed, extended_refs[rep][0:tok, :]).astype(jnp.bfloat16)
        for k, sent_ref in enumerate(sent_refs):
            sent_ref[rep * hot_capacity : (rep + 1) * hot_capacity] = rows[
                k * hot_capacity : (k + 1) * hot_capacity
            ]


def fold_blocks(ids_ref, begin_ref, tasks, reps, states, bias_ref):
    lanes = 128
    per = lanes // HD
    scale = math.log2(math.e) / math.sqrt(HD)
    spreads = {}
    lowest = {}
    for k, query_ref, unused_pair, unused_first in tasks:
        if k in spreads:
            continue
        lowest[k] = jnp.min(begin_ref[k : k + 1, :])
        tok = begin_ref.shape[1]
        turned = query_ref[...].T
        head_of_row = lax.broadcasted_iota(jnp.int32, (lanes, tok), 0) // HD
        spreads[k] = []
        for group in range(turned.shape[0] // lanes):
            part = turned[group * lanes : (group + 1) * lanes]
            spreads[k].append(
                jnp.concatenate(
                    [
                        jnp.where(head_of_row == head, part, jnp.zeros_like(part))
                        for head in range(per)
                    ],
                    axis=1,
                )
            )

    def fold(place, k, pair_ref, block, begin, fresh):
        top_ref, total_ref, sum_ref = states[k]
        tok = begin.shape[1]
        position = ids_ref[k] * tok + lax.broadcasted_iota(jnp.int32, (1, tok), 1)
        key_position = block * tok + lax.broadcasted_iota(jnp.int32, (tok, tok), 0)
        visible = (key_position >= begin) & (key_position <= position)
        bias_ref[place] = jnp.where(visible, 0.0, masked_score)
        bias = bias_ref[place]
        key_ref, value_ref = pair_ref
        values = value_ref[...].T
        for group, spread in enumerate(spreads[k]):
            columns = slice(group * lanes, (group + 1) * lanes)
            scores = dot(key_ref[:, columns], spread)
            weights, factors = [], []
            for head in range(per):
                row = group * per + head
                part = scores[:, head * tok : (head + 1) * tok] + bias
                top = jnp.max(part, axis=0, keepdims=True)
                if not fresh:
                    old = top_ref[row : row + 1, :]
                    top = jnp.maximum(top, old)
                    factors.append(jnp.exp2((old - top) * scale))
                weight = jnp.exp2((part - top) * scale)
                total = jnp.sum(weight, axis=0, keepdims=True)
                if not fresh:
                    total = total + total_ref[row : row + 1, :] * factors[head]
                top_ref[row : row + 1, :] = top
                total_ref[row : row + 1, :] = total
                weights.append(weight.astype(jnp.bfloat16))
            summed = dot(values[columns], jnp.concatenate(weights, axis=1))
            for head in range(per):
                rows = slice((group * per + head) * HD, (group * per + head + 1) * HD)
                piece = summed[head * HD : (head + 1) * HD, head * tok : (head + 1) * tok]
                if not fresh:
                    piece = piece + sum_ref[rows, :] * factors[head]
                sum_ref[rows, :] = piece

    for place, (k, unused_query, pair_ref, first) in enumerate(tasks):
        block = ids_ref[reps + place]
        begin = begin_ref[k : k + 1, :]
        tok = begin.shape[1]
        if first and k == 0:
            fold(place, k, pair_ref, block, begin, True)
            continue
        if first:
            top_ref, total_ref, sum_ref = states[k]
            top_ref[...] = jnp.full(top_ref.shape, masked_score, jnp.float32)
            total_ref[...] = jnp.zeros(total_ref.shape, jnp.float32)
            sum_ref[...] = jnp.zeros(sum_ref.shape, jnp.float32)

        @pl.when((block >= 0) & ((block + 1) * tok > lowest[k]))
        def unused(place=place, k=k, pair_ref=pair_ref, block=block, begin=begin):
            fold(place, k, pair_ref, block, begin, False)


def attend_kernel(plan, reps, counts, packed, ahead, ids_ref, begin_ref, *refs):
    ks = sorted({k for k, unused_pair, unused_first in plan})
    old_ks = [k for k in ks if not any(first for j, unused_pair, first in plan if j == k)]
    query_refs, refs = dict(zip(ks, refs)), refs[len(ks) + ahead :]
    pair_refs = [refs[2 * place : 2 * place + 2] for place in range(counts)]
    refs = refs[2 * counts :]
    old_refs, refs = refs[: 3 * len(old_ks)], refs[3 * len(old_ks) :]
    bias_ref, refs = refs[-1], refs[:-1]
    packed_refs, state_refs = (refs[: len(ks)], refs[len(ks) :]) if packed else ((), refs)
    states = {k: state_refs[3 * place : 3 * place + 3] for place, k in enumerate(ks)}
    for place, k in enumerate(old_ks):
        for old_ref, new_ref in zip(old_refs[3 * place : 3 * place + 3], states[k]):
            new_ref[...] = old_ref[...]
    tasks = [(k, query_refs[k], pair_refs[pair], first) for k, pair, first in plan]
    fold_blocks(ids_ref, begin_ref, tasks, reps, states, bias_ref)
    for k, packed_ref in zip(ks, packed_refs):
        top_ref, total_ref, sum_ref = states[k]
        heads, width = top_ref.shape[0], sum_ref.shape[0]
        packed_ref[0:width, :] = sum_ref[...].astype(jnp.bfloat16)
        first = width
        for ref, pieces in ((top_ref, 3), (total_ref, 2)):
            rest = ref[...]
            for unused in range(pieces):
                piece = rest.astype(jnp.bfloat16)
                packed_ref[first : first + heads, :] = piece
                rest = rest - piece.astype(jnp.float32)
                first += heads


def mix_kernel(expert_count, hot_capacity, own_ref, extended_ref, residual_ref, proj_ref, *refs):
    top_ref, total_ref, sum_ref = refs[0:3]
    mixed_ref, sent_refs = refs[-1 - expert_count], refs[len(refs) - expert_count :]
    packed_refs = refs[3 : -1 - expert_count]
    tok, width = mixed_ref.shape
    heads = top_ref.shape[0]
    scale = math.log2(math.e) / math.sqrt(HD)
    tops, totals = [top_ref[...]], [total_ref[...]]
    for packed_ref in packed_refs:
        pieces = [
            packed_ref[width + place * heads : width + (place + 1) * heads, :].astype(jnp.float32)
            for place in range(5)
        ]
        tops.append((pieces[0] + pieces[1]) + pieces[2])
        totals.append(pieces[3] + pieces[4])
    top = functools.reduce(jnp.maximum, tops)
    factors = [jnp.exp2((one - top) * scale) for one in tops]
    total = sum(one * factor for one, factor in zip(totals, factors))
    factors = [factor / total for factor in factors]
    pieces = []
    for head in range(heads):
        rows = slice(head * HD, (head + 1) * HD)
        piece = sum_ref[rows, :] * factors[0][head : head + 1, :]
        for packed_ref, factor in zip(packed_refs, factors[1:]):
            piece = piece + packed_ref[rows, :].astype(jnp.float32) * factor[head : head + 1, :]
        pieces.append(piece.astype(jnp.bfloat16))
    attended = jnp.concatenate(pieces, axis=0).T
    mixed = (residual_ref[...].astype(jnp.float32) + dot(attended, proj_ref[...])).astype(
        jnp.bfloat16
    )
    mixed_ref[...] = mixed
    mixed_f = mixed.astype(jnp.float32)
    inv_rms = lax.rsqrt(jnp.mean(mixed_f * mixed_f, axis=1, keepdims=True) + norm_eps)
    normed = (mixed_f * inv_rms).astype(jnp.bfloat16)
    placed = slot_matrix(chosen_of(extended_ref, tok), own_ref[0], len(sent_refs), hot_capacity)
    rows = dot(placed, normed).astype(jnp.bfloat16)
    for k, sent_ref in enumerate(sent_refs):
        sent_ref[...] = rows[k * hot_capacity : (k + 1) * hot_capacity]


def expert_kernel(
    reps,
    rep_list,
    sources,
    tok,
    strip,
    counts,
    own_ref,
    part_ref,
    up_ref,
    down_ref,
    extended_ref,
    *refs,
):
    row_count, grad_count = counts
    row_refs, refs = refs[:row_count], refs[row_count:]
    per_rep = row_count // len(rep_list)
    grad_refs, refs = refs[:grad_count], refs[grad_count:]
    own_rows = rep_list[0] == 0
    held_ref, refs = refs[-1], refs[:-1]
    if own_rows:
        up_old, down_old, activated_ref, pre_grad_ref = refs[:4]
        term_refs, kept_ref = refs[4:-1], refs[-1]
    else:
        up_acc, down_acc = refs
    total_grads = sum(ref.shape[0] for ref in grad_refs)
    capacity = total_grads // (sources * reps)
    count = sources * capacity
    parts = part_ref.shape[0]
    up = up_ref[...]
    down = down_ref[...]
    router = router_of(extended_ref, tok, sources)
    expert_lane = lax.broadcasted_iota(jnp.int32, (count, router.shape[0]), 1) == own_ref[0]

    def strips(rows, place):
        held_ref[place] = rows.T
        taken = []
        for k in range(parts):
            first = pl.multiple_of(part_ref[k] * strip, strip)
            taken.append(held_ref[place, pl.ds(first, strip), :])
        return jnp.concatenate(taken, axis=0)

    up_term = down_term = None
    for place, rep in enumerate(rep_list):
        rows = chunk_rows(
            row_refs[place * per_rep : (place + 1) * per_rep], sources, 0, capacity
        )
        grads = chunk_rows(grad_refs, sources, rep * capacity, (rep + 1) * capacity)
        pre = dot(rows, up)
        sigmoid_pre = jax.nn.sigmoid(pre)
        activated = (pre * sigmoid_pre).astype(jnp.bfloat16)
        logits = dot(rows, router, NT)
        gate = jax.nn.sigmoid(
            jnp.sum(jnp.where(expert_lane, logits, 0.0), axis=1, keepdims=True)
        )
        scaled = (gate * grads.astype(jnp.float32)).astype(jnp.bfloat16)
        act_grad = dot(scaled, down, NT)
        pre_grad = (act_grad * sigmoid_pre * (1.0 + pre * (1.0 - sigmoid_pre))).astype(
            jnp.bfloat16
        )
        if own_rows:
            activated_ref[...] = activated
            pre_grad_ref[...] = pre_grad
        more_up = dot(strips(rows, 2 * place), pre_grad)
        more_down = dot(strips(activated, 2 * place + 1), scaled)
        up_term = more_up if up_term is None else up_term + more_up
        down_term = more_down if down_term is None else down_term + more_down
    if not own_rows:
        up_acc[...] = up_term
        down_acc[...] = down_term
        return
    up_term = up_term + up_old[...]
    down_term = down_term + down_old[...]
    for k, ref in enumerate((kept_ref, *term_refs)):
        rows = slice(k * strip, (k + 1) * strip)
        ref[0] = up_term[rows].astype(ref.dtype)
        ref[1] = down_term[rows].astype(ref.dtype)


def back_kernel(sources, up_ref, down_ref, activated_ref, pre_grad_ref, *back_refs):
    capacity = activated_ref.shape[0] // sources
    produced = dot(activated_ref[...], down_ref[...]).astype(jnp.bfloat16)
    token_grad = dot(pre_grad_ref[...], up_ref[...], NT).astype(jnp.bfloat16)
    for k, back_ref in enumerate(back_refs):
        rows = slice(k * capacity, (k + 1) * capacity)
        back_ref[0:capacity] = produced[rows]
        back_ref[capacity : 2 * capacity] = token_grad[rows]


def prepare_kernel(
    hot_capacity,
    expert_count,
    own_ref,
    mixed_ref,
    extended_ref,
    placed_ref,
    factors_ref,
    router_cols_ref,
):
    tok = mixed_ref.shape[0]
    choice = chosen_of(extended_ref, tok)
    placed = slot_matrix(choice, own_ref[0], expert_count, hot_capacity)
    placed_ref[...] = placed.T
    router = router_of(extended_ref, tok, expert_count)
    mixed_f = mixed_ref[...].astype(jnp.float32)
    inv_rms = lax.rsqrt(jnp.mean(mixed_f * mixed_f, axis=1, keepdims=True) + norm_eps)
    normed = (mixed_f * inv_rms).astype(jnp.bfloat16)
    one_hot = lax.broadcasted_iota(jnp.int32, (expert_count, tok), 0) == choice
    logits = dot(router, normed, NT)
    logit_row = jnp.sum(jnp.where(one_hot, logits, 0.0), axis=0, keepdims=True)
    gate = jax.nn.sigmoid(jnp.broadcast_to(logit_row, (8, tok)).T[:, 0:1])
    lane = lax.broadcasted_iota(jnp.int32, factors_ref.shape, 1)
    factors_ref[...] = jnp.where(lane == 0, inv_rms, gate)
    router_cols_ref[...] = dot(one_hot.astype(jnp.float32).astype(jnp.bfloat16), router, TN)


def finish_kernel(
    hot_capacity,
    parts,
    placed_ref,
    factors_ref,
    router_cols_ref,
    mixed_ref,
    extended_ref,
    *refs,
):
    refs, (layer_ref, grad_mixed_ref, *share_refs) = refs[:-4], refs[-4:]
    (kept_ref, *term_refs), back_refs = refs[:parts], refs[parts:][::-1]
    for kind, share_ref in enumerate(share_refs):
        total = kept_ref[kind]
        for ref in term_refs:
            total = total + ref[kind].astype(jnp.float32)
        share_ref[...] = total
    tok = mixed_ref.shape[0]
    mixed_f = mixed_ref[...].astype(jnp.float32)
    inv_rms = factors_ref[:, 0:1]
    gate = factors_ref[:, 1:2]
    pair = 2 * hot_capacity
    chunks = [
        ref[first : first + pair] for ref in back_refs for first in range(0, ref.shape[0], pair)
    ]
    results = jnp.concatenate([chunk[:hot_capacity] for chunk in chunks], axis=0)
    grads = jnp.concatenate([chunk[hot_capacity:] for chunk in chunks], axis=0)
    placed = placed_ref[...]
    result_f = dot(placed, results)
    normed_grad = dot(placed, grads)
    grad_f = extended_ref[0:tok, :].astype(jnp.float32)
    layer_ref[...] = (mixed_f + gate * result_f).astype(jnp.bfloat16)
    gate_grad = jnp.sum(grad_f * result_f, axis=1, keepdims=True)
    logit_grad = gate_grad * gate * (1.0 - gate)
    total_grad = normed_grad + logit_grad * router_cols_ref[...]
    mean_term = jnp.mean(total_grad * mixed_f, axis=1, keepdims=True)
    input_grad = inv_rms * total_grad - mixed_f * inv_rms * inv_rms * inv_rms * mean_term
    grad_mixed_ref[...] = (grad_f + input_grad).astype(jnp.bfloat16)


def shape(dims, dtype=jnp.bfloat16):
    return jax.ShapeDtypeStruct(dims, dtype)


SMEM = pl.BlockSpec(memory_space=pltpu.SMEM)
VMEM = pl.BlockSpec(memory_space=pltpu.VMEM)
HBM = pl.BlockSpec(memory_space=pltpu.HBM)


def call(body, out_shape, specs, scratch=(), cost=0.5):
    return pl.pallas_call(
        body,
        cost_estimate=pl.CostEstimate(
            flops=int(cost * 1e9), bytes_accessed=0, transcendentals=0
        ),
        out_shape=out_shape,
        in_specs=specs,
        out_specs=jax.tree.map(lambda unused: VMEM, out_shape),
        scratch_shapes=list(scratch),
        compiler_params=pltpu.CompilerParams(vmem_limit_bytes=VMEM_LIMIT),
    )


def local(
    seq_count,
    expert_count,
    rep_count,
    query_rows,
    key_rows,
    value_rows,
    doc_lengths,
    residual,
    out_proj,
    router,
    expert_choice,
    weight_in,
    weight_out,
    grad_out,
):
    tok, width = query_rows.shape[1:]
    hidden = weight_in.shape[2]
    heads = width // HD
    experts = Group(("expert",), (expert_count,))
    reps = Group(("rep",), (rep_count,))
    owners = Group(("expert", "rep"), (expert_count, rep_count))
    parts = Group(("seq",), (seq_count,))
    strip = width // (seq_count * rep_count)
    capacity = max(2, (3 * tok + 2 * expert_count - 1) // (2 * expert_count))
    hot_capacity = min(4 * capacity, tok // 2)
    choice = expert_choice.reshape(1, tok)
    seq_index = lax.axis_index("seq")
    rep_index = lax.axis_index("rep")
    rank = seq_index * rep_count + rep_index
    own = jnp.stack([lax.axis_index("expert")]).astype(jnp.int32)
    part_to = jnp.stack(
        [parts.target(seq_index, k) * rep_count + rep_index for k in range(seq_count)]
    ).astype(jnp.int32)

    def forward(array):
        return lax.ppermute(array, "seq", [(i, (i + 1) % seq_count) for i in range(seq_count)])

    reach = (seq_count + 1) // 2
    longest = (seq_count * rep_count + 1) // 2
    query_ranks = [
        seq_index * rep_count + reps.source(rep_index, k) for k in range(rep_count)
    ]

    def task_ids(plan, steps):
        ids = list(query_ranks)
        for k, pair, unused_first in plan:
            block = rank - steps[pair] * rep_count
            behind = query_ranks[k] - block
            ids.append(jnp.where((block >= 0) & (behind >= 0) & (behind <= longest), block, -1))
        return jnp.stack(ids).astype(jnp.int32)

    state_shapes = [
        shape((heads, tok), jnp.float32),
        shape((heads, tok), jnp.float32),
        shape((width, tok), jnp.float32),
    ]
    tail = 16 + -(-expert_count // 16) * 16
    extended, begin = call(
        extend_kernel,
        [shape((tok + tail, width)), shape((rep_count, tok), jnp.int32)],
        [SMEM, SMEM] + [VMEM] * 3,
    )(
        jnp.stack(query_ranks).astype(jnp.int32), doc_lengths, choice, router.T, grad_out[0]
    )

    def attend(plan, pairs, steps, queries, states, packed, cost, ahead=()):
        ks = sorted({k for k, unused_pair, unused_first in plan})
        old = [one for k in ks if k in states for one in states[k]]
        state_out = state_shapes * len(ks)
        if packed:
            out_shape = [shape((width + 5 * heads, tok))] * len(ks)
            scratch = [pltpu.VMEM(one.shape, one.dtype) for one in state_out]
        else:
            out_shape, scratch = state_out, []
        outs = call(
            functools.partial(
                attend_kernel, plan, rep_count, len(pairs), packed, len(ahead)
            ),
            out_shape,
            [SMEM] + [VMEM] * (1 + len(ks) + len(ahead) + 2 * len(pairs) + len(old)),
            scratch + [pltpu.VMEM((len(plan), tok, tok), jnp.float32)],
            cost=cost,
        )(task_ids(plan, steps), begin, *[queries[k] for k in ks], *ahead, *[one for both in pairs for one in both], *old)
        if packed:
            return dict(zip(ks, outs))
        return {k: list(outs[3 * place : 3 * place + 3]) for place, k in enumerate(ks)}

    others = range(1, rep_count)
    lines = [(key_rows[0], value_rows[0])]
    lines.append(tuple(forward(one) for one in lines[0]))
    queries = reps.exchange([query_rows[0]] * rep_count)
    extendeds = reps.exchange([extended] * rep_count)
    states = attend(((0, 0, True),), lines[:1], [0], queries, {}, False, 2.0)
    ahead, *states[0] = lax.optimization_barrier((lines[1][0], *states[0]))
    lines[1] = (ahead, lines[1][1])
    for unused in range(1, reach):
        lines.append(tuple(forward(one) for one in lines[-1]))
    middle = tuple((0, step, False) for step in range(1, reach)) + tuple(
        (k, step, step == 0) for k in others for step in range(reach)
    )
    states = attend(middle, lines[:-1], list(range(reach)), queries, states, False, 4.0)
    states[1][0], *extendeds[1:] = lax.optimization_barrier((states[1][0], *extendeds[1:]))
    sent_grads = call(
        functools.partial(dispatch_kernel, rep_count, tok, hot_capacity),
        [shape((rep_count * hot_capacity, width))] * expert_count,
        [SMEM] + [VMEM] * rep_count,
    )(own, *extendeds)
    partial = attend(
        tuple((k, 0, False) for k in others),
        lines[-1:],
        [reach],
        queries,
        states,
        True,
        1.5,
        ahead=sent_grads[:1],
    )
    returned = reps.exchange([None] + [partial[k] for k in others], inverse=True)[1:]
    states = attend(((0, 0, False),), lines[-1:], [reach], queries, states, False, 1.5)
    got_grads = merged(experts.exchange(sent_grads), MOST_PERMUTES)

    mixed, *sent_rows = call(
        functools.partial(mix_kernel, expert_count, hot_capacity),
        [shape((tok, width))] + [shape((hot_capacity, width))] * expert_count,
        [SMEM] + [VMEM] * (6 + len(returned)),
        cost=2.0,
    )(own, extendeds[0], residual[0], out_proj, *states[0], *returned)
    arrived = owners.exchange([sent_rows[k // rep_count] for k in range(owners.count)])
    got_rows = merged(arrived[0::rep_count], MOST_PERMUTES)
    got_more = [
        one for k in others for one in merged(arrived[k::rep_count], MOST_PERMUTES)
    ]

    def expert_call(rep_list, rows, out_shape, extra):
        return call(
            functools.partial(
                expert_kernel,
                rep_count,
                rep_list,
                expert_count,
                tok,
                strip,
                (len(rows), len(got_grads)),
            ),
            out_shape,
            [SMEM, SMEM] + [VMEM] * (3 + len(rows) + len(got_grads) + len(extra)),
            [pltpu.VMEM((2 * len(rep_list), width, expert_count * hot_capacity), jnp.bfloat16)],
            cost=2.0,
        )(own, part_to, weight_in[0], weight_out[0], extendeds[0], *rows, *got_grads, *extra)

    slots = expert_count * hot_capacity
    sums = expert_call(
        tuple(others),
        got_more,
        [
            shape((seq_count * strip, hidden), jnp.float32),
            shape((seq_count * strip, width), jnp.float32),
        ],
        [],
    )
    activated, pre_grad, *terms, kept = expert_call(
        (0,),
        got_rows,
        [shape((slots, hidden))] * 2
        + [shape((2, strip, hidden))] * (seq_count - 1)
        + [shape((2, strip, hidden), jnp.float32)],
        list(sums),
    )
    got_terms = parts.exchange([None] + terms)[1:]
    activated, mixed, kept = lax.optimization_barrier((activated, mixed, kept))
    back = call(
        functools.partial(back_kernel, expert_count),
        [shape((2 * hot_capacity, width))] * expert_count,
        [VMEM] * 4,
        cost=1.0,
    )(weight_in[0], weight_out[0], activated, pre_grad)
    got_back = merged(experts.exchange(back, inverse=True), MOST_PERMUTES)
    prepared = call(
        functools.partial(prepare_kernel, hot_capacity, expert_count),
        [
            shape((tok, slots)),
            shape((tok, 128), jnp.float32),
            shape((tok, width), jnp.float32),
        ],
        [SMEM, VMEM, VMEM],
        cost=1.0,
    )(own, mixed, extended)
    layer_out, grad_mixed, share_in, share_out = call(
        functools.partial(finish_kernel, hot_capacity, seq_count),
        [
            shape((tok, width)),
            shape((tok, width)),
            shape((strip, hidden), jnp.float32),
            shape((strip, width), jnp.float32),
        ],
        [VMEM] * (5 + seq_count + len(got_back)),
        cost=1.0,
    )(*prepared, mixed, extended, kept, *got_terms[::-1], *got_back[::-1])
    return (layer_out[None], grad_mixed[None], share_in[None], share_out[None])


def solution(mesh):
    rows = P("expert", ("seq", "rep"), None)
    in_specs = (
        rows,
        rows,
        rows,
        P("expert", None),
        rows,
        P(),
        P(),
        rows,
        P("expert", None, None),
        P("expert", None, None),
        rows,
    )
    body = functools.partial(
        local, mesh.shape["seq"], mesh.shape["expert"], mesh.shape["rep"]
    )
    return jax.shard_map(
        body, mesh=mesh, in_specs=in_specs, out_specs=(rows, rows, rows, rows), check_vma=False
    )
```

```python
import functools
import math

import jax
import jax.numpy as jnp
from jax import lax
from jax.experimental import pallas as pl
from jax.experimental.pallas import tpu as pltpu
from jax.sharding import PartitionSpec as P

HD = 32
norm_eps = 1e-06
masked_score = -1e30
VMEM_LIMIT = 48 * 1024 * 1024
MOST_PERMUTES = 16
NT = (((1,), (1,)), ((), ()))
TN = (((0,), (0,)), ((), ()))


def dot(a, b, dims=None):
    if dims is None:
        return jnp.dot(a, b, preferred_element_type=jnp.float32)
    return lax.dot_general(a, b, dims, preferred_element_type=jnp.float32)


def away(index, offset, size):
    if size & (size - 1) == 0:
        return index ^ offset
    return (index + offset) % size


def back_from(index, offset, size):
    if size & (size - 1) == 0:
        return index ^ offset
    return (index - offset + size) % size


class Group:
    def __init__(self, axes, sizes):
        self.axes, self.sizes = tuple(axes), tuple(sizes)
        self.count = math.prod(sizes)

    def split(self, flat):
        coords = []
        for size in reversed(self.sizes):
            coords.append(flat % size)
            flat = flat // size
        return coords[::-1]

    def moved(self, flat, offset, step):
        place = 0
        for coord, part, size in zip(self.split(flat), self.split(offset), self.sizes):
            place = place * size + step(coord, part, size)
        return place

    def target(self, flat, offset):
        return self.moved(flat, offset, away)

    def source(self, flat, offset):
        return self.moved(flat, offset, back_from)

    def exchange(self, chunks, inverse=False):
        to, start = (self.source, self.target) if inverse else (self.target, self.source)
        if self.count <= MOST_PERMUTES:
            order = sorted(range(1, self.count), key=lambda k: -k)
            got = {0: chunks[0]}
            for k in order:
                pairs = [(i, to(i, k)) for i in range(self.count)]
                got[k] = lax.ppermute(chunks[k], self.axes, pairs)
            return [got[k] for k in range(self.count)]
        me = lax.axis_index(self.axes)
        steps = jnp.arange(self.count, dtype=jnp.int32)
        sent_to = jax.vmap(lambda k: to(me, k))(steps)
        placed = jnp.zeros((self.count,), jnp.int32).at[sent_to].set(steps)
        stacked = jnp.stack(chunks)[placed]
        got = lax.all_to_all(stacked, self.axes, split_axis=0, concat_axis=0, tiled=True)
        came_from = jax.vmap(lambda k: start(me, k))(steps)
        ordered = got[came_from]
        return [ordered[k] for k in range(self.count)]


def merged(chunks, most):
    if len(chunks) <= most:
        return list(chunks)
    return [jnp.concatenate(chunks, axis=0)]


def chunk_rows(refs, count, low, high):
    size = sum(ref.shape[0] for ref in refs) // count
    parts = []
    for chunk in range(count):
        ref, first = (refs[chunk], 0) if len(refs) == count else (refs[0], chunk * size)
        parts.append(ref[first + low : first + high, :])
    return parts[0] if count == 1 else jnp.concatenate(parts, axis=0)


def slot_matrix(choice, own, expert_count, hot_capacity):
    tok = choice.shape[1]
    offset = back_from(choice, own, expert_count)
    one_hot = lax.broadcasted_iota(jnp.int32, (expert_count, tok), 0) == offset
    hits = one_hot.astype(jnp.float32).astype(jnp.bfloat16)
    earlier = lax.broadcasted_iota(jnp.int32, (tok, tok), 0) <= lax.broadcasted_iota(
        jnp.int32, (tok, tok), 1
    )
    counted = dot(hits, earlier.astype(jnp.float32).astype(jnp.bfloat16))
    rank = jnp.sum(jnp.where(one_hot, counted, 0.0), axis=0, keepdims=True) - 1.0
    slots = offset * hot_capacity + rank.astype(jnp.int32)
    rows = lax.broadcasted_iota(jnp.int32, (expert_count * hot_capacity, tok), 0)
    return (rows == slots).astype(jnp.float32).astype(jnp.bfloat16)


def extend_kernel(
    ranks_ref, lengths_ref, choice_ref, router_ref, grad_ref, extended_ref, begin_ref
):
    tok, width = grad_ref.shape
    extended_ref[0:tok, :] = grad_ref[...]
    chosen = jnp.broadcast_to(choice_ref[...].astype(jnp.float32), (16, tok))
    extended_ref[tok : tok + 16, 0:tok] = chosen.astype(jnp.bfloat16)
    extended_ref[tok : tok + 16, tok:width] = jnp.zeros((16, width - tok), jnp.bfloat16)
    routed = router_ref[...].astype(jnp.float32)
    spare = extended_ref.shape[0] - tok - 16 - routed.shape[0]
    if spare:
        routed = jnp.concatenate([routed, jnp.zeros((spare, width), jnp.float32)], axis=0)
    extended_ref[tok + 16 :, :] = routed.astype(jnp.bfloat16)
    for k in range(begin_ref.shape[0]):
        position = ranks_ref[k] * tok + lax.broadcasted_iota(jnp.int32, (1, tok), 1)
        begin = jnp.zeros((1, tok), jnp.int32)
        bound = jnp.int32(0)
        for doc in range(lengths_ref.shape[1] - 1):
            bound = bound + lengths_ref[0, doc]
            begin = jnp.maximum(begin, jnp.where(position >= bound, bound, 0))
        begin_ref[k : k + 1, :] = begin


def chosen_of(extended_ref, tok):
    return extended_ref[tok : tok + 16, 0:tok].astype(jnp.float32)[0:1].astype(jnp.int32)


def router_of(extended_ref, tok, expert_count):
    whole = extended_ref[tok + 16 :, :].astype(jnp.float32)
    return whole[0:expert_count].astype(jnp.bfloat16)


def dispatch_kernel(reps, tok, hot_capacity, own_ref, *refs):
    extended_refs, sent_refs = refs[:reps], refs[reps:]
    for rep in range(reps):
        choice = chosen_of(extended_refs[rep], tok)
        placed = slot_matrix(choice, own_ref[0], len(sent_refs), hot_capacity)
        rows = dot(placed, extended_refs[rep][0:tok, :]).astype(jnp.bfloat16)
        for k, sent_ref in enumerate(sent_refs):
            sent_ref[rep * hot_capacity : (rep + 1) * hot_capacity] = rows[
                k * hot_capacity : (k + 1) * hot_capacity
            ]


def fold_blocks(ids_ref, begin_ref, tasks, reps, states, bias_ref):
    lanes = 128
    per = lanes // HD
    scale = math.log2(math.e) / math.sqrt(HD)
    spreads = {}
    lowest = {}
    for k, query_ref, unused_pair, unused_first in tasks:
        if k in spreads:
            continue
        lowest[k] = jnp.min(begin_ref[k : k + 1, :])
        tok = begin_ref.shape[1]
        turned = query_ref[...].T
        head_of_row = lax.broadcasted_iota(jnp.int32, (lanes, tok), 0) // HD
        spreads[k] = []
        for group in range(turned.shape[0] // lanes):
            part = turned[group * lanes : (group + 1) * lanes]
            spreads[k].append(
                jnp.concatenate(
                    [
                        jnp.where(head_of_row == head, part, jnp.zeros_like(part))
                        for head in range(per)
                    ],
                    axis=1,
                )
            )

    def fold(place, k, pair_ref, block, begin, fresh):
        top_ref, total_ref, sum_ref = states[k]
        tok = begin.shape[1]
        position = ids_ref[k] * tok + lax.broadcasted_iota(jnp.int32, (1, tok), 1)
        key_position = block * tok + lax.broadcasted_iota(jnp.int32, (tok, tok), 0)
        visible = (key_position >= begin) & (key_position <= position)
        bias_ref[place] = jnp.where(visible, 0.0, masked_score)
        bias = bias_ref[place]
        key_ref, value_ref = pair_ref
        values = value_ref[...].T
        for group, spread in enumerate(spreads[k]):
            columns = slice(group * lanes, (group + 1) * lanes)
            scores = dot(key_ref[:, columns], spread)
            weights, factors = [], []
            for head in range(per):
                row = group * per + head
                part = scores[:, head * tok : (head + 1) * tok] + bias
                top = jnp.max(part, axis=0, keepdims=True)
                if not fresh:
                    old = top_ref[row : row + 1, :]
                    top = jnp.maximum(top, old)
                    factors.append(jnp.exp2((old - top) * scale))
                weight = jnp.exp2((part - top) * scale)
                total = jnp.sum(weight, axis=0, keepdims=True)
                if not fresh:
                    total = total + total_ref[row : row + 1, :] * factors[head]
                top_ref[row : row + 1, :] = top
                total_ref[row : row + 1, :] = total
                weights.append(weight.astype(jnp.bfloat16))
            summed = dot(values[columns], jnp.concatenate(weights, axis=1))
            for head in range(per):
                rows = slice((group * per + head) * HD, (group * per + head + 1) * HD)
                piece = summed[head * HD : (head + 1) * HD, head * tok : (head + 1) * tok]
                if not fresh:
                    piece = piece + sum_ref[rows, :] * factors[head]
                sum_ref[rows, :] = piece

    for place, (k, unused_query, pair_ref, first) in enumerate(tasks):
        block = ids_ref[reps + place]
        begin = begin_ref[k : k + 1, :]
        tok = begin.shape[1]
        if first and k == 0:
            fold(place, k, pair_ref, block, begin, True)
            continue
        if first:
            top_ref, total_ref, sum_ref = states[k]
            top_ref[...] = jnp.full(top_ref.shape, masked_score, jnp.float32)
            total_ref[...] = jnp.zeros(total_ref.shape, jnp.float32)
            sum_ref[...] = jnp.zeros(sum_ref.shape, jnp.float32)

        @pl.when((block >= 0) & ((block + 1) * tok > lowest[k]))
        def unused(place=place, k=k, pair_ref=pair_ref, block=block, begin=begin):
            fold(place, k, pair_ref, block, begin, False)


def attend_kernel(plan, reps, counts, packed, ahead, ids_ref, begin_ref, *refs):
    ks = sorted({k for k, unused_pair, unused_first in plan})
    old_ks = [k for k in ks if not any(first for j, unused_pair, first in plan if j == k)]
    query_refs, refs = dict(zip(ks, refs)), refs[len(ks) + ahead :]
    pair_refs = [refs[2 * place : 2 * place + 2] for place in range(counts)]
    refs = refs[2 * counts :]
    old_refs, refs = refs[: 3 * len(old_ks)], refs[3 * len(old_ks) :]
    bias_ref, refs = refs[-1], refs[:-1]
    packed_refs, state_refs = (refs[: len(ks)], refs[len(ks) :]) if packed else ((), refs)
    states = {k: state_refs[3 * place : 3 * place + 3] for place, k in enumerate(ks)}
    for place, k in enumerate(old_ks):
        for old_ref, new_ref in zip(old_refs[3 * place : 3 * place + 3], states[k]):
            new_ref[...] = old_ref[...]
    tasks = [(k, query_refs[k], pair_refs[pair], first) for k, pair, first in plan]
    fold_blocks(ids_ref, begin_ref, tasks, reps, states, bias_ref)
    for k, packed_ref in zip(ks, packed_refs):
        top_ref, total_ref, sum_ref = states[k]
        heads, width = top_ref.shape[0], sum_ref.shape[0]
        packed_ref[0:width, :] = sum_ref[...].astype(jnp.bfloat16)
        first = width
        for ref, pieces in ((top_ref, 3), (total_ref, 2)):
            rest = ref[...]
            for unused in range(pieces):
                piece = rest.astype(jnp.bfloat16)
                packed_ref[first : first + heads, :] = piece
                rest = rest - piece.astype(jnp.float32)
                first += heads


def mix_kernel(expert_count, hot_capacity, own_ref, extended_ref, residual_ref, proj_ref, *refs):
    top_ref, total_ref, sum_ref = refs[0:3]
    mixed_ref, sent_refs = refs[-1 - expert_count], refs[len(refs) - expert_count :]
    packed_refs = refs[3 : -1 - expert_count]
    tok, width = mixed_ref.shape
    heads = top_ref.shape[0]
    scale = math.log2(math.e) / math.sqrt(HD)
    tops, totals = [top_ref[...]], [total_ref[...]]
    for packed_ref in packed_refs:
        pieces = [
            packed_ref[width + place * heads : width + (place + 1) * heads, :].astype(jnp.float32)
            for place in range(5)
        ]
        tops.append((pieces[0] + pieces[1]) + pieces[2])
        totals.append(pieces[3] + pieces[4])
    top = functools.reduce(jnp.maximum, tops)
    factors = [jnp.exp2((one - top) * scale) for one in tops]
    total = sum(one * factor for one, factor in zip(totals, factors))
    factors = [factor / total for factor in factors]
    pieces = []
    for head in range(heads):
        rows = slice(head * HD, (head + 1) * HD)
        piece = sum_ref[rows, :] * factors[0][head : head + 1, :]
        for packed_ref, factor in zip(packed_refs, factors[1:]):
            piece = piece + packed_ref[rows, :].astype(jnp.float32) * factor[head : head + 1, :]
        pieces.append(piece.astype(jnp.bfloat16))
    attended = jnp.concatenate(pieces, axis=0).T
    mixed = (residual_ref[...].astype(jnp.float32) + dot(attended, proj_ref[...])).astype(
        jnp.bfloat16
    )
    mixed_ref[...] = mixed
    mixed_f = mixed.astype(jnp.float32)
    inv_rms = lax.rsqrt(jnp.mean(mixed_f * mixed_f, axis=1, keepdims=True) + norm_eps)
    normed = (mixed_f * inv_rms).astype(jnp.bfloat16)
    placed = slot_matrix(chosen_of(extended_ref, tok), own_ref[0], len(sent_refs), hot_capacity)
    rows = dot(placed, normed).astype(jnp.bfloat16)
    for k, sent_ref in enumerate(sent_refs):
        sent_ref[...] = rows[k * hot_capacity : (k + 1) * hot_capacity]


def expert_kernel(
    reps,
    rep_list,
    sources,
    tok,
    strip,
    counts,
    own_ref,
    part_ref,
    up_ref,
    down_ref,
    extended_ref,
    *refs,
):
    row_count, grad_count = counts
    row_refs, refs = refs[:row_count][::-1], refs[row_count:]
    per_rep = row_count // len(rep_list)
    grad_refs, refs = refs[:grad_count], refs[grad_count:]
    own_rows = rep_list[0] == 0
    held_ref, refs = refs[-1], refs[:-1]
    if own_rows:
        up_old, down_old, activated_ref, pre_grad_ref = refs[:4]
        term_refs, kept_ref = refs[4:-1], refs[-1]
    else:
        up_acc, down_acc = refs
    total_grads = sum(ref.shape[0] for ref in grad_refs)
    capacity = total_grads // (sources * reps)
    count = sources * capacity
    parts = part_ref.shape[0]
    up = up_ref[...]
    down = down_ref[...]
    router = router_of(extended_ref, tok, sources)
    expert_lane = lax.broadcasted_iota(jnp.int32, (count, router.shape[0]), 1) == own_ref[0]

    def strips(rows, place):
        held_ref[place] = rows.T
        taken = []
        for k in range(parts):
            first = pl.multiple_of(part_ref[k] * strip, strip)
            taken.append(held_ref[place, pl.ds(first, strip), :])
        return jnp.concatenate(taken, axis=0)

    up_term = down_term = None
    for place, rep in enumerate(rep_list):
        rows = chunk_rows(
            row_refs[place * per_rep : (place + 1) * per_rep], sources, 0, capacity
        )
        grads = chunk_rows(grad_refs, sources, rep * capacity, (rep + 1) * capacity)
        pre = dot(rows, up)
        sigmoid_pre = jax.nn.sigmoid(pre)
        activated = (pre * sigmoid_pre).astype(jnp.bfloat16)
        logits = dot(rows, router, NT)
        gate = jax.nn.sigmoid(
            jnp.sum(jnp.where(expert_lane, logits, 0.0), axis=1, keepdims=True)
        )
        scaled = (gate * grads.astype(jnp.float32)).astype(jnp.bfloat16)
        act_grad = dot(scaled, down, NT)
        pre_grad = (act_grad * sigmoid_pre * (1.0 + pre * (1.0 - sigmoid_pre))).astype(
            jnp.bfloat16
        )
        if own_rows:
            activated_ref[...] = activated
            pre_grad_ref[...] = pre_grad
        more_up = dot(strips(rows, 2 * place), pre_grad)
        more_down = dot(strips(activated, 2 * place + 1), scaled)
        up_term = more_up if up_term is None else up_term + more_up
        down_term = more_down if down_term is None else down_term + more_down
    if not own_rows:
        up_acc[...] = up_term
        down_acc[...] = down_term
        return
    up_term = up_term + up_old[...]
    down_term = down_term + down_old[...]
    for k, ref in enumerate((kept_ref, *term_refs)):
        rows = slice(k * strip, (k + 1) * strip)
        ref[0] = up_term[rows].astype(ref.dtype)
        ref[1] = down_term[rows].astype(ref.dtype)


def back_kernel(sources, up_ref, down_ref, activated_ref, pre_grad_ref, *back_refs):
    capacity = activated_ref.shape[0] // sources
    produced = dot(activated_ref[...], down_ref[...]).astype(jnp.bfloat16)
    token_grad = dot(pre_grad_ref[...], up_ref[...], NT).astype(jnp.bfloat16)
    for k, back_ref in enumerate(back_refs):
        rows = slice(k * capacity, (k + 1) * capacity)
        back_ref[0:capacity] = produced[rows]
        back_ref[capacity : 2 * capacity] = token_grad[rows]


def prepare_kernel(
    hot_capacity,
    expert_count,
    own_ref,
    mixed_ref,
    extended_ref,
    placed_ref,
    factors_ref,
    router_cols_ref,
):
    tok = mixed_ref.shape[0]
    choice = chosen_of(extended_ref, tok)
    placed = slot_matrix(choice, own_ref[0], expert_count, hot_capacity)
    placed_ref[...] = placed.T
    router = router_of(extended_ref, tok, expert_count)
    mixed_f = mixed_ref[...].astype(jnp.float32)
    inv_rms = lax.rsqrt(jnp.mean(mixed_f * mixed_f, axis=1, keepdims=True) + norm_eps)
    normed = (mixed_f * inv_rms).astype(jnp.bfloat16)
    one_hot = lax.broadcasted_iota(jnp.int32, (expert_count, tok), 0) == choice
    logits = dot(router, normed, NT)
    logit_row = jnp.sum(jnp.where(one_hot, logits, 0.0), axis=0, keepdims=True)
    gate = jax.nn.sigmoid(jnp.broadcast_to(logit_row, (8, tok)).T[:, 0:1])
    lane = lax.broadcasted_iota(jnp.int32, factors_ref.shape, 1)
    factors_ref[...] = jnp.where(lane == 0, inv_rms, gate)
    router_cols_ref[...] = dot(one_hot.astype(jnp.float32).astype(jnp.bfloat16), router, TN)


def finish_kernel(
    hot_capacity,
    parts,
    placed_ref,
    factors_ref,
    router_cols_ref,
    mixed_ref,
    extended_ref,
    *refs,
):
    refs, (layer_ref, grad_mixed_ref, *share_refs) = refs[:-4], refs[-4:]
    (kept_ref, *term_refs), back_refs = refs[:parts], refs[parts:][::-1]
    for kind, share_ref in enumerate(share_refs):
        total = kept_ref[kind]
        for ref in term_refs:
            total = total + ref[kind].astype(jnp.float32)
        share_ref[...] = total
    tok = mixed_ref.shape[0]
    mixed_f = mixed_ref[...].astype(jnp.float32)
    inv_rms = factors_ref[:, 0:1]
    gate = factors_ref[:, 1:2]
    pair = 2 * hot_capacity
    chunks = [
        ref[first : first + pair] for ref in back_refs for first in range(0, ref.shape[0], pair)
    ]
    results = jnp.concatenate([chunk[:hot_capacity] for chunk in chunks], axis=0)
    grads = jnp.concatenate([chunk[hot_capacity:] for chunk in chunks], axis=0)
    placed = placed_ref[...]
    result_f = dot(placed, results)
    normed_grad = dot(placed, grads)
    grad_f = extended_ref[0:tok, :].astype(jnp.float32)
    layer_ref[...] = (mixed_f + gate * result_f).astype(jnp.bfloat16)
    gate_grad = jnp.sum(grad_f * result_f, axis=1, keepdims=True)
    logit_grad = gate_grad * gate * (1.0 - gate)
    total_grad = normed_grad + logit_grad * router_cols_ref[...]
    mean_term = jnp.mean(total_grad * mixed_f, axis=1, keepdims=True)
    input_grad = inv_rms * total_grad - mixed_f * inv_rms * inv_rms * inv_rms * mean_term
    grad_mixed_ref[...] = (grad_f + input_grad).astype(jnp.bfloat16)


def shape(dims, dtype=jnp.bfloat16):
    return jax.ShapeDtypeStruct(dims, dtype)


SMEM = pl.BlockSpec(memory_space=pltpu.SMEM)
VMEM = pl.BlockSpec(memory_space=pltpu.VMEM)
HBM = pl.BlockSpec(memory_space=pltpu.HBM)


def call(body, out_shape, specs, scratch=(), cost=0.5):
    return pl.pallas_call(
        body,
        cost_estimate=pl.CostEstimate(
            flops=int(cost * 1e9), bytes_accessed=0, transcendentals=0
        ),
        out_shape=out_shape,
        in_specs=specs,
        out_specs=jax.tree.map(lambda unused: VMEM, out_shape),
        scratch_shapes=list(scratch),
        compiler_params=pltpu.CompilerParams(vmem_limit_bytes=VMEM_LIMIT),
    )


def local(
    seq_count,
    expert_count,
    rep_count,
    query_rows,
    key_rows,
    value_rows,
    doc_lengths,
    residual,
    out_proj,
    router,
    expert_choice,
    weight_in,
    weight_out,
    grad_out,
):
    tok, width = query_rows.shape[1:]
    hidden = weight_in.shape[2]
    heads = width // HD
    experts = Group(("expert",), (expert_count,))
    reps = Group(("rep",), (rep_count,))
    owners = Group(("expert", "rep"), (expert_count, rep_count))
    parts = Group(("seq",), (seq_count,))
    strip = width // (seq_count * rep_count)
    capacity = max(2, (3 * tok + 2 * expert_count - 1) // (2 * expert_count))
    hot_capacity = min(4 * capacity, tok // 2)
    choice = expert_choice.reshape(1, tok)
    seq_index = lax.axis_index("seq")
    rep_index = lax.axis_index("rep")
    rank = seq_index * rep_count + rep_index
    own = jnp.stack([lax.axis_index("expert")]).astype(jnp.int32)
    part_to = jnp.stack(
        [parts.target(seq_index, k) * rep_count + rep_index for k in range(seq_count)]
    ).astype(jnp.int32)

    def forward(array):
        return lax.ppermute(array, "seq", [(i, (i + 1) % seq_count) for i in range(seq_count)])

    reach = (seq_count + 1) // 2
    longest = (seq_count * rep_count + 1) // 2
    query_ranks = [
        seq_index * rep_count + reps.source(rep_index, k) for k in range(rep_count)
    ]

    def task_ids(plan, steps):
        ids = list(query_ranks)
        for k, pair, unused_first in plan:
            block = rank - steps[pair] * rep_count
            behind = query_ranks[k] - block
            ids.append(jnp.where((block >= 0) & (behind >= 0) & (behind <= longest), block, -1))
        return jnp.stack(ids).astype(jnp.int32)

    state_shapes = [
        shape((heads, tok), jnp.float32),
        shape((heads, tok), jnp.float32),
        shape((width, tok), jnp.float32),
    ]
    tail = 16 + -(-expert_count // 16) * 16
    extended, begin = call(
        extend_kernel,
        [shape((tok + tail, width)), shape((rep_count, tok), jnp.int32)],
        [SMEM, SMEM] + [VMEM] * 3,
    )(
        jnp.stack(query_ranks).astype(jnp.int32), doc_lengths, choice, router.T, grad_out[0]
    )

    def attend(plan, pairs, steps, queries, states, packed, cost, ahead=()):
        ks = sorted({k for k, unused_pair, unused_first in plan})
        old = [one for k in ks if k in states for one in states[k]]
        state_out = state_shapes * len(ks)
        if packed:
            out_shape = [shape((width + 5 * heads, tok))] * len(ks)
            scratch = [pltpu.VMEM(one.shape, one.dtype) for one in state_out]
        else:
            out_shape, scratch = state_out, []
        outs = call(
            functools.partial(
                attend_kernel, plan, rep_count, len(pairs), packed, len(ahead)
            ),
            out_shape,
            [SMEM] + [VMEM] * (1 + len(ks) + len(ahead) + 2 * len(pairs) + len(old)),
            scratch + [pltpu.VMEM((len(plan), tok, tok), jnp.float32)],
            cost=cost,
        )(task_ids(plan, steps), begin, *[queries[k] for k in ks], *ahead, *[one for both in pairs for one in both], *old)
        if packed:
            return dict(zip(ks, outs))
        return {k: list(outs[3 * place : 3 * place + 3]) for place, k in enumerate(ks)}

    others = range(1, rep_count)
    lines = [(key_rows[0], value_rows[0])]
    lines.append(tuple(forward(one) for one in lines[0]))
    queries = reps.exchange([query_rows[0]] * rep_count)
    extendeds = reps.exchange([extended] * rep_count)
    states = attend(((0, 0, True),), lines[:1], [0], queries, {}, False, 2.0)
    ahead, *states[0] = lax.optimization_barrier((lines[1][0], *states[0]))
    lines[1] = (ahead, lines[1][1])
    for unused in range(1, reach):
        lines.append(tuple(forward(one) for one in lines[-1]))
    middle = tuple((0, step, False) for step in range(1, reach)) + tuple(
        (k, step, step == 0) for k in others for step in range(reach)
    )
    states = attend(middle, lines[:-1], list(range(reach)), queries, states, False, 4.0)
    states[1][0], *extendeds[1:] = lax.optimization_barrier((states[1][0], *extendeds[1:]))
    sent_grads = call(
        functools.partial(dispatch_kernel, rep_count, tok, hot_capacity),
        [shape((rep_count * hot_capacity, width))] * expert_count,
        [SMEM] + [VMEM] * rep_count,
    )(own, *extendeds)
    partial = attend(
        tuple((k, 0, False) for k in others),
        lines[-1:],
        [reach],
        queries,
        states,
        True,
        1.5,
        ahead=sent_grads[:1],
    )
    returned = reps.exchange([None] + [partial[k] for k in others], inverse=True)[1:]
    states = attend(((0, 0, False),), lines[-1:], [reach], queries, states, False, 1.5)
    got_grads = merged(experts.exchange(sent_grads), MOST_PERMUTES)

    mixed, *sent_rows = call(
        functools.partial(mix_kernel, expert_count, hot_capacity),
        [shape((tok, width))] + [shape((hot_capacity, width))] * expert_count,
        [SMEM] + [VMEM] * (6 + len(returned)),
        cost=2.0,
    )(own, extendeds[0], residual[0], out_proj, *states[0], *returned)
    arrived = owners.exchange([sent_rows[k // rep_count] for k in range(owners.count)])
    got_rows = merged(arrived[0::rep_count], MOST_PERMUTES)
    got_more = [
        one for k in others for one in merged(arrived[k::rep_count], MOST_PERMUTES)
    ]

    def expert_call(rep_list, rows, out_shape, extra):
        return call(
            functools.partial(
                expert_kernel,
                rep_count,
                rep_list,
                expert_count,
                tok,
                strip,
                (len(rows), len(got_grads)),
            ),
            out_shape,
            [SMEM, SMEM] + [VMEM] * (3 + len(rows) + len(got_grads) + len(extra)),
            [pltpu.VMEM((2 * len(rep_list), width, expert_count * hot_capacity), jnp.bfloat16)],
            cost=2.0,
        )(own, part_to, weight_in[0], weight_out[0], extendeds[0], *rows[::-1], *got_grads, *extra)

    slots = expert_count * hot_capacity
    sums = expert_call(
        tuple(others),
        got_more,
        [
            shape((seq_count * strip, hidden), jnp.float32),
            shape((seq_count * strip, width), jnp.float32),
        ],
        [],
    )
    activated, pre_grad, *terms, kept = expert_call(
        (0,),
        got_rows,
        [shape((slots, hidden))] * 2
        + [shape((2, strip, hidden))] * (seq_count - 1)
        + [shape((2, strip, hidden), jnp.float32)],
        list(sums),
    )
    got_terms = parts.exchange([None] + terms)[1:]
    activated, mixed, kept = lax.optimization_barrier((activated, mixed, kept))
    back = call(
        functools.partial(back_kernel, expert_count),
        [shape((2 * hot_capacity, width))] * expert_count,
        [VMEM] * 4,
        cost=1.0,
    )(weight_in[0], weight_out[0], activated, pre_grad)
    got_back = merged(experts.exchange(back, inverse=True), MOST_PERMUTES)
    prepared = call(
        functools.partial(prepare_kernel, hot_capacity, expert_count),
        [
            shape((tok, slots)),
            shape((tok, 128), jnp.float32),
            shape((tok, width), jnp.float32),
        ],
        [SMEM, VMEM, VMEM],
        cost=1.0,
    )(own, mixed, extended)
    layer_out, grad_mixed, share_in, share_out = call(
        functools.partial(finish_kernel, hot_capacity, seq_count),
        [
            shape((tok, width)),
            shape((tok, width)),
            shape((strip, hidden), jnp.float32),
            shape((strip, width), jnp.float32),
        ],
        [VMEM] * (5 + seq_count + len(got_back)),
        cost=1.0,
    )(*prepared, mixed, extended, kept, *got_terms[::-1], *got_back[::-1])
    return (layer_out[None], grad_mixed[None], share_in[None], share_out[None])


def solution(mesh):
    rows = P("expert", ("seq", "rep"), None)
    in_specs = (
        rows,
        rows,
        rows,
        P("expert", None),
        rows,
        P(),
        P(),
        rows,
        P("expert", None, None),
        P("expert", None, None),
        rows,
    )
    body = functools.partial(
        local, mesh.shape["seq"], mesh.shape["expert"], mesh.shape["rep"]
    )
    return jax.shard_map(
        body, mesh=mesh, in_specs=in_specs, out_specs=(rows, rows, rows, rows), check_vma=False
    )
```

```python
import functools
import math

import jax
import jax.numpy as jnp
from jax import lax
from jax.experimental import pallas as pl
from jax.experimental.pallas import tpu as pltpu
from jax.sharding import PartitionSpec as P

HD = 32
norm_eps = 1e-06
masked_score = -1e30
VMEM_LIMIT = 48 * 1024 * 1024
MOST_PERMUTES = 16
NT = (((1,), (1,)), ((), ()))
TN = (((0,), (0,)), ((), ()))


def dot(a, b, dims=None):
    if dims is None:
        return jnp.dot(a, b, preferred_element_type=jnp.float32)
    return lax.dot_general(a, b, dims, preferred_element_type=jnp.float32)


def away(index, offset, size):
    if size & (size - 1) == 0:
        return index ^ offset
    return (index + offset) % size


def back_from(index, offset, size):
    if size & (size - 1) == 0:
        return index ^ offset
    return (index - offset + size) % size


class Group:
    def __init__(self, axes, sizes):
        self.axes, self.sizes = tuple(axes), tuple(sizes)
        self.count = math.prod(sizes)

    def split(self, flat):
        coords = []
        for size in reversed(self.sizes):
            coords.append(flat % size)
            flat = flat // size
        return coords[::-1]

    def moved(self, flat, offset, step):
        place = 0
        for coord, part, size in zip(self.split(flat), self.split(offset), self.sizes):
            place = place * size + step(coord, part, size)
        return place

    def target(self, flat, offset):
        return self.moved(flat, offset, away)

    def source(self, flat, offset):
        return self.moved(flat, offset, back_from)

    def exchange(self, chunks, inverse=False):
        to, start = (self.source, self.target) if inverse else (self.target, self.source)
        if self.count <= MOST_PERMUTES:
            order = sorted(range(1, self.count), key=lambda k: -k)
            got = {0: chunks[0]}
            for k in order:
                pairs = [(i, to(i, k)) for i in range(self.count)]
                got[k] = lax.ppermute(chunks[k], self.axes, pairs)
            return [got[k] for k in range(self.count)]
        me = lax.axis_index(self.axes)
        steps = jnp.arange(self.count, dtype=jnp.int32)
        sent_to = jax.vmap(lambda k: to(me, k))(steps)
        placed = jnp.zeros((self.count,), jnp.int32).at[sent_to].set(steps)
        stacked = jnp.stack(chunks)[placed]
        got = lax.all_to_all(stacked, self.axes, split_axis=0, concat_axis=0, tiled=True)
        came_from = jax.vmap(lambda k: start(me, k))(steps)
        ordered = got[came_from]
        return [ordered[k] for k in range(self.count)]


def merged(chunks, most):
    if len(chunks) <= most:
        return list(chunks)
    return [jnp.concatenate(chunks, axis=0)]


def chunk_rows(refs, count, low, high):
    size = sum(ref.shape[0] for ref in refs) // count
    parts = []
    for chunk in range(count):
        ref, first = (refs[chunk], 0) if len(refs) == count else (refs[0], chunk * size)
        parts.append(ref[first + low : first + high, :])
    return parts[0] if count == 1 else jnp.concatenate(parts, axis=0)


def slot_matrix(choice, own, expert_count, hot_capacity):
    tok = choice.shape[1]
    offset = back_from(choice, own, expert_count)
    one_hot = lax.broadcasted_iota(jnp.int32, (expert_count, tok), 0) == offset
    hits = one_hot.astype(jnp.float32).astype(jnp.bfloat16)
    earlier = lax.broadcasted_iota(jnp.int32, (tok, tok), 0) <= lax.broadcasted_iota(
        jnp.int32, (tok, tok), 1
    )
    counted = dot(hits, earlier.astype(jnp.float32).astype(jnp.bfloat16))
    rank = jnp.sum(jnp.where(one_hot, counted, 0.0), axis=0, keepdims=True) - 1.0
    slots = offset * hot_capacity + rank.astype(jnp.int32)
    rows = lax.broadcasted_iota(jnp.int32, (expert_count * hot_capacity, tok), 0)
    return (rows == slots).astype(jnp.float32).astype(jnp.bfloat16)


def extend_kernel(
    ranks_ref, lengths_ref, choice_ref, router_ref, grad_ref, extended_ref, begin_ref
):
    tok, width = grad_ref.shape
    extended_ref[0:tok, :] = grad_ref[...]
    chosen = jnp.broadcast_to(choice_ref[...].astype(jnp.float32), (16, tok))
    extended_ref[tok : tok + 16, 0:tok] = chosen.astype(jnp.bfloat16)
    extended_ref[tok : tok + 16, tok:width] = jnp.zeros((16, width - tok), jnp.bfloat16)
    routed = router_ref[...].astype(jnp.float32)
    spare = extended_ref.shape[0] - tok - 16 - routed.shape[0]
    if spare:
        routed = jnp.concatenate([routed, jnp.zeros((spare, width), jnp.float32)], axis=0)
    extended_ref[tok + 16 :, :] = routed.astype(jnp.bfloat16)
    for k in range(begin_ref.shape[0]):
        position = ranks_ref[k] * tok + lax.broadcasted_iota(jnp.int32, (1, tok), 1)
        begin = jnp.zeros((1, tok), jnp.int32)
        bound = jnp.int32(0)
        for doc in range(lengths_ref.shape[1] - 1):
            bound = bound + lengths_ref[0, doc]
            begin = jnp.maximum(begin, jnp.where(position >= bound, bound, 0))
        begin_ref[k : k + 1, :] = begin


def chosen_of(extended_ref, tok):
    return extended_ref[tok : tok + 16, 0:tok].astype(jnp.float32)[0:1].astype(jnp.int32)


def router_of(extended_ref, tok, expert_count):
    whole = extended_ref[tok + 16 :, :].astype(jnp.float32)
    return whole[0:expert_count].astype(jnp.bfloat16)


def dispatch_kernel(reps, tok, hot_capacity, own_ref, *refs):
    extended_refs, sent_refs = refs[:reps], refs[reps:]
    for rep in range(reps):
        choice = chosen_of(extended_refs[rep], tok)
        placed = slot_matrix(choice, own_ref[0], len(sent_refs), hot_capacity)
        rows = dot(placed, extended_refs[rep][0:tok, :]).astype(jnp.bfloat16)
        for k, sent_ref in enumerate(sent_refs):
            sent_ref[rep * hot_capacity : (rep + 1) * hot_capacity] = rows[
                k * hot_capacity : (k + 1) * hot_capacity
            ]


def fold_blocks(ids_ref, begin_ref, tasks, reps, states, bias_ref):
    lanes = 128
    per = lanes // HD
    scale = math.log2(math.e) / math.sqrt(HD)
    spreads = {}
    lowest = {}
    for k, query_ref, unused_pair, unused_first in tasks:
        if k in spreads:
            continue
        lowest[k] = jnp.min(begin_ref[k : k + 1, :])
        tok = begin_ref.shape[1]
        turned = query_ref[...].T
        head_of_row = lax.broadcasted_iota(jnp.int32, (lanes, tok), 0) // HD
        spreads[k] = []
        for group in range(turned.shape[0] // lanes):
            part = turned[group * lanes : (group + 1) * lanes]
            spreads[k].append(
                jnp.concatenate(
                    [
                        jnp.where(head_of_row == head, part, jnp.zeros_like(part))
                        for head in range(per)
                    ],
                    axis=1,
                )
            )

    def fold(place, k, pair_ref, block, begin, fresh):
        top_ref, total_ref, sum_ref = states[k]
        tok = begin.shape[1]
        position = ids_ref[k] * tok + lax.broadcasted_iota(jnp.int32, (1, tok), 1)
        key_position = block * tok + lax.broadcasted_iota(jnp.int32, (tok, tok), 0)
        visible = (key_position >= begin) & (key_position <= position)
        bias_ref[place] = jnp.where(visible, 0.0, masked_score)
        bias = bias_ref[place]
        key_ref, value_ref = pair_ref
        values = value_ref[...].T
        for group, spread in enumerate(spreads[k]):
            columns = slice(group * lanes, (group + 1) * lanes)
            scores = dot(key_ref[:, columns], spread)
            weights, factors = [], []
            for head in range(per):
                row = group * per + head
                part = scores[:, head * tok : (head + 1) * tok] + bias
                top = jnp.max(part, axis=0, keepdims=True)
                if not fresh:
                    old = top_ref[row : row + 1, :]
                    top = jnp.maximum(top, old)
                    factors.append(jnp.exp2((old - top) * scale))
                weight = jnp.exp2((part - top) * scale)
                total = jnp.sum(weight, axis=0, keepdims=True)
                if not fresh:
                    total = total + total_ref[row : row + 1, :] * factors[head]
                top_ref[row : row + 1, :] = top
                total_ref[row : row + 1, :] = total
                weights.append(weight.astype(jnp.bfloat16))
            summed = dot(values[columns], jnp.concatenate(weights, axis=1))
            for head in range(per):
                rows = slice((group * per + head) * HD, (group * per + head + 1) * HD)
                piece = summed[head * HD : (head + 1) * HD, head * tok : (head + 1) * tok]
                if not fresh:
                    piece = piece + sum_ref[rows, :] * factors[head]
                sum_ref[rows, :] = piece

    for place, (k, unused_query, pair_ref, first) in enumerate(tasks):
        block = ids_ref[reps + place]
        begin = begin_ref[k : k + 1, :]
        tok = begin.shape[1]
        if first and k == 0:
            fold(place, k, pair_ref, block, begin, True)
            continue
        if first:
            top_ref, total_ref, sum_ref = states[k]
            top_ref[...] = jnp.full(top_ref.shape, masked_score, jnp.float32)
            total_ref[...] = jnp.zeros(total_ref.shape, jnp.float32)
            sum_ref[...] = jnp.zeros(sum_ref.shape, jnp.float32)

        @pl.when((block >= 0) & ((block + 1) * tok > lowest[k]))
        def unused(place=place, k=k, pair_ref=pair_ref, block=block, begin=begin):
            fold(place, k, pair_ref, block, begin, False)


def attend_kernel(plan, reps, counts, packed, ahead, ids_ref, begin_ref, *refs):
    ks = sorted({k for k, unused_pair, unused_first in plan})
    old_ks = [k for k in ks if not any(first for j, unused_pair, first in plan if j == k)]
    query_refs, refs = dict(zip(ks, refs)), refs[len(ks) + ahead :]
    pair_refs = [refs[2 * place : 2 * place + 2] for place in range(counts)]
    refs = refs[2 * counts :]
    old_refs, refs = refs[: 3 * len(old_ks)], refs[3 * len(old_ks) :]
    bias_ref, refs = refs[-1], refs[:-1]
    packed_refs, state_refs = (refs[: len(ks)], refs[len(ks) :]) if packed else ((), refs)
    states = {k: state_refs[3 * place : 3 * place + 3] for place, k in enumerate(ks)}
    for place, k in enumerate(old_ks):
        for old_ref, new_ref in zip(old_refs[3 * place : 3 * place + 3], states[k]):
            new_ref[...] = old_ref[...]
    tasks = [(k, query_refs[k], pair_refs[pair], first) for k, pair, first in plan]
    fold_blocks(ids_ref, begin_ref, tasks, reps, states, bias_ref)
    for k, packed_ref in zip(ks, packed_refs):
        top_ref, total_ref, sum_ref = states[k]
        heads, width = top_ref.shape[0], sum_ref.shape[0]
        packed_ref[0:width, :] = sum_ref[...].astype(jnp.bfloat16)
        first = width
        for ref, pieces in ((top_ref, 3), (total_ref, 2)):
            rest = ref[...]
            for unused in range(pieces):
                piece = rest.astype(jnp.bfloat16)
                packed_ref[first : first + heads, :] = piece
                rest = rest - piece.astype(jnp.float32)
                first += heads


def mix_kernel(expert_count, hot_capacity, own_ref, extended_ref, residual_ref, proj_ref, *refs):
    top_ref, total_ref, sum_ref = refs[0:3]
    mixed_ref, sent_refs = refs[-1 - expert_count], refs[len(refs) - expert_count :]
    packed_refs = refs[3 : -1 - expert_count]
    tok, width = mixed_ref.shape
    heads = top_ref.shape[0]
    scale = math.log2(math.e) / math.sqrt(HD)
    tops, totals = [top_ref[...]], [total_ref[...]]
    for packed_ref in packed_refs:
        pieces = [
            packed_ref[width + place * heads : width + (place + 1) * heads, :].astype(jnp.float32)
            for place in range(5)
        ]
        tops.append((pieces[0] + pieces[1]) + pieces[2])
        totals.append(pieces[3] + pieces[4])
    top = functools.reduce(jnp.maximum, tops)
    factors = [jnp.exp2((one - top) * scale) for one in tops]
    total = sum(one * factor for one, factor in zip(totals, factors))
    factors = [factor / total for factor in factors]
    pieces = []
    for head in range(heads):
        rows = slice(head * HD, (head + 1) * HD)
        piece = sum_ref[rows, :] * factors[0][head : head + 1, :]
        for packed_ref, factor in zip(packed_refs, factors[1:]):
            piece = piece + packed_ref[rows, :].astype(jnp.float32) * factor[head : head + 1, :]
        pieces.append(piece.astype(jnp.bfloat16))
    attended = jnp.concatenate(pieces, axis=0).T
    mixed = (residual_ref[...].astype(jnp.float32) + dot(attended, proj_ref[...])).astype(
        jnp.bfloat16
    )
    mixed_ref[...] = mixed
    mixed_f = mixed.astype(jnp.float32)
    inv_rms = lax.rsqrt(jnp.mean(mixed_f * mixed_f, axis=1, keepdims=True) + norm_eps)
    normed = (mixed_f * inv_rms).astype(jnp.bfloat16)
    placed = slot_matrix(chosen_of(extended_ref, tok), own_ref[0], len(sent_refs), hot_capacity)
    rows = dot(placed, normed).astype(jnp.bfloat16)
    for k, sent_ref in enumerate(sent_refs):
        sent_ref[...] = rows[k * hot_capacity : (k + 1) * hot_capacity]


def expert_kernel(
    reps,
    rep_list,
    sources,
    tok,
    strip,
    counts,
    own_ref,
    part_ref,
    up_ref,
    down_ref,
    extended_ref,
    *refs,
):
    row_count, grad_count = counts
    row_refs, refs = refs[:row_count], refs[row_count:]
    per_rep = row_count // len(rep_list)
    if rep_list == (0,) and per_rep == sources:
        row_refs = row_refs[:1] + row_refs[1:][::-1]
    grad_refs, refs = refs[:grad_count], refs[grad_count:]
    own_rows = rep_list[0] == 0
    held_ref, refs = refs[-1], refs[:-1]
    if own_rows:
        up_old, down_old, activated_ref, pre_grad_ref = refs[:4]
        term_refs, kept_ref = refs[4:-1], refs[-1]
    else:
        up_acc, down_acc = refs
    total_grads = sum(ref.shape[0] for ref in grad_refs)
    capacity = total_grads // (sources * reps)
    count = sources * capacity
    parts = part_ref.shape[0]
    up = up_ref[...]
    down = down_ref[...]
    router = router_of(extended_ref, tok, sources)
    expert_lane = lax.broadcasted_iota(jnp.int32, (count, router.shape[0]), 1) == own_ref[0]

    def strips(rows, place):
        held_ref[place] = rows.T
        taken = []
        for k in range(parts):
            first = pl.multiple_of(part_ref[k] * strip, strip)
            taken.append(held_ref[place, pl.ds(first, strip), :])
        return jnp.concatenate(taken, axis=0)

    up_term = down_term = None
    for place, rep in enumerate(rep_list):
        rows = chunk_rows(
            row_refs[place * per_rep : (place + 1) * per_rep], sources, 0, capacity
        )
        grads = chunk_rows(grad_refs, sources, rep * capacity, (rep + 1) * capacity)
        pre = dot(rows, up)
        sigmoid_pre = jax.nn.sigmoid(pre)
        activated = (pre * sigmoid_pre).astype(jnp.bfloat16)
        logits = dot(rows, router, NT)
        gate = jax.nn.sigmoid(
            jnp.sum(jnp.where(expert_lane, logits, 0.0), axis=1, keepdims=True)
        )
        scaled = (gate * grads.astype(jnp.float32)).astype(jnp.bfloat16)
        act_grad = dot(scaled, down, NT)
        pre_grad = (act_grad * sigmoid_pre * (1.0 + pre * (1.0 - sigmoid_pre))).astype(
            jnp.bfloat16
        )
        if own_rows:
            activated_ref[...] = activated
            pre_grad_ref[...] = pre_grad
        more_up = dot(strips(rows, 2 * place), pre_grad)
        more_down = dot(strips(activated, 2 * place + 1), scaled)
        up_term = more_up if up_term is None else up_term + more_up
        down_term = more_down if down_term is None else down_term + more_down
    if not own_rows:
        up_acc[...] = up_term
        down_acc[...] = down_term
        return
    up_term = up_term + up_old[...]
    down_term = down_term + down_old[...]
    for k, ref in enumerate((kept_ref, *term_refs)):
        rows = slice(k * strip, (k + 1) * strip)
        ref[0] = up_term[rows].astype(ref.dtype)
        ref[1] = down_term[rows].astype(ref.dtype)


def back_kernel(sources, up_ref, down_ref, activated_ref, pre_grad_ref, *back_refs):
    capacity = activated_ref.shape[0] // sources
    produced = dot(activated_ref[...], down_ref[...]).astype(jnp.bfloat16)
    token_grad = dot(pre_grad_ref[...], up_ref[...], NT).astype(jnp.bfloat16)
    for k, back_ref in enumerate(back_refs):
        rows = slice(k * capacity, (k + 1) * capacity)
        back_ref[0:capacity] = produced[rows]
        back_ref[capacity : 2 * capacity] = token_grad[rows]


def prepare_kernel(
    hot_capacity,
    expert_count,
    own_ref,
    mixed_ref,
    extended_ref,
    placed_ref,
    factors_ref,
    router_cols_ref,
):
    tok = mixed_ref.shape[0]
    choice = chosen_of(extended_ref, tok)
    placed = slot_matrix(choice, own_ref[0], expert_count, hot_capacity)
    placed_ref[...] = placed.T
    router = router_of(extended_ref, tok, expert_count)
    mixed_f = mixed_ref[...].astype(jnp.float32)
    inv_rms = lax.rsqrt(jnp.mean(mixed_f * mixed_f, axis=1, keepdims=True) + norm_eps)
    normed = (mixed_f * inv_rms).astype(jnp.bfloat16)
    one_hot = lax.broadcasted_iota(jnp.int32, (expert_count, tok), 0) == choice
    logits = dot(router, normed, NT)
    logit_row = jnp.sum(jnp.where(one_hot, logits, 0.0), axis=0, keepdims=True)
    gate = jax.nn.sigmoid(jnp.broadcast_to(logit_row, (8, tok)).T[:, 0:1])
    lane = lax.broadcasted_iota(jnp.int32, factors_ref.shape, 1)
    factors_ref[...] = jnp.where(lane == 0, inv_rms, gate)
    router_cols_ref[...] = dot(one_hot.astype(jnp.float32).astype(jnp.bfloat16), router, TN)


def finish_kernel(
    hot_capacity,
    parts,
    placed_ref,
    factors_ref,
    router_cols_ref,
    mixed_ref,
    extended_ref,
    *refs,
):
    refs, (layer_ref, grad_mixed_ref, *share_refs) = refs[:-4], refs[-4:]
    (kept_ref, *term_refs), back_refs = refs[:parts], refs[parts:][::-1]
    for kind, share_ref in enumerate(share_refs):
        total = kept_ref[kind]
        for ref in term_refs:
            total = total + ref[kind].astype(jnp.float32)
        share_ref[...] = total
    tok = mixed_ref.shape[0]
    mixed_f = mixed_ref[...].astype(jnp.float32)
    inv_rms = factors_ref[:, 0:1]
    gate = factors_ref[:, 1:2]
    pair = 2 * hot_capacity
    chunks = [
        ref[first : first + pair] for ref in back_refs for first in range(0, ref.shape[0], pair)
    ]
    results = jnp.concatenate([chunk[:hot_capacity] for chunk in chunks], axis=0)
    grads = jnp.concatenate([chunk[hot_capacity:] for chunk in chunks], axis=0)
    placed = placed_ref[...]
    result_f = dot(placed, results)
    normed_grad = dot(placed, grads)
    grad_f = extended_ref[0:tok, :].astype(jnp.float32)
    layer_ref[...] = (mixed_f + gate * result_f).astype(jnp.bfloat16)
    gate_grad = jnp.sum(grad_f * result_f, axis=1, keepdims=True)
    logit_grad = gate_grad * gate * (1.0 - gate)
    total_grad = normed_grad + logit_grad * router_cols_ref[...]
    mean_term = jnp.mean(total_grad * mixed_f, axis=1, keepdims=True)
    input_grad = inv_rms * total_grad - mixed_f * inv_rms * inv_rms * inv_rms * mean_term
    grad_mixed_ref[...] = (grad_f + input_grad).astype(jnp.bfloat16)


def shape(dims, dtype=jnp.bfloat16):
    return jax.ShapeDtypeStruct(dims, dtype)


SMEM = pl.BlockSpec(memory_space=pltpu.SMEM)
VMEM = pl.BlockSpec(memory_space=pltpu.VMEM)
HBM = pl.BlockSpec(memory_space=pltpu.HBM)


def call(body, out_shape, specs, scratch=(), cost=0.5):
    return pl.pallas_call(
        body,
        cost_estimate=pl.CostEstimate(
            flops=int(cost * 1e9), bytes_accessed=0, transcendentals=0
        ),
        out_shape=out_shape,
        in_specs=specs,
        out_specs=jax.tree.map(lambda unused: VMEM, out_shape),
        scratch_shapes=list(scratch),
        compiler_params=pltpu.CompilerParams(vmem_limit_bytes=VMEM_LIMIT),
    )


def local(
    seq_count,
    expert_count,
    rep_count,
    query_rows,
    key_rows,
    value_rows,
    doc_lengths,
    residual,
    out_proj,
    router,
    expert_choice,
    weight_in,
    weight_out,
    grad_out,
):
    tok, width = query_rows.shape[1:]
    hidden = weight_in.shape[2]
    heads = width // HD
    experts = Group(("expert",), (expert_count,))
    reps = Group(("rep",), (rep_count,))
    owners = Group(("expert", "rep"), (expert_count, rep_count))
    parts = Group(("seq",), (seq_count,))
    strip = width // (seq_count * rep_count)
    capacity = max(2, (3 * tok + 2 * expert_count - 1) // (2 * expert_count))
    hot_capacity = min(4 * capacity, tok // 2)
    choice = expert_choice.reshape(1, tok)
    seq_index = lax.axis_index("seq")
    rep_index = lax.axis_index("rep")
    rank = seq_index * rep_count + rep_index
    own = jnp.stack([lax.axis_index("expert")]).astype(jnp.int32)
    part_to = jnp.stack(
        [parts.target(seq_index, k) * rep_count + rep_index for k in range(seq_count)]
    ).astype(jnp.int32)

    def forward(array):
        return lax.ppermute(array, "seq", [(i, (i + 1) % seq_count) for i in range(seq_count)])

    reach = (seq_count + 1) // 2
    longest = (seq_count * rep_count + 1) // 2
    query_ranks = [
        seq_index * rep_count + reps.source(rep_index, k) for k in range(rep_count)
    ]

    def task_ids(plan, steps):
        ids = list(query_ranks)
        for k, pair, unused_first in plan:
            block = rank - steps[pair] * rep_count
            behind = query_ranks[k] - block
            ids.append(jnp.where((block >= 0) & (behind >= 0) & (behind <= longest), block, -1))
        return jnp.stack(ids).astype(jnp.int32)

    state_shapes = [
        shape((heads, tok), jnp.float32),
        shape((heads, tok), jnp.float32),
        shape((width, tok), jnp.float32),
    ]
    tail = 16 + -(-expert_count // 16) * 16
    extended, begin = call(
        extend_kernel,
        [shape((tok + tail, width)), shape((rep_count, tok), jnp.int32)],
        [SMEM, SMEM] + [VMEM] * 3,
    )(
        jnp.stack(query_ranks).astype(jnp.int32), doc_lengths, choice, router.T, grad_out[0]
    )

    def attend(plan, pairs, steps, queries, states, packed, cost, ahead=()):
        ks = sorted({k for k, unused_pair, unused_first in plan})
        old = [one for k in ks if k in states for one in states[k]]
        state_out = state_shapes * len(ks)
        if packed:
            out_shape = [shape((width + 5 * heads, tok))] * len(ks)
            scratch = [pltpu.VMEM(one.shape, one.dtype) for one in state_out]
        else:
            out_shape, scratch = state_out, []
        outs = call(
            functools.partial(
                attend_kernel, plan, rep_count, len(pairs), packed, len(ahead)
            ),
            out_shape,
            [SMEM] + [VMEM] * (1 + len(ks) + len(ahead) + 2 * len(pairs) + len(old)),
            scratch + [pltpu.VMEM((len(plan), tok, tok), jnp.float32)],
            cost=cost,
        )(task_ids(plan, steps), begin, *[queries[k] for k in ks], *ahead, *[one for both in pairs for one in both], *old)
        if packed:
            return dict(zip(ks, outs))
        return {k: list(outs[3 * place : 3 * place + 3]) for place, k in enumerate(ks)}

    others = range(1, rep_count)
    lines = [(key_rows[0], value_rows[0])]
    lines.append(tuple(forward(one) for one in lines[0]))
    queries = reps.exchange([query_rows[0]] * rep_count)
    extendeds = reps.exchange([extended] * rep_count)
    states = attend(((0, 0, True),), lines[:1], [0], queries, {}, False, 2.0)
    ahead, *states[0] = lax.optimization_barrier((lines[1][0], *states[0]))
    lines[1] = (ahead, lines[1][1])
    for unused in range(1, reach):
        lines.append(tuple(forward(one) for one in lines[-1]))
    middle = tuple((0, step, False) for step in range(1, reach)) + tuple(
        (k, step, step == 0) for k in others for step in range(reach)
    )
    states = attend(middle, lines[:-1], list(range(reach)), queries, states, False, 4.0)
    states[1][0], *extendeds[1:] = lax.optimization_barrier((states[1][0], *extendeds[1:]))
    sent_grads = call(
        functools.partial(dispatch_kernel, rep_count, tok, hot_capacity),
        [shape((rep_count * hot_capacity, width))] * expert_count,
        [SMEM] + [VMEM] * rep_count,
    )(own, *extendeds)
    partial = attend(
        tuple((k, 0, False) for k in others),
        lines[-1:],
        [reach],
        queries,
        states,
        True,
        1.5,
        ahead=sent_grads[:1],
    )
    returned = reps.exchange([None] + [partial[k] for k in others], inverse=True)[1:]
    states = attend(((0, 0, False),), lines[-1:], [reach], queries, states, False, 1.5)
    got_grads = merged(experts.exchange(sent_grads), MOST_PERMUTES)

    mixed, *sent_rows = call(
        functools.partial(mix_kernel, expert_count, hot_capacity),
        [shape((tok, width))] + [shape((hot_capacity, width))] * expert_count,
        [SMEM] + [VMEM] * (6 + len(returned)),
        cost=2.0,
    )(own, extendeds[0], residual[0], out_proj, *states[0], *returned)
    arrived = owners.exchange([sent_rows[k // rep_count] for k in range(owners.count)])
    got_rows = merged(arrived[0::rep_count], MOST_PERMUTES)
    got_more = [
        one for k in others for one in merged(arrived[k::rep_count], MOST_PERMUTES)
    ]

    def expert_call(rep_list, rows, out_shape, extra):
        return call(
            functools.partial(
                expert_kernel,
                rep_count,
                rep_list,
                expert_count,
                tok,
                strip,
                (len(rows), len(got_grads)),
            ),
            out_shape,
            [SMEM, SMEM] + [VMEM] * (3 + len(rows) + len(got_grads) + len(extra)),
            [pltpu.VMEM((2 * len(rep_list), width, expert_count * hot_capacity), jnp.bfloat16)],
            cost=2.0,
        )(own, part_to, weight_in[0], weight_out[0], extendeds[0], *rows, *got_grads, *extra)

    slots = expert_count * hot_capacity
    sums = expert_call(
        tuple(others),
        got_more,
        [
            shape((seq_count * strip, hidden), jnp.float32),
            shape((seq_count * strip, width), jnp.float32),
        ],
        [],
    )
    activated, pre_grad, *terms, kept = expert_call(
        (0,),
        got_rows[:1] + got_rows[1:][::-1],
        [shape((slots, hidden))] * 2
        + [shape((2, strip, hidden))] * (seq_count - 1)
        + [shape((2, strip, hidden), jnp.float32)],
        list(sums),
    )
    got_terms = parts.exchange([None] + terms)[1:]
    activated, mixed, kept = lax.optimization_barrier((activated, mixed, kept))
    back = call(
        functools.partial(back_kernel, expert_count),
        [shape((2 * hot_capacity, width))] * expert_count,
        [VMEM] * 4,
        cost=1.0,
    )(weight_in[0], weight_out[0], activated, pre_grad)
    got_back = merged(experts.exchange(back, inverse=True), MOST_PERMUTES)
    prepared = call(
        functools.partial(prepare_kernel, hot_capacity, expert_count),
        [
            shape((tok, slots)),
            shape((tok, 128), jnp.float32),
            shape((tok, width), jnp.float32),
        ],
        [SMEM, VMEM, VMEM],
        cost=1.0,
    )(own, mixed, extended)
    layer_out, grad_mixed, share_in, share_out = call(
        functools.partial(finish_kernel, hot_capacity, seq_count),
        [
            shape((tok, width)),
            shape((tok, width)),
            shape((strip, hidden), jnp.float32),
            shape((strip, width), jnp.float32),
        ],
        [VMEM] * (5 + seq_count + len(got_back)),
        cost=1.0,
    )(*prepared, mixed, extended, kept, *got_terms[::-1], *got_back[::-1])
    return (layer_out[None], grad_mixed[None], share_in[None], share_out[None])


def solution(mesh):
    rows = P("expert", ("seq", "rep"), None)
    in_specs = (
        rows,
        rows,
        rows,
        P("expert", None),
        rows,
        P(),
        P(),
        rows,
        P("expert", None, None),
        P("expert", None, None),
        rows,
    )
    body = functools.partial(
        local, mesh.shape["seq"], mesh.shape["expert"], mesh.shape["rep"]
    )
    return jax.shard_map(
        body, mesh=mesh, in_specs=in_specs, out_specs=(rows, rows, rows, rows), check_vma=False
    )
```

```python
import functools
import math

import jax
import jax.numpy as jnp
from jax import lax
from jax.experimental import pallas as pl
from jax.experimental.pallas import tpu as pltpu
from jax.sharding import PartitionSpec as P

HD = 32
norm_eps = 1e-06
masked_score = -1e30
VMEM_LIMIT = 48 * 1024 * 1024
MOST_PERMUTES = 16
NT = (((1,), (1,)), ((), ()))
TN = (((0,), (0,)), ((), ()))


def dot(a, b, dims=None):
    if dims is None:
        return jnp.dot(a, b, preferred_element_type=jnp.float32)
    return lax.dot_general(a, b, dims, preferred_element_type=jnp.float32)


def away(index, offset, size):
    if size & (size - 1) == 0:
        return index ^ offset
    return (index + offset) % size


def back_from(index, offset, size):
    if size & (size - 1) == 0:
        return index ^ offset
    return (index - offset + size) % size


class Group:
    def __init__(self, axes, sizes):
        self.axes, self.sizes = tuple(axes), tuple(sizes)
        self.count = math.prod(sizes)

    def split(self, flat):
        coords = []
        for size in reversed(self.sizes):
            coords.append(flat % size)
            flat = flat // size
        return coords[::-1]

    def moved(self, flat, offset, step):
        place = 0
        for coord, part, size in zip(self.split(flat), self.split(offset), self.sizes):
            place = place * size + step(coord, part, size)
        return place

    def target(self, flat, offset):
        return self.moved(flat, offset, away)

    def source(self, flat, offset):
        return self.moved(flat, offset, back_from)

    def exchange(self, chunks, inverse=False):
        to, start = (self.source, self.target) if inverse else (self.target, self.source)
        if self.count <= MOST_PERMUTES:
            order = sorted(range(1, self.count), key=lambda k: -k)
            got = {0: chunks[0]}
            for k in order:
                pairs = [(i, to(i, k)) for i in range(self.count)]
                got[k] = lax.ppermute(chunks[k], self.axes, pairs)
            return [got[k] for k in range(self.count)]
        me = lax.axis_index(self.axes)
        steps = jnp.arange(self.count, dtype=jnp.int32)
        sent_to = jax.vmap(lambda k: to(me, k))(steps)
        placed = jnp.zeros((self.count,), jnp.int32).at[sent_to].set(steps)
        stacked = jnp.stack(chunks)[placed]
        got = lax.all_to_all(stacked, self.axes, split_axis=0, concat_axis=0, tiled=True)
        came_from = jax.vmap(lambda k: start(me, k))(steps)
        ordered = got[came_from]
        return [ordered[k] for k in range(self.count)]


def merged(chunks, most):
    if len(chunks) <= most:
        return list(chunks)
    return [jnp.concatenate(chunks, axis=0)]


def chunk_rows(refs, count, low, high):
    size = sum(ref.shape[0] for ref in refs) // count
    parts = []
    for chunk in range(count):
        ref, first = (refs[chunk], 0) if len(refs) == count else (refs[0], chunk * size)
        parts.append(ref[first + low : first + high, :])
    return parts[0] if count == 1 else jnp.concatenate(parts, axis=0)


def slot_matrix(choice, own, expert_count, hot_capacity):
    tok = choice.shape[1]
    offset = back_from(choice, own, expert_count)
    one_hot = lax.broadcasted_iota(jnp.int32, (expert_count, tok), 0) == offset
    hits = one_hot.astype(jnp.float32).astype(jnp.bfloat16)
    earlier = lax.broadcasted_iota(jnp.int32, (tok, tok), 0) <= lax.broadcasted_iota(
        jnp.int32, (tok, tok), 1
    )
    counted = dot(hits, earlier.astype(jnp.float32).astype(jnp.bfloat16))
    rank = jnp.sum(jnp.where(one_hot, counted, 0.0), axis=0, keepdims=True) - 1.0
    slots = offset * hot_capacity + rank.astype(jnp.int32)
    rows = lax.broadcasted_iota(jnp.int32, (expert_count * hot_capacity, tok), 0)
    return (rows == slots).astype(jnp.float32).astype(jnp.bfloat16)


def extend_kernel(
    ranks_ref, lengths_ref, choice_ref, router_ref, grad_ref, extended_ref, begin_ref
):
    tok, width = grad_ref.shape
    extended_ref[0:tok, :] = grad_ref[...]
    chosen = jnp.broadcast_to(choice_ref[...].astype(jnp.float32), (16, tok))
    extended_ref[tok : tok + 16, 0:tok] = chosen.astype(jnp.bfloat16)
    extended_ref[tok : tok + 16, tok:width] = jnp.zeros((16, width - tok), jnp.bfloat16)
    routed = router_ref[...].astype(jnp.float32)
    spare = extended_ref.shape[0] - tok - 16 - routed.shape[0]
    if spare:
        routed = jnp.concatenate([routed, jnp.zeros((spare, width), jnp.float32)], axis=0)
    extended_ref[tok + 16 :, :] = routed.astype(jnp.bfloat16)
    for k in range(begin_ref.shape[0]):
        position = ranks_ref[k] * tok + lax.broadcasted_iota(jnp.int32, (1, tok), 1)
        begin = jnp.zeros((1, tok), jnp.int32)
        bound = jnp.int32(0)
        for doc in range(lengths_ref.shape[1] - 1):
            bound = bound + lengths_ref[0, doc]
            begin = jnp.maximum(begin, jnp.where(position >= bound, bound, 0))
        begin_ref[k : k + 1, :] = begin


def chosen_of(extended_ref, tok):
    return extended_ref[tok : tok + 16, 0:tok].astype(jnp.float32)[0:1].astype(jnp.int32)


def router_of(extended_ref, tok, expert_count):
    whole = extended_ref[tok + 16 :, :].astype(jnp.float32)
    return whole[0:expert_count].astype(jnp.bfloat16)


def dispatch_kernel(reps, tok, hot_capacity, own_ref, *refs):
    extended_refs, sent_refs = refs[:reps], refs[reps:]
    for rep in range(reps):
        choice = chosen_of(extended_refs[rep], tok)
        placed = slot_matrix(choice, own_ref[0], len(sent_refs), hot_capacity)
        rows = dot(placed, extended_refs[rep][0:tok, :]).astype(jnp.bfloat16)
        for k, sent_ref in enumerate(sent_refs):
            sent_ref[rep * hot_capacity : (rep + 1) * hot_capacity] = rows[
                k * hot_capacity : (k + 1) * hot_capacity
            ]


def fold_blocks(ids_ref, begin_ref, tasks, reps, states, bias_ref):
    lanes = 128
    per = lanes // HD
    scale = math.log2(math.e) / math.sqrt(HD)
    spreads = {}
    lowest = {}
    for k, query_ref, unused_pair, unused_first in tasks:
        if k in spreads:
            continue
        lowest[k] = jnp.min(begin_ref[k : k + 1, :])
        tok = begin_ref.shape[1]
        turned = query_ref[...].T
        head_of_row = lax.broadcasted_iota(jnp.int32, (lanes, tok), 0) // HD
        spreads[k] = []
        for group in range(turned.shape[0] // lanes):
            part = turned[group * lanes : (group + 1) * lanes]
            spreads[k].append(
                jnp.concatenate(
                    [
                        jnp.where(head_of_row == head, part, jnp.zeros_like(part))
                        for head in range(per)
                    ],
                    axis=1,
                )
            )

    def fold(place, k, pair_ref, block, begin, fresh):
        top_ref, total_ref, sum_ref = states[k]
        tok = begin.shape[1]
        position = ids_ref[k] * tok + lax.broadcasted_iota(jnp.int32, (1, tok), 1)
        key_position = block * tok + lax.broadcasted_iota(jnp.int32, (tok, tok), 0)
        visible = (key_position >= begin) & (key_position <= position)
        bias_ref[place] = jnp.where(visible, 0.0, masked_score)
        bias = bias_ref[place]
        key_ref, value_ref = pair_ref
        values = value_ref[...].T
        for group, spread in enumerate(spreads[k]):
            columns = slice(group * lanes, (group + 1) * lanes)
            scores = dot(key_ref[:, columns], spread)
            weights, factors = [], []
            for head in range(per):
                row = group * per + head
                part = scores[:, head * tok : (head + 1) * tok] + bias
                top = jnp.max(part, axis=0, keepdims=True)
                if not fresh:
                    old = top_ref[row : row + 1, :]
                    top = jnp.maximum(top, old)
                    factors.append(jnp.exp2((old - top) * scale))
                weight = jnp.exp2((part - top) * scale)
                total = jnp.sum(weight, axis=0, keepdims=True)
                if not fresh:
                    total = total + total_ref[row : row + 1, :] * factors[head]
                top_ref[row : row + 1, :] = top
                total_ref[row : row + 1, :] = total
                weights.append(weight.astype(jnp.bfloat16))
            summed = dot(values[columns], jnp.concatenate(weights, axis=1))
            for head in range(per):
                rows = slice((group * per + head) * HD, (group * per + head + 1) * HD)
                piece = summed[head * HD : (head + 1) * HD, head * tok : (head + 1) * tok]
                if not fresh:
                    piece = piece + sum_ref[rows, :] * factors[head]
                sum_ref[rows, :] = piece

    for place, (k, unused_query, pair_ref, first) in enumerate(tasks):
        block = ids_ref[reps + place]
        begin = begin_ref[k : k + 1, :]
        tok = begin.shape[1]
        if first and k == 0:
            fold(place, k, pair_ref, block, begin, True)
            continue
        if first:
            top_ref, total_ref, sum_ref = states[k]
            top_ref[...] = jnp.full(top_ref.shape, masked_score, jnp.float32)
            total_ref[...] = jnp.zeros(total_ref.shape, jnp.float32)
            sum_ref[...] = jnp.zeros(sum_ref.shape, jnp.float32)

        @pl.when((block >= 0) & ((block + 1) * tok > lowest[k]))
        def unused(place=place, k=k, pair_ref=pair_ref, block=block, begin=begin):
            fold(place, k, pair_ref, block, begin, False)


def attend_kernel(plan, reps, counts, packed, ahead, ids_ref, begin_ref, *refs):
    ks = sorted({k for k, unused_pair, unused_first in plan})
    old_ks = [k for k in ks if not any(first for j, unused_pair, first in plan if j == k)]
    query_refs, refs = dict(zip(ks, refs)), refs[len(ks) + ahead :]
    pair_refs = [refs[2 * place : 2 * place + 2] for place in range(counts)]
    refs = refs[2 * counts :]
    old_refs, refs = refs[: 3 * len(old_ks)], refs[3 * len(old_ks) :]
    bias_ref, refs = refs[-1], refs[:-1]
    packed_refs, state_refs = (refs[: len(ks)], refs[len(ks) :]) if packed else ((), refs)
    states = {k: state_refs[3 * place : 3 * place + 3] for place, k in enumerate(ks)}
    for place, k in enumerate(old_ks):
        for old_ref, new_ref in zip(old_refs[3 * place : 3 * place + 3], states[k]):
            new_ref[...] = old_ref[...]
    tasks = [(k, query_refs[k], pair_refs[pair], first) for k, pair, first in plan]
    fold_blocks(ids_ref, begin_ref, tasks, reps, states, bias_ref)
    for k, packed_ref in zip(ks, packed_refs):
        top_ref, total_ref, sum_ref = states[k]
        heads, width = top_ref.shape[0], sum_ref.shape[0]
        packed_ref[0:width, :] = sum_ref[...].astype(jnp.bfloat16)
        first = width
        for ref, pieces in ((top_ref, 3), (total_ref, 2)):
            rest = ref[...]
            for unused in range(pieces):
                piece = rest.astype(jnp.bfloat16)
                packed_ref[first : first + heads, :] = piece
                rest = rest - piece.astype(jnp.float32)
                first += heads


def mix_kernel(expert_count, hot_capacity, own_ref, extended_ref, residual_ref, proj_ref, *refs):
    top_ref, total_ref, sum_ref = refs[0:3]
    mixed_ref, sent_refs = refs[-1 - expert_count], refs[len(refs) - expert_count :]
    packed_refs = refs[3 : -1 - expert_count]
    tok, width = mixed_ref.shape
    heads = top_ref.shape[0]
    scale = math.log2(math.e) / math.sqrt(HD)
    tops, totals = [top_ref[...]], [total_ref[...]]
    for packed_ref in packed_refs:
        pieces = [
            packed_ref[width + place * heads : width + (place + 1) * heads, :].astype(jnp.float32)
            for place in range(5)
        ]
        tops.append((pieces[0] + pieces[1]) + pieces[2])
        totals.append(pieces[3] + pieces[4])
    top = functools.reduce(jnp.maximum, tops)
    factors = [jnp.exp2((one - top) * scale) for one in tops]
    total = sum(one * factor for one, factor in zip(totals, factors))
    factors = [factor / total for factor in factors]
    pieces = []
    for head in range(heads):
        rows = slice(head * HD, (head + 1) * HD)
        piece = sum_ref[rows, :] * factors[0][head : head + 1, :]
        for packed_ref, factor in zip(packed_refs, factors[1:]):
            piece = piece + packed_ref[rows, :].astype(jnp.float32) * factor[head : head + 1, :]
        pieces.append(piece.astype(jnp.bfloat16))
    attended = jnp.concatenate(pieces, axis=0).T
    mixed = (residual_ref[...].astype(jnp.float32) + dot(attended, proj_ref[...])).astype(
        jnp.bfloat16
    )
    mixed_ref[...] = mixed
    mixed_f = mixed.astype(jnp.float32)
    inv_rms = lax.rsqrt(jnp.mean(mixed_f * mixed_f, axis=1, keepdims=True) + norm_eps)
    normed = (mixed_f * inv_rms).astype(jnp.bfloat16)
    placed = slot_matrix(chosen_of(extended_ref, tok), own_ref[0], len(sent_refs), hot_capacity)
    rows = dot(placed, normed).astype(jnp.bfloat16)
    for k, sent_ref in enumerate(sent_refs):
        sent_ref[...] = rows[k * hot_capacity : (k + 1) * hot_capacity]


def expert_kernel(
    reps,
    rep_list,
    sources,
    tok,
    strip,
    counts,
    own_ref,
    part_ref,
    up_ref,
    down_ref,
    extended_ref,
    *refs,
):
    row_count, grad_count = counts
    row_refs, refs = refs[:row_count], refs[row_count:]
    per_rep = row_count // len(rep_list)
    if rep_list == (0,) and per_rep == sources:
        row_refs = row_refs[:1] + row_refs[1:][::-1]
    grad_refs, refs = refs[:grad_count], refs[grad_count:]
    own_rows = rep_list[0] == 0
    held_ref, refs = refs[-1], refs[:-1]
    if own_rows:
        up_old, down_old, activated_ref, pre_grad_ref = refs[:4]
        term_refs, kept_ref = refs[4:-1], refs[-1]
    else:
        up_acc, down_acc = refs
    total_grads = sum(ref.shape[0] for ref in grad_refs)
    capacity = total_grads // (sources * reps)
    count = sources * capacity
    parts = part_ref.shape[0]
    up = up_ref[...]
    down = down_ref[...]
    router = router_of(extended_ref, tok, sources)
    expert_lane = lax.broadcasted_iota(jnp.int32, (count, router.shape[0]), 1) == own_ref[0]

    def strips(rows, place):
        held_ref[place] = rows.T
        taken = []
        for k in range(parts):
            first = pl.multiple_of(part_ref[k] * strip, strip)
            taken.append(held_ref[place, pl.ds(first, strip), :])
        return jnp.concatenate(taken, axis=0)

    up_term = down_term = None
    for place, rep in enumerate(rep_list):
        rows = chunk_rows(
            row_refs[place * per_rep : (place + 1) * per_rep], sources, 0, capacity
        )
        grads = chunk_rows(grad_refs, sources, rep * capacity, (rep + 1) * capacity)
        pre = dot(rows, up)
        sigmoid_pre = jax.nn.sigmoid(pre)
        activated = (pre * sigmoid_pre).astype(jnp.bfloat16)
        logits = dot(rows, router, NT)
        gate = jax.nn.sigmoid(
            jnp.sum(jnp.where(expert_lane, logits, 0.0), axis=1, keepdims=True)
        )
        scaled = (gate * grads.astype(jnp.float32)).astype(jnp.bfloat16)
        act_grad = dot(scaled, down, NT)
        pre_grad = (act_grad * sigmoid_pre * (1.0 + pre * (1.0 - sigmoid_pre))).astype(
            jnp.bfloat16
        )
        if own_rows:
            activated_ref[...] = activated
            pre_grad_ref[...] = pre_grad
        more_up = dot(strips(rows, 2 * place), pre_grad)
        more_down = dot(strips(activated, 2 * place + 1), scaled)
        up_term = more_up if up_term is None else up_term + more_up
        down_term = more_down if down_term is None else down_term + more_down
    if not own_rows:
        up_acc[...] = up_term
        down_acc[...] = down_term
        return
    up_term = up_term + up_old[...]
    down_term = down_term + down_old[...]
    for k, ref in enumerate((kept_ref, *term_refs)):
        rows = slice(k * strip, (k + 1) * strip)
        ref[0] = up_term[rows].astype(ref.dtype)
        ref[1] = down_term[rows].astype(ref.dtype)


def back_kernel(sources, up_ref, down_ref, activated_ref, pre_grad_ref, *back_refs):
    capacity = activated_ref.shape[0] // sources
    produced = dot(activated_ref[...], down_ref[...]).astype(jnp.bfloat16)
    token_grad = dot(pre_grad_ref[...], up_ref[...], NT).astype(jnp.bfloat16)
    for k, back_ref in enumerate(back_refs):
        rows = slice(k * capacity, (k + 1) * capacity)
        back_ref[0:capacity] = produced[rows]
        back_ref[capacity : 2 * capacity] = token_grad[rows]


def prepare_kernel(
    hot_capacity,
    expert_count,
    own_ref,
    mixed_ref,
    extended_ref,
    placed_ref,
    factors_ref,
    router_cols_ref,
):
    tok = mixed_ref.shape[0]
    choice = chosen_of(extended_ref, tok)
    placed = slot_matrix(choice, own_ref[0], expert_count, hot_capacity)
    placed_ref[...] = placed.T
    router = router_of(extended_ref, tok, expert_count)
    mixed_f = mixed_ref[...].astype(jnp.float32)
    inv_rms = lax.rsqrt(jnp.mean(mixed_f * mixed_f, axis=1, keepdims=True) + norm_eps)
    normed = (mixed_f * inv_rms).astype(jnp.bfloat16)
    one_hot = lax.broadcasted_iota(jnp.int32, (expert_count, tok), 0) == choice
    logits = dot(router, normed, NT)
    logit_row = jnp.sum(jnp.where(one_hot, logits, 0.0), axis=0, keepdims=True)
    gate = jax.nn.sigmoid(jnp.broadcast_to(logit_row, (8, tok)).T[:, 0:1])
    lane = lax.broadcasted_iota(jnp.int32, factors_ref.shape, 1)
    factors_ref[...] = jnp.where(lane == 0, inv_rms, gate)
    router_cols_ref[...] = dot(one_hot.astype(jnp.float32).astype(jnp.bfloat16), router, TN)


def finish_kernel(
    hot_capacity,
    parts,
    placed_ref,
    factors_ref,
    router_cols_ref,
    mixed_ref,
    extended_ref,
    *refs,
):
    refs, (layer_ref, grad_mixed_ref, *share_refs) = refs[:-4], refs[-4:]
    (kept_ref, *term_refs), back_refs = refs[:parts], refs[parts:][::-1]
    for kind, share_ref in enumerate(share_refs):
        total = kept_ref[kind]
        for ref in term_refs:
            total = total + ref[kind].astype(jnp.float32)
        share_ref[...] = total
    tok = mixed_ref.shape[0]
    mixed_f = mixed_ref[...].astype(jnp.float32)
    inv_rms = factors_ref[:, 0:1]
    gate = factors_ref[:, 1:2]
    pair = 2 * hot_capacity
    chunks = [
        ref[first : first + pair] for ref in back_refs for first in range(0, ref.shape[0], pair)
    ]
    results = jnp.concatenate([chunk[:hot_capacity] for chunk in chunks], axis=0)
    grads = jnp.concatenate([chunk[hot_capacity:] for chunk in chunks], axis=0)
    placed = placed_ref[...]
    result_f = dot(placed, results)
    normed_grad = dot(placed, grads)
    grad_f = extended_ref[0:tok, :].astype(jnp.float32)
    layer_ref[...] = (mixed_f + gate * result_f).astype(jnp.bfloat16)
    gate_grad = jnp.sum(grad_f * result_f, axis=1, keepdims=True)
    logit_grad = gate_grad * gate * (1.0 - gate)
    total_grad = normed_grad + logit_grad * router_cols_ref[...]
    mean_term = jnp.mean(total_grad * mixed_f, axis=1, keepdims=True)
    input_grad = inv_rms * total_grad - mixed_f * inv_rms * inv_rms * inv_rms * mean_term
    grad_mixed_ref[...] = (grad_f + input_grad).astype(jnp.bfloat16)


def shape(dims, dtype=jnp.bfloat16):
    return jax.ShapeDtypeStruct(dims, dtype)


SMEM = pl.BlockSpec(memory_space=pltpu.SMEM)
VMEM = pl.BlockSpec(memory_space=pltpu.VMEM)
HBM = pl.BlockSpec(memory_space=pltpu.HBM)


def call(body, out_shape, specs, scratch=(), cost=0.5):
    return pl.pallas_call(
        body,
        cost_estimate=pl.CostEstimate(
            flops=int(cost * 1e9), bytes_accessed=0, transcendentals=0
        ),
        out_shape=out_shape,
        in_specs=specs,
        out_specs=jax.tree.map(lambda unused: VMEM, out_shape),
        scratch_shapes=list(scratch),
        compiler_params=pltpu.CompilerParams(vmem_limit_bytes=VMEM_LIMIT),
    )


def local(
    seq_count,
    expert_count,
    rep_count,
    query_rows,
    key_rows,
    value_rows,
    doc_lengths,
    residual,
    out_proj,
    router,
    expert_choice,
    weight_in,
    weight_out,
    grad_out,
):
    tok, width = query_rows.shape[1:]
    hidden = weight_in.shape[2]
    heads = width // HD
    experts = Group(("expert",), (expert_count,))
    reps = Group(("rep",), (rep_count,))
    owners = Group(("expert", "rep"), (expert_count, rep_count))
    parts = Group(("seq",), (seq_count,))
    strip = width // (seq_count * rep_count)
    capacity = max(2, (3 * tok + 2 * expert_count - 1) // (2 * expert_count))
    hot_capacity = min(4 * capacity, tok // 2)
    choice = expert_choice.reshape(1, tok)
    seq_index = lax.axis_index("seq")
    rep_index = lax.axis_index("rep")
    rank = seq_index * rep_count + rep_index
    own = jnp.stack([lax.axis_index("expert")]).astype(jnp.int32)
    part_to = jnp.stack(
        [parts.target(seq_index, k) * rep_count + rep_index for k in range(seq_count)]
    ).astype(jnp.int32)

    def forward(array):
        return lax.ppermute(array, "seq", [(i, (i + 1) % seq_count) for i in range(seq_count)])

    reach = (seq_count + 1) // 2
    longest = (seq_count * rep_count + 1) // 2
    query_ranks = [
        seq_index * rep_count + reps.source(rep_index, k) for k in range(rep_count)
    ]

    def task_ids(plan, steps):
        ids = list(query_ranks)
        for k, pair, unused_first in plan:
            block = rank - steps[pair] * rep_count
            behind = query_ranks[k] - block
            ids.append(jnp.where((block >= 0) & (behind >= 0) & (behind <= longest), block, -1))
        return jnp.stack(ids).astype(jnp.int32)

    state_shapes = [
        shape((heads, tok), jnp.float32),
        shape((heads, tok), jnp.float32),
        shape((width, tok), jnp.float32),
    ]
    tail = 16 + -(-expert_count // 16) * 16
    extended, begin = call(
        extend_kernel,
        [shape((tok + tail, width)), shape((rep_count, tok), jnp.int32)],
        [SMEM, SMEM] + [VMEM] * 3,
    )(
        jnp.stack(query_ranks).astype(jnp.int32), doc_lengths, choice, router.T, grad_out[0]
    )

    def attend(plan, pairs, steps, queries, states, packed, cost, ahead=()):
        ks = sorted({k for k, unused_pair, unused_first in plan})
        old = [one for k in ks if k in states for one in states[k]]
        state_out = state_shapes * len(ks)
        if packed:
            out_shape = [shape((width + 5 * heads, tok))] * len(ks)
            scratch = [pltpu.VMEM(one.shape, one.dtype) for one in state_out]
        else:
            out_shape, scratch = state_out, []
        outs = call(
            functools.partial(
                attend_kernel, plan, rep_count, len(pairs), packed, len(ahead)
            ),
            out_shape,
            [SMEM] + [VMEM] * (1 + len(ks) + len(ahead) + 2 * len(pairs) + len(old)),
            scratch + [pltpu.VMEM((len(plan), tok, tok), jnp.float32)],
            cost=cost,
        )(task_ids(plan, steps), begin, *[queries[k] for k in ks], *ahead, *[one for both in pairs for one in both], *old)
        if packed:
            return dict(zip(ks, outs))
        return {k: list(outs[3 * place : 3 * place + 3]) for place, k in enumerate(ks)}

    others = range(1, rep_count)
    lines = [(key_rows[0], value_rows[0])]
    lines.append(tuple(forward(one) for one in lines[0]))
    queries = reps.exchange([query_rows[0]] * rep_count)
    extendeds = reps.exchange([extended] * rep_count)
    states = attend(((0, 0, True),), lines[:1], [0], queries, {}, False, 2.0)
    ahead, *states[0] = lax.optimization_barrier((lines[1][0], *states[0]))
    lines[1] = (ahead, lines[1][1])
    for unused in range(1, reach):
        lines.append(tuple(forward(one) for one in lines[-1]))
    own_state = states
    middle = tuple((k, step, step == 0) for k in others for step in range(reach))
    states = attend(middle, lines[:-1], list(range(reach)), queries, {}, False, 3.0)
    states[1][0], *extendeds[1:] = lax.optimization_barrier((states[1][0], *extendeds[1:]))
    sent_grads = call(
        functools.partial(dispatch_kernel, rep_count, tok, hot_capacity),
        [shape((rep_count * hot_capacity, width))] * expert_count,
        [SMEM] + [VMEM] * rep_count,
    )(own, *extendeds)
    partial = attend(
        tuple((k, 0, False) for k in others),
        lines[-1:],
        [reach],
        queries,
        states,
        True,
        1.5,
        ahead=sent_grads[:1],
    )
    returned = reps.exchange([None] + [partial[k] for k in others], inverse=True)[1:]
    states = attend(
        tuple((0, step, False) for step in range(reach)),
        lines[1:],
        list(range(1, reach + 1)),
        queries,
        own_state,
        False,
        2.5,
    )
    got_grads = merged(experts.exchange(sent_grads), MOST_PERMUTES)

    mixed, *sent_rows = call(
        functools.partial(mix_kernel, expert_count, hot_capacity),
        [shape((tok, width))] + [shape((hot_capacity, width))] * expert_count,
        [SMEM] + [VMEM] * (6 + len(returned)),
        cost=2.0,
    )(own, extendeds[0], residual[0], out_proj, *states[0], *returned)
    arrived = owners.exchange([sent_rows[k // rep_count] for k in range(owners.count)])
    got_rows = merged(arrived[0::rep_count], MOST_PERMUTES)
    got_more = [
        one for k in others for one in merged(arrived[k::rep_count], MOST_PERMUTES)
    ]

    def expert_call(rep_list, rows, out_shape, extra):
        return call(
            functools.partial(
                expert_kernel,
                rep_count,
                rep_list,
                expert_count,
                tok,
                strip,
                (len(rows), len(got_grads)),
            ),
            out_shape,
            [SMEM, SMEM] + [VMEM] * (3 + len(rows) + len(got_grads) + len(extra)),
            [pltpu.VMEM((2 * len(rep_list), width, expert_count * hot_capacity), jnp.bfloat16)],
            cost=2.0,
        )(own, part_to, weight_in[0], weight_out[0], extendeds[0], *rows, *got_grads, *extra)

    slots = expert_count * hot_capacity
    sums = expert_call(
        tuple(others),
        got_more,
        [
            shape((seq_count * strip, hidden), jnp.float32),
            shape((seq_count * strip, width), jnp.float32),
        ],
        [],
    )
    activated, pre_grad, *terms, kept = expert_call(
        (0,),
        got_rows[:1] + got_rows[1:][::-1],
        [shape((slots, hidden))] * 2
        + [shape((2, strip, hidden))] * (seq_count - 1)
        + [shape((2, strip, hidden), jnp.float32)],
        list(sums),
    )
    got_terms = parts.exchange([None] + terms)[1:]
    activated, mixed, kept = lax.optimization_barrier((activated, mixed, kept))
    back = call(
        functools.partial(back_kernel, expert_count),
        [shape((2 * hot_capacity, width))] * expert_count,
        [VMEM] * 4,
        cost=1.0,
    )(weight_in[0], weight_out[0], activated, pre_grad)
    got_back = merged(experts.exchange(back, inverse=True), MOST_PERMUTES)
    prepared = call(
        functools.partial(prepare_kernel, hot_capacity, expert_count),
        [
            shape((tok, slots)),
            shape((tok, 128), jnp.float32),
            shape((tok, width), jnp.float32),
        ],
        [SMEM, VMEM, VMEM],
        cost=1.0,
    )(own, mixed, extended)
    layer_out, grad_mixed, share_in, share_out = call(
        functools.partial(finish_kernel, hot_capacity, seq_count),
        [
            shape((tok, width)),
            shape((tok, width)),
            shape((strip, hidden), jnp.float32),
            shape((strip, width), jnp.float32),
        ],
        [VMEM] * (5 + seq_count + len(got_back)),
        cost=1.0,
    )(*prepared, mixed, extended, kept, *got_terms[::-1], *got_back[::-1])
    return (layer_out[None], grad_mixed[None], share_in[None], share_out[None])


def solution(mesh):
    rows = P("expert", ("seq", "rep"), None)
    in_specs = (
        rows,
        rows,
        rows,
        P("expert", None),
        rows,
        P(),
        P(),
        rows,
        P("expert", None, None),
        P("expert", None, None),
        rows,
    )
    body = functools.partial(
        local, mesh.shape["seq"], mesh.shape["expert"], mesh.shape["rep"]
    )
    return jax.shard_map(
        body, mesh=mesh, in_specs=in_specs, out_specs=(rows, rows, rows, rows), check_vma=False
    )
```

```python
import functools
import math

import jax
import jax.numpy as jnp
from jax import lax
from jax.experimental import pallas as pl
from jax.experimental.pallas import tpu as pltpu
from jax.sharding import PartitionSpec as P

HD = 32
norm_eps = 1e-06
masked_score = -1e30
VMEM_LIMIT = 48 * 1024 * 1024
MOST_PERMUTES = 16
NT = (((1,), (1,)), ((), ()))
TN = (((0,), (0,)), ((), ()))


def dot(a, b, dims=None):
    if dims is None:
        return jnp.dot(a, b, preferred_element_type=jnp.float32)
    return lax.dot_general(a, b, dims, preferred_element_type=jnp.float32)


def away(index, offset, size):
    if size & (size - 1) == 0:
        return index ^ offset
    return (index + offset) % size


def back_from(index, offset, size):
    if size & (size - 1) == 0:
        return index ^ offset
    return (index - offset + size) % size


class Group:
    def __init__(self, axes, sizes):
        self.axes, self.sizes = tuple(axes), tuple(sizes)
        self.count = math.prod(sizes)

    def split(self, flat):
        coords = []
        for size in reversed(self.sizes):
            coords.append(flat % size)
            flat = flat // size
        return coords[::-1]

    def moved(self, flat, offset, step):
        place = 0
        for coord, part, size in zip(self.split(flat), self.split(offset), self.sizes):
            place = place * size + step(coord, part, size)
        return place

    def target(self, flat, offset):
        return self.moved(flat, offset, away)

    def source(self, flat, offset):
        return self.moved(flat, offset, back_from)

    def exchange(self, chunks, inverse=False):
        to, start = (self.source, self.target) if inverse else (self.target, self.source)
        if self.count <= MOST_PERMUTES:
            order = sorted(range(1, self.count), key=lambda k: -k)
            got = {0: chunks[0]}
            for k in order:
                pairs = [(i, to(i, k)) for i in range(self.count)]
                got[k] = lax.ppermute(chunks[k], self.axes, pairs)
            return [got[k] for k in range(self.count)]
        me = lax.axis_index(self.axes)
        steps = jnp.arange(self.count, dtype=jnp.int32)
        sent_to = jax.vmap(lambda k: to(me, k))(steps)
        placed = jnp.zeros((self.count,), jnp.int32).at[sent_to].set(steps)
        stacked = jnp.stack(chunks)[placed]
        got = lax.all_to_all(stacked, self.axes, split_axis=0, concat_axis=0, tiled=True)
        came_from = jax.vmap(lambda k: start(me, k))(steps)
        ordered = got[came_from]
        return [ordered[k] for k in range(self.count)]


def merged(chunks, most):
    if len(chunks) <= most:
        return list(chunks)
    return [jnp.concatenate(chunks, axis=0)]


def chunk_rows(refs, count, low, high):
    size = sum(ref.shape[0] for ref in refs) // count
    parts = []
    for chunk in range(count):
        ref, first = (refs[chunk], 0) if len(refs) == count else (refs[0], chunk * size)
        parts.append(ref[first + low : first + high, :])
    return parts[0] if count == 1 else jnp.concatenate(parts, axis=0)


def slot_matrix(choice, own, expert_count, hot_capacity):
    tok = choice.shape[1]
    offset = back_from(choice, own, expert_count)
    one_hot = lax.broadcasted_iota(jnp.int32, (expert_count, tok), 0) == offset
    hits = one_hot.astype(jnp.float32).astype(jnp.bfloat16)
    earlier = lax.broadcasted_iota(jnp.int32, (tok, tok), 0) <= lax.broadcasted_iota(
        jnp.int32, (tok, tok), 1
    )
    counted = dot(hits, earlier.astype(jnp.float32).astype(jnp.bfloat16))
    rank = jnp.sum(jnp.where(one_hot, counted, 0.0), axis=0, keepdims=True) - 1.0
    slots = offset * hot_capacity + rank.astype(jnp.int32)
    rows = lax.broadcasted_iota(jnp.int32, (expert_count * hot_capacity, tok), 0)
    return (rows == slots).astype(jnp.float32).astype(jnp.bfloat16)


def extend_kernel(
    ranks_ref, lengths_ref, choice_ref, router_ref, grad_ref, extended_ref, begin_ref
):
    tok, width = grad_ref.shape
    extended_ref[0:tok, :] = grad_ref[...]
    chosen = jnp.broadcast_to(choice_ref[...].astype(jnp.float32), (16, tok))
    extended_ref[tok : tok + 16, 0:tok] = chosen.astype(jnp.bfloat16)
    extended_ref[tok : tok + 16, tok:width] = jnp.zeros((16, width - tok), jnp.bfloat16)
    routed = router_ref[...].astype(jnp.float32)
    spare = extended_ref.shape[0] - tok - 16 - routed.shape[0]
    if spare:
        routed = jnp.concatenate([routed, jnp.zeros((spare, width), jnp.float32)], axis=0)
    extended_ref[tok + 16 :, :] = routed.astype(jnp.bfloat16)
    for k in range(begin_ref.shape[0]):
        position = ranks_ref[k] * tok + lax.broadcasted_iota(jnp.int32, (1, tok), 1)
        begin = jnp.zeros((1, tok), jnp.int32)
        bound = jnp.int32(0)
        for doc in range(lengths_ref.shape[1] - 1):
            bound = bound + lengths_ref[0, doc]
            begin = jnp.maximum(begin, jnp.where(position >= bound, bound, 0))
        begin_ref[k : k + 1, :] = begin


def chosen_of(extended_ref, tok):
    return extended_ref[tok : tok + 16, 0:tok].astype(jnp.float32)[0:1].astype(jnp.int32)


def router_of(extended_ref, tok, expert_count):
    whole = extended_ref[tok + 16 :, :].astype(jnp.float32)
    return whole[0:expert_count].astype(jnp.bfloat16)


def dispatch_kernel(reps, tok, hot_capacity, own_ref, *refs):
    extended_refs, sent_refs = refs[:reps], refs[reps:]
    for rep in range(reps):
        choice = chosen_of(extended_refs[rep], tok)
        placed = slot_matrix(choice, own_ref[0], len(sent_refs), hot_capacity)
        rows = dot(placed, extended_refs[rep][0:tok, :]).astype(jnp.bfloat16)
        for k, sent_ref in enumerate(sent_refs):
            sent_ref[rep * hot_capacity : (rep + 1) * hot_capacity] = rows[
                k * hot_capacity : (k + 1) * hot_capacity
            ]


def fold_blocks(ids_ref, begin_ref, tasks, reps, states, bias_ref):
    lanes = 128
    per = lanes // HD
    scale = math.log2(math.e) / math.sqrt(HD)
    spreads = {}
    lowest = {}
    for k, query_ref, unused_pair, unused_first in tasks:
        if k in spreads:
            continue
        lowest[k] = jnp.min(begin_ref[k : k + 1, :])
        tok = begin_ref.shape[1]
        turned = query_ref[...].T
        head_of_row = lax.broadcasted_iota(jnp.int32, (lanes, tok), 0) // HD
        spreads[k] = []
        for group in range(turned.shape[0] // lanes):
            part = turned[group * lanes : (group + 1) * lanes]
            spreads[k].append(
                jnp.concatenate(
                    [
                        jnp.where(head_of_row == head, part, jnp.zeros_like(part))
                        for head in range(per)
                    ],
                    axis=1,
                )
            )

    def fold(place, k, pair_ref, block, begin, fresh):
        top_ref, total_ref, sum_ref = states[k]
        tok = begin.shape[1]
        position = ids_ref[k] * tok + lax.broadcasted_iota(jnp.int32, (1, tok), 1)
        key_position = block * tok + lax.broadcasted_iota(jnp.int32, (tok, tok), 0)
        visible = (key_position >= begin) & (key_position <= position)
        bias_ref[place] = jnp.where(visible, 0.0, masked_score)
        bias = bias_ref[place]
        key_ref, value_ref = pair_ref
        values = value_ref[...].T
        for group, spread in enumerate(spreads[k]):
            columns = slice(group * lanes, (group + 1) * lanes)
            scores = dot(key_ref[:, columns], spread)
            weights, factors = [], []
            for head in range(per):
                row = group * per + head
                part = scores[:, head * tok : (head + 1) * tok] + bias
                top = jnp.max(part, axis=0, keepdims=True)
                if not fresh:
                    old = top_ref[row : row + 1, :]
                    top = jnp.maximum(top, old)
                    factors.append(jnp.exp2((old - top) * scale))
                weight = jnp.exp2((part - top) * scale)
                total = jnp.sum(weight, axis=0, keepdims=True)
                if not fresh:
                    total = total + total_ref[row : row + 1, :] * factors[head]
                top_ref[row : row + 1, :] = top
                total_ref[row : row + 1, :] = total
                weights.append(weight.astype(jnp.bfloat16))
            summed = dot(values[columns], jnp.concatenate(weights, axis=1))
            for head in range(per):
                rows = slice((group * per + head) * HD, (group * per + head + 1) * HD)
                piece = summed[head * HD : (head + 1) * HD, head * tok : (head + 1) * tok]
                if not fresh:
                    piece = piece + sum_ref[rows, :] * factors[head]
                sum_ref[rows, :] = piece

    for place, (k, unused_query, pair_ref, first) in enumerate(tasks):
        block = ids_ref[reps + place]
        begin = begin_ref[k : k + 1, :]
        tok = begin.shape[1]
        if first and k == 0:
            fold(place, k, pair_ref, block, begin, True)
            continue
        if first:
            top_ref, total_ref, sum_ref = states[k]
            top_ref[...] = jnp.full(top_ref.shape, masked_score, jnp.float32)
            total_ref[...] = jnp.zeros(total_ref.shape, jnp.float32)
            sum_ref[...] = jnp.zeros(sum_ref.shape, jnp.float32)

        @pl.when((block >= 0) & ((block + 1) * tok > lowest[k]))
        def unused(place=place, k=k, pair_ref=pair_ref, block=block, begin=begin):
            fold(place, k, pair_ref, block, begin, False)


def attend_kernel(plan, reps, counts, packed, ahead, ids_ref, begin_ref, *refs):
    ks = sorted({k for k, unused_pair, unused_first in plan})
    old_ks = [k for k in ks if not any(first for j, unused_pair, first in plan if j == k)]
    query_refs, refs = dict(zip(ks, refs)), refs[len(ks) + ahead :]
    pair_refs = [refs[2 * place : 2 * place + 2] for place in range(counts)]
    refs = refs[2 * counts :]
    old_refs, refs = refs[: 3 * len(old_ks)], refs[3 * len(old_ks) :]
    bias_ref, refs = refs[-1], refs[:-1]
    packed_refs, state_refs = (refs[: len(ks)], refs[len(ks) :]) if packed else ((), refs)
    states = {k: state_refs[3 * place : 3 * place + 3] for place, k in enumerate(ks)}
    for place, k in enumerate(old_ks):
        for old_ref, new_ref in zip(old_refs[3 * place : 3 * place + 3], states[k]):
            new_ref[...] = old_ref[...]
    tasks = [(k, query_refs[k], pair_refs[pair], first) for k, pair, first in plan]
    fold_blocks(ids_ref, begin_ref, tasks, reps, states, bias_ref)
    for k, packed_ref in zip(ks, packed_refs):
        top_ref, total_ref, sum_ref = states[k]
        heads, width = top_ref.shape[0], sum_ref.shape[0]
        packed_ref[0:width, :] = sum_ref[...].astype(jnp.bfloat16)
        first = width
        for ref, pieces in ((top_ref, 3), (total_ref, 2)):
            rest = ref[...]
            for unused in range(pieces):
                piece = rest.astype(jnp.bfloat16)
                packed_ref[first : first + heads, :] = piece
                rest = rest - piece.astype(jnp.float32)
                first += heads


def mix_kernel(expert_count, hot_capacity, own_ref, extended_ref, residual_ref, proj_ref, *refs):
    top_ref, total_ref, sum_ref = refs[0:3]
    mixed_ref, sent_refs = refs[-1 - expert_count], refs[len(refs) - expert_count :]
    packed_refs = refs[3 : -1 - expert_count]
    tok, width = mixed_ref.shape
    heads = top_ref.shape[0]
    scale = math.log2(math.e) / math.sqrt(HD)
    tops, totals = [top_ref[...]], [total_ref[...]]
    for packed_ref in packed_refs:
        pieces = [
            packed_ref[width + place * heads : width + (place + 1) * heads, :].astype(jnp.float32)
            for place in range(5)
        ]
        tops.append((pieces[0] + pieces[1]) + pieces[2])
        totals.append(pieces[3] + pieces[4])
    top = functools.reduce(jnp.maximum, tops)
    factors = [jnp.exp2((one - top) * scale) for one in tops]
    total = sum(one * factor for one, factor in zip(totals, factors))
    factors = [factor / total for factor in factors]
    pieces = []
    for head in range(heads):
        rows = slice(head * HD, (head + 1) * HD)
        piece = sum_ref[rows, :] * factors[0][head : head + 1, :]
        for packed_ref, factor in zip(packed_refs, factors[1:]):
            piece = piece + packed_ref[rows, :].astype(jnp.float32) * factor[head : head + 1, :]
        pieces.append(piece.astype(jnp.bfloat16))
    attended = jnp.concatenate(pieces, axis=0).T
    mixed = (residual_ref[...].astype(jnp.float32) + dot(attended, proj_ref[...])).astype(
        jnp.bfloat16
    )
    mixed_ref[...] = mixed
    mixed_f = mixed.astype(jnp.float32)
    inv_rms = lax.rsqrt(jnp.mean(mixed_f * mixed_f, axis=1, keepdims=True) + norm_eps)
    normed = (mixed_f * inv_rms).astype(jnp.bfloat16)
    placed = slot_matrix(chosen_of(extended_ref, tok), own_ref[0], len(sent_refs), hot_capacity)
    rows = dot(placed, normed).astype(jnp.bfloat16)
    for k, sent_ref in enumerate(sent_refs):
        sent_ref[...] = rows[k * hot_capacity : (k + 1) * hot_capacity]


def expert_kernel(
    reps,
    rep_list,
    sources,
    tok,
    strip,
    counts,
    own_ref,
    part_ref,
    up_ref,
    down_ref,
    extended_ref,
    *refs,
):
    row_count, grad_count = counts
    row_refs, refs = refs[:row_count], refs[row_count:]
    per_rep = row_count // len(rep_list)
    if rep_list == (0,) and per_rep == sources:
        row_refs = row_refs[:1] + row_refs[1:][::-1]
    grad_refs, refs = refs[:grad_count], refs[grad_count:]
    own_rows = rep_list[0] == 0
    held_ref, refs = refs[-1], refs[:-1]
    if own_rows:
        up_old, down_old, activated_ref, pre_grad_ref = refs[:4]
        term_refs, kept_ref = refs[4:-1], refs[-1]
    else:
        up_acc, down_acc = refs
    total_grads = sum(ref.shape[0] for ref in grad_refs)
    capacity = total_grads // (sources * reps)
    count = sources * capacity
    parts = part_ref.shape[0]
    up = up_ref[...]
    down = down_ref[...]
    router = router_of(extended_ref, tok, sources)
    expert_lane = lax.broadcasted_iota(jnp.int32, (count, router.shape[0]), 1) == own_ref[0]

    def strips(rows, place):
        held_ref[place] = rows.T
        taken = []
        for k in range(parts):
            first = pl.multiple_of(part_ref[k] * strip, strip)
            taken.append(held_ref[place, pl.ds(first, strip), :])
        return jnp.concatenate(taken, axis=0)

    up_term = down_term = None
    for place, rep in enumerate(rep_list):
        rows = chunk_rows(
            row_refs[place * per_rep : (place + 1) * per_rep], sources, 0, capacity
        )
        grads = chunk_rows(grad_refs, sources, rep * capacity, (rep + 1) * capacity)
        pre = dot(rows, up)
        sigmoid_pre = jax.nn.sigmoid(pre)
        activated = (pre * sigmoid_pre).astype(jnp.bfloat16)
        logits = dot(rows, router, NT)
        gate = jax.nn.sigmoid(
            jnp.sum(jnp.where(expert_lane, logits, 0.0), axis=1, keepdims=True)
        )
        scaled = (gate * grads.astype(jnp.float32)).astype(jnp.bfloat16)
        act_grad = dot(scaled, down, NT)
        pre_grad = (act_grad * sigmoid_pre * (1.0 + pre * (1.0 - sigmoid_pre))).astype(
            jnp.bfloat16
        )
        if own_rows:
            activated_ref[...] = activated
            pre_grad_ref[...] = pre_grad
        more_up = dot(strips(rows, 2 * place), pre_grad)
        more_down = dot(strips(activated, 2 * place + 1), scaled)
        up_term = more_up if up_term is None else up_term + more_up
        down_term = more_down if down_term is None else down_term + more_down
    if not own_rows:
        up_acc[...] = up_term
        down_acc[...] = down_term
        return
    up_term = up_term + up_old[...]
    down_term = down_term + down_old[...]
    for k, ref in enumerate((kept_ref, *term_refs)):
        rows = slice(k * strip, (k + 1) * strip)
        ref[0] = up_term[rows].astype(ref.dtype)
        ref[1] = down_term[rows].astype(ref.dtype)


def back_kernel(sources, up_ref, down_ref, activated_ref, pre_grad_ref, *back_refs):
    capacity = activated_ref.shape[0] // sources
    produced = dot(activated_ref[...], down_ref[...]).astype(jnp.bfloat16)
    token_grad = dot(pre_grad_ref[...], up_ref[...], NT).astype(jnp.bfloat16)
    for k, back_ref in enumerate(back_refs):
        rows = slice(k * capacity, (k + 1) * capacity)
        back_ref[0:capacity] = produced[rows]
        back_ref[capacity : 2 * capacity] = token_grad[rows]


def prepare_kernel(
    hot_capacity,
    expert_count,
    own_ref,
    mixed_ref,
    extended_ref,
    placed_ref,
    factors_ref,
    router_cols_ref,
):
    tok = mixed_ref.shape[0]
    choice = chosen_of(extended_ref, tok)
    placed = slot_matrix(choice, own_ref[0], expert_count, hot_capacity)
    placed_ref[...] = placed.T
    router = router_of(extended_ref, tok, expert_count)
    mixed_f = mixed_ref[...].astype(jnp.float32)
    inv_rms = lax.rsqrt(jnp.mean(mixed_f * mixed_f, axis=1, keepdims=True) + norm_eps)
    normed = (mixed_f * inv_rms).astype(jnp.bfloat16)
    one_hot = lax.broadcasted_iota(jnp.int32, (expert_count, tok), 0) == choice
    logits = dot(router, normed, NT)
    logit_row = jnp.sum(jnp.where(one_hot, logits, 0.0), axis=0, keepdims=True)
    gate = jax.nn.sigmoid(jnp.broadcast_to(logit_row, (8, tok)).T[:, 0:1])
    lane = lax.broadcasted_iota(jnp.int32, factors_ref.shape, 1)
    factors_ref[...] = jnp.where(lane == 0, inv_rms, gate)
    router_cols_ref[...] = dot(one_hot.astype(jnp.float32).astype(jnp.bfloat16), router, TN)


def finish_kernel(
    hot_capacity,
    parts,
    placed_ref,
    factors_ref,
    router_cols_ref,
    mixed_ref,
    extended_ref,
    *refs,
):
    refs, (layer_ref, grad_mixed_ref, *share_refs) = refs[:-4], refs[-4:]
    (kept_ref, *term_refs), back_refs = refs[:parts], refs[parts:][::-1]
    for kind, share_ref in enumerate(share_refs):
        total = kept_ref[kind]
        for ref in term_refs:
            total = total + ref[kind].astype(jnp.float32)
        share_ref[...] = total
    tok = mixed_ref.shape[0]
    mixed_f = mixed_ref[...].astype(jnp.float32)
    inv_rms = factors_ref[:, 0:1]
    gate = factors_ref[:, 1:2]
    pair = 2 * hot_capacity
    chunks = [
        ref[first : first + pair] for ref in back_refs for first in range(0, ref.shape[0], pair)
    ]
    results = jnp.concatenate([chunk[:hot_capacity] for chunk in chunks], axis=0)
    grads = jnp.concatenate([chunk[hot_capacity:] for chunk in chunks], axis=0)
    placed = placed_ref[...]
    result_f = dot(placed, results)
    normed_grad = dot(placed, grads)
    grad_f = extended_ref[0:tok, :].astype(jnp.float32)
    layer_ref[...] = (mixed_f + gate * result_f).astype(jnp.bfloat16)
    gate_grad = jnp.sum(grad_f * result_f, axis=1, keepdims=True)
    logit_grad = gate_grad * gate * (1.0 - gate)
    total_grad = normed_grad + logit_grad * router_cols_ref[...]
    mean_term = jnp.mean(total_grad * mixed_f, axis=1, keepdims=True)
    input_grad = inv_rms * total_grad - mixed_f * inv_rms * inv_rms * inv_rms * mean_term
    grad_mixed_ref[...] = (grad_f + input_grad).astype(jnp.bfloat16)


def shape(dims, dtype=jnp.bfloat16):
    return jax.ShapeDtypeStruct(dims, dtype)


SMEM = pl.BlockSpec(memory_space=pltpu.SMEM)
VMEM = pl.BlockSpec(memory_space=pltpu.VMEM)
HBM = pl.BlockSpec(memory_space=pltpu.HBM)


def call(body, out_shape, specs, scratch=(), cost=0.5):
    return pl.pallas_call(
        body,
        cost_estimate=pl.CostEstimate(
            flops=int(cost * 1e9), bytes_accessed=0, transcendentals=0
        ),
        out_shape=out_shape,
        in_specs=specs,
        out_specs=jax.tree.map(lambda unused: VMEM, out_shape),
        scratch_shapes=list(scratch),
        compiler_params=pltpu.CompilerParams(vmem_limit_bytes=VMEM_LIMIT),
    )


def local(
    seq_count,
    expert_count,
    rep_count,
    query_rows,
    key_rows,
    value_rows,
    doc_lengths,
    residual,
    out_proj,
    router,
    expert_choice,
    weight_in,
    weight_out,
    grad_out,
):
    tok, width = query_rows.shape[1:]
    hidden = weight_in.shape[2]
    heads = width // HD
    experts = Group(("expert",), (expert_count,))
    reps = Group(("rep",), (rep_count,))
    owners = Group(("expert", "rep"), (expert_count, rep_count))
    parts = Group(("seq",), (seq_count,))
    strip = width // (seq_count * rep_count)
    capacity = max(2, (3 * tok + 2 * expert_count - 1) // (2 * expert_count))
    hot_capacity = min(4 * capacity, tok // 2)
    choice = expert_choice.reshape(1, tok)
    seq_index = lax.axis_index("seq")
    rep_index = lax.axis_index("rep")
    rank = seq_index * rep_count + rep_index
    own = jnp.stack([lax.axis_index("expert")]).astype(jnp.int32)
    part_to = jnp.stack(
        [parts.target(seq_index, k) * rep_count + rep_index for k in range(seq_count)]
    ).astype(jnp.int32)

    def forward(array):
        return lax.ppermute(array, "seq", [(i, (i + 1) % seq_count) for i in range(seq_count)])

    reach = (seq_count + 1) // 2
    longest = (seq_count * rep_count + 1) // 2
    query_ranks = [
        seq_index * rep_count + reps.source(rep_index, k) for k in range(rep_count)
    ]

    def task_ids(plan, steps):
        ids = list(query_ranks)
        for k, pair, unused_first in plan:
            block = rank - steps[pair] * rep_count
            behind = query_ranks[k] - block
            ids.append(jnp.where((block >= 0) & (behind >= 0) & (behind <= longest), block, -1))
        return jnp.stack(ids).astype(jnp.int32)

    state_shapes = [
        shape((heads, tok), jnp.float32),
        shape((heads, tok), jnp.float32),
        shape((width, tok), jnp.float32),
    ]
    tail = 16 + -(-expert_count // 16) * 16
    extended, begin = call(
        extend_kernel,
        [shape((tok + tail, width)), shape((rep_count, tok), jnp.int32)],
        [SMEM, SMEM] + [VMEM] * 3,
    )(
        jnp.stack(query_ranks).astype(jnp.int32), doc_lengths, choice, router.T, grad_out[0]
    )

    def attend(plan, pairs, steps, queries, states, packed, cost, ahead=()):
        ks = sorted({k for k, unused_pair, unused_first in plan})
        old = [one for k in ks if k in states for one in states[k]]
        state_out = state_shapes * len(ks)
        if packed:
            out_shape = [shape((width + 5 * heads, tok))] * len(ks)
            scratch = [pltpu.VMEM(one.shape, one.dtype) for one in state_out]
        else:
            out_shape, scratch = state_out, []
        outs = call(
            functools.partial(
                attend_kernel, plan, rep_count, len(pairs), packed, len(ahead)
            ),
            out_shape,
            [SMEM] + [VMEM] * (1 + len(ks) + len(ahead) + 2 * len(pairs) + len(old)),
            scratch + [pltpu.VMEM((len(plan), tok, tok), jnp.float32)],
            cost=cost,
        )(task_ids(plan, steps), begin, *[queries[k] for k in ks], *ahead, *[one for both in pairs for one in both], *old)
        if packed:
            return dict(zip(ks, outs))
        return {k: list(outs[3 * place : 3 * place + 3]) for place, k in enumerate(ks)}

    others = range(1, rep_count)
    lines = [(key_rows[0], value_rows[0])]
    lines.append(tuple(forward(one) for one in lines[0]))
    queries = reps.exchange([query_rows[0]] * rep_count)
    extendeds = reps.exchange([extended] * rep_count)
    states = attend(((0, 0, True),), lines[:1], [0], queries, {}, False, 2.0)
    ahead, *states[0] = lax.optimization_barrier((lines[1][0], *states[0]))
    lines[1] = (ahead, lines[1][1])
    for unused in range(1, reach):
        lines.append(tuple(forward(one) for one in lines[-1]))
    own_state = states
    middle = tuple((k, step, step == 0) for k in others for step in range(reach))
    states = attend(middle, lines[:-1], list(range(reach)), queries, {}, False, 3.0)
    states[1][0], *extendeds[1:] = lax.optimization_barrier((states[1][0], *extendeds[1:]))
    sent_grads = call(
        functools.partial(dispatch_kernel, rep_count, tok, hot_capacity),
        [shape((rep_count * hot_capacity, width))] * expert_count,
        [SMEM] + [VMEM] * rep_count,
    )(own, *extendeds)
    partial = attend(
        tuple((k, 0, False) for k in others),
        lines[-1:],
        [reach],
        queries,
        states,
        True,
        1.5,
        ahead=sent_grads[:1],
    )
    returned = reps.exchange([None] + [partial[k] for k in others], inverse=True)[1:]
    states = attend(
        tuple((0, step, False) for step in range(reach)),
        lines[1:],
        list(range(1, reach + 1)),
        queries,
        own_state,
        False,
        1.5,
    )
    got_grads = merged(experts.exchange(sent_grads), MOST_PERMUTES)

    mixed, *sent_rows = call(
        functools.partial(mix_kernel, expert_count, hot_capacity),
        [shape((tok, width))] + [shape((hot_capacity, width))] * expert_count,
        [SMEM] + [VMEM] * (6 + len(returned)),
        cost=2.0,
    )(own, extendeds[0], residual[0], out_proj, *states[0], *returned)
    arrived = owners.exchange([sent_rows[k // rep_count] for k in range(owners.count)])
    got_rows = merged(arrived[0::rep_count], MOST_PERMUTES)
    got_more = [
        one for k in others for one in merged(arrived[k::rep_count], MOST_PERMUTES)
    ]

    def expert_call(rep_list, rows, out_shape, extra):
        return call(
            functools.partial(
                expert_kernel,
                rep_count,
                rep_list,
                expert_count,
                tok,
                strip,
                (len(rows), len(got_grads)),
            ),
            out_shape,
            [SMEM, SMEM] + [VMEM] * (3 + len(rows) + len(got_grads) + len(extra)),
            [pltpu.VMEM((2 * len(rep_list), width, expert_count * hot_capacity), jnp.bfloat16)],
            cost=2.0,
        )(own, part_to, weight_in[0], weight_out[0], extendeds[0], *rows, *got_grads, *extra)

    slots = expert_count * hot_capacity
    sums = expert_call(
        tuple(others),
        got_more,
        [
            shape((seq_count * strip, hidden), jnp.float32),
            shape((seq_count * strip, width), jnp.float32),
        ],
        [],
    )
    activated, pre_grad, *terms, kept = expert_call(
        (0,),
        got_rows[:1] + got_rows[1:][::-1],
        [shape((slots, hidden))] * 2
        + [shape((2, strip, hidden))] * (seq_count - 1)
        + [shape((2, strip, hidden), jnp.float32)],
        list(sums),
    )
    got_terms = parts.exchange([None] + terms)[1:]
    activated, mixed, kept = lax.optimization_barrier((activated, mixed, kept))
    back = call(
        functools.partial(back_kernel, expert_count),
        [shape((2 * hot_capacity, width))] * expert_count,
        [VMEM] * 4,
        cost=1.0,
    )(weight_in[0], weight_out[0], activated, pre_grad)
    got_back = merged(experts.exchange(back, inverse=True), MOST_PERMUTES)
    prepared = call(
        functools.partial(prepare_kernel, hot_capacity, expert_count),
        [
            shape((tok, slots)),
            shape((tok, 128), jnp.float32),
            shape((tok, width), jnp.float32),
        ],
        [SMEM, VMEM, VMEM],
        cost=1.0,
    )(own, mixed, extended)
    layer_out, grad_mixed, share_in, share_out = call(
        functools.partial(finish_kernel, hot_capacity, seq_count),
        [
            shape((tok, width)),
            shape((tok, width)),
            shape((strip, hidden), jnp.float32),
            shape((strip, width), jnp.float32),
        ],
        [VMEM] * (5 + seq_count + len(got_back)),
        cost=1.0,
    )(*prepared, mixed, extended, kept, *got_terms[::-1], *got_back[::-1])
    return (layer_out[None], grad_mixed[None], share_in[None], share_out[None])


def solution(mesh):
    rows = P("expert", ("seq", "rep"), None)
    in_specs = (
        rows,
        rows,
        rows,
        P("expert", None),
        rows,
        P(),
        P(),
        rows,
        P("expert", None, None),
        P("expert", None, None),
        rows,
    )
    body = functools.partial(
        local, mesh.shape["seq"], mesh.shape["expert"], mesh.shape["rep"]
    )
    return jax.shard_map(
        body, mesh=mesh, in_specs=in_specs, out_specs=(rows, rows, rows, rows), check_vma=False
    )
```

```python
import functools
import math

import jax
import jax.numpy as jnp
from jax import lax
from jax.experimental import pallas as pl
from jax.experimental.pallas import tpu as pltpu
from jax.sharding import PartitionSpec as P

HD = 32
norm_eps = 1e-06
masked_score = -1e30
VMEM_LIMIT = 48 * 1024 * 1024
MOST_PERMUTES = 16
NT = (((1,), (1,)), ((), ()))
TN = (((0,), (0,)), ((), ()))


def dot(a, b, dims=None):
    if dims is None:
        return jnp.dot(a, b, preferred_element_type=jnp.float32)
    return lax.dot_general(a, b, dims, preferred_element_type=jnp.float32)


def away(index, offset, size):
    if size & (size - 1) == 0:
        return index ^ offset
    return (index + offset) % size


def back_from(index, offset, size):
    if size & (size - 1) == 0:
        return index ^ offset
    return (index - offset + size) % size


class Group:
    def __init__(self, axes, sizes):
        self.axes, self.sizes = tuple(axes), tuple(sizes)
        self.count = math.prod(sizes)

    def split(self, flat):
        coords = []
        for size in reversed(self.sizes):
            coords.append(flat % size)
            flat = flat // size
        return coords[::-1]

    def moved(self, flat, offset, step):
        place = 0
        for coord, part, size in zip(self.split(flat), self.split(offset), self.sizes):
            place = place * size + step(coord, part, size)
        return place

    def target(self, flat, offset):
        return self.moved(flat, offset, away)

    def source(self, flat, offset):
        return self.moved(flat, offset, back_from)

    def exchange(self, chunks, inverse=False):
        to, start = (self.source, self.target) if inverse else (self.target, self.source)
        if self.count <= MOST_PERMUTES:
            order = sorted(range(1, self.count), key=lambda k: -k)
            got = {0: chunks[0]}
            for k in order:
                pairs = [(i, to(i, k)) for i in range(self.count)]
                got[k] = lax.ppermute(chunks[k], self.axes, pairs)
            return [got[k] for k in range(self.count)]
        me = lax.axis_index(self.axes)
        steps = jnp.arange(self.count, dtype=jnp.int32)
        sent_to = jax.vmap(lambda k: to(me, k))(steps)
        placed = jnp.zeros((self.count,), jnp.int32).at[sent_to].set(steps)
        stacked = jnp.stack(chunks)[placed]
        got = lax.all_to_all(stacked, self.axes, split_axis=0, concat_axis=0, tiled=True)
        came_from = jax.vmap(lambda k: start(me, k))(steps)
        ordered = got[came_from]
        return [ordered[k] for k in range(self.count)]


def merged(chunks, most):
    if len(chunks) <= most:
        return list(chunks)
    return [jnp.concatenate(chunks, axis=0)]


def chunk_rows(refs, count, low, high):
    size = sum(ref.shape[0] for ref in refs) // count
    parts = []
    for chunk in range(count):
        ref, first = (refs[chunk], 0) if len(refs) == count else (refs[0], chunk * size)
        parts.append(ref[first + low : first + high, :])
    return parts[0] if count == 1 else jnp.concatenate(parts, axis=0)


def slot_matrix(choice, own, expert_count, hot_capacity):
    tok = choice.shape[1]
    offset = back_from(choice, own, expert_count)
    one_hot = lax.broadcasted_iota(jnp.int32, (expert_count, tok), 0) == offset
    hits = one_hot.astype(jnp.float32).astype(jnp.bfloat16)
    earlier = lax.broadcasted_iota(jnp.int32, (tok, tok), 0) <= lax.broadcasted_iota(
        jnp.int32, (tok, tok), 1
    )
    counted = dot(hits, earlier.astype(jnp.float32).astype(jnp.bfloat16))
    rank = jnp.sum(jnp.where(one_hot, counted, 0.0), axis=0, keepdims=True) - 1.0
    slots = offset * hot_capacity + rank.astype(jnp.int32)
    rows = lax.broadcasted_iota(jnp.int32, (expert_count * hot_capacity, tok), 0)
    return (rows == slots).astype(jnp.float32).astype(jnp.bfloat16)


def extend_kernel(
    ranks_ref, lengths_ref, choice_ref, router_ref, grad_ref, extended_ref, begin_ref
):
    tok, width = grad_ref.shape
    extended_ref[0:tok, :] = grad_ref[...]
    chosen = jnp.broadcast_to(choice_ref[...].astype(jnp.float32), (16, tok))
    extended_ref[tok : tok + 16, 0:tok] = chosen.astype(jnp.bfloat16)
    extended_ref[tok : tok + 16, tok:width] = jnp.zeros((16, width - tok), jnp.bfloat16)
    routed = router_ref[...].astype(jnp.float32)
    spare = extended_ref.shape[0] - tok - 16 - routed.shape[0]
    if spare:
        routed = jnp.concatenate([routed, jnp.zeros((spare, width), jnp.float32)], axis=0)
    extended_ref[tok + 16 :, :] = routed.astype(jnp.bfloat16)
    for k in range(begin_ref.shape[0]):
        position = ranks_ref[k] * tok + lax.broadcasted_iota(jnp.int32, (1, tok), 1)
        begin = jnp.zeros((1, tok), jnp.int32)
        bound = jnp.int32(0)
        for doc in range(lengths_ref.shape[1] - 1):
            bound = bound + lengths_ref[0, doc]
            begin = jnp.maximum(begin, jnp.where(position >= bound, bound, 0))
        begin_ref[k : k + 1, :] = begin


def chosen_of(extended_ref, tok):
    return extended_ref[tok : tok + 16, 0:tok].astype(jnp.float32)[0:1].astype(jnp.int32)


def router_of(extended_ref, tok, expert_count):
    whole = extended_ref[tok + 16 :, :].astype(jnp.float32)
    return whole[0:expert_count].astype(jnp.bfloat16)


def dispatch_kernel(reps, tok, hot_capacity, own_ref, *refs):
    extended_refs, sent_refs = refs[:reps], refs[reps:]
    for rep in range(reps):
        choice = chosen_of(extended_refs[rep], tok)
        placed = slot_matrix(choice, own_ref[0], len(sent_refs), hot_capacity)
        rows = dot(placed, extended_refs[rep][0:tok, :]).astype(jnp.bfloat16)
        for k, sent_ref in enumerate(sent_refs):
            sent_ref[rep * hot_capacity : (rep + 1) * hot_capacity] = rows[
                k * hot_capacity : (k + 1) * hot_capacity
            ]


def fold_blocks(ids_ref, begin_ref, tasks, reps, states, bias_ref):
    lanes = 128
    per = lanes // HD
    scale = math.log2(math.e) / math.sqrt(HD)
    spreads = {}
    lowest = {}
    for k, query_ref, unused_pair, unused_first in tasks:
        if k in spreads:
            continue
        lowest[k] = jnp.min(begin_ref[k : k + 1, :])
        tok = begin_ref.shape[1]
        turned = query_ref[...].T
        head_of_row = lax.broadcasted_iota(jnp.int32, (lanes, tok), 0) // HD
        spreads[k] = []
        for group in range(turned.shape[0] // lanes):
            part = turned[group * lanes : (group + 1) * lanes]
            spreads[k].append(
                jnp.concatenate(
                    [
                        jnp.where(head_of_row == head, part, jnp.zeros_like(part))
                        for head in range(per)
                    ],
                    axis=1,
                )
            )

    def fold(place, k, pair_ref, block, begin, fresh):
        top_ref, total_ref, sum_ref = states[k]
        tok = begin.shape[1]
        position = ids_ref[k] * tok + lax.broadcasted_iota(jnp.int32, (1, tok), 1)
        key_position = block * tok + lax.broadcasted_iota(jnp.int32, (tok, tok), 0)
        visible = (key_position >= begin) & (key_position <= position)
        bias_ref[place] = jnp.where(visible, 0.0, masked_score)
        bias = bias_ref[place]
        key_ref, value_ref = pair_ref
        values = value_ref[...].T
        for group, spread in enumerate(spreads[k]):
            columns = slice(group * lanes, (group + 1) * lanes)
            scores = dot(key_ref[:, columns], spread)
            weights, factors = [], []
            for head in range(per):
                row = group * per + head
                part = scores[:, head * tok : (head + 1) * tok] + bias
                top = jnp.max(part, axis=0, keepdims=True)
                if not fresh:
                    old = top_ref[row : row + 1, :]
                    top = jnp.maximum(top, old)
                    factors.append(jnp.exp2((old - top) * scale))
                weight = jnp.exp2((part - top) * scale)
                total = jnp.sum(weight, axis=0, keepdims=True)
                if not fresh:
                    total = total + total_ref[row : row + 1, :] * factors[head]
                top_ref[row : row + 1, :] = top
                total_ref[row : row + 1, :] = total
                weights.append(weight.astype(jnp.bfloat16))
            summed = dot(values[columns], jnp.concatenate(weights, axis=1))
            for head in range(per):
                rows = slice((group * per + head) * HD, (group * per + head + 1) * HD)
                piece = summed[head * HD : (head + 1) * HD, head * tok : (head + 1) * tok]
                if not fresh:
                    piece = piece + sum_ref[rows, :] * factors[head]
                sum_ref[rows, :] = piece

    for place, (k, unused_query, pair_ref, first) in enumerate(tasks):
        block = ids_ref[reps + place]
        begin = begin_ref[k : k + 1, :]
        tok = begin.shape[1]
        if first and k == 0:
            fold(place, k, pair_ref, block, begin, True)
            continue
        if first:
            top_ref, total_ref, sum_ref = states[k]
            top_ref[...] = jnp.full(top_ref.shape, masked_score, jnp.float32)
            total_ref[...] = jnp.zeros(total_ref.shape, jnp.float32)
            sum_ref[...] = jnp.zeros(sum_ref.shape, jnp.float32)

        @pl.when((block >= 0) & ((block + 1) * tok > lowest[k]))
        def unused(place=place, k=k, pair_ref=pair_ref, block=block, begin=begin):
            fold(place, k, pair_ref, block, begin, False)


def attend_kernel(plan, reps, counts, packed, ahead, ids_ref, begin_ref, *refs):
    ks = sorted({k for k, unused_pair, unused_first in plan})
    old_ks = [k for k in ks if not any(first for j, unused_pair, first in plan if j == k)]
    query_refs, refs = dict(zip(ks, refs)), refs[len(ks) + ahead :]
    pair_refs = [refs[2 * place : 2 * place + 2] for place in range(counts)]
    refs = refs[2 * counts :]
    old_refs, refs = refs[: 3 * len(old_ks)], refs[3 * len(old_ks) :]
    bias_ref, refs = refs[-1], refs[:-1]
    packed_refs, state_refs = (refs[: len(ks)], refs[len(ks) :]) if packed else ((), refs)
    states = {k: state_refs[3 * place : 3 * place + 3] for place, k in enumerate(ks)}
    for place, k in enumerate(old_ks):
        for old_ref, new_ref in zip(old_refs[3 * place : 3 * place + 3], states[k]):
            new_ref[...] = old_ref[...]
    tasks = [(k, query_refs[k], pair_refs[pair], first) for k, pair, first in plan]
    fold_blocks(ids_ref, begin_ref, tasks, reps, states, bias_ref)
    for k, packed_ref in zip(ks, packed_refs):
        top_ref, total_ref, sum_ref = states[k]
        heads, width = top_ref.shape[0], sum_ref.shape[0]
        packed_ref[0:width, :] = sum_ref[...].astype(jnp.bfloat16)
        first = width
        for ref, pieces in ((top_ref, 3), (total_ref, 2)):
            rest = ref[...]
            for unused in range(pieces):
                piece = rest.astype(jnp.bfloat16)
                packed_ref[first : first + heads, :] = piece
                rest = rest - piece.astype(jnp.float32)
                first += heads


def mix_kernel(expert_count, hot_capacity, own_ref, extended_ref, residual_ref, proj_ref, *refs):
    top_ref, total_ref, sum_ref = refs[0:3]
    mixed_ref, sent_refs = refs[-1 - expert_count], refs[len(refs) - expert_count :]
    packed_refs = refs[3 : -1 - expert_count]
    tok, width = mixed_ref.shape
    heads = top_ref.shape[0]
    scale = math.log2(math.e) / math.sqrt(HD)
    tops, totals = [top_ref[...]], [total_ref[...]]
    for packed_ref in packed_refs:
        pieces = [
            packed_ref[width + place * heads : width + (place + 1) * heads, :].astype(jnp.float32)
            for place in range(5)
        ]
        tops.append((pieces[0] + pieces[1]) + pieces[2])
        totals.append(pieces[3] + pieces[4])
    top = functools.reduce(jnp.maximum, tops)
    factors = [jnp.exp2((one - top) * scale) for one in tops]
    total = sum(one * factor for one, factor in zip(totals, factors))
    factors = [factor / total for factor in factors]
    pieces = []
    for head in range(heads):
        rows = slice(head * HD, (head + 1) * HD)
        piece = sum_ref[rows, :] * factors[0][head : head + 1, :]
        for packed_ref, factor in zip(packed_refs, factors[1:]):
            piece = piece + packed_ref[rows, :].astype(jnp.float32) * factor[head : head + 1, :]
        pieces.append(piece.astype(jnp.bfloat16))
    attended = jnp.concatenate(pieces, axis=0).T
    mixed = (residual_ref[...].astype(jnp.float32) + dot(attended, proj_ref[...])).astype(
        jnp.bfloat16
    )
    mixed_ref[...] = mixed
    mixed_f = mixed.astype(jnp.float32)
    inv_rms = lax.rsqrt(jnp.mean(mixed_f * mixed_f, axis=1, keepdims=True) + norm_eps)
    normed = (mixed_f * inv_rms).astype(jnp.bfloat16)
    placed = slot_matrix(chosen_of(extended_ref, tok), own_ref[0], len(sent_refs), hot_capacity)
    rows = dot(placed, normed).astype(jnp.bfloat16)
    for k, sent_ref in enumerate(sent_refs):
        sent_ref[...] = rows[k * hot_capacity : (k + 1) * hot_capacity]


def expert_kernel(
    reps,
    rep_list,
    sources,
    tok,
    strip,
    counts,
    own_ref,
    part_ref,
    up_ref,
    down_ref,
    extended_ref,
    *refs,
):
    row_count, grad_count = counts
    row_refs, refs = refs[:row_count], refs[row_count:]
    per_rep = row_count // len(rep_list)
    if rep_list == (0,) and per_rep == sources:
        row_refs = row_refs[:1] + row_refs[1:][::-1]
    grad_refs, refs = refs[:grad_count], refs[grad_count:]
    own_rows = rep_list[0] == 0
    held_ref, refs = refs[-1], refs[:-1]
    if own_rows:
        up_old, down_old, activated_ref, pre_grad_ref = refs[:4]
        term_refs, kept_ref = refs[4:-1], refs[-1]
    else:
        up_acc, down_acc = refs
    total_grads = sum(ref.shape[0] for ref in grad_refs)
    capacity = total_grads // (sources * reps)
    count = sources * capacity
    parts = part_ref.shape[0]
    up = up_ref[...]
    down = down_ref[...]
    router = router_of(extended_ref, tok, sources)
    expert_lane = lax.broadcasted_iota(jnp.int32, (count, router.shape[0]), 1) == own_ref[0]

    def strips(rows, place):
        held_ref[place] = rows.T
        taken = []
        for k in range(parts):
            first = pl.multiple_of(part_ref[k] * strip, strip)
            taken.append(held_ref[place, pl.ds(first, strip), :])
        return jnp.concatenate(taken, axis=0)

    up_term = down_term = None
    for place, rep in enumerate(rep_list):
        rows = chunk_rows(
            row_refs[place * per_rep : (place + 1) * per_rep], sources, 0, capacity
        )
        grads = chunk_rows(grad_refs, sources, rep * capacity, (rep + 1) * capacity)
        pre = dot(rows, up)
        sigmoid_pre = jax.nn.sigmoid(pre)
        activated = (pre * sigmoid_pre).astype(jnp.bfloat16)
        logits = dot(rows, router, NT)
        gate = jax.nn.sigmoid(
            jnp.sum(jnp.where(expert_lane, logits, 0.0), axis=1, keepdims=True)
        )
        scaled = (gate * grads.astype(jnp.float32)).astype(jnp.bfloat16)
        act_grad = dot(scaled, down, NT)
        pre_grad = (act_grad * sigmoid_pre * (1.0 + pre * (1.0 - sigmoid_pre))).astype(
            jnp.bfloat16
        )
        if own_rows:
            activated_ref[...] = activated
            pre_grad_ref[...] = pre_grad
        more_up = dot(strips(rows, 2 * place), pre_grad)
        more_down = dot(strips(activated, 2 * place + 1), scaled)
        up_term = more_up if up_term is None else up_term + more_up
        down_term = more_down if down_term is None else down_term + more_down
    if not own_rows:
        up_acc[...] = up_term
        down_acc[...] = down_term
        return
    up_term = up_term + up_old[...]
    down_term = down_term + down_old[...]
    for k, ref in enumerate((kept_ref, *term_refs)):
        rows = slice(k * strip, (k + 1) * strip)
        ref[0] = up_term[rows].astype(ref.dtype)
        ref[1] = down_term[rows].astype(ref.dtype)


def back_kernel(sources, up_ref, down_ref, activated_ref, pre_grad_ref, *back_refs):
    capacity = activated_ref.shape[0] // sources
    produced = dot(activated_ref[...], down_ref[...]).astype(jnp.bfloat16)
    token_grad = dot(pre_grad_ref[...], up_ref[...], NT).astype(jnp.bfloat16)
    for k, back_ref in enumerate(back_refs):
        rows = slice(k * capacity, (k + 1) * capacity)
        back_ref[0:capacity] = produced[rows]
        back_ref[capacity : 2 * capacity] = token_grad[rows]


def prepare_kernel(
    hot_capacity,
    expert_count,
    own_ref,
    mixed_ref,
    extended_ref,
    placed_ref,
    factors_ref,
    router_cols_ref,
):
    tok = mixed_ref.shape[0]
    choice = chosen_of(extended_ref, tok)
    placed = slot_matrix(choice, own_ref[0], expert_count, hot_capacity)
    placed_ref[...] = placed.T
    router = router_of(extended_ref, tok, expert_count)
    mixed_f = mixed_ref[...].astype(jnp.float32)
    inv_rms = lax.rsqrt(jnp.mean(mixed_f * mixed_f, axis=1, keepdims=True) + norm_eps)
    normed = (mixed_f * inv_rms).astype(jnp.bfloat16)
    one_hot = lax.broadcasted_iota(jnp.int32, (expert_count, tok), 0) == choice
    logits = dot(router, normed, NT)
    logit_row = jnp.sum(jnp.where(one_hot, logits, 0.0), axis=0, keepdims=True)
    gate = jax.nn.sigmoid(jnp.broadcast_to(logit_row, (8, tok)).T[:, 0:1])
    lane = lax.broadcasted_iota(jnp.int32, factors_ref.shape, 1)
    factors_ref[...] = jnp.where(lane == 0, inv_rms, gate)
    router_cols_ref[...] = dot(one_hot.astype(jnp.float32).astype(jnp.bfloat16), router, TN)


def finish_kernel(
    hot_capacity,
    parts,
    placed_ref,
    factors_ref,
    router_cols_ref,
    mixed_ref,
    extended_ref,
    *refs,
):
    refs, (layer_ref, grad_mixed_ref, *share_refs) = refs[:-4], refs[-4:]
    (kept_ref, *term_refs), back_refs = refs[:parts], refs[parts:][::-1]
    for kind, share_ref in enumerate(share_refs):
        total = kept_ref[kind]
        for ref in term_refs:
            total = total + ref[kind].astype(jnp.float32)
        share_ref[...] = total
    tok = mixed_ref.shape[0]
    mixed_f = mixed_ref[...].astype(jnp.float32)
    inv_rms = factors_ref[:, 0:1]
    gate = factors_ref[:, 1:2]
    pair = 2 * hot_capacity
    chunks = [
        ref[first : first + pair] for ref in back_refs for first in range(0, ref.shape[0], pair)
    ]
    results = jnp.concatenate([chunk[:hot_capacity] for chunk in chunks], axis=0)
    grads = jnp.concatenate([chunk[hot_capacity:] for chunk in chunks], axis=0)
    placed = placed_ref[...]
    result_f = dot(placed, results)
    normed_grad = dot(placed, grads)
    grad_f = extended_ref[0:tok, :].astype(jnp.float32)
    layer_ref[...] = (mixed_f + gate * result_f).astype(jnp.bfloat16)
    gate_grad = jnp.sum(grad_f * result_f, axis=1, keepdims=True)
    logit_grad = gate_grad * gate * (1.0 - gate)
    total_grad = normed_grad + logit_grad * router_cols_ref[...]
    mean_term = jnp.mean(total_grad * mixed_f, axis=1, keepdims=True)
    input_grad = inv_rms * total_grad - mixed_f * inv_rms * inv_rms * inv_rms * mean_term
    grad_mixed_ref[...] = (grad_f + input_grad).astype(jnp.bfloat16)


def shape(dims, dtype=jnp.bfloat16):
    return jax.ShapeDtypeStruct(dims, dtype)


SMEM = pl.BlockSpec(memory_space=pltpu.SMEM)
VMEM = pl.BlockSpec(memory_space=pltpu.VMEM)
HBM = pl.BlockSpec(memory_space=pltpu.HBM)


def call(body, out_shape, specs, scratch=(), cost=0.5):
    return pl.pallas_call(
        body,
        cost_estimate=pl.CostEstimate(
            flops=int(cost * 1e9), bytes_accessed=0, transcendentals=0
        ),
        out_shape=out_shape,
        in_specs=specs,
        out_specs=jax.tree.map(lambda unused: VMEM, out_shape),
        scratch_shapes=list(scratch),
        compiler_params=pltpu.CompilerParams(vmem_limit_bytes=VMEM_LIMIT),
    )


def local(
    seq_count,
    expert_count,
    rep_count,
    query_rows,
    key_rows,
    value_rows,
    doc_lengths,
    residual,
    out_proj,
    router,
    expert_choice,
    weight_in,
    weight_out,
    grad_out,
):
    tok, width = query_rows.shape[1:]
    hidden = weight_in.shape[2]
    heads = width // HD
    experts = Group(("expert",), (expert_count,))
    reps = Group(("rep",), (rep_count,))
    owners = Group(("expert", "rep"), (expert_count, rep_count))
    parts = Group(("seq",), (seq_count,))
    strip = width // (seq_count * rep_count)
    capacity = max(2, (3 * tok + 2 * expert_count - 1) // (2 * expert_count))
    hot_capacity = min(4 * capacity, tok // 2)
    choice = expert_choice.reshape(1, tok)
    seq_index = lax.axis_index("seq")
    rep_index = lax.axis_index("rep")
    rank = seq_index * rep_count + rep_index
    own = jnp.stack([lax.axis_index("expert")]).astype(jnp.int32)
    part_to = jnp.stack(
        [parts.target(seq_index, k) * rep_count + rep_index for k in range(seq_count)]
    ).astype(jnp.int32)

    def forward(array):
        return lax.ppermute(array, "seq", [(i, (i + 1) % seq_count) for i in range(seq_count)])

    reach = (seq_count + 1) // 2
    longest = (seq_count * rep_count + 1) // 2
    query_ranks = [
        seq_index * rep_count + reps.source(rep_index, k) for k in range(rep_count)
    ]

    def task_ids(plan, steps):
        ids = list(query_ranks)
        for k, pair, unused_first in plan:
            block = rank - steps[pair] * rep_count
            behind = query_ranks[k] - block
            ids.append(jnp.where((block >= 0) & (behind >= 0) & (behind <= longest), block, -1))
        return jnp.stack(ids).astype(jnp.int32)

    state_shapes = [
        shape((heads, tok), jnp.float32),
        shape((heads, tok), jnp.float32),
        shape((width, tok), jnp.float32),
    ]
    tail = 16 + -(-expert_count // 16) * 16
    extended, begin = call(
        extend_kernel,
        [shape((tok + tail, width)), shape((rep_count, tok), jnp.int32)],
        [SMEM, SMEM] + [VMEM] * 3,
    )(
        jnp.stack(query_ranks).astype(jnp.int32), doc_lengths, choice, router.T, grad_out[0]
    )

    def attend(plan, pairs, steps, queries, states, packed, cost, ahead=()):
        ks = sorted({k for k, unused_pair, unused_first in plan})
        old = [one for k in ks if k in states for one in states[k]]
        state_out = state_shapes * len(ks)
        if packed:
            out_shape = [shape((width + 5 * heads, tok))] * len(ks)
            scratch = [pltpu.VMEM(one.shape, one.dtype) for one in state_out]
        else:
            out_shape, scratch = state_out, []
        outs = call(
            functools.partial(
                attend_kernel, plan, rep_count, len(pairs), packed, len(ahead)
            ),
            out_shape,
            [SMEM] + [VMEM] * (1 + len(ks) + len(ahead) + 2 * len(pairs) + len(old)),
            scratch + [pltpu.VMEM((len(plan), tok, tok), jnp.float32)],
            cost=cost,
        )(task_ids(plan, steps), begin, *[queries[k] for k in ks], *ahead, *[one for both in pairs for one in both], *old)
        if packed:
            return dict(zip(ks, outs))
        return {k: list(outs[3 * place : 3 * place + 3]) for place, k in enumerate(ks)}

    others = range(1, rep_count)
    lines = [(key_rows[0], value_rows[0])]
    lines.append(tuple(forward(one) for one in lines[0]))
    queries = reps.exchange([query_rows[0]] * rep_count)
    extendeds = reps.exchange([extended] * rep_count)
    for unused in range(1, reach):
        lines.append(tuple(forward(one) for one in lines[-1]))
    middle = tuple((k, step, step == 0) for k in others for step in range(reach))
    states = attend(middle, lines[:-1], list(range(reach)), queries, {}, False, 3.0)
    states[1][0], *extendeds[1:] = lax.optimization_barrier((states[1][0], *extendeds[1:]))
    sent_grads = call(
        functools.partial(dispatch_kernel, rep_count, tok, hot_capacity),
        [shape((rep_count * hot_capacity, width))] * expert_count,
        [SMEM] + [VMEM] * rep_count,
    )(own, *extendeds)
    partial = attend(
        tuple((k, 0, False) for k in others),
        lines[-1:],
        [reach],
        queries,
        states,
        True,
        1.5,
        ahead=sent_grads[:1],
    )
    returned = reps.exchange([None] + [partial[k] for k in others], inverse=True)[1:]
    states = attend(
        tuple((0, step, step == 0) for step in range(reach + 1)),
        lines,
        list(range(reach + 1)),
        queries,
        {},
        False,
        1.5,
    )
    got_grads = merged(experts.exchange(sent_grads), MOST_PERMUTES)

    mixed, *sent_rows = call(
        functools.partial(mix_kernel, expert_count, hot_capacity),
        [shape((tok, width))] + [shape((hot_capacity, width))] * expert_count,
        [SMEM] + [VMEM] * (6 + len(returned)),
        cost=2.0,
    )(own, extendeds[0], residual[0], out_proj, *states[0], *returned)
    arrived = owners.exchange([sent_rows[k // rep_count] for k in range(owners.count)])
    got_rows = merged(arrived[0::rep_count], MOST_PERMUTES)
    got_more = [
        one for k in others for one in merged(arrived[k::rep_count], MOST_PERMUTES)
    ]

    def expert_call(rep_list, rows, out_shape, extra):
        return call(
            functools.partial(
                expert_kernel,
                rep_count,
                rep_list,
                expert_count,
                tok,
                strip,
                (len(rows), len(got_grads)),
            ),
            out_shape,
            [SMEM, SMEM] + [VMEM] * (3 + len(rows) + len(got_grads) + len(extra)),
            [pltpu.VMEM((2 * len(rep_list), width, expert_count * hot_capacity), jnp.bfloat16)],
            cost=2.0,
        )(own, part_to, weight_in[0], weight_out[0], extendeds[0], *rows, *got_grads, *extra)

    slots = expert_count * hot_capacity
    sums = expert_call(
        tuple(others),
        got_more,
        [
            shape((seq_count * strip, hidden), jnp.float32),
            shape((seq_count * strip, width), jnp.float32),
        ],
        [],
    )
    activated, pre_grad, *terms, kept = expert_call(
        (0,),
        got_rows[:1] + got_rows[1:][::-1],
        [shape((slots, hidden))] * 2
        + [shape((2, strip, hidden))] * (seq_count - 1)
        + [shape((2, strip, hidden), jnp.float32)],
        list(sums),
    )
    got_terms = parts.exchange([None] + terms)[1:]
    activated, mixed, kept = lax.optimization_barrier((activated, mixed, kept))
    back = call(
        functools.partial(back_kernel, expert_count),
        [shape((2 * hot_capacity, width))] * expert_count,
        [VMEM] * 4,
        cost=1.0,
    )(weight_in[0], weight_out[0], activated, pre_grad)
    got_back = merged(experts.exchange(back, inverse=True), MOST_PERMUTES)
    prepared = call(
        functools.partial(prepare_kernel, hot_capacity, expert_count),
        [
            shape((tok, slots)),
            shape((tok, 128), jnp.float32),
            shape((tok, width), jnp.float32),
        ],
        [SMEM, VMEM, VMEM],
        cost=1.0,
    )(own, mixed, extended)
    layer_out, grad_mixed, share_in, share_out = call(
        functools.partial(finish_kernel, hot_capacity, seq_count),
        [
            shape((tok, width)),
            shape((tok, width)),
            shape((strip, hidden), jnp.float32),
            shape((strip, width), jnp.float32),
        ],
        [VMEM] * (5 + seq_count + len(got_back)),
        cost=1.0,
    )(*prepared, mixed, extended, kept, *got_terms[::-1], *got_back[::-1])
    return (layer_out[None], grad_mixed[None], share_in[None], share_out[None])


def solution(mesh):
    rows = P("expert", ("seq", "rep"), None)
    in_specs = (
        rows,
        rows,
        rows,
        P("expert", None),
        rows,
        P(),
        P(),
        rows,
        P("expert", None, None),
        P("expert", None, None),
        rows,
    )
    body = functools.partial(
        local, mesh.shape["seq"], mesh.shape["expert"], mesh.shape["rep"]
    )
    return jax.shard_map(
        body, mesh=mesh, in_specs=in_specs, out_specs=(rows, rows, rows, rows), check_vma=False
    )
```

```python
import functools
import math

import jax
import jax.numpy as jnp
from jax import lax
from jax.experimental import pallas as pl
from jax.experimental.pallas import tpu as pltpu
from jax.sharding import PartitionSpec as P

HD = 32
norm_eps = 1e-06
masked_score = -1e30
VMEM_LIMIT = 48 * 1024 * 1024
MOST_PERMUTES = 16
NT = (((1,), (1,)), ((), ()))
TN = (((0,), (0,)), ((), ()))


def dot(a, b, dims=None):
    if dims is None:
        return jnp.dot(a, b, preferred_element_type=jnp.float32)
    return lax.dot_general(a, b, dims, preferred_element_type=jnp.float32)


def away(index, offset, size):
    if size & (size - 1) == 0:
        return index ^ offset
    return (index + offset) % size


def back_from(index, offset, size):
    if size & (size - 1) == 0:
        return index ^ offset
    return (index - offset + size) % size


class Group:
    def __init__(self, axes, sizes):
        self.axes, self.sizes = tuple(axes), tuple(sizes)
        self.count = math.prod(sizes)

    def split(self, flat):
        coords = []
        for size in reversed(self.sizes):
            coords.append(flat % size)
            flat = flat // size
        return coords[::-1]

    def moved(self, flat, offset, step):
        place = 0
        for coord, part, size in zip(self.split(flat), self.split(offset), self.sizes):
            place = place * size + step(coord, part, size)
        return place

    def target(self, flat, offset):
        return self.moved(flat, offset, away)

    def source(self, flat, offset):
        return self.moved(flat, offset, back_from)

    def exchange(self, chunks, inverse=False):
        to, start = (self.source, self.target) if inverse else (self.target, self.source)
        if self.count <= MOST_PERMUTES:
            order = sorted(range(1, self.count), key=lambda k: -k)
            got = {0: chunks[0]}
            for k in order:
                pairs = [(i, to(i, k)) for i in range(self.count)]
                got[k] = lax.ppermute(chunks[k], self.axes, pairs)
            return [got[k] for k in range(self.count)]
        me = lax.axis_index(self.axes)
        steps = jnp.arange(self.count, dtype=jnp.int32)
        sent_to = jax.vmap(lambda k: to(me, k))(steps)
        placed = jnp.zeros((self.count,), jnp.int32).at[sent_to].set(steps)
        stacked = jnp.stack(chunks)[placed]
        got = lax.all_to_all(stacked, self.axes, split_axis=0, concat_axis=0, tiled=True)
        came_from = jax.vmap(lambda k: start(me, k))(steps)
        ordered = got[came_from]
        return [ordered[k] for k in range(self.count)]


def merged(chunks, most):
    if len(chunks) <= most:
        return list(chunks)
    return [jnp.concatenate(chunks, axis=0)]


def chunk_rows(refs, count, low, high):
    size = sum(ref.shape[0] for ref in refs) // count
    parts = []
    for chunk in range(count):
        ref, first = (refs[chunk], 0) if len(refs) == count else (refs[0], chunk * size)
        parts.append(ref[first + low : first + high, :])
    return parts[0] if count == 1 else jnp.concatenate(parts, axis=0)


def slot_matrix(choice, own, expert_count, hot_capacity):
    tok = choice.shape[1]
    offset = back_from(choice, own, expert_count)
    one_hot = lax.broadcasted_iota(jnp.int32, (expert_count, tok), 0) == offset
    hits = one_hot.astype(jnp.float32).astype(jnp.bfloat16)
    earlier = lax.broadcasted_iota(jnp.int32, (tok, tok), 0) <= lax.broadcasted_iota(
        jnp.int32, (tok, tok), 1
    )
    counted = dot(hits, earlier.astype(jnp.float32).astype(jnp.bfloat16))
    rank = jnp.sum(jnp.where(one_hot, counted, 0.0), axis=0, keepdims=True) - 1.0
    slots = offset * hot_capacity + rank.astype(jnp.int32)
    rows = lax.broadcasted_iota(jnp.int32, (expert_count * hot_capacity, tok), 0)
    return (rows == slots).astype(jnp.float32).astype(jnp.bfloat16)


def extend_kernel(
    ranks_ref, lengths_ref, choice_ref, router_ref, grad_ref, extended_ref, begin_ref
):
    tok, width = grad_ref.shape
    extended_ref[0:tok, :] = grad_ref[...]
    chosen = jnp.broadcast_to(choice_ref[...].astype(jnp.float32), (16, tok))
    extended_ref[tok : tok + 16, 0:tok] = chosen.astype(jnp.bfloat16)
    extended_ref[tok : tok + 16, tok:width] = jnp.zeros((16, width - tok), jnp.bfloat16)
    routed = router_ref[...].astype(jnp.float32)
    spare = extended_ref.shape[0] - tok - 16 - routed.shape[0]
    if spare:
        routed = jnp.concatenate([routed, jnp.zeros((spare, width), jnp.float32)], axis=0)
    extended_ref[tok + 16 :, :] = routed.astype(jnp.bfloat16)
    for k in range(begin_ref.shape[0]):
        position = ranks_ref[k] * tok + lax.broadcasted_iota(jnp.int32, (1, tok), 1)
        begin = jnp.zeros((1, tok), jnp.int32)
        bound = jnp.int32(0)
        for doc in range(lengths_ref.shape[1] - 1):
            bound = bound + lengths_ref[0, doc]
            begin = jnp.maximum(begin, jnp.where(position >= bound, bound, 0))
        begin_ref[k : k + 1, :] = begin


def chosen_of(extended_ref, tok):
    return extended_ref[tok : tok + 16, 0:tok].astype(jnp.float32)[0:1].astype(jnp.int32)


def router_of(extended_ref, tok, expert_count):
    whole = extended_ref[tok + 16 :, :].astype(jnp.float32)
    return whole[0:expert_count].astype(jnp.bfloat16)


def dispatch_kernel(reps, tok, hot_capacity, own_ref, *refs):
    extended_refs, sent_refs = refs[:reps], refs[reps:]
    for rep in range(reps):
        choice = chosen_of(extended_refs[rep], tok)
        placed = slot_matrix(choice, own_ref[0], len(sent_refs), hot_capacity)
        rows = dot(placed, extended_refs[rep][0:tok, :]).astype(jnp.bfloat16)
        for k, sent_ref in enumerate(sent_refs):
            sent_ref[rep * hot_capacity : (rep + 1) * hot_capacity] = rows[
                k * hot_capacity : (k + 1) * hot_capacity
            ]


def fold_blocks(ids_ref, begin_ref, tasks, reps, states, bias_ref):
    lanes = 128
    per = lanes // HD
    scale = math.log2(math.e) / math.sqrt(HD)
    spreads = {}
    lowest = {}
    for k, query_ref, unused_pair, unused_first in tasks:
        if k in spreads:
            continue
        lowest[k] = jnp.min(begin_ref[k : k + 1, :])
        tok = begin_ref.shape[1]
        turned = query_ref[...].T
        head_of_row = lax.broadcasted_iota(jnp.int32, (lanes, tok), 0) // HD
        spreads[k] = []
        for group in range(turned.shape[0] // lanes):
            part = turned[group * lanes : (group + 1) * lanes]
            spreads[k].append(
                jnp.concatenate(
                    [
                        jnp.where(head_of_row == head, part, jnp.zeros_like(part))
                        for head in range(per)
                    ],
                    axis=1,
                )
            )

    def fold(place, k, pair_ref, block, begin, fresh):
        top_ref, total_ref, sum_ref = states[k]
        tok = begin.shape[1]
        position = ids_ref[k] * tok + lax.broadcasted_iota(jnp.int32, (1, tok), 1)
        key_position = block * tok + lax.broadcasted_iota(jnp.int32, (tok, tok), 0)
        visible = (key_position >= begin) & (key_position <= position)
        bias_ref[place] = jnp.where(visible, 0.0, masked_score)
        bias = bias_ref[place]
        key_ref, value_ref = pair_ref
        values = value_ref[...].T
        for group, spread in enumerate(spreads[k]):
            columns = slice(group * lanes, (group + 1) * lanes)
            scores = dot(key_ref[:, columns], spread)
            weights, factors = [], []
            for head in range(per):
                row = group * per + head
                part = scores[:, head * tok : (head + 1) * tok] + bias
                top = jnp.max(part, axis=0, keepdims=True)
                if not fresh:
                    old = top_ref[row : row + 1, :]
                    top = jnp.maximum(top, old)
                    factors.append(jnp.exp2((old - top) * scale))
                weight = jnp.exp2((part - top) * scale)
                total = jnp.sum(weight, axis=0, keepdims=True)
                if not fresh:
                    total = total + total_ref[row : row + 1, :] * factors[head]
                top_ref[row : row + 1, :] = top
                total_ref[row : row + 1, :] = total
                weights.append(weight.astype(jnp.bfloat16))
            summed = dot(values[columns], jnp.concatenate(weights, axis=1))
            for head in range(per):
                rows = slice((group * per + head) * HD, (group * per + head + 1) * HD)
                piece = summed[head * HD : (head + 1) * HD, head * tok : (head + 1) * tok]
                if not fresh:
                    piece = piece + sum_ref[rows, :] * factors[head]
                sum_ref[rows, :] = piece

    for place, (k, unused_query, pair_ref, first) in enumerate(tasks):
        block = ids_ref[reps + place]
        begin = begin_ref[k : k + 1, :]
        tok = begin.shape[1]
        if first and k == 0:
            fold(place, k, pair_ref, block, begin, True)
            continue
        if first:
            top_ref, total_ref, sum_ref = states[k]
            top_ref[...] = jnp.full(top_ref.shape, masked_score, jnp.float32)
            total_ref[...] = jnp.zeros(total_ref.shape, jnp.float32)
            sum_ref[...] = jnp.zeros(sum_ref.shape, jnp.float32)

        @pl.when((block >= 0) & ((block + 1) * tok > lowest[k]))
        def unused(place=place, k=k, pair_ref=pair_ref, block=block, begin=begin):
            fold(place, k, pair_ref, block, begin, False)


def attend_kernel(plan, reps, counts, packed, ahead, ids_ref, begin_ref, *refs):
    ks = sorted({k for k, unused_pair, unused_first in plan})
    old_ks = [k for k in ks if not any(first for j, unused_pair, first in plan if j == k)]
    query_refs, refs = dict(zip(ks, refs)), refs[len(ks) + ahead :]
    pair_refs = [refs[2 * place : 2 * place + 2] for place in range(counts)]
    refs = refs[2 * counts :]
    old_refs, refs = refs[: 3 * len(old_ks)], refs[3 * len(old_ks) :]
    bias_ref, refs = refs[-1], refs[:-1]
    packed_refs, state_refs = (refs[: len(ks)], refs[len(ks) :]) if packed else ((), refs)
    states = {k: state_refs[3 * place : 3 * place + 3] for place, k in enumerate(ks)}
    for place, k in enumerate(old_ks):
        for old_ref, new_ref in zip(old_refs[3 * place : 3 * place + 3], states[k]):
            new_ref[...] = old_ref[...]
    tasks = [(k, query_refs[k], pair_refs[pair], first) for k, pair, first in plan]
    fold_blocks(ids_ref, begin_ref, tasks, reps, states, bias_ref)
    for k, packed_ref in zip(ks, packed_refs):
        top_ref, total_ref, sum_ref = states[k]
        heads, width = top_ref.shape[0], sum_ref.shape[0]
        packed_ref[0:width, :] = sum_ref[...].astype(jnp.bfloat16)
        first = width
        for ref, pieces in ((top_ref, 3), (total_ref, 2)):
            rest = ref[...]
            for unused in range(pieces):
                piece = rest.astype(jnp.bfloat16)
                packed_ref[first : first + heads, :] = piece
                rest = rest - piece.astype(jnp.float32)
                first += heads


def mix_kernel(expert_count, hot_capacity, own_ref, extended_ref, residual_ref, proj_ref, *refs):
    top_ref, total_ref, sum_ref = refs[0:3]
    mixed_ref, sent_refs = refs[-1 - expert_count], refs[len(refs) - expert_count :]
    packed_refs = refs[3 : -1 - expert_count]
    tok, width = mixed_ref.shape
    heads = top_ref.shape[0]
    scale = math.log2(math.e) / math.sqrt(HD)
    tops, totals = [top_ref[...]], [total_ref[...]]
    for packed_ref in packed_refs:
        pieces = [
            packed_ref[width + place * heads : width + (place + 1) * heads, :].astype(jnp.float32)
            for place in range(5)
        ]
        tops.append((pieces[0] + pieces[1]) + pieces[2])
        totals.append(pieces[3] + pieces[4])
    top = functools.reduce(jnp.maximum, tops)
    factors = [jnp.exp2((one - top) * scale) for one in tops]
    total = sum(one * factor for one, factor in zip(totals, factors))
    factors = [factor / total for factor in factors]
    pieces = []
    for head in range(heads):
        rows = slice(head * HD, (head + 1) * HD)
        piece = sum_ref[rows, :] * factors[0][head : head + 1, :]
        for packed_ref, factor in zip(packed_refs, factors[1:]):
            piece = piece + packed_ref[rows, :].astype(jnp.float32) * factor[head : head + 1, :]
        pieces.append(piece.astype(jnp.bfloat16))
    attended = jnp.concatenate(pieces, axis=0).T
    mixed = (residual_ref[...].astype(jnp.float32) + dot(attended, proj_ref[...])).astype(
        jnp.bfloat16
    )
    mixed_ref[...] = mixed
    mixed_f = mixed.astype(jnp.float32)
    inv_rms = lax.rsqrt(jnp.mean(mixed_f * mixed_f, axis=1, keepdims=True) + norm_eps)
    normed = (mixed_f * inv_rms).astype(jnp.bfloat16)
    placed = slot_matrix(chosen_of(extended_ref, tok), own_ref[0], len(sent_refs), hot_capacity)
    rows = dot(placed, normed).astype(jnp.bfloat16)
    for k, sent_ref in enumerate(sent_refs):
        sent_ref[...] = rows[k * hot_capacity : (k + 1) * hot_capacity]


def expert_kernel(
    reps,
    rep_list,
    sources,
    tok,
    strip,
    counts,
    own_ref,
    part_ref,
    up_ref,
    down_ref,
    extended_ref,
    *refs,
):
    row_count, grad_count = counts
    row_refs, refs = refs[:row_count], refs[row_count:]
    per_rep = row_count // len(rep_list)
    if rep_list == (0,) and per_rep == sources:
        row_refs = row_refs[:1] + row_refs[1:][::-1]
    grad_refs, refs = refs[:grad_count], refs[grad_count:]
    own_rows = rep_list[0] == 0
    held_ref, refs = refs[-1], refs[:-1]
    if own_rows:
        up_old, down_old, activated_ref, pre_grad_ref = refs[:4]
        term_refs, kept_ref = refs[4:-1], refs[-1]
    else:
        up_acc, down_acc = refs
    total_grads = sum(ref.shape[0] for ref in grad_refs)
    capacity = total_grads // (sources * reps)
    count = sources * capacity
    parts = part_ref.shape[0]
    up = up_ref[...]
    down = down_ref[...]
    router = router_of(extended_ref, tok, sources)
    expert_lane = lax.broadcasted_iota(jnp.int32, (count, router.shape[0]), 1) == own_ref[0]

    def strips(rows, place):
        held_ref[place] = rows.T
        taken = []
        for k in range(parts):
            first = pl.multiple_of(part_ref[k] * strip, strip)
            taken.append(held_ref[place, pl.ds(first, strip), :])
        return jnp.concatenate(taken, axis=0)

    up_term = down_term = None
    for place, rep in enumerate(rep_list):
        rows = chunk_rows(
            row_refs[place * per_rep : (place + 1) * per_rep], sources, 0, capacity
        )
        grads = chunk_rows(grad_refs, sources, rep * capacity, (rep + 1) * capacity)
        pre = dot(rows, up)
        sigmoid_pre = jax.nn.sigmoid(pre)
        activated = (pre * sigmoid_pre).astype(jnp.bfloat16)
        logits = dot(rows, router, NT)
        gate = jax.nn.sigmoid(
            jnp.sum(jnp.where(expert_lane, logits, 0.0), axis=1, keepdims=True)
        )
        scaled = (gate * grads.astype(jnp.float32)).astype(jnp.bfloat16)
        act_grad = dot(scaled, down, NT)
        pre_grad = (act_grad * sigmoid_pre * (1.0 + pre * (1.0 - sigmoid_pre))).astype(
            jnp.bfloat16
        )
        if own_rows:
            activated_ref[...] = activated
            pre_grad_ref[...] = pre_grad
        more_up = dot(strips(rows, 2 * place), pre_grad)
        more_down = dot(strips(activated, 2 * place + 1), scaled)
        up_term = more_up if up_term is None else up_term + more_up
        down_term = more_down if down_term is None else down_term + more_down
    if not own_rows:
        up_acc[...] = up_term
        down_acc[...] = down_term
        return
    up_term = up_term + up_old[...]
    down_term = down_term + down_old[...]
    for k, ref in enumerate((kept_ref, *term_refs)):
        rows = slice(k * strip, (k + 1) * strip)
        ref[0] = up_term[rows].astype(ref.dtype)
        ref[1] = down_term[rows].astype(ref.dtype)


def back_kernel(sources, up_ref, down_ref, activated_ref, pre_grad_ref, *back_refs):
    capacity = activated_ref.shape[0] // sources
    produced = dot(activated_ref[...], down_ref[...]).astype(jnp.bfloat16)
    token_grad = dot(pre_grad_ref[...], up_ref[...], NT).astype(jnp.bfloat16)
    for k, back_ref in enumerate(back_refs):
        rows = slice(k * capacity, (k + 1) * capacity)
        back_ref[0:capacity] = produced[rows]
        back_ref[capacity : 2 * capacity] = token_grad[rows]


def prepare_kernel(
    hot_capacity,
    expert_count,
    own_ref,
    mixed_ref,
    extended_ref,
    placed_ref,
    factors_ref,
    router_cols_ref,
):
    tok = mixed_ref.shape[0]
    choice = chosen_of(extended_ref, tok)
    placed = slot_matrix(choice, own_ref[0], expert_count, hot_capacity)
    placed_ref[...] = placed.T
    router = router_of(extended_ref, tok, expert_count)
    mixed_f = mixed_ref[...].astype(jnp.float32)
    inv_rms = lax.rsqrt(jnp.mean(mixed_f * mixed_f, axis=1, keepdims=True) + norm_eps)
    normed = (mixed_f * inv_rms).astype(jnp.bfloat16)
    one_hot = lax.broadcasted_iota(jnp.int32, (expert_count, tok), 0) == choice
    logits = dot(router, normed, NT)
    logit_row = jnp.sum(jnp.where(one_hot, logits, 0.0), axis=0, keepdims=True)
    gate = jax.nn.sigmoid(jnp.broadcast_to(logit_row, (8, tok)).T[:, 0:1])
    lane = lax.broadcasted_iota(jnp.int32, factors_ref.shape, 1)
    factors_ref[...] = jnp.where(lane == 0, inv_rms, gate)
    router_cols_ref[...] = dot(one_hot.astype(jnp.float32).astype(jnp.bfloat16), router, TN)


def finish_kernel(
    hot_capacity,
    parts,
    placed_ref,
    factors_ref,
    router_cols_ref,
    mixed_ref,
    extended_ref,
    *refs,
):
    refs, (layer_ref, grad_mixed_ref, *share_refs) = refs[:-4], refs[-4:]
    (kept_ref, *term_refs), back_refs = refs[:parts], refs[parts:][::-1]
    for kind, share_ref in enumerate(share_refs):
        total = kept_ref[kind]
        for ref in term_refs:
            total = total + ref[kind].astype(jnp.float32)
        share_ref[...] = total
    tok = mixed_ref.shape[0]
    mixed_f = mixed_ref[...].astype(jnp.float32)
    inv_rms = factors_ref[:, 0:1]
    gate = factors_ref[:, 1:2]
    pair = 2 * hot_capacity
    chunks = [
        ref[first : first + pair] for ref in back_refs for first in range(0, ref.shape[0], pair)
    ]
    results = jnp.concatenate([chunk[:hot_capacity] for chunk in chunks], axis=0)
    grads = jnp.concatenate([chunk[hot_capacity:] for chunk in chunks], axis=0)
    placed = placed_ref[...]
    result_f = dot(placed, results)
    normed_grad = dot(placed, grads)
    grad_f = extended_ref[0:tok, :].astype(jnp.float32)
    layer_ref[...] = (mixed_f + gate * result_f).astype(jnp.bfloat16)
    gate_grad = jnp.sum(grad_f * result_f, axis=1, keepdims=True)
    logit_grad = gate_grad * gate * (1.0 - gate)
    total_grad = normed_grad + logit_grad * router_cols_ref[...]
    mean_term = jnp.mean(total_grad * mixed_f, axis=1, keepdims=True)
    input_grad = inv_rms * total_grad - mixed_f * inv_rms * inv_rms * inv_rms * mean_term
    grad_mixed_ref[...] = (grad_f + input_grad).astype(jnp.bfloat16)


def shape(dims, dtype=jnp.bfloat16):
    return jax.ShapeDtypeStruct(dims, dtype)


SMEM = pl.BlockSpec(memory_space=pltpu.SMEM)
VMEM = pl.BlockSpec(memory_space=pltpu.VMEM)
HBM = pl.BlockSpec(memory_space=pltpu.HBM)


def call(body, out_shape, specs, scratch=(), cost=0.5):
    return pl.pallas_call(
        body,
        cost_estimate=pl.CostEstimate(
            flops=int(cost * 1e9), bytes_accessed=0, transcendentals=0
        ),
        out_shape=out_shape,
        in_specs=specs,
        out_specs=jax.tree.map(lambda unused: VMEM, out_shape),
        scratch_shapes=list(scratch),
        compiler_params=pltpu.CompilerParams(vmem_limit_bytes=VMEM_LIMIT),
    )


def local(
    seq_count,
    expert_count,
    rep_count,
    query_rows,
    key_rows,
    value_rows,
    doc_lengths,
    residual,
    out_proj,
    router,
    expert_choice,
    weight_in,
    weight_out,
    grad_out,
):
    tok, width = query_rows.shape[1:]
    hidden = weight_in.shape[2]
    heads = width // HD
    experts = Group(("expert",), (expert_count,))
    reps = Group(("rep",), (rep_count,))
    owners = Group(("expert", "rep"), (expert_count, rep_count))
    parts = Group(("seq",), (seq_count,))
    strip = width // (seq_count * rep_count)
    capacity = max(2, (3 * tok + 2 * expert_count - 1) // (2 * expert_count))
    hot_capacity = min(4 * capacity, tok // 2)
    choice = expert_choice.reshape(1, tok)
    seq_index = lax.axis_index("seq")
    rep_index = lax.axis_index("rep")
    rank = seq_index * rep_count + rep_index
    own = jnp.stack([lax.axis_index("expert")]).astype(jnp.int32)
    part_to = jnp.stack(
        [parts.target(seq_index, k) * rep_count + rep_index for k in range(seq_count)]
    ).astype(jnp.int32)

    def forward(array):
        return lax.ppermute(array, "seq", [(i, (i + 1) % seq_count) for i in range(seq_count)])

    reach = (seq_count + 1) // 2
    longest = (seq_count * rep_count + 1) // 2
    query_ranks = [
        seq_index * rep_count + reps.source(rep_index, k) for k in range(rep_count)
    ]

    def task_ids(plan, steps):
        ids = list(query_ranks)
        for k, pair, unused_first in plan:
            block = rank - steps[pair] * rep_count
            behind = query_ranks[k] - block
            ids.append(jnp.where((block >= 0) & (behind >= 0) & (behind <= longest), block, -1))
        return jnp.stack(ids).astype(jnp.int32)

    state_shapes = [
        shape((heads, tok), jnp.float32),
        shape((heads, tok), jnp.float32),
        shape((width, tok), jnp.float32),
    ]
    tail = 16 + -(-expert_count // 16) * 16
    extended, begin = call(
        extend_kernel,
        [shape((tok + tail, width)), shape((rep_count, tok), jnp.int32)],
        [SMEM, SMEM] + [VMEM] * 3,
    )(
        jnp.stack(query_ranks).astype(jnp.int32), doc_lengths, choice, router.T, grad_out[0]
    )

    def attend(plan, pairs, steps, queries, states, packed, cost, ahead=()):
        ks = sorted({k for k, unused_pair, unused_first in plan})
        old = [one for k in ks if k in states for one in states[k]]
        state_out = state_shapes * len(ks)
        if packed:
            out_shape = [shape((width + 5 * heads, tok))] * len(ks)
            scratch = [pltpu.VMEM(one.shape, one.dtype) for one in state_out]
        else:
            out_shape, scratch = state_out, []
        outs = call(
            functools.partial(
                attend_kernel, plan, rep_count, len(pairs), packed, len(ahead)
            ),
            out_shape,
            [SMEM] + [VMEM] * (1 + len(ks) + len(ahead) + 2 * len(pairs) + len(old)),
            scratch + [pltpu.VMEM((len(plan), tok, tok), jnp.float32)],
            cost=cost,
        )(task_ids(plan, steps), begin, *[queries[k] for k in ks], *ahead, *[one for both in pairs for one in both], *old)
        if packed:
            return dict(zip(ks, outs))
        return {k: list(outs[3 * place : 3 * place + 3]) for place, k in enumerate(ks)}

    others = range(1, rep_count)
    lines = [(key_rows[0], value_rows[0])]
    lines.append(tuple(forward(one) for one in lines[0]))
    queries = reps.exchange([query_rows[0]] * rep_count)
    extendeds = reps.exchange([extended] * rep_count)
    ahead, begin = lax.optimization_barrier((lines[1][0], begin))
    states = attend(((0, 0, True),), lines[:1], [0], queries, {}, False, 2.0)
    behind, *states[0] = lax.optimization_barrier((lines[1][1], *states[0]))
    lines[1] = (ahead, behind)
    for unused in range(1, reach):
        lines.append(tuple(forward(one) for one in lines[-1]))
    own_state = states
    middle = tuple((k, step, step == 0) for k in others for step in range(reach))
    states = attend(middle, lines[:-1], list(range(reach)), queries, {}, False, 3.0)
    states[1][0], *extendeds[1:] = lax.optimization_barrier((states[1][0], *extendeds[1:]))
    sent_grads = call(
        functools.partial(dispatch_kernel, rep_count, tok, hot_capacity),
        [shape((rep_count * hot_capacity, width))] * expert_count,
        [SMEM] + [VMEM] * rep_count,
    )(own, *extendeds)
    partial = attend(
        tuple((k, 0, False) for k in others),
        lines[-1:],
        [reach],
        queries,
        states,
        True,
        1.5,
        ahead=sent_grads[:1],
    )
    returned = reps.exchange([None] + [partial[k] for k in others], inverse=True)[1:]
    states = attend(
        tuple((0, step, False) for step in range(reach)),
        lines[1:],
        list(range(1, reach + 1)),
        queries,
        own_state,
        False,
        1.5,
    )
    got_grads = merged(experts.exchange(sent_grads), MOST_PERMUTES)

    mixed, *sent_rows = call(
        functools.partial(mix_kernel, expert_count, hot_capacity),
        [shape((tok, width))] + [shape((hot_capacity, width))] * expert_count,
        [SMEM] + [VMEM] * (6 + len(returned)),
        cost=2.0,
    )(own, extendeds[0], residual[0], out_proj, *states[0], *returned)
    arrived = owners.exchange([sent_rows[k // rep_count] for k in range(owners.count)])
    got_rows = merged(arrived[0::rep_count], MOST_PERMUTES)
    got_more = [
        one for k in others for one in merged(arrived[k::rep_count], MOST_PERMUTES)
    ]

    def expert_call(rep_list, rows, out_shape, extra):
        return call(
            functools.partial(
                expert_kernel,
                rep_count,
                rep_list,
                expert_count,
                tok,
                strip,
                (len(rows), len(got_grads)),
            ),
            out_shape,
            [SMEM, SMEM] + [VMEM] * (3 + len(rows) + len(got_grads) + len(extra)),
            [pltpu.VMEM((2 * len(rep_list), width, expert_count * hot_capacity), jnp.bfloat16)],
            cost=2.0,
        )(own, part_to, weight_in[0], weight_out[0], extendeds[0], *rows, *got_grads, *extra)

    slots = expert_count * hot_capacity
    sums = expert_call(
        tuple(others),
        got_more,
        [
            shape((seq_count * strip, hidden), jnp.float32),
            shape((seq_count * strip, width), jnp.float32),
        ],
        [],
    )
    activated, pre_grad, *terms, kept = expert_call(
        (0,),
        got_rows[:1] + got_rows[1:][::-1],
        [shape((slots, hidden))] * 2
        + [shape((2, strip, hidden))] * (seq_count - 1)
        + [shape((2, strip, hidden), jnp.float32)],
        list(sums),
    )
    got_terms = parts.exchange([None] + terms)[1:]
    activated, mixed, kept = lax.optimization_barrier((activated, mixed, kept))
    back = call(
        functools.partial(back_kernel, expert_count),
        [shape((2 * hot_capacity, width))] * expert_count,
        [VMEM] * 4,
        cost=1.0,
    )(weight_in[0], weight_out[0], activated, pre_grad)
    got_back = merged(experts.exchange(back, inverse=True), MOST_PERMUTES)
    prepared = call(
        functools.partial(prepare_kernel, hot_capacity, expert_count),
        [
            shape((tok, slots)),
            shape((tok, 128), jnp.float32),
            shape((tok, width), jnp.float32),
        ],
        [SMEM, VMEM, VMEM],
        cost=1.0,
    )(own, mixed, extended)
    layer_out, grad_mixed, share_in, share_out = call(
        functools.partial(finish_kernel, hot_capacity, seq_count),
        [
            shape((tok, width)),
            shape((tok, width)),
            shape((strip, hidden), jnp.float32),
            shape((strip, width), jnp.float32),
        ],
        [VMEM] * (5 + seq_count + len(got_back)),
        cost=1.0,
    )(*prepared, mixed, extended, kept, *got_terms[::-1], *got_back[::-1])
    return (layer_out[None], grad_mixed[None], share_in[None], share_out[None])


def solution(mesh):
    rows = P("expert", ("seq", "rep"), None)
    in_specs = (
        rows,
        rows,
        rows,
        P("expert", None),
        rows,
        P(),
        P(),
        rows,
        P("expert", None, None),
        P("expert", None, None),
        rows,
    )
    body = functools.partial(
        local, mesh.shape["seq"], mesh.shape["expert"], mesh.shape["rep"]
    )
    return jax.shard_map(
        body, mesh=mesh, in_specs=in_specs, out_specs=(rows, rows, rows, rows), check_vma=False
    )
```

```python
import functools
import math

import jax
import jax.numpy as jnp
from jax import lax
from jax.experimental import pallas as pl
from jax.experimental.pallas import tpu as pltpu
from jax.sharding import PartitionSpec as P

HD = 32
norm_eps = 1e-06
masked_score = -1e30
VMEM_LIMIT = 48 * 1024 * 1024
MOST_PERMUTES = 16
NT = (((1,), (1,)), ((), ()))
TN = (((0,), (0,)), ((), ()))


def dot(a, b, dims=None):
    if dims is None:
        return jnp.dot(a, b, preferred_element_type=jnp.float32)
    return lax.dot_general(a, b, dims, preferred_element_type=jnp.float32)


def away(index, offset, size):
    if size & (size - 1) == 0:
        return index ^ offset
    return (index + offset) % size


def back_from(index, offset, size):
    if size & (size - 1) == 0:
        return index ^ offset
    return (index - offset + size) % size


class Group:
    def __init__(self, axes, sizes):
        self.axes, self.sizes = tuple(axes), tuple(sizes)
        self.count = math.prod(sizes)

    def split(self, flat):
        coords = []
        for size in reversed(self.sizes):
            coords.append(flat % size)
            flat = flat // size
        return coords[::-1]

    def moved(self, flat, offset, step):
        place = 0
        for coord, part, size in zip(self.split(flat), self.split(offset), self.sizes):
            place = place * size + step(coord, part, size)
        return place

    def target(self, flat, offset):
        return self.moved(flat, offset, away)

    def source(self, flat, offset):
        return self.moved(flat, offset, back_from)

    def exchange(self, chunks, inverse=False):
        to, start = (self.source, self.target) if inverse else (self.target, self.source)
        if self.count <= MOST_PERMUTES:
            order = sorted(range(1, self.count), key=lambda k: -k)
            got = {0: chunks[0]}
            for k in order:
                pairs = [(i, to(i, k)) for i in range(self.count)]
                got[k] = lax.ppermute(chunks[k], self.axes, pairs)
            return [got[k] for k in range(self.count)]
        me = lax.axis_index(self.axes)
        steps = jnp.arange(self.count, dtype=jnp.int32)
        sent_to = jax.vmap(lambda k: to(me, k))(steps)
        placed = jnp.zeros((self.count,), jnp.int32).at[sent_to].set(steps)
        stacked = jnp.stack(chunks)[placed]
        got = lax.all_to_all(stacked, self.axes, split_axis=0, concat_axis=0, tiled=True)
        came_from = jax.vmap(lambda k: start(me, k))(steps)
        ordered = got[came_from]
        return [ordered[k] for k in range(self.count)]


def merged(chunks, most):
    if len(chunks) <= most:
        return list(chunks)
    return [jnp.concatenate(chunks, axis=0)]


def chunk_rows(refs, count, low, high):
    size = sum(ref.shape[0] for ref in refs) // count
    parts = []
    for chunk in range(count):
        ref, first = (refs[chunk], 0) if len(refs) == count else (refs[0], chunk * size)
        parts.append(ref[first + low : first + high, :])
    return parts[0] if count == 1 else jnp.concatenate(parts, axis=0)


def slot_matrix(choice, own, expert_count, hot_capacity):
    tok = choice.shape[1]
    offset = back_from(choice, own, expert_count)
    one_hot = lax.broadcasted_iota(jnp.int32, (expert_count, tok), 0) == offset
    hits = one_hot.astype(jnp.float32).astype(jnp.bfloat16)
    earlier = lax.broadcasted_iota(jnp.int32, (tok, tok), 0) <= lax.broadcasted_iota(
        jnp.int32, (tok, tok), 1
    )
    counted = dot(hits, earlier.astype(jnp.float32).astype(jnp.bfloat16))
    rank = jnp.sum(jnp.where(one_hot, counted, 0.0), axis=0, keepdims=True) - 1.0
    slots = offset * hot_capacity + rank.astype(jnp.int32)
    rows = lax.broadcasted_iota(jnp.int32, (expert_count * hot_capacity, tok), 0)
    return (rows == slots).astype(jnp.float32).astype(jnp.bfloat16)


def extend_kernel(
    ranks_ref, lengths_ref, choice_ref, router_ref, grad_ref, extended_ref, begin_ref
):
    tok, width = grad_ref.shape
    extended_ref[0:tok, :] = grad_ref[...]
    chosen = jnp.broadcast_to(choice_ref[...].astype(jnp.float32), (16, tok))
    extended_ref[tok : tok + 16, 0:tok] = chosen.astype(jnp.bfloat16)
    extended_ref[tok : tok + 16, tok:width] = jnp.zeros((16, width - tok), jnp.bfloat16)
    routed = router_ref[...].astype(jnp.float32)
    spare = extended_ref.shape[0] - tok - 16 - routed.shape[0]
    if spare:
        routed = jnp.concatenate([routed, jnp.zeros((spare, width), jnp.float32)], axis=0)
    extended_ref[tok + 16 :, :] = routed.astype(jnp.bfloat16)
    for k in range(begin_ref.shape[0]):
        position = ranks_ref[k] * tok + lax.broadcasted_iota(jnp.int32, (1, tok), 1)
        begin = jnp.zeros((1, tok), jnp.int32)
        bound = jnp.int32(0)
        for doc in range(lengths_ref.shape[1] - 1):
            bound = bound + lengths_ref[0, doc]
            begin = jnp.maximum(begin, jnp.where(position >= bound, bound, 0))
        begin_ref[k : k + 1, :] = begin


def chosen_of(extended_ref, tok):
    return extended_ref[tok : tok + 16, 0:tok].astype(jnp.float32)[0:1].astype(jnp.int32)


def router_of(extended_ref, tok, expert_count):
    whole = extended_ref[tok + 16 :, :].astype(jnp.float32)
    return whole[0:expert_count].astype(jnp.bfloat16)


def dispatch_kernel(reps, tok, hot_capacity, own_ref, *refs):
    extended_refs, sent_refs = refs[:reps], refs[reps:]
    for rep in range(reps):
        choice = chosen_of(extended_refs[rep], tok)
        placed = slot_matrix(choice, own_ref[0], len(sent_refs), hot_capacity)
        rows = dot(placed, extended_refs[rep][0:tok, :]).astype(jnp.bfloat16)
        for k, sent_ref in enumerate(sent_refs):
            sent_ref[rep * hot_capacity : (rep + 1) * hot_capacity] = rows[
                k * hot_capacity : (k + 1) * hot_capacity
            ]


def fold_blocks(ids_ref, begin_ref, tasks, reps, states, bias_ref):
    lanes = 128
    per = lanes // HD
    scale = math.log2(math.e) / math.sqrt(HD)
    spreads = {}
    lowest = {}
    for k, query_ref, unused_pair, unused_first in tasks:
        if k in spreads:
            continue
        lowest[k] = jnp.min(begin_ref[k : k + 1, :])
        tok = begin_ref.shape[1]
        turned = query_ref[...].T
        head_of_row = lax.broadcasted_iota(jnp.int32, (lanes, tok), 0) // HD
        spreads[k] = []
        for group in range(turned.shape[0] // lanes):
            part = turned[group * lanes : (group + 1) * lanes]
            spreads[k].append(
                jnp.concatenate(
                    [
                        jnp.where(head_of_row == head, part, jnp.zeros_like(part))
                        for head in range(per)
                    ],
                    axis=1,
                )
            )

    def fold(place, k, pair_ref, block, begin, fresh):
        top_ref, total_ref, sum_ref = states[k]
        tok = begin.shape[1]
        position = ids_ref[k] * tok + lax.broadcasted_iota(jnp.int32, (1, tok), 1)
        key_position = block * tok + lax.broadcasted_iota(jnp.int32, (tok, tok), 0)
        visible = (key_position >= begin) & (key_position <= position)
        bias_ref[place] = jnp.where(visible, 0.0, masked_score)
        bias = bias_ref[place]
        key_ref, value_ref = pair_ref
        values = value_ref[...].T
        for group, spread in enumerate(spreads[k]):
            columns = slice(group * lanes, (group + 1) * lanes)
            scores = dot(key_ref[:, columns], spread)
            weights, factors = [], []
            for head in range(per):
                row = group * per + head
                part = scores[:, head * tok : (head + 1) * tok] + bias
                top = jnp.max(part, axis=0, keepdims=True)
                if not fresh:
                    old = top_ref[row : row + 1, :]
                    top = jnp.maximum(top, old)
                    factors.append(jnp.exp2((old - top) * scale))
                weight = jnp.exp2((part - top) * scale)
                total = jnp.sum(weight, axis=0, keepdims=True)
                if not fresh:
                    total = total + total_ref[row : row + 1, :] * factors[head]
                top_ref[row : row + 1, :] = top
                total_ref[row : row + 1, :] = total
                weights.append(weight.astype(jnp.bfloat16))
            summed = dot(values[columns], jnp.concatenate(weights, axis=1))
            for head in range(per):
                rows = slice((group * per + head) * HD, (group * per + head + 1) * HD)
                piece = summed[head * HD : (head + 1) * HD, head * tok : (head + 1) * tok]
                if not fresh:
                    piece = piece + sum_ref[rows, :] * factors[head]
                sum_ref[rows, :] = piece

    for place, (k, unused_query, pair_ref, first) in enumerate(tasks):
        block = ids_ref[reps + place]
        begin = begin_ref[k : k + 1, :]
        tok = begin.shape[1]
        if first and k == 0:
            fold(place, k, pair_ref, block, begin, True)
            continue
        if first:
            top_ref, total_ref, sum_ref = states[k]
            top_ref[...] = jnp.full(top_ref.shape, masked_score, jnp.float32)
            total_ref[...] = jnp.zeros(total_ref.shape, jnp.float32)
            sum_ref[...] = jnp.zeros(sum_ref.shape, jnp.float32)

        @pl.when((block >= 0) & ((block + 1) * tok > lowest[k]))
        def unused(place=place, k=k, pair_ref=pair_ref, block=block, begin=begin):
            fold(place, k, pair_ref, block, begin, False)


def attend_kernel(plan, reps, counts, packed, ahead, ids_ref, begin_ref, *refs):
    ks = sorted({k for k, unused_pair, unused_first in plan})
    old_ks = [k for k in ks if not any(first for j, unused_pair, first in plan if j == k)]
    query_refs, refs = dict(zip(ks, refs)), refs[len(ks) + ahead :]
    pair_refs = [refs[2 * place : 2 * place + 2] for place in range(counts)]
    refs = refs[2 * counts :]
    old_refs, refs = refs[: 3 * len(old_ks)], refs[3 * len(old_ks) :]
    bias_ref, refs = refs[-1], refs[:-1]
    packed_refs, state_refs = (refs[: len(ks)], refs[len(ks) :]) if packed else ((), refs)
    states = {k: state_refs[3 * place : 3 * place + 3] for place, k in enumerate(ks)}
    for place, k in enumerate(old_ks):
        for old_ref, new_ref in zip(old_refs[3 * place : 3 * place + 3], states[k]):
            new_ref[...] = old_ref[...]
    tasks = [(k, query_refs[k], pair_refs[pair], first) for k, pair, first in plan]
    fold_blocks(ids_ref, begin_ref, tasks, reps, states, bias_ref)
    for k, packed_ref in zip(ks, packed_refs):
        top_ref, total_ref, sum_ref = states[k]
        heads, width = top_ref.shape[0], sum_ref.shape[0]
        packed_ref[0:width, :] = sum_ref[...].astype(jnp.bfloat16)
        first = width
        for ref, pieces in ((top_ref, 3), (total_ref, 2)):
            rest = ref[...]
            for unused in range(pieces):
                piece = rest.astype(jnp.bfloat16)
                packed_ref[first : first + heads, :] = piece
                rest = rest - piece.astype(jnp.float32)
                first += heads


def mix_kernel(expert_count, hot_capacity, own_ref, extended_ref, residual_ref, proj_ref, *refs):
    top_ref, total_ref, sum_ref = refs[0:3]
    mixed_ref, sent_refs = refs[-1 - expert_count], refs[len(refs) - expert_count :]
    packed_refs = refs[3 : -1 - expert_count]
    tok, width = mixed_ref.shape
    heads = top_ref.shape[0]
    scale = math.log2(math.e) / math.sqrt(HD)
    tops, totals = [top_ref[...]], [total_ref[...]]
    for packed_ref in packed_refs:
        pieces = [
            packed_ref[width + place * heads : width + (place + 1) * heads, :].astype(jnp.float32)
            for place in range(5)
        ]
        tops.append((pieces[0] + pieces[1]) + pieces[2])
        totals.append(pieces[3] + pieces[4])
    top = functools.reduce(jnp.maximum, tops)
    factors = [jnp.exp2((one - top) * scale) for one in tops]
    total = sum(one * factor for one, factor in zip(totals, factors))
    factors = [factor / total for factor in factors]
    pieces = []
    for head in range(heads):
        rows = slice(head * HD, (head + 1) * HD)
        piece = sum_ref[rows, :] * factors[0][head : head + 1, :]
        for packed_ref, factor in zip(packed_refs, factors[1:]):
            piece = piece + packed_ref[rows, :].astype(jnp.float32) * factor[head : head + 1, :]
        pieces.append(piece.astype(jnp.bfloat16))
    attended = jnp.concatenate(pieces, axis=0).T
    mixed = (residual_ref[...].astype(jnp.float32) + dot(attended, proj_ref[...])).astype(
        jnp.bfloat16
    )
    mixed_ref[...] = mixed
    mixed_f = mixed.astype(jnp.float32)
    inv_rms = lax.rsqrt(jnp.mean(mixed_f * mixed_f, axis=1, keepdims=True) + norm_eps)
    normed = (mixed_f * inv_rms).astype(jnp.bfloat16)
    placed = slot_matrix(chosen_of(extended_ref, tok), own_ref[0], len(sent_refs), hot_capacity)
    rows = dot(placed, normed).astype(jnp.bfloat16)
    for k, sent_ref in enumerate(sent_refs):
        sent_ref[...] = rows[k * hot_capacity : (k + 1) * hot_capacity]


def expert_kernel(
    reps,
    rep_list,
    sources,
    tok,
    strip,
    counts,
    own_ref,
    part_ref,
    up_ref,
    down_ref,
    extended_ref,
    *refs,
):
    row_count, grad_count = counts
    row_refs, refs = refs[:row_count], refs[row_count:]
    per_rep = row_count // len(rep_list)
    if rep_list == (0,) and per_rep == sources:
        row_refs = row_refs[:1] + row_refs[-1:] + row_refs[1:-1]
    grad_refs, refs = refs[:grad_count], refs[grad_count:]
    own_rows = rep_list[0] == 0
    held_ref, refs = refs[-1], refs[:-1]
    if own_rows:
        up_old, down_old, activated_ref, pre_grad_ref = refs[:4]
        term_refs, kept_ref = refs[4:-1], refs[-1]
    else:
        up_acc, down_acc = refs
    total_grads = sum(ref.shape[0] for ref in grad_refs)
    capacity = total_grads // (sources * reps)
    count = sources * capacity
    parts = part_ref.shape[0]
    up = up_ref[...]
    down = down_ref[...]
    router = router_of(extended_ref, tok, sources)
    expert_lane = lax.broadcasted_iota(jnp.int32, (count, router.shape[0]), 1) == own_ref[0]

    def strips(rows, place):
        held_ref[place] = rows.T
        taken = []
        for k in range(parts):
            first = pl.multiple_of(part_ref[k] * strip, strip)
            taken.append(held_ref[place, pl.ds(first, strip), :])
        return jnp.concatenate(taken, axis=0)

    up_term = down_term = None
    for place, rep in enumerate(rep_list):
        rows = chunk_rows(
            row_refs[place * per_rep : (place + 1) * per_rep], sources, 0, capacity
        )
        grads = chunk_rows(grad_refs, sources, rep * capacity, (rep + 1) * capacity)
        pre = dot(rows, up)
        sigmoid_pre = jax.nn.sigmoid(pre)
        activated = (pre * sigmoid_pre).astype(jnp.bfloat16)
        logits = dot(rows, router, NT)
        gate = jax.nn.sigmoid(
            jnp.sum(jnp.where(expert_lane, logits, 0.0), axis=1, keepdims=True)
        )
        scaled = (gate * grads.astype(jnp.float32)).astype(jnp.bfloat16)
        act_grad = dot(scaled, down, NT)
        pre_grad = (act_grad * sigmoid_pre * (1.0 + pre * (1.0 - sigmoid_pre))).astype(
            jnp.bfloat16
        )
        if own_rows:
            activated_ref[...] = activated
            pre_grad_ref[...] = pre_grad
        more_up = dot(strips(rows, 2 * place), pre_grad)
        more_down = dot(strips(activated, 2 * place + 1), scaled)
        up_term = more_up if up_term is None else up_term + more_up
        down_term = more_down if down_term is None else down_term + more_down
    if not own_rows:
        up_acc[...] = up_term
        down_acc[...] = down_term
        return
    up_term = up_term + up_old[...]
    down_term = down_term + down_old[...]
    for k, ref in enumerate((kept_ref, *term_refs)):
        rows = slice(k * strip, (k + 1) * strip)
        ref[0] = up_term[rows].astype(ref.dtype)
        ref[1] = down_term[rows].astype(ref.dtype)


def back_kernel(sources, up_ref, down_ref, activated_ref, pre_grad_ref, *back_refs):
    capacity = activated_ref.shape[0] // sources
    produced = dot(activated_ref[...], down_ref[...]).astype(jnp.bfloat16)
    token_grad = dot(pre_grad_ref[...], up_ref[...], NT).astype(jnp.bfloat16)
    for k, back_ref in enumerate(back_refs):
        rows = slice(k * capacity, (k + 1) * capacity)
        back_ref[0:capacity] = produced[rows]
        back_ref[capacity : 2 * capacity] = token_grad[rows]


def prepare_kernel(
    hot_capacity,
    expert_count,
    own_ref,
    mixed_ref,
    extended_ref,
    placed_ref,
    factors_ref,
    router_cols_ref,
):
    tok = mixed_ref.shape[0]
    choice = chosen_of(extended_ref, tok)
    placed = slot_matrix(choice, own_ref[0], expert_count, hot_capacity)
    placed_ref[...] = placed.T
    router = router_of(extended_ref, tok, expert_count)
    mixed_f = mixed_ref[...].astype(jnp.float32)
    inv_rms = lax.rsqrt(jnp.mean(mixed_f * mixed_f, axis=1, keepdims=True) + norm_eps)
    normed = (mixed_f * inv_rms).astype(jnp.bfloat16)
    one_hot = lax.broadcasted_iota(jnp.int32, (expert_count, tok), 0) == choice
    logits = dot(router, normed, NT)
    logit_row = jnp.sum(jnp.where(one_hot, logits, 0.0), axis=0, keepdims=True)
    gate = jax.nn.sigmoid(jnp.broadcast_to(logit_row, (8, tok)).T[:, 0:1])
    lane = lax.broadcasted_iota(jnp.int32, factors_ref.shape, 1)
    factors_ref[...] = jnp.where(lane == 0, inv_rms, gate)
    router_cols_ref[...] = dot(one_hot.astype(jnp.float32).astype(jnp.bfloat16), router, TN)


def finish_kernel(
    hot_capacity,
    parts,
    placed_ref,
    factors_ref,
    router_cols_ref,
    mixed_ref,
    extended_ref,
    *refs,
):
    refs, (layer_ref, grad_mixed_ref, *share_refs) = refs[:-4], refs[-4:]
    (kept_ref, *term_refs), back_refs = refs[:parts], refs[parts:][::-1]
    for kind, share_ref in enumerate(share_refs):
        total = kept_ref[kind]
        for ref in term_refs:
            total = total + ref[kind].astype(jnp.float32)
        share_ref[...] = total
    tok = mixed_ref.shape[0]
    mixed_f = mixed_ref[...].astype(jnp.float32)
    inv_rms = factors_ref[:, 0:1]
    gate = factors_ref[:, 1:2]
    pair = 2 * hot_capacity
    chunks = [
        ref[first : first + pair] for ref in back_refs for first in range(0, ref.shape[0], pair)
    ]
    results = jnp.concatenate([chunk[:hot_capacity] for chunk in chunks], axis=0)
    grads = jnp.concatenate([chunk[hot_capacity:] for chunk in chunks], axis=0)
    placed = placed_ref[...]
    result_f = dot(placed, results)
    normed_grad = dot(placed, grads)
    grad_f = extended_ref[0:tok, :].astype(jnp.float32)
    layer_ref[...] = (mixed_f + gate * result_f).astype(jnp.bfloat16)
    gate_grad = jnp.sum(grad_f * result_f, axis=1, keepdims=True)
    logit_grad = gate_grad * gate * (1.0 - gate)
    total_grad = normed_grad + logit_grad * router_cols_ref[...]
    mean_term = jnp.mean(total_grad * mixed_f, axis=1, keepdims=True)
    input_grad = inv_rms * total_grad - mixed_f * inv_rms * inv_rms * inv_rms * mean_term
    grad_mixed_ref[...] = (grad_f + input_grad).astype(jnp.bfloat16)


def shape(dims, dtype=jnp.bfloat16):
    return jax.ShapeDtypeStruct(dims, dtype)


SMEM = pl.BlockSpec(memory_space=pltpu.SMEM)
VMEM = pl.BlockSpec(memory_space=pltpu.VMEM)
HBM = pl.BlockSpec(memory_space=pltpu.HBM)


def call(body, out_shape, specs, scratch=(), cost=0.5):
    return pl.pallas_call(
        body,
        cost_estimate=pl.CostEstimate(
            flops=int(cost * 1e9), bytes_accessed=0, transcendentals=0
        ),
        out_shape=out_shape,
        in_specs=specs,
        out_specs=jax.tree.map(lambda unused: VMEM, out_shape),
        scratch_shapes=list(scratch),
        compiler_params=pltpu.CompilerParams(vmem_limit_bytes=VMEM_LIMIT),
    )


def local(
    seq_count,
    expert_count,
    rep_count,
    query_rows,
    key_rows,
    value_rows,
    doc_lengths,
    residual,
    out_proj,
    router,
    expert_choice,
    weight_in,
    weight_out,
    grad_out,
):
    tok, width = query_rows.shape[1:]
    hidden = weight_in.shape[2]
    heads = width // HD
    experts = Group(("expert",), (expert_count,))
    reps = Group(("rep",), (rep_count,))
    owners = Group(("expert", "rep"), (expert_count, rep_count))
    parts = Group(("seq",), (seq_count,))
    strip = width // (seq_count * rep_count)
    capacity = max(2, (3 * tok + 2 * expert_count - 1) // (2 * expert_count))
    hot_capacity = min(4 * capacity, tok // 2)
    choice = expert_choice.reshape(1, tok)
    seq_index = lax.axis_index("seq")
    rep_index = lax.axis_index("rep")
    rank = seq_index * rep_count + rep_index
    own = jnp.stack([lax.axis_index("expert")]).astype(jnp.int32)
    part_to = jnp.stack(
        [parts.target(seq_index, k) * rep_count + rep_index for k in range(seq_count)]
    ).astype(jnp.int32)

    def forward(array):
        return lax.ppermute(array, "seq", [(i, (i + 1) % seq_count) for i in range(seq_count)])

    reach = (seq_count + 1) // 2
    longest = (seq_count * rep_count + 1) // 2
    query_ranks = [
        seq_index * rep_count + reps.source(rep_index, k) for k in range(rep_count)
    ]

    def task_ids(plan, steps):
        ids = list(query_ranks)
        for k, pair, unused_first in plan:
            block = rank - steps[pair] * rep_count
            behind = query_ranks[k] - block
            ids.append(jnp.where((block >= 0) & (behind >= 0) & (behind <= longest), block, -1))
        return jnp.stack(ids).astype(jnp.int32)

    state_shapes = [
        shape((heads, tok), jnp.float32),
        shape((heads, tok), jnp.float32),
        shape((width, tok), jnp.float32),
    ]
    tail = 16 + -(-expert_count // 16) * 16
    extended, begin = call(
        extend_kernel,
        [shape((tok + tail, width)), shape((rep_count, tok), jnp.int32)],
        [SMEM, SMEM] + [VMEM] * 3,
    )(
        jnp.stack(query_ranks).astype(jnp.int32), doc_lengths, choice, router.T, grad_out[0]
    )

    def attend(plan, pairs, steps, queries, states, packed, cost, ahead=()):
        ks = sorted({k for k, unused_pair, unused_first in plan})
        old = [one for k in ks if k in states for one in states[k]]
        state_out = state_shapes * len(ks)
        if packed:
            out_shape = [shape((width + 5 * heads, tok))] * len(ks)
            scratch = [pltpu.VMEM(one.shape, one.dtype) for one in state_out]
        else:
            out_shape, scratch = state_out, []
        outs = call(
            functools.partial(
                attend_kernel, plan, rep_count, len(pairs), packed, len(ahead)
            ),
            out_shape,
            [SMEM] + [VMEM] * (1 + len(ks) + len(ahead) + 2 * len(pairs) + len(old)),
            scratch + [pltpu.VMEM((len(plan), tok, tok), jnp.float32)],
            cost=cost,
        )(task_ids(plan, steps), begin, *[queries[k] for k in ks], *ahead, *[one for both in pairs for one in both], *old)
        if packed:
            return dict(zip(ks, outs))
        return {k: list(outs[3 * place : 3 * place + 3]) for place, k in enumerate(ks)}

    others = range(1, rep_count)
    lines = [(key_rows[0], value_rows[0])]
    lines.append(tuple(forward(one) for one in lines[0]))
    queries = reps.exchange([query_rows[0]] * rep_count)
    extendeds = reps.exchange([extended] * rep_count)
    states = attend(((0, 0, True),), lines[:1], [0], queries, {}, False, 2.0)
    ahead, *states[0] = lax.optimization_barrier((lines[1][0], *states[0]))
    lines[1] = (ahead, lines[1][1])
    for unused in range(1, reach):
        lines.append(tuple(forward(one) for one in lines[-1]))
    middle = tuple((0, step, False) for step in range(1, reach)) + tuple(
        (k, step, step == 0) for k in others for step in range(reach)
    )
    states = attend(middle, lines[:-1], list(range(reach)), queries, states, False, 4.0)
    states[1][0], *extendeds[1:] = lax.optimization_barrier((states[1][0], *extendeds[1:]))
    sent_grads = call(
        functools.partial(dispatch_kernel, rep_count, tok, hot_capacity),
        [shape((rep_count * hot_capacity, width))] * expert_count,
        [SMEM] + [VMEM] * rep_count,
    )(own, *extendeds)
    partial = attend(
        tuple((k, 0, False) for k in others),
        lines[-1:],
        [reach],
        queries,
        states,
        True,
        1.5,
        ahead=sent_grads[:1],
    )
    returned = reps.exchange([None] + [partial[k] for k in others], inverse=True)[1:]
    states = attend(((0, 0, False),), lines[-1:], [reach], queries, states, False, 1.5)
    got_grads = merged(experts.exchange(sent_grads), MOST_PERMUTES)

    mixed, *sent_rows = call(
        functools.partial(mix_kernel, expert_count, hot_capacity),
        [shape((tok, width))] + [shape((hot_capacity, width))] * expert_count,
        [SMEM] + [VMEM] * (6 + len(returned)),
        cost=2.0,
    )(own, extendeds[0], residual[0], out_proj, *states[0], *returned)
    arrived = owners.exchange([sent_rows[k // rep_count] for k in range(owners.count)])
    got_rows = merged(arrived[0::rep_count], MOST_PERMUTES)
    got_more = [
        one for k in others for one in merged(arrived[k::rep_count], MOST_PERMUTES)
    ]

    def expert_call(rep_list, rows, out_shape, extra):
        return call(
            functools.partial(
                expert_kernel,
                rep_count,
                rep_list,
                expert_count,
                tok,
                strip,
                (len(rows), len(got_grads)),
            ),
            out_shape,
            [SMEM, SMEM] + [VMEM] * (3 + len(rows) + len(got_grads) + len(extra)),
            [pltpu.VMEM((2 * len(rep_list), width, expert_count * hot_capacity), jnp.bfloat16)],
            cost=2.0,
        )(own, part_to, weight_in[0], weight_out[0], extendeds[0], *rows, *got_grads, *extra)

    slots = expert_count * hot_capacity
    sums = expert_call(
        tuple(others),
        got_more,
        [
            shape((seq_count * strip, hidden), jnp.float32),
            shape((seq_count * strip, width), jnp.float32),
        ],
        [],
    )
    activated, pre_grad, *terms, kept = expert_call(
        (0,),
        got_rows[:1] + got_rows[2:] + got_rows[1:2],
        [shape((slots, hidden))] * 2
        + [shape((2, strip, hidden))] * (seq_count - 1)
        + [shape((2, strip, hidden), jnp.float32)],
        list(sums),
    )
    got_terms = parts.exchange([None] + terms)[1:]
    activated, mixed, kept = lax.optimization_barrier((activated, mixed, kept))
    back = call(
        functools.partial(back_kernel, expert_count),
        [shape((2 * hot_capacity, width))] * expert_count,
        [VMEM] * 4,
        cost=1.0,
    )(weight_in[0], weight_out[0], activated, pre_grad)
    got_back = merged(experts.exchange(back, inverse=True), MOST_PERMUTES)
    prepared = call(
        functools.partial(prepare_kernel, hot_capacity, expert_count),
        [
            shape((tok, slots)),
            shape((tok, 128), jnp.float32),
            shape((tok, width), jnp.float32),
        ],
        [SMEM, VMEM, VMEM],
        cost=1.0,
    )(own, mixed, extended)
    layer_out, grad_mixed, share_in, share_out = call(
        functools.partial(finish_kernel, hot_capacity, seq_count),
        [
            shape((tok, width)),
            shape((tok, width)),
            shape((strip, hidden), jnp.float32),
            shape((strip, width), jnp.float32),
        ],
        [VMEM] * (5 + seq_count + len(got_back)),
        cost=1.0,
    )(*prepared, mixed, extended, kept, *got_terms[::-1], *got_back[::-1])
    return (layer_out[None], grad_mixed[None], share_in[None], share_out[None])


def solution(mesh):
    rows = P("expert", ("seq", "rep"), None)
    in_specs = (
        rows,
        rows,
        rows,
        P("expert", None),
        rows,
        P(),
        P(),
        rows,
        P("expert", None, None),
        P("expert", None, None),
        rows,
    )
    body = functools.partial(
        local, mesh.shape["seq"], mesh.shape["expert"], mesh.shape["rep"]
    )
    return jax.shard_map(
        body, mesh=mesh, in_specs=in_specs, out_specs=(rows, rows, rows, rows), check_vma=False
    )
```
